32 devices in a mesh: groups: 2 (over y), band: 4 (over z), inner: 4 (over x, core).
Axes of the slice: x: 2, y: 2, z: 4, core: 2. Of those that a mesh axis runs over, the one named last changes fastest.
Arguments:
- grid_rows: bfloat16 [32768, 512], P(('groups', 'band', 'inner')), parts along dimension 0, may hold values from -6 to 6
- mesh_rows: bfloat16 [8192, 512], P(('groups', 'band', 'inner')), parts along dimension 0, may hold values from -6 to 6
- edge_source: int32 [8, 4, 3, 4, 128], P(('groups', 'band'), 'inner'), parts along dimension 0, may hold values from 0 to 1023
- edge_target: int32 [8, 4, 3, 4, 128], P(('groups', 'band'), 'inner'), parts along dimension 0, may hold values from 0 to 255
- edge_count: int32 [8, 4, 3, 4], P(('groups', 'band'), 'inner'), parts along dimension 0, may hold values from 0 to 128, as said below
- w_message: bfloat16 [512, 512], replicated, may hold values from -0.25 to 0.25
- w_merge: bfloat16 [512, 512], replicated, may hold values from -0.25 to 0.25
- gain_attn: float32 [512], replicated, may hold values from 0.1 to 1.9
- w_qkv: bfloat16 [512, 1536], replicated, may hold values from -5 to 5
- window: int32 [32], P('groups'), parts along dimension 0, may hold values from 32 to 512, as said below
- w_out: bfloat16 [512, 512], replicated, may hold values from -0.25 to 0.25
- gain_mlp: float32 [512], replicated, may hold values from 0.1 to 1.9
- w_up: bfloat16 [512, 2048], replicated, may hold values from -0.25 to 0.25
- w_down: bfloat16 [2048, 512], replicated, may hold values from -0.125 to 0.125
Outputs:
- mesh_out: bfloat16 [8192, 512], P(('groups', 'band', 'inner')), parts along dimension 0
The draws below stay inside these ranges and needn't reach their ends.
There are 2 independent parts, one for each index of `groups`. The reference program is written for one: setup_inputs(seed, part) draws one part's arguments, and reference() takes and returns one part's arrays. A program takes and returns all parts, laid end to end along the dimension named above; an argument that names none is the same for every part. Nothing has to cross between parts.
Inputs may be any that keep to these rules, and one draw needn't show every extreme that they name: `edge_count`: entries whose target band b + o - 1 lies outside the bands are 0; on every device some block with o = 1 is full (128). Each window is 512 divided by a power of two of at most 16; some head has exactly 512.
All inputs are finite; a program needn't handle non-finite values.
Results may differ from the reference program's by a relative error of at most 0.0061.
Values may be sent and summed in bfloat16 or wider, within the bound.
No kernel may reach another device: no remote copies, remote signals or barrier semaphores. Data moves between devices by JAX's collectives and lax.ppermute only.
A program may use at most 128 MiB of HBM per device.

```python
import math
import jax
import jax.numpy as jnp
from jax import lax

D = 512
HEADS = 16
HEAD_DIM = 32
HID = 2048
WMAX = 512
CAP = 128
GRID_DEV = 1024
MESH_DEV = 256
GRID = 16384
MESH = 4096
N_BAND = 4
N_INNER = 4


def draw_edge_count(key, part):
    key = jax.random.fold_in(key, 5)
    key_near, key_far, key_pick = jax.random.split(key, 3)
    near = jax.random.randint(key_near, (N_BAND, N_INNER, 1, N_INNER), CAP // 2, CAP + 1)
    far = jax.random.randint(key_far, (N_BAND, N_INNER, 2, N_INNER), 0, CAP // 2 + 1)
    pick = jax.random.randint(key_pick, (N_BAND, N_INNER, 1, 1), 0, N_INNER)
    column = jnp.arange(N_INNER, dtype=jnp.int32)[None, None, None, :]
    near = jnp.where(column == pick, CAP, near)
    counts = jnp.concatenate([far[:, :, :1], near, far[:, :, 1:]], axis=2)
    band_at = jnp.arange(N_BAND, dtype=jnp.int32)[:, None, None, None]
    offset = jnp.arange(3, dtype=jnp.int32)[None, None, :, None]
    target_band = band_at + offset - 1
    inside = (target_band >= 0) & (target_band < N_BAND)
    return jnp.where(inside, counts, 0).astype(jnp.int32)


def draw_window(key, part):
    key = jax.random.fold_in(key, 7)
    key_exp, key_top = jax.random.split(key)
    powers = jax.random.randint(key_exp, (HEADS,), 0, 5)
    top = jax.random.randint(key_top, (), 0, HEADS)
    powers = jnp.where(jnp.arange(HEADS, dtype=jnp.int32) == top, 0, powers)
    return (WMAX // jnp.left_shift(jnp.ones((HEADS,), jnp.int32), powers)).astype(jnp.int32)


def draw_w_qkv(key, part):
    key = jax.random.fold_in(key, 11)
    key_base = jax.random.fold_in(key, 0)
    values = jnp.clip(jax.random.normal(key_base, (D, HEADS, 3, HEAD_DIM), jnp.float32), -5.0, 5.0) * D ** (-0.5)
    return jnp.clip(values, -5.0, 5.0).reshape(D, 3 * D).astype(jnp.bfloat16)


def set_ends(entries, rng, smallest, top_value):
    dims = entries.shape
    index_at = [jax.random.randint(jax.random.fold_in(rng, axis), (), 0, dims[axis]) for axis in range(len(dims))]
    entries = entries.at[tuple(index_at)].set(smallest)
    longest = dims.index(max(dims))
    index_at[longest] = (index_at[longest] + 1) % dims[longest]
    return entries.at[tuple(index_at)].set(top_value)


def levels(key, extent, cuts, least, largest):
    factor_of, own = 1.0, jax.random.fold_in(key, 6)
    for position, blocks in cuts:
        heights = jnp.exp(jax.random.uniform(jax.random.fold_in(own, position), (blocks,), jnp.float32, least / len(cuts), largest / len(cuts)))
        factor_of = factor_of * jnp.repeat(heights, extent[position] // blocks).reshape([-1 if axis == position else 1 for axis in range(len(extent))])
    return factor_of


def centred(rng, dims, scale, bound, cuts=(), kind=jnp.bfloat16):
    level = levels(rng, dims, cuts, -0.22, 0.18) if cuts else 1.0
    result = jax.random.normal(rng, dims, jnp.float32) * scale * level
    return jnp.minimum(jnp.maximum(result, -bound), bound).astype(kind)


def setup_inputs(seed: int = 0, part: int = 0) -> dict:
    key_of = jax.random.split(jax.random.key(seed), 15)
    own_keys = jax.random.split(jax.random.fold_in(key_of[14], part), 15)
    grid_rows = centred(own_keys[0], (GRID, D), 1.0, 6.0, ((0, 16),))
    mesh_rows = centred(own_keys[1], (MESH, D), 1.0, 6.0, ((0, 16),))
    edge_source = set_ends(jax.random.randint(own_keys[2], (N_BAND, N_INNER, 3, N_INNER, CAP), 0, GRID_DEV), jax.random.fold_in(own_keys[2], 1), 0, GRID_DEV - 1).astype(jnp.int32)
    edge_target = set_ends(jax.random.randint(own_keys[3], (N_BAND, N_INNER, 3, N_INNER, CAP), 0, MESH_DEV), jax.random.fold_in(own_keys[3], 1), 0, MESH_DEV - 1).astype(jnp.int32)
    edge_count = draw_edge_count(jax.random.fold_in(jax.random.fold_in(key_of[14], part), 71), part)
    w_message = centred(key_of[5], (D, D), D ** -0.5, 0.25)
    w_merge = centred(key_of[6], (D, D), D ** -0.5, 0.25)
    gain_attn = jnp.clip(1.0 + 0.18 * jax.random.normal(key_of[7], (D,), jnp.float32), 0.1, 1.9)
    w_qkv = draw_w_qkv(jax.random.fold_in(key_of[14], 71), part)
    window = draw_window(jax.random.fold_in(jax.random.fold_in(key_of[14], part), 71), part)
    w_out = centred(key_of[10], (D, D), D ** -0.5, 0.25)
    gain_mlp = jnp.clip(1.0 + 0.18 * jax.random.normal(key_of[11], (D,), jnp.float32), 0.1, 1.9)
    w_up = centred(key_of[12], (D, HID), D ** -0.5, 0.25)
    w_down = centred(key_of[13], (HID, D), HID ** -0.5, 0.125)
    return dict(grid_rows=grid_rows, mesh_rows=mesh_rows, edge_source=edge_source, edge_target=edge_target, edge_count=edge_count, w_message=w_message, w_merge=w_merge, gain_attn=gain_attn, w_qkv=w_qkv, window=window, w_out=w_out, gain_mlp=gain_mlp, w_up=w_up, w_down=w_down)


norm_eps = 1e-05

def layer_norm(values, gain):
    center = values - lax.optimization_barrier(jnp.mean(values, axis=-1, keepdims=True))
    spread = lax.optimization_barrier(jnp.mean(center * center, axis=-1, keepdims=True))
    return center * lax.rsqrt(spread + norm_eps) * gain.astype(jnp.float32)

def reference(grid_rows, mesh_rows, edge_source, edge_target, edge_count, w_message, w_merge, gain_attn, w_qkv, window, w_out, gain_mlp, w_up, w_down):
    band_count = N_BAND
    inner_count = N_INNER
    total_nodes = MESH_DEV * band_count * inner_count
    message_rows = jax.nn.silu(jnp.dot(grid_rows, w_message, preferred_element_type=jnp.float32)).astype(jnp.bfloat16)
    sources = edge_source.reshape(band_count * inner_count, 3, inner_count, CAP)
    targets = edge_target.reshape(band_count * inner_count, 3, inner_count, CAP)
    counts = edge_count.reshape(band_count * inner_count, 3, inner_count)
    offsets = jnp.arange(3, dtype=jnp.int32)[:, None, None]
    columns = jnp.arange(inner_count, dtype=jnp.int32)[None, :, None]
    slots = jnp.arange(CAP, dtype=jnp.int32)[None, None, :]

    def accumulate(totals, sender):
        band_at = sender // inner_count
        live = slots < counts[sender][:, :, None]
        target_band = band_at + offsets - 1
        live = live & (target_band >= 0) & (target_band < band_count)
        nodes = jnp.where(live, (target_band * inner_count + columns) * MESH_DEV + targets[sender], total_nodes)
        rows = jnp.take(message_rows, (sender * GRID_DEV + sources[sender]).reshape(-1).astype(jnp.int32), axis=0)
        totals = totals.at[nodes.reshape(-1).astype(jnp.int32)].add(rows.astype(jnp.float32))
        return (totals, None)
    start_sum = jnp.zeros((total_nodes + 1, D), jnp.float32)
    summed, unused = lax.scan(accumulate, start_sum, jnp.arange(band_count * inner_count, dtype=jnp.int32))
    aggregated = summed[:total_nodes].astype(jnp.bfloat16)
    mesh_state = mesh_rows.astype(jnp.float32) + jnp.dot(aggregated, w_merge, preferred_element_type=jnp.float32)
    normed = layer_norm(mesh_state, gain_attn).astype(jnp.bfloat16)
    qkv = jnp.dot(normed, w_qkv, preferred_element_type=jnp.float32).astype(jnp.bfloat16)
    qkv = qkv.reshape(total_nodes, HEADS, 3, HEAD_DIM)
    queries = qkv[:, :, 0, :]
    padded_keys = jnp.pad(qkv[:, :, 1, :], ((WMAX, WMAX), (0, 0), (0, 0)))
    padded_vals = jnp.pad(qkv[:, :, 2, :], ((WMAX, WMAX), (0, 0), (0, 0)))
    qblock = math.gcd(512, total_nodes)
    scale = HEAD_DIM ** (-0.5)

    def attend(start):
        block_q = lax.dynamic_slice_in_dim(queries, start, qblock, 0).astype(jnp.float32)
        block_k = lax.dynamic_slice_in_dim(padded_keys, start, qblock + 2 * WMAX, 0).astype(jnp.float32)
        block_v = lax.dynamic_slice_in_dim(padded_vals, start, qblock + 2 * WMAX, 0).astype(jnp.float32)
        scores = jnp.einsum('qhd,khd->hqk', block_q, block_k, precision=lax.Precision.HIGHEST) * scale
        qpos = start + jnp.arange(qblock, dtype=jnp.int32)
        kpos = start - WMAX + jnp.arange(qblock + 2 * WMAX, dtype=jnp.int32)
        gap = jnp.abs(qpos[:, None] - kpos[None, :])
        inside = (kpos >= 0) & (kpos < total_nodes)
        visible = (gap[None, :, :] <= window[:, None, None]) & inside[None, None, :]
        scores = jnp.where(visible, scores, -1e+30)
        maximum = lax.optimization_barrier(jnp.max(scores, axis=-1, keepdims=True))
        expo = jnp.where(visible, jnp.exp(scores - maximum), 0.0)
        probs = (expo / lax.optimization_barrier(jnp.sum(expo, axis=-1, keepdims=True))).astype(jnp.bfloat16)
        return jnp.einsum('hqk,khd->qhd', probs.astype(jnp.float32), block_v, precision=lax.Precision.HIGHEST).astype(jnp.bfloat16)
    starts = jnp.arange(total_nodes // qblock, dtype=jnp.int32) * qblock
    attended = lax.map(attend, starts).reshape(total_nodes, D)
    mid = mesh_state + jnp.dot(attended, w_out, preferred_element_type=jnp.float32)
    normed_mlp = layer_norm(mid, gain_mlp).astype(jnp.bfloat16)
    hidden = jax.nn.silu(jnp.dot(normed_mlp, w_up, preferred_element_type=jnp.float32)).astype(jnp.bfloat16)
    return (mid + jnp.dot(hidden, w_down, preferred_element_type=jnp.float32)).astype(jnp.bfloat16)
```

```python
import functools
import math

import jax
import jax.numpy as jnp
from jax import lax
from jax.experimental import pallas as pl
from jax.experimental.pallas import tpu as pltpu
from jax.sharding import PartitionSpec as P

HEADS = 16
WMAX = 512
LANES = 128
NEAR = 128

norm_eps = 1e-05
NODES = ("band", "inner")
VMEM = pl.BlockSpec(memory_space=pltpu.VMEM)
SMEM = pl.BlockSpec(memory_space=pltpu.SMEM)


def params(mib):
    return pltpu.CompilerParams(vmem_limit_bytes=mib * 1024 * 1024)


def dot(a, b):
    return jnp.dot(a, b, preferred_element_type=jnp.float32)


def dot_t(a, b):
    return lax.dot_general(a, b, (((1,), (1,)), ((), ())), preferred_element_type=jnp.float32)


def layer_norm(values, gain):
    center = values - jnp.mean(values, axis=-1, keepdims=True)
    spread = jnp.mean(center * center, axis=-1, keepdims=True)
    return center * lax.rsqrt(spread + norm_eps) * gain


def message_kernel(inner_count, grid_ref, w_ref, source_ref, *out_refs):
    rows = grid_ref.shape[0]
    blocks, cap = source_ref.shape
    message = jax.nn.silu(dot(grid_ref[...], w_ref[...])).astype(jnp.bfloat16)
    inner = lax.axis_index("inner")
    sources = jnp.concatenate(
        [
            source_ref[pl.ds(o * inner_count + (inner ^ d), 1), :]
            for o in range(3)
            for d in range(inner_count)
        ],
        axis=0,
    )
    by_slot = jnp.transpose(sources.astype(jnp.float32)).astype(jnp.int32)
    row = lax.broadcasted_iota(jnp.int32, (cap, rows), 1)
    step = math.gcd(blocks, 4)
    for first in range(0, blocks, step):
        picks = jnp.concatenate(
            [
                jnp.where(row == by_slot[:, n : n + 1], 1.0, 0.0).astype(jnp.bfloat16)
                for n in range(first, first + step)
            ],
            axis=0,
        )
        taken = dot(picks, message).astype(jnp.bfloat16)
        for n in range(first, first + step):
            out_refs[n][...] = taken[(n - first) * cap : (n - first + 1) * cap]


def merge_kernel(inner_count, band_count, *refs):
    blocks = 3 * inner_count
    row_refs = refs[:blocks]
    target_ref, mesh_ref, w_ref, gain_ref, state_ref, normed_ref = refs[blocks:]
    nodes = mesh_ref.shape[0]
    cap = row_refs[0].shape[0]
    band = lax.axis_index("band")
    inner = lax.axis_index("inner")
    node = lax.broadcasted_iota(jnp.int32, (nodes, cap), 0)
    hits = []
    for o in range(3):
        sender_band = band + 1 - o
        present = (sender_band >= 0) & (sender_band < band_count)
        for d in range(inner_count):
            sender = sender_band * inner_count + (inner ^ d)
            place = jnp.where(present, (sender * 3 + o) * inner_count + inner, 0)
            target = jnp.where(present, target_ref[pl.ds(place, 1), :], -1)
            hits.append(jnp.where(node == target, 1.0, 0.0).astype(jnp.bfloat16))
    aggregated = dot(
        jnp.concatenate(hits, axis=1), jnp.concatenate([r[...] for r in row_refs], axis=0)
    ).astype(jnp.bfloat16)
    state = mesh_ref[...].astype(jnp.float32) + dot(aggregated, w_ref[...])
    state_ref[...] = state
    normed_ref[...] = layer_norm(state, gain_ref[...]).astype(jnp.bfloat16)


def project_keys(rows, wk_ref, wv_ref, key_ref, value_ref, start):
    count = rows.shape[0]
    groups = key_ref.shape[0]
    heads = value_ref.shape[0]
    keys = dot(rows, wk_ref[...]).astype(jnp.bfloat16)
    for g in range(groups):
        key_ref[g, start : start + count, :] = keys[:, g * LANES : (g + 1) * LANES]
    values = dot_t(wv_ref[...], rows).astype(jnp.bfloat16)
    value_ref[:, 0 : values.shape[0] // heads, start : start + count] = values.reshape(
        heads, -1, count
    )


def near_kernel(
    own_ref, side_ref, wq_ref, wk_ref, wv_ref, order_ref, window_ref,
    query_ref, sums_ref, top_ref,
    key_ref, value_ref, gap_ref,
):
    nodes, width = own_ref.shape
    head_dim = width // HEADS
    per_group = LANES // head_dim
    odd = lax.rem(lax.axis_index("inner"), 2)
    side = 1 - 2 * odd
    first = odd * (nodes - NEAR)
    second = (1 - odd) * NEAR
    scale = head_dim ** (-0.5) / math.log(2.0)

    queries = dot_t(wq_ref[...], own_ref[...]).astype(jnp.bfloat16)
    part = lax.broadcasted_iota(jnp.int32, (LANES, nodes), 0) // head_dim
    for h in range(HEADS):
        g = h // per_group
        lanes = queries[g * LANES : (g + 1) * LANES]
        query_ref[h] = jnp.where(part == h % per_group, lanes, jnp.zeros_like(lanes))
    value_ref[:, head_dim:, :] = jnp.ones_like(value_ref[:, head_dim:, :])
    project_keys(own_ref[...], wk_ref, wv_ref, key_ref, value_ref, 0)
    project_keys(side_ref[pl.ds(pl.multiple_of(first, NEAR), NEAR), :], wk_ref, wv_ref, key_ref, value_ref, nodes)
    project_keys(
        side_ref[pl.ds(pl.multiple_of(second, NEAR), NEAR), :], wk_ref, wv_ref, key_ref, value_ref, nodes + NEAR
    )
    lag = lax.broadcasted_iota(jnp.int32, (nodes, nodes), 0) - lax.broadcasted_iota(
        jnp.int32, (nodes, nodes), 1
    )
    gap_ref[0:nodes] = jnp.abs(lag)
    gap_ref[nodes : nodes + NEAR] = jnp.abs(lag[0:NEAR] + (side * nodes + first))
    gap_ref[nodes + NEAR : 2 * nodes] = jnp.abs(lag[0:NEAR] + (side * nodes + second))

    def attend(h, rows):
        scores = dot(key_ref[h // per_group, 0:rows, :], query_ref[h])
        scores = jnp.where(gap_ref[0:rows] <= window_ref[h], scores, -1e30)
        top = jnp.max(scores, axis=0, keepdims=True)
        expo = jnp.exp2((scores - top) * scale).astype(jnp.bfloat16)
        sums_ref[h] = dot(value_ref[h, :, 0:rows], expo)
        top_ref[h] = jnp.broadcast_to(top, top_ref.shape[1:])

    def pair(i, carry):
        a, b = order_ref[2 * i], order_ref[2 * i + 1]
        widest = jnp.maximum(window_ref[a], window_ref[b])

        @pl.when(widest <= NEAR)
        def _():
            attend(a, nodes + NEAR)
            attend(b, nodes + NEAR)

        @pl.when(widest > NEAR)
        def _():
            attend(a, 2 * nodes)
            attend(b, 2 * nodes)

        return carry

    lax.fori_loop(0, HEADS // 2, pair, 0)


def far_kernel(
    beyond_ref, before_ref, after_ref, wk_ref, wv_ref, order_ref, window_ref,
    query_ref, sums_ref, top_ref, state_ref, w_out_ref, gain_ref, up_ref, down_ref,
    out_ref,
    key_ref, value_ref, gap_ref, attended_ref, up_vmem, down_vmem, sems,
):
    nodes, width = beyond_ref.shape
    head_dim = width // HEADS
    per_group = LANES // head_dim
    total = lax.axis_size("band") * lax.axis_size("inner")
    me = lax.axis_index("band") * lax.axis_size("inner") + lax.axis_index("inner")
    odd = lax.rem(lax.axis_index("inner"), 2)
    side = 2 * odd - 1
    first = (1 - odd) * (nodes - NEAR)
    second = odd * NEAR
    scale = head_dim ** (-0.5) / math.log(2.0)
    absent = 1 << 20

    fetch_up = pltpu.make_async_copy(up_ref, up_vmem, sems.at[0])
    fetch_down = pltpu.make_async_copy(down_ref, down_vmem, sems.at[1])
    fetch_up.start()
    fetch_down.start()

    value_ref[:, head_dim:, :] = jnp.ones_like(value_ref[:, head_dim:, :])
    project_keys(beyond_ref[pl.ds(pl.multiple_of(first, NEAR), NEAR), :], wk_ref, wv_ref, key_ref, value_ref, 0)
    project_keys(
        beyond_ref[pl.ds(pl.multiple_of(second, NEAR), NEAR), :], wk_ref, wv_ref, key_ref, value_ref, NEAR
    )
    project_keys(before_ref[...], wk_ref, wv_ref, key_ref, value_ref, nodes)
    project_keys(after_ref[...], wk_ref, wv_ref, key_ref, value_ref, 2 * nodes)
    lag = lax.broadcasted_iota(jnp.int32, (nodes, nodes), 0) - lax.broadcasted_iota(
        jnp.int32, (nodes, nodes), 1
    )

    def gap(rows, device, offset):
        inside = (me + device >= 0) & (me + device < total)
        return jnp.where(inside, jnp.abs(rows + (device * nodes + offset)), absent)

    gap_ref[0:NEAR] = gap(lag[0:NEAR], side, first)
    gap_ref[NEAR:nodes] = gap(lag[0:NEAR], side, second)
    gap_ref[nodes : 2 * nodes] = gap(lag, -2, 0)
    gap_ref[2 * nodes : 3 * nodes] = gap(lag, 2, 0)

    def attend(h, rows):
        scores = dot(key_ref[h // per_group, 0:rows, :], query_ref[h])
        scores = jnp.where(gap_ref[0:rows] <= window_ref[h], scores, -1e30)
        before = top_ref[h, 0:1, :]
        top = jnp.maximum(before, jnp.max(scores, axis=0, keepdims=True))
        expo = jnp.exp2((scores - top) * scale).astype(jnp.bfloat16)
        sums = sums_ref[h] * jnp.exp2((before - top) * scale) + dot(value_ref[h, :, 0:rows], expo)
        attended_ref[h] = (sums[0:head_dim] / sums[head_dim : head_dim + 1]).astype(jnp.bfloat16)

    def pair(i, carry):
        a, b = order_ref[2 * i], order_ref[2 * i + 1]
        widest = jnp.maximum(window_ref[a], window_ref[b])

        @pl.when(widest <= NEAR)
        def _():
            attend(a, NEAR)
            attend(b, NEAR)

        @pl.when((widest > NEAR) & (widest <= nodes))
        def _():
            attend(a, nodes)
            attend(b, nodes)

        @pl.when(widest > nodes)
        def _():
            attend(a, 3 * nodes)
            attend(b, 3 * nodes)

        return carry

    lax.fori_loop(0, HEADS // 2, pair, 0)

    attended = attended_ref[...].reshape(width, nodes)
    mixed = lax.dot_general(
        attended, w_out_ref[...], (((0,), (0,)), ((), ())), preferred_element_type=jnp.float32
    )
    mid = state_ref[...] + mixed
    normed = layer_norm(mid, gain_ref[...]).astype(jnp.bfloat16)
    fetch_up.wait()
    hidden = jax.nn.silu(dot(normed, up_vmem[...])).astype(jnp.bfloat16)
    fetch_down.wait()
    out_ref[...] = (mid + dot(hidden, down_vmem[...])).astype(jnp.bfloat16)


def cost(flops, size):
    return pl.CostEstimate(flops=flops, bytes_accessed=size, transcendentals=0)


def local(
    grid_rows,
    mesh_rows,
    edge_source,
    edge_target,
    edge_count,
    w_message,
    w_merge,
    gain_attn,
    w_qkv,
    window,
    w_out,
    gain_mlp,
    w_up,
    w_down,
):
    bands = lax.axis_size("band")
    inners = lax.axis_size("inner")
    devices = bands * inners
    grid_dev = grid_rows.shape[0]
    nodes, width = mesh_rows.shape
    cap = edge_source.shape[-1]
    head_dim = width // HEADS
    blocks = 3 * inners
    f32, bf16, i32 = jnp.float32, jnp.bfloat16, jnp.int32

    live = lax.broadcasted_iota(i32, (blocks, cap), 1) < edge_count.reshape(blocks)[:, None]
    targets = jnp.where(live, edge_target.reshape(blocks, cap), -1)
    targets = lax.all_gather(targets, NODES, axis=0, tiled=True)

    outgoing = pl.pallas_call(
        functools.partial(message_kernel, inners),
        out_shape=[jax.ShapeDtypeStruct((cap, width), bf16)] * blocks,
        in_specs=[VMEM] * 3,
        out_specs=[VMEM] * blocks,
        compiler_params=params(24),
        cost_estimate=cost(2 * grid_dev * width * (width + blocks * cap), 4 << 20),
        name="messages",
    )(grid_rows, w_message, edge_source.reshape(blocks, cap))

    arrived = []
    for o in range(3):
        for d in range(inners):
            route = [
                (b * inners + i, (b + o - 1) * inners + (i ^ d))
                for b in range(bands)
                for i in range(inners)
                if 0 <= b + o - 1 < bands
            ]
            block = outgoing[o * inners + d]
            arrived.append(block if o == 1 and d == 0 else lax.ppermute(block, NODES, route))

    w_parts = w_qkv.reshape(width, HEADS, 3, head_dim)
    w_query = w_parts[:, :, 0].reshape(width, width).T
    w_key = w_parts[:, :, 1].reshape(width, width)
    w_value = w_parts[:, :, 2].reshape(width, width).T
    ahead = (window[None, :] > window[:, None]) | (
        (window[None, :] == window[:, None]) & (jnp.arange(HEADS)[None, :] < jnp.arange(HEADS)[:, None])
    )
    rank = jnp.sum(ahead.astype(i32), axis=1)
    order = jnp.sum(
        jnp.where(rank[None, :] == jnp.arange(HEADS)[:, None], jnp.arange(HEADS)[None, :], 0), axis=1
    ).astype(i32)

    state, normed = pl.pallas_call(
        functools.partial(merge_kernel, inners, bands),
        out_shape=[
            jax.ShapeDtypeStruct((nodes, width), f32),
            jax.ShapeDtypeStruct((nodes, width), bf16),
        ],
        in_specs=[VMEM] * (blocks + 4),
        out_specs=[VMEM] * 2,
        compiler_params=params(24),
        cost_estimate=cost(2 * nodes * width * (width + blocks * cap), 4 << 20),
        name="merge",
    )(*arrived, targets, mesh_rows, w_merge, gain_attn.reshape(1, width))

    side = lax.ppermute(normed, NODES, [(g, g ^ 1) for g in range(devices)])
    beyond = lax.ppermute(
        normed,
        NODES,
        [(g, g + 1) for g in range(1, devices - 1, 2)] + [(g, g - 1) for g in range(2, devices, 2)],
    )
    before = lax.ppermute(normed, NODES, [(g, g + 2) for g in range(devices - 2)])
    after = lax.ppermute(normed, NODES, [(g + 2, g) for g in range(devices - 2)])

    extra = head_dim + 16
    query, sums, top = pl.pallas_call(
        near_kernel,
        out_shape=[
            jax.ShapeDtypeStruct((HEADS, LANES, nodes), bf16),
            jax.ShapeDtypeStruct((HEADS, extra, nodes), f32),
            jax.ShapeDtypeStruct((HEADS, 8, nodes), f32),
        ],
        in_specs=[VMEM] * 5 + [SMEM] * 2,
        out_specs=[VMEM] * 3,
        scratch_shapes=[
            pltpu.VMEM((width // LANES, 2 * nodes, LANES), bf16),
            pltpu.VMEM((HEADS, extra, 2 * nodes), bf16),
            pltpu.VMEM((2 * nodes, nodes), i32),
        ],
        compiler_params=params(32),
        cost_estimate=cost(8 << 30, 4 << 20),
        name="near",
    )(normed, side, w_query, w_key, w_value, order, window)

    return pl.pallas_call(
        far_kernel,
        out_shape=jax.ShapeDtypeStruct((nodes, width), bf16),
        in_specs=[VMEM] * 5 + [SMEM] * 2 + [VMEM] * 6 + [pl.BlockSpec(memory_space=pl.ANY)] * 2,
        out_specs=VMEM,
        scratch_shapes=[
            pltpu.VMEM((width // LANES, 3 * nodes, LANES), bf16),
            pltpu.VMEM((HEADS, extra, 3 * nodes), bf16),
            pltpu.VMEM((3 * nodes, nodes), i32),
            pltpu.VMEM((HEADS, head_dim, nodes), bf16),
            pltpu.VMEM(w_up.shape, bf16),
            pltpu.VMEM(w_down.shape, bf16),
            pltpu.SemaphoreType.DMA((2,)),
        ],
        compiler_params=params(40),
        cost_estimate=cost(8 << 30, 8 << 20),
        name="far",
    )(
        beyond, before, after, w_key, w_value, order, window,
        query, sums, top, state, w_out, gain_mlp.reshape(1, width), w_up, w_down,
    )


def solution(mesh):
    placed = (
        P(("groups", "band", "inner"), None),
        P(("groups", "band", "inner"), None),
        P(("groups", "band"), "inner", None, None, None),
        P(("groups", "band"), "inner", None, None, None),
        P(("groups", "band"), "inner", None, None),
        P(),
        P(),
        P(),
        P(),
        P("groups"),
        P(),
        P(),
        P(),
        P(),
    )
    return jax.shard_map(
        local,
        mesh=mesh,
        in_specs=placed,
        out_specs=P(("groups", "band", "inner"), None),
        check_vma=False,
    )
```

```python
import functools
import math

import jax
import jax.numpy as jnp
from jax import lax
from jax.experimental import pallas as pl
from jax.experimental.pallas import tpu as pltpu
from jax.sharding import PartitionSpec as P

HEADS = 16
WMAX = 512
LANES = 128
NEAR = 128
TILE = 16
GRID_PARTS = 4

norm_eps = 1e-05
NODES = ("band", "inner")
VMEM = pl.BlockSpec(memory_space=pltpu.VMEM)
SMEM = pl.BlockSpec(memory_space=pltpu.SMEM)
ANY = pl.BlockSpec(memory_space=pl.ANY)


def params(mib):
    return pltpu.CompilerParams(vmem_limit_bytes=mib * 1024 * 1024)


def dot(a, b):
    return jnp.dot(a, b, preferred_element_type=jnp.float32)


def dot_t(a, b):
    return lax.dot_general(a, b, (((1,), (1,)), ((), ())), preferred_element_type=jnp.float32)


def layer_norm(values, gain):
    center = values - jnp.mean(values, axis=-1, keepdims=True)
    spread = jnp.mean(center * center, axis=-1, keepdims=True)
    return center * lax.rsqrt(spread + norm_eps) * gain


def message_kernel(
    inner_count, grid_ref, w_ref, source_ref, target_ref, count_ref, *refs
):
    out_refs = refs[: 3 * inner_count]
    grid_vmem, w_vmem, message_ref, sems = refs[3 * inner_count :]
    rows = grid_ref.shape[0]
    cap = source_ref.shape[-1]
    part = rows // GRID_PARTS
    fetches = [pltpu.make_async_copy(w_ref, w_vmem, sems.at[GRID_PARTS])]
    for k in range(GRID_PARTS):
        span = pl.ds(k * part, part)
        fetches.append(pltpu.make_async_copy(grid_ref.at[span], grid_vmem.at[span], sems.at[k]))
    for fetch in fetches:
        fetch.start()
    inner = lax.axis_index("inner")
    blocks = [(o, inner ^ d) for o in range(3) for d in range(inner_count)]
    sources = jnp.concatenate([source_ref[0, 0, o, pl.ds(j, 1), :] for o, j in blocks], axis=0)
    by_slot = jnp.transpose(sources.astype(jnp.float32)).astype(jnp.int32)
    slot = lax.broadcasted_iota(jnp.int32, (1, cap), 1)
    for n, (o, j) in enumerate(blocks):
        target = jnp.where(slot < count_ref[0, 0, o, j], target_ref[0, 0, o, pl.ds(j, 1), :], -1)
        tile = jnp.broadcast_to(target.astype(jnp.float32), (TILE, cap)).astype(jnp.bfloat16)
        out_refs[n][cap:, :] = jnp.concatenate([tile] * (w_ref.shape[1] // cap), axis=1)
    fetches[0].wait()
    for k in range(GRID_PARTS):
        span = pl.ds(k * part, part)
        fetches[k + 1].wait()
        message_ref[span] = jax.nn.silu(dot(grid_vmem[span], w_vmem[...])).astype(jnp.bfloat16)
    message = message_ref[...]
    row = lax.broadcasted_iota(jnp.int32, (cap, rows), 1)
    step = inner_count
    for first in range(0, len(blocks), step):
        picks = jnp.concatenate(
            [
                jnp.where(row == by_slot[:, n : n + 1], 1.0, 0.0).astype(jnp.bfloat16)
                for n in range(first, first + step)
            ],
            axis=0,
        )
        taken = dot(picks, message).astype(jnp.bfloat16)
        for n in range(first, first + step):
            out_refs[n][0:cap, :] = taken[(n - first) * cap : (n - first + 1) * cap]


def weights_kernel(w_ref, window_ref, after_ref, query_ref, key_ref, value_ref, order_ref):
    width = w_ref.shape[0]
    head_dim = width // HEADS
    for c in range(3):
        out_ref = (query_ref, key_ref, value_ref)[c]
        for g in range(width // LANES):
            heads = range(g * LANES // head_dim, (g + 1) * LANES // head_dim)
            columns = jnp.concatenate(
                [w_ref[:, (3 * h + c) * head_dim : (3 * h + c + 1) * head_dim] for h in heads], axis=1
            )
            out_ref[g * LANES : (g + 1) * LANES, :] = jnp.transpose(
                columns.astype(jnp.float32)
            ).astype(jnp.bfloat16)

    def place(h, carry):
        def ahead(k, count):
            wider = (window_ref[k] > window_ref[h]) | ((window_ref[k] == window_ref[h]) & (k < h))
            return count + wider.astype(jnp.int32)

        order_ref[lax.fori_loop(0, HEADS, ahead, 0)] = h
        return carry

    lax.fori_loop(0, HEADS, place, 0)


def merge_kernel(inner_count, band_count, *refs):
    blocks = 3 * inner_count
    row_refs = refs[:blocks]
    mesh_ref, w_ref, gain_ref, _, state_ref, normed_ref = refs[blocks:]
    nodes = mesh_ref.shape[0]
    cap = row_refs[0].shape[0] - TILE
    band = lax.axis_index("band")
    node = lax.broadcasted_iota(jnp.int32, (nodes, cap), 0)
    hits = []
    for o in range(3):
        present = (band + 1 - o >= 0) & (band + 1 - o < band_count)
        for d in range(inner_count):
            target = row_refs[o * inner_count + d][cap:, 0:cap].astype(jnp.float32)[0:1].astype(jnp.int32)
            target = jnp.where(present, target, -1)
            hits.append(jnp.where(node == target, 1.0, 0.0).astype(jnp.bfloat16))
    aggregated = dot(
        jnp.concatenate(hits, axis=1), jnp.concatenate([r[0:cap, :] for r in row_refs], axis=0)
    ).astype(jnp.bfloat16)
    state = mesh_ref[...].astype(jnp.float32) + dot(aggregated, w_ref[...])
    state_ref[...] = state
    normed_ref[...] = layer_norm(state, gain_ref[...]).astype(jnp.bfloat16)


def project_keys(rows, wk_ref, wv_ref, key_ref, value_ref, start):
    count = rows.shape[0]
    groups = key_ref.shape[0]
    heads = value_ref.shape[0]
    keys = dot_t(rows, wk_ref[...]).astype(jnp.bfloat16)
    for g in range(groups):
        key_ref[g, start : start + count, :] = keys[:, g * LANES : (g + 1) * LANES]
    values = dot_t(wv_ref[...], rows).astype(jnp.bfloat16)
    value_ref[:, 0 : values.shape[0] // heads, start : start + count] = values.reshape(
        heads, -1, count
    )


def near_kernel(
    own_ref, side_ref, wq_ref, wk_ref, wv_ref, order_ref, window_ref,
    query_ref, sums_ref, top_ref,
    key_ref, value_ref, gap_ref,
):
    nodes, width = own_ref.shape
    head_dim = width // HEADS
    per_group = LANES // head_dim
    odd = lax.rem(lax.axis_index("inner"), 2)
    side = 1 - 2 * odd
    first = odd * (nodes - NEAR)
    second = (1 - odd) * NEAR
    scale = head_dim ** (-0.5) / math.log(2.0)

    queries = dot_t(wq_ref[...], own_ref[...]).astype(jnp.bfloat16)
    part = lax.broadcasted_iota(jnp.int32, (LANES, nodes), 0) // head_dim
    for h in range(HEADS):
        g = h // per_group
        lanes = queries[g * LANES : (g + 1) * LANES]
        query_ref[h] = jnp.where(part == h % per_group, lanes, jnp.zeros_like(lanes))
    value_ref[:, head_dim:, :] = jnp.ones_like(value_ref[:, head_dim:, :])
    project_keys(own_ref[...], wk_ref, wv_ref, key_ref, value_ref, 0)
    project_keys(side_ref[pl.ds(pl.multiple_of(first, NEAR), NEAR), :], wk_ref, wv_ref, key_ref, value_ref, nodes)
    project_keys(
        side_ref[pl.ds(pl.multiple_of(second, NEAR), NEAR), :], wk_ref, wv_ref, key_ref, value_ref, nodes + NEAR
    )
    lag = lax.broadcasted_iota(jnp.int32, (nodes, nodes), 0) - lax.broadcasted_iota(
        jnp.int32, (nodes, nodes), 1
    )
    gap_ref[0:nodes] = jnp.abs(lag)
    gap_ref[nodes : nodes + NEAR] = jnp.abs(lag[0:NEAR] + (side * nodes + first))
    gap_ref[nodes + NEAR : 2 * nodes] = jnp.abs(lag[0:NEAR] + (side * nodes + second))

    def attend(h, rows):
        scores = dot(key_ref[h // per_group, 0:rows, :], query_ref[h])
        scores = jnp.where(gap_ref[0:rows] <= window_ref[h], scores, -1e30)
        top = jnp.max(scores, axis=0, keepdims=True)
        expo = jnp.exp2((scores - top) * scale).astype(jnp.bfloat16)
        sums_ref[h] = dot(value_ref[h, :, 0:rows], expo)
        top_ref[h] = jnp.broadcast_to(top, top_ref.shape[1:])

    def pair(i, carry):
        a, b = order_ref[2 * i], order_ref[2 * i + 1]
        widest = jnp.maximum(window_ref[a], window_ref[b])

        @pl.when(widest <= NEAR)
        def _():
            attend(a, nodes + NEAR)
            attend(b, nodes + NEAR)

        @pl.when(widest > NEAR)
        def _():
            attend(a, 2 * nodes)
            attend(b, 2 * nodes)

        return carry

    lax.fori_loop(0, HEADS // 2, pair, 0)


def far_kernel(
    beyond_ref, before_ref, after_ref, wk_ref, wv_ref, order_ref, window_ref,
    query_ref, sums_ref, top_ref, state_ref, w_out_ref, gain_ref, up_ref, down_ref,
    out_ref,
    key_ref, value_ref, gap_ref, attended_ref, up_vmem, down_vmem, sems,
):
    nodes, width = beyond_ref.shape
    head_dim = width // HEADS
    per_group = LANES // head_dim
    total = lax.axis_size("band") * lax.axis_size("inner")
    me = lax.axis_index("band") * lax.axis_size("inner") + lax.axis_index("inner")
    odd = lax.rem(lax.axis_index("inner"), 2)
    side = 2 * odd - 1
    first = (1 - odd) * (nodes - NEAR)
    second = odd * NEAR
    scale = head_dim ** (-0.5) / math.log(2.0)
    absent = 1 << 20

    fetch_up = pltpu.make_async_copy(up_ref, up_vmem, sems.at[0])
    fetch_down = pltpu.make_async_copy(down_ref, down_vmem, sems.at[1])
    fetch_up.start()
    fetch_down.start()

    value_ref[:, head_dim:, :] = jnp.ones_like(value_ref[:, head_dim:, :])
    project_keys(beyond_ref[pl.ds(pl.multiple_of(first, NEAR), NEAR), :], wk_ref, wv_ref, key_ref, value_ref, 0)
    project_keys(
        beyond_ref[pl.ds(pl.multiple_of(second, NEAR), NEAR), :], wk_ref, wv_ref, key_ref, value_ref, NEAR
    )
    project_keys(before_ref[...], wk_ref, wv_ref, key_ref, value_ref, nodes)
    project_keys(after_ref[...], wk_ref, wv_ref, key_ref, value_ref, 2 * nodes)
    lag = lax.broadcasted_iota(jnp.int32, (nodes, nodes), 0) - lax.broadcasted_iota(
        jnp.int32, (nodes, nodes), 1
    )

    def gap(rows, device, offset):
        inside = (me + device >= 0) & (me + device < total)
        return jnp.where(inside, jnp.abs(rows + (device * nodes + offset)), absent)

    gap_ref[0:NEAR] = gap(lag[0:NEAR], side, first)
    gap_ref[NEAR:nodes] = gap(lag[0:NEAR], side, second)
    gap_ref[nodes : 2 * nodes] = gap(lag, -2, 0)
    gap_ref[2 * nodes : 3 * nodes] = gap(lag, 2, 0)

    def attend(h, rows):
        scores = dot(key_ref[h // per_group, 0:rows, :], query_ref[h])
        scores = jnp.where(gap_ref[0:rows] <= window_ref[h], scores, -1e30)
        before = top_ref[h, 0:1, :]
        top = jnp.maximum(before, jnp.max(scores, axis=0, keepdims=True))
        expo = jnp.exp2((scores - top) * scale).astype(jnp.bfloat16)
        sums = sums_ref[h] * jnp.exp2((before - top) * scale) + dot(value_ref[h, :, 0:rows], expo)
        attended_ref[h] = (sums[0:head_dim] / sums[head_dim : head_dim + 1]).astype(jnp.bfloat16)

    def pair(i, carry):
        a, b = order_ref[2 * i], order_ref[2 * i + 1]
        widest = jnp.maximum(window_ref[a], window_ref[b])

        @pl.when(widest <= NEAR)
        def _():
            attend(a, NEAR)
            attend(b, NEAR)

        @pl.when((widest > NEAR) & (widest <= nodes))
        def _():
            attend(a, nodes)
            attend(b, nodes)

        @pl.when(widest > nodes)
        def _():
            attend(a, 3 * nodes)
            attend(b, 3 * nodes)

        return carry

    lax.fori_loop(0, HEADS // 2, pair, 0)

    attended = attended_ref[...].reshape(width, nodes)
    mixed = lax.dot_general(
        attended, w_out_ref[...], (((0,), (0,)), ((), ())), preferred_element_type=jnp.float32
    )
    mid = state_ref[...] + mixed
    normed = layer_norm(mid, gain_ref[...]).astype(jnp.bfloat16)
    fetch_up.wait()
    hidden = jax.nn.silu(dot(normed, up_vmem[...])).astype(jnp.bfloat16)
    fetch_down.wait()
    out_ref[...] = (mid + dot(hidden, down_vmem[...])).astype(jnp.bfloat16)


def cost(flops, size):
    return pl.CostEstimate(flops=flops, bytes_accessed=size, transcendentals=0)


def local(
    grid_rows,
    mesh_rows,
    edge_source,
    edge_target,
    edge_count,
    w_message,
    w_merge,
    gain_attn,
    w_qkv,
    window,
    w_out,
    gain_mlp,
    w_up,
    w_down,
):
    bands = lax.axis_size("band")
    inners = lax.axis_size("inner")
    devices = bands * inners
    grid_dev = grid_rows.shape[0]
    nodes, width = mesh_rows.shape
    cap = edge_source.shape[-1]
    head_dim = width // HEADS
    blocks = 3 * inners
    f32, bf16, i32 = jnp.float32, jnp.bfloat16, jnp.int32

    outgoing = pl.pallas_call(
        functools.partial(message_kernel, inners),
        out_shape=[jax.ShapeDtypeStruct((cap + TILE, width), bf16)] * blocks,
        in_specs=[ANY] * 2 + [VMEM] * 2 + [SMEM],
        out_specs=[VMEM] * blocks,
        scratch_shapes=[
            pltpu.VMEM(grid_rows.shape, bf16),
            pltpu.VMEM(w_message.shape, bf16),
            pltpu.VMEM((grid_dev, width), bf16),
            pltpu.SemaphoreType.DMA((GRID_PARTS + 1,)),
        ],
        compiler_params=params(24),
        cost_estimate=cost(2 * grid_dev * width * (width + blocks * cap), 4 << 20),
        name="messages",
    )(grid_rows, w_message, edge_source, edge_target, edge_count)

    arrived = []
    for o in range(3):
        for d in range(inners):
            route = [
                (b * inners + i, (b + o - 1) * inners + (i ^ d))
                for b in range(bands)
                for i in range(inners)
                if 0 <= b + o - 1 < bands
            ]
            block = outgoing[o * inners + d]
            arrived.append(block if o == 1 and d == 0 else lax.ppermute(block, NODES, route))

    w_query, w_key, w_value, order = pl.pallas_call(
        weights_kernel,
        out_shape=[jax.ShapeDtypeStruct((width, width), bf16)] * 3
        + [jax.ShapeDtypeStruct((HEADS,), i32)],
        in_specs=[VMEM, SMEM, ANY],
        out_specs=[VMEM] * 3 + [SMEM],
        compiler_params=params(16),
        cost_estimate=cost(1 << 24, 3 << 20),
        name="weights",
    )(w_qkv, window, outgoing[inners])

    state, normed = pl.pallas_call(
        functools.partial(merge_kernel, inners, bands),
        out_shape=[
            jax.ShapeDtypeStruct((nodes, width), f32),
            jax.ShapeDtypeStruct((nodes, width), bf16),
        ],
        in_specs=[VMEM] * (blocks + 3) + [ANY],
        out_specs=[VMEM] * 2,
        compiler_params=params(24),
        cost_estimate=cost(2 * nodes * width * (width + blocks * cap), 4 << 20),
        name="merge",
    )(*arrived, mesh_rows, w_merge, gain_attn.reshape(1, width), w_query)

    side = lax.ppermute(normed, NODES, [(g, g ^ 1) for g in range(devices)])
    beyond = lax.ppermute(
        normed,
        NODES,
        [(g, g + 1) for g in range(1, devices - 1, 2)] + [(g, g - 1) for g in range(2, devices, 2)],
    )
    before = lax.ppermute(normed, NODES, [(g, g + 2) for g in range(devices - 2)])
    after = lax.ppermute(normed, NODES, [(g + 2, g) for g in range(devices - 2)])

    extra = head_dim + 16
    query, sums, top = pl.pallas_call(
        near_kernel,
        out_shape=[
            jax.ShapeDtypeStruct((HEADS, LANES, nodes), bf16),
            jax.ShapeDtypeStruct((HEADS, extra, nodes), f32),
            jax.ShapeDtypeStruct((HEADS, 8, nodes), f32),
        ],
        in_specs=[VMEM] * 5 + [SMEM] * 2,
        out_specs=[VMEM] * 3,
        scratch_shapes=[
            pltpu.VMEM((width // LANES, 2 * nodes, LANES), bf16),
            pltpu.VMEM((HEADS, extra, 2 * nodes), bf16),
            pltpu.VMEM((2 * nodes, nodes), i32),
        ],
        compiler_params=params(32),
        cost_estimate=cost(8 << 30, 4 << 20),
        name="near",
    )(normed, side, w_query, w_key, w_value, order, window)

    return pl.pallas_call(
        far_kernel,
        out_shape=jax.ShapeDtypeStruct((nodes, width), bf16),
        in_specs=[VMEM] * 5 + [SMEM] * 2 + [VMEM] * 6 + [ANY] * 2,
        out_specs=VMEM,
        scratch_shapes=[
            pltpu.VMEM((width // LANES, 3 * nodes, LANES), bf16),
            pltpu.VMEM((HEADS, extra, 3 * nodes), bf16),
            pltpu.VMEM((3 * nodes, nodes), i32),
            pltpu.VMEM((HEADS, head_dim, nodes), bf16),
            pltpu.VMEM(w_up.shape, bf16),
            pltpu.VMEM(w_down.shape, bf16),
            pltpu.SemaphoreType.DMA((2,)),
        ],
        compiler_params=params(40),
        cost_estimate=cost(8 << 30, 8 << 20),
        name="far",
    )(
        beyond, before, after, w_key, w_value, order, window,
        query, sums, top, state, w_out, gain_mlp.reshape(1, width), w_up, w_down,
    )


def solution(mesh):
    placed = (
        P(("groups", "band", "inner"), None),
        P(("groups", "band", "inner"), None),
        P(("groups", "band"), "inner", None, None, None),
        P(("groups", "band"), "inner", None, None, None),
        P(("groups", "band"), "inner", None, None),
        P(),
        P(),
        P(),
        P(),
        P("groups"),
        P(),
        P(),
        P(),
        P(),
    )
    return jax.shard_map(
        local,
        mesh=mesh,
        in_specs=placed,
        out_specs=P(("groups", "band", "inner"), None),
        check_vma=False,
    )
```

```python
import functools
import math

import jax
import jax.numpy as jnp
from jax import lax
from jax.experimental import pallas as pl
from jax.experimental.pallas import tpu as pltpu
from jax.sharding import PartitionSpec as P

HEADS = 16
WMAX = 512
LANES = 128
NEAR = 128
TILE = 16
GRID_PARTS = 4
MOST = 56

norm_eps = 1e-05
NODES = ("band", "inner")
VMEM = pl.BlockSpec(memory_space=pltpu.VMEM)
SMEM = pl.BlockSpec(memory_space=pltpu.SMEM)
ANY = pl.BlockSpec(memory_space=pl.ANY)


def params(mib):
    return pltpu.CompilerParams(vmem_limit_bytes=mib * 1024 * 1024)


def dot(a, b):
    return jnp.dot(a, b, preferred_element_type=jnp.float32)


def dot_t(a, b):
    return lax.dot_general(a, b, (((1,), (1,)), ((), ())), preferred_element_type=jnp.float32)


def layer_norm(values, gain):
    center = values - jnp.mean(values, axis=-1, keepdims=True)
    spread = jnp.mean(center * center, axis=-1, keepdims=True)
    return center * lax.rsqrt(spread + norm_eps) * gain


def message_kernel(pair_count, grid_ref, w_ref, source_ref, target_ref, count_ref, *refs):
    out_refs, (grid_vmem, w_vmem, message_ref, sems) = refs[:6], refs[6:]
    rows = grid_ref.shape[0]
    cap = source_ref.shape[-1]
    part = rows // GRID_PARTS
    fetches = [pltpu.make_async_copy(w_ref, w_vmem, sems.at[GRID_PARTS])]
    for k in range(GRID_PARTS):
        span = pl.ds(k * part, part)
        fetches.append(pltpu.make_async_copy(grid_ref.at[span], grid_vmem.at[span], sems.at[k]))
    for fetch in fetches:
        fetch.start()
    inner = lax.axis_index("inner")
    blocks = [(o, inner ^ (2 * p + k)) for o in range(3) for k in range(2) for p in range(pair_count)]
    sources = jnp.concatenate([source_ref[0, 0, o, pl.ds(j, 1), :] for o, j in blocks], axis=0)
    by_slot = jnp.transpose(sources.astype(jnp.float32)).astype(jnp.int32)
    slot = lax.broadcasted_iota(jnp.int32, (1, cap), 1)
    for n, (o, j) in enumerate(blocks):
        target = jnp.where(slot < count_ref[0, 0, o, j], target_ref[0, 0, o, pl.ds(j, 1), :], -1)
        tile = jnp.broadcast_to(target.astype(jnp.float32), (TILE, cap)).astype(jnp.bfloat16)
        p = n % pair_count
        out_refs[n // pair_count][pair_count * cap :, p * cap : (p + 1) * cap] = tile
    fetches[0].wait()
    for k in range(GRID_PARTS):
        span = pl.ds(k * part, part)
        fetches[k + 1].wait()
        message_ref[span] = jax.nn.silu(dot(grid_vmem[span], w_vmem[...])).astype(jnp.bfloat16)
    message = message_ref[...]
    row = lax.broadcasted_iota(jnp.int32, (cap, rows), 1)
    for n in range(6):
        picks = jnp.concatenate(
            [
                jnp.where(row == by_slot[:, m : m + 1], 1.0, 0.0).astype(jnp.bfloat16)
                for m in range(n * pair_count, (n + 1) * pair_count)
            ],
            axis=0,
        )
        out_refs[n][0 : pair_count * cap, :] = dot(picks, message).astype(jnp.bfloat16)
        rest = out_refs[n].shape[1] - pair_count * cap
        if rest:
            out_refs[n][pair_count * cap :, pair_count * cap :] = jnp.zeros((TILE, rest), jnp.bfloat16)


def weights_kernel(w_ref, window_ref, query_ref, key_ref, value_ref, order_ref):
    width = w_ref.shape[0]
    head_dim = width // HEADS
    span = 3 * LANES
    row = lax.broadcasted_iota(jnp.int32, (LANES, span), 0)
    column = lax.broadcasted_iota(jnp.int32, (LANES, span), 1)
    wanted = row // head_dim * (3 * head_dim) + row % head_dim
    for c, out_ref in enumerate((query_ref, key_ref, value_ref)):
        pick = jnp.where(column == wanted + c * head_dim, 1.0, 0.0).astype(jnp.bfloat16)
        for g in range(width // LANES):
            part = dot_t(pick, w_ref[:, g * span : (g + 1) * span])
            out_ref[g * LANES : (g + 1) * LANES, :] = part.astype(jnp.bfloat16)

    def place(h, carry):
        def ahead(k, count):
            wider = (window_ref[k] > window_ref[h]) | ((window_ref[k] == window_ref[h]) & (k < h))
            return count + wider.astype(jnp.int32)

        order_ref[lax.fori_loop(0, HEADS, ahead, 0)] = h
        return carry

    lax.fori_loop(0, HEADS, place, 0)


def reduce_kernel(pair_count, band_count, *refs):
    row_refs, (_, own_ref), part_refs = refs[:6], refs[6:8], refs[8:]
    nodes = own_ref.shape[0]
    cap = (row_refs[0].shape[0] - TILE) // pair_count
    band = lax.axis_index("band")
    node = lax.broadcasted_iota(jnp.int32, (nodes, cap), 0)
    targets = [r[pair_count * cap :, :].astype(jnp.float32)[0:1].astype(jnp.int32) for r in row_refs]
    for n in range(2):
        targets[n] = jnp.where(band > 0, targets[n], -1)
        targets[n + 2] = jnp.where(band < band_count - 1, targets[n + 2], -1)
    for p in reversed(range(pair_count)):
        span = slice(p * cap, (p + 1) * cap)
        hits = [jnp.where(node == t[:, span], 1.0, 0.0).astype(jnp.bfloat16) for t in targets]
        total = dot(jnp.concatenate(hits, axis=1), jnp.concatenate([r[span, :] for r in row_refs], axis=0))
        if p:
            part_refs[p - 1][...] = total.astype(jnp.bfloat16)
        else:
            own_ref[...] = total


def merge_kernel(own_ref, *refs):
    part_refs, (mesh_ref, w_ref, gain_ref, state_ref, normed_ref) = refs[:-5], refs[-5:]
    total = own_ref[...]
    for part_ref in part_refs:
        total = total + part_ref[...].astype(jnp.float32)
    state = mesh_ref[...].astype(jnp.float32) + dot(total.astype(jnp.bfloat16), w_ref[...])
    state_ref[...] = state
    normed_ref[...] = layer_norm(state, gain_ref[...]).astype(jnp.bfloat16)


def project_keys(rows, wk_ref, wv_ref, key_ref, value_ref, start):
    count = rows.shape[0]
    groups = key_ref.shape[0]
    heads = value_ref.shape[0]
    keys = dot_t(rows, wk_ref[...]).astype(jnp.bfloat16)
    for g in range(groups):
        key_ref[g, start : start + count, :] = keys[:, g * LANES : (g + 1) * LANES]
    values = dot_t(wv_ref[...], rows).astype(jnp.bfloat16)
    value_ref[:, 0 : values.shape[0] // heads, start : start + count] = values.reshape(
        heads, -1, count
    )


def near_kernel(
    own_ref, side_ref, wq_ref, wk_ref, wv_ref, order_ref, window_ref,
    query_ref, sums_ref, top_ref,
    key_ref, value_ref, gap_ref,
):
    nodes, width = own_ref.shape
    head_dim = width // HEADS
    per_group = LANES // head_dim
    odd = lax.rem(lax.axis_index("inner"), 2)
    side = 1 - 2 * odd
    first = odd * (nodes - NEAR)
    second = (1 - odd) * NEAR
    scale = head_dim ** (-0.5) / math.log(2.0)

    queries = dot_t(wq_ref[...], own_ref[...]).astype(jnp.bfloat16)
    part = lax.broadcasted_iota(jnp.int32, (LANES, nodes), 0) // head_dim
    for h in range(HEADS):
        g = h // per_group
        lanes = queries[g * LANES : (g + 1) * LANES]
        query_ref[h] = jnp.where(part == h % per_group, lanes, jnp.zeros_like(lanes))
    value_ref[:, head_dim:, :] = jnp.ones_like(value_ref[:, head_dim:, :])
    project_keys(own_ref[...], wk_ref, wv_ref, key_ref, value_ref, 0)
    project_keys(side_ref[pl.ds(pl.multiple_of(first, NEAR), NEAR), :], wk_ref, wv_ref, key_ref, value_ref, nodes)
    project_keys(
        side_ref[pl.ds(pl.multiple_of(second, NEAR), NEAR), :], wk_ref, wv_ref, key_ref, value_ref, nodes + NEAR
    )
    lag = lax.broadcasted_iota(jnp.int32, (nodes, nodes), 0) - lax.broadcasted_iota(
        jnp.int32, (nodes, nodes), 1
    )
    gap_ref[0:nodes] = jnp.abs(lag)
    gap_ref[nodes : nodes + NEAR] = jnp.abs(lag[0:NEAR] + (side * nodes + first))
    gap_ref[nodes + NEAR : 2 * nodes] = jnp.abs(lag[0:NEAR] + (side * nodes + second))

    def attend(h, rows):
        scores = dot(key_ref[h // per_group, 0:rows, :], query_ref[h])
        scores = jnp.where(gap_ref[0:rows] <= window_ref[h], scores, -1e30)
        top = jnp.max(scores, axis=0, keepdims=True)
        expo = jnp.exp2((scores - top) * scale).astype(jnp.bfloat16)
        sums_ref[h] = dot(value_ref[h, :, 0:rows], expo)
        top_ref[h] = jnp.broadcast_to(top, top_ref.shape[1:])

    def pair(i, carry):
        a, b = order_ref[2 * i], order_ref[2 * i + 1]
        widest = jnp.maximum(window_ref[a], window_ref[b])

        @pl.when(widest <= NEAR)
        def _():
            attend(a, nodes + NEAR)
            attend(b, nodes + NEAR)

        @pl.when(widest > NEAR)
        def _():
            attend(a, 2 * nodes)
            attend(b, 2 * nodes)

        return carry

    lax.fori_loop(0, HEADS // 2, pair, 0)


def far_kernel(
    first_ref, second_ref, even_ref, odd_ref, wk_ref, wv_ref, order_ref, window_ref,
    query_ref, sums_ref, top_ref, state_ref, w_out_ref, gain_ref, up_ref, down_ref,
    out_ref,
    key_ref, value_ref, gap_ref, attended_ref,
):
    nodes, width = even_ref.shape
    head_dim = width // HEADS
    per_group = LANES // head_dim
    total = lax.axis_size("band") * lax.axis_size("inner")
    me = lax.axis_index("band") * lax.axis_size("inner") + lax.axis_index("inner")
    odd = lax.rem(me, 2)
    far = 2 - 4 * lax.rem(me // 2, 2)
    side = 2 * odd - 1
    first = (1 - odd) * (nodes - NEAR)
    second = odd * NEAR
    scale = head_dim ** (-0.5) / math.log(2.0)
    absent = 1 << 20

    value_ref[:, head_dim:, :] = jnp.ones_like(value_ref[:, head_dim:, :])
    by_even = odd == lax.rem(me // 2 + 1, 2)
    beyond = jnp.where(by_even, first_ref[...], second_ref[...])
    beyond = jnp.where(odd == 0, jnp.concatenate([beyond[NEAR:], beyond[:NEAR]], axis=0), beyond)
    project_keys(beyond, wk_ref, wv_ref, key_ref, value_ref, 0)
    project_keys(even_ref[...], wk_ref, wv_ref, key_ref, value_ref, nodes)
    project_keys(odd_ref[...], wk_ref, wv_ref, key_ref, value_ref, 2 * nodes)
    lag = lax.broadcasted_iota(jnp.int32, (nodes, nodes), 0) - lax.broadcasted_iota(
        jnp.int32, (nodes, nodes), 1
    )

    def gap(rows, device, offset):
        inside = (me + device >= 0) & (me + device < total)
        return jnp.where(inside, jnp.abs(rows + (device * nodes + offset)), absent)

    gap_ref[0:NEAR] = gap(lag[0:NEAR], side, first)
    gap_ref[NEAR:nodes] = gap(lag[0:NEAR], side, second)
    gap_ref[nodes : 2 * nodes] = gap(lag, far, 0)
    gap_ref[2 * nodes : 3 * nodes] = gap(lag, -far, 0)

    def attend(h, rows):
        scores = dot(key_ref[h // per_group, 0:rows, :], query_ref[h])
        scores = jnp.where(gap_ref[0:rows] <= window_ref[h], scores, -1e30)
        before = top_ref[h, 0:1, :]
        top = jnp.maximum(before, jnp.max(scores, axis=0, keepdims=True))
        expo = jnp.exp2((scores - top) * scale).astype(jnp.bfloat16)
        sums = sums_ref[h] * jnp.exp2((before - top) * scale) + dot(value_ref[h, :, 0:rows], expo)
        attended_ref[h] = (sums[0:head_dim] / sums[head_dim : head_dim + 1]).astype(jnp.bfloat16)

    def pair(i, carry):
        a, b = order_ref[2 * i], order_ref[2 * i + 1]
        widest = jnp.maximum(window_ref[a], window_ref[b])

        @pl.when(widest <= NEAR)
        def _():
            attend(a, NEAR)
            attend(b, NEAR)

        @pl.when((widest > NEAR) & (widest <= nodes))
        def _():
            attend(a, nodes)
            attend(b, nodes)

        @pl.when(widest > nodes)
        def _():
            attend(a, 3 * nodes)
            attend(b, 3 * nodes)

        return carry

    lax.fori_loop(0, HEADS // 2, pair, 0)

    attended = attended_ref[...].reshape(width, nodes)
    mixed = lax.dot_general(
        attended, w_out_ref[...], (((0,), (0,)), ((), ())), preferred_element_type=jnp.float32
    )
    mid = state_ref[...] + mixed
    normed = layer_norm(mid, gain_ref[...]).astype(jnp.bfloat16)
    hidden = jax.nn.silu(dot(normed, up_ref[...])).astype(jnp.bfloat16)
    out_ref[...] = (mid + dot(hidden, down_ref[...])).astype(jnp.bfloat16)


def cost(flops, size):
    return pl.CostEstimate(flops=flops, bytes_accessed=size, transcendentals=0)


def local(
    grid_rows,
    mesh_rows,
    edge_source,
    edge_target,
    edge_count,
    w_message,
    w_merge,
    gain_attn,
    w_qkv,
    window,
    w_out,
    gain_mlp,
    w_up,
    w_down,
):
    bands = lax.axis_size("band")
    inners = lax.axis_size("inner")
    devices = bands * inners
    grid_dev = grid_rows.shape[0]
    nodes, width = mesh_rows.shape
    cap = edge_source.shape[-1]
    head_dim = width // HEADS
    pairs = inners // 2
    slots = pairs * cap
    f32, bf16, i32 = jnp.float32, jnp.bfloat16, jnp.int32

    down, down_other, own, own_other, up, up_other = pl.pallas_call(
        functools.partial(message_kernel, pairs),
        out_shape=[jax.ShapeDtypeStruct((slots + TILE, width), bf16)] * 6,
        in_specs=[ANY] * 2 + [VMEM] * 2 + [SMEM],
        out_specs=[VMEM] * 6,
        scratch_shapes=[
            pltpu.VMEM(grid_rows.shape, bf16),
            pltpu.VMEM(w_message.shape, bf16),
            pltpu.VMEM((grid_dev, width), bf16),
            pltpu.SemaphoreType.DMA((GRID_PARTS + 1,)),
        ],
        compiler_params=params(MOST),
        cost_estimate=cost(2 * grid_dev * width * (width + 6 * slots), 4 << 20),
        name="messages",
    )(grid_rows, w_message, edge_source, edge_target, edge_count)

    beside = [(g, g ^ 1) for g in range(devices)]
    to_next = [(g, g + inners) for g in range(devices - inners)]
    to_last = [(g + inners, g) for g in range(devices - inners)]
    up_other = lax.ppermute(up_other, NODES, beside)
    up = lax.ppermute(up, NODES, to_next)
    down_other = lax.ppermute(down_other, NODES, beside)
    down = lax.ppermute(down, NODES, to_last)
    up_other = lax.ppermute(up_other, NODES, to_next)
    down_other = lax.ppermute(down_other, NODES, to_last)
    own_other = lax.ppermute(own_other, NODES, beside)

    w_qkv, own = lax.optimization_barrier((w_qkv, own))
    w_query, w_key, w_value, order = pl.pallas_call(
        weights_kernel,
        out_shape=[jax.ShapeDtypeStruct((width, width), bf16)] * 3
        + [jax.ShapeDtypeStruct((HEADS,), i32)],
        in_specs=[VMEM, SMEM],
        out_specs=[VMEM] * 3 + [SMEM],
        compiler_params=params(16),
        cost_estimate=cost(1 << 24, 3 << 20),
        name="weights",
    )(w_qkv, window)

    sums = pl.pallas_call(
        functools.partial(reduce_kernel, pairs, bands),
        out_shape=[jax.ShapeDtypeStruct((nodes, width), f32)]
        + [jax.ShapeDtypeStruct((nodes, width), bf16)] * (pairs - 1),
        in_specs=[VMEM] * 6 + [ANY],
        out_specs=[VMEM] * pairs,
        compiler_params=params(24),
        cost_estimate=cost(2 * nodes * width * 6 * slots, 3 << 20),
        name="reduce",
    )(up, up_other, down, down_other, own, own_other, w_query)
    parts = [
        lax.ppermute(sums[p], NODES, [(g, g ^ (2 * p)) for g in range(devices)]) for p in range(1, pairs)
    ]

    state, normed = pl.pallas_call(
        merge_kernel,
        out_shape=[
            jax.ShapeDtypeStruct((nodes, width), f32),
            jax.ShapeDtypeStruct((nodes, width), bf16),
        ],
        in_specs=[VMEM] * (pairs + 3),
        out_specs=[VMEM] * 2,
        compiler_params=params(24),
        cost_estimate=cost(2 * nodes * width * width, 2 << 20),
        name="merge",
    )(sums[0], *parts, mesh_rows, w_merge, gain_attn.reshape(1, width))

    chips = devices // 2
    side = lax.ppermute(normed, NODES, beside)
    even = lax.ppermute(normed, NODES, [(g, g ^ 2) for g in range(devices)])
    odd = lax.ppermute(
        normed,
        NODES,
        [(2 * q + c, 2 * t + c) for q in range(chips) for c in range(2) for t in [q + 2 * (q % 2) - 1] if 0 <= t < chips],
    )
    extra = head_dim + 16
    query, near, top = pl.pallas_call(
        near_kernel,
        out_shape=[
            jax.ShapeDtypeStruct((HEADS, LANES, nodes), bf16),
            jax.ShapeDtypeStruct((HEADS, extra, nodes), f32),
            jax.ShapeDtypeStruct((HEADS, 8, nodes), f32),
        ],
        in_specs=[VMEM] * 5 + [SMEM] * 2,
        out_specs=[VMEM] * 3,
        scratch_shapes=[
            pltpu.VMEM((width // LANES, 2 * nodes, LANES), bf16),
            pltpu.VMEM((HEADS, extra, 2 * nodes), bf16),
            pltpu.VMEM((2 * nodes, nodes), i32),
        ],
        compiler_params=params(32),
        cost_estimate=cost(8 << 30, 4 << 20),
        name="near",
    )(normed, side, w_query, w_key, w_value, order, window)

    even, odd, near, top = lax.optimization_barrier((even, odd, near, top))
    first = lax.ppermute(even, NODES, [(2 * q + q % 2, 2 * q + 1 - q % 2) for q in range(chips)])
    second = lax.ppermute(odd, NODES, [(2 * q + 1 - q % 2, 2 * q + q % 2) for q in range(chips)])

    return pl.pallas_call(
        far_kernel,
        out_shape=jax.ShapeDtypeStruct((nodes, width), bf16),
        in_specs=[VMEM] * 6 + [SMEM] * 2 + [VMEM] * 8,
        out_specs=VMEM,
        scratch_shapes=[
            pltpu.VMEM((width // LANES, 3 * nodes, LANES), bf16),
            pltpu.VMEM((HEADS, extra, 3 * nodes), bf16),
            pltpu.VMEM((3 * nodes, nodes), i32),
            pltpu.VMEM((HEADS, head_dim, nodes), bf16),
        ],
        compiler_params=params(40),
        cost_estimate=cost(8 << 30, 8 << 20),
        name="far",
    )(
        first, second, even, odd, w_key, w_value, order, window,
        query, near, top, state, w_out, gain_mlp.reshape(1, width), w_up, w_down,
    )


def solution(mesh):
    placed = (
        P(("groups", "band", "inner"), None),
        P(("groups", "band", "inner"), None),
        P(("groups", "band"), "inner", None, None, None),
        P(("groups", "band"), "inner", None, None, None),
        P(("groups", "band"), "inner", None, None),
        P(),
        P(),
        P(),
        P(),
        P("groups"),
        P(),
        P(),
        P(),
        P(),
    )
    return jax.shard_map(
        local,
        mesh=mesh,
        in_specs=placed,
        out_specs=P(("groups", "band", "inner"), None),
        check_vma=False,
    )
```

```python
import functools
import math

import jax
import jax.numpy as jnp
from jax import lax
from jax.experimental import pallas as pl
from jax.experimental.pallas import tpu as pltpu
from jax.sharding import PartitionSpec as P

HEADS = 16
WMAX = 512
LANES = 128
NEAR = 128
TILE = 16
GRID_PARTS = 4
MOST = 56

norm_eps = 1e-05
NODES = ("band", "inner")
VMEM = pl.BlockSpec(memory_space=pltpu.VMEM)
SMEM = pl.BlockSpec(memory_space=pltpu.SMEM)
ANY = pl.BlockSpec(memory_space=pl.ANY)


def params(mib):
    return pltpu.CompilerParams(vmem_limit_bytes=mib * 1024 * 1024)


def dot(a, b):
    return jnp.dot(a, b, preferred_element_type=jnp.float32)


def dot_t(a, b):
    return lax.dot_general(a, b, (((1,), (1,)), ((), ())), preferred_element_type=jnp.float32)


def layer_norm(values, gain):
    center = values - jnp.mean(values, axis=-1, keepdims=True)
    spread = jnp.mean(center * center, axis=-1, keepdims=True)
    return center * lax.rsqrt(spread + norm_eps) * gain


def message_kernel(pair_count, grid_ref, w_ref, source_ref, target_ref, count_ref, *refs):
    out_refs, (grid_vmem, w_vmem, message_ref, out_vmem, in_sems, out_sems) = refs[:6], refs[6:]
    rows = grid_ref.shape[0]
    cap = source_ref.shape[-1]
    slots = pair_count * cap
    part = rows // GRID_PARTS
    fetches = [pltpu.make_async_copy(w_ref, w_vmem, in_sems.at[GRID_PARTS])]
    for k in range(GRID_PARTS):
        span = pl.ds(k * part, part)
        fetches.append(pltpu.make_async_copy(grid_ref.at[span], grid_vmem.at[span], in_sems.at[k]))
    for fetch in fetches:
        fetch.start()
    inner = lax.axis_index("inner")
    ahead = lax.rem(lax.axis_index("band"), 2) * 2
    blocks = [(o, inner ^ (2 * p + k)) for o in (2 - ahead, ahead, 1) for k in range(2) for p in range(pair_count)]
    sources = jnp.concatenate([source_ref[0, 0, o, pl.ds(j, 1), :] for o, j in blocks], axis=0)
    by_slot = jnp.transpose(sources.astype(jnp.float32)).astype(jnp.int32)
    slot = lax.broadcasted_iota(jnp.int32, (1, cap), 1)
    for m, (o, j) in enumerate(blocks):
        target = jnp.where(slot < count_ref[0, o, 0, j], target_ref[0, 0, o, pl.ds(j, 1), :], -1)
        tile = jnp.broadcast_to(target.astype(jnp.float32), (TILE, cap)).astype(jnp.bfloat16)
        p = m % pair_count
        out_vmem[m // pair_count, slots:, p * cap : (p + 1) * cap] = tile
    if out_vmem.shape[2] > slots:
        rest = jnp.zeros((6, TILE, out_vmem.shape[2] - slots), jnp.bfloat16)
        out_vmem[:, slots:, slots:] = rest
    fetches[0].wait()
    for k in range(GRID_PARTS):
        span = pl.ds(k * part, part)
        fetches[k + 1].wait()
        message_ref[span] = jax.nn.silu(dot(grid_vmem[span], w_vmem[...])).astype(jnp.bfloat16)
    message = message_ref[...]
    row = lax.broadcasted_iota(jnp.int32, (cap, rows), 1)
    sends = []
    for n in range(6):
        picks = jnp.concatenate(
            [
                jnp.where(row == by_slot[:, m : m + 1], 1.0, 0.0).astype(jnp.bfloat16)
                for m in range(n * pair_count, (n + 1) * pair_count)
            ],
            axis=0,
        )
        out_vmem[n, 0:slots, :] = dot(picks, message).astype(jnp.bfloat16)
        send = pltpu.make_async_copy(out_vmem.at[n], out_refs[n], out_sems.at[n])
        send.start()
        sends.append(send)
    for send in sends:
        send.wait()


def node_sums(row_refs, pair_count, nodes):
    cap = (row_refs[0].shape[0] - TILE) // pair_count
    node = lax.broadcasted_iota(jnp.int32, (nodes, cap), 0)
    targets = [r[pair_count * cap :, :].astype(jnp.float32)[0:1].astype(jnp.int32) for r in row_refs]
    for p in range(pair_count):
        span = slice(p * cap, (p + 1) * cap)
        hits = [jnp.where(node == t[:, span], 1.0, 0.0).astype(jnp.bfloat16) for t in targets]
        yield p, dot(jnp.concatenate(hits, axis=1), jnp.concatenate([r[span, :] for r in row_refs], axis=0))


def early_kernel(pair_count, w_ref, own_ref, other_ref, query_ref, key_ref, value_ref, sum_ref):
    width = w_ref.shape[0]
    head_dim = width // HEADS
    span = 3 * LANES
    row = lax.broadcasted_iota(jnp.int32, (LANES, span), 0)
    column = lax.broadcasted_iota(jnp.int32, (LANES, span), 1)
    wanted = row // head_dim * (3 * head_dim) + row % head_dim
    for c, out_ref in enumerate((query_ref, key_ref, value_ref)):
        pick = jnp.where(column == wanted + c * head_dim, 1.0, 0.0).astype(jnp.bfloat16)
        for g in range(width // LANES):
            part = dot_t(pick, w_ref[:, g * span : (g + 1) * span])
            out_ref[g * LANES : (g + 1) * LANES, :] = part.astype(jnp.bfloat16)
    for p, total in node_sums((own_ref, other_ref), pair_count, sum_ref.shape[1]):
        sum_ref[p] = total


def reduce_kernel(pair_count, *refs):
    row_refs, sum_ref, (own_ref, *part_refs) = refs[:4], refs[4], refs[5:]
    for p, total in node_sums(row_refs, pair_count, own_ref.shape[0]):
        total = total + sum_ref[p]
        if p:
            part_refs[p - 1][...] = total.astype(jnp.bfloat16)
        else:
            own_ref[...] = total


def merge_kernel(own_ref, *refs):
    part_refs, (mesh_ref, w_ref, gain_ref, state_ref, normed_ref) = refs[:-5], refs[-5:]
    total = own_ref[...]
    for part_ref in part_refs:
        total = total + part_ref[...].astype(jnp.float32)
    state = mesh_ref[...].astype(jnp.float32) + dot(total.astype(jnp.bfloat16), w_ref[...])
    state_ref[...] = state
    normed_ref[...] = layer_norm(state, gain_ref[...]).astype(jnp.bfloat16)


def project_keys(rows, wk_ref, wv_ref, key_ref, value_ref, start):
    count = rows.shape[0]
    groups = key_ref.shape[0]
    heads = value_ref.shape[0]
    keys = dot_t(rows, wk_ref[...]).astype(jnp.bfloat16)
    for g in range(groups):
        key_ref[g, start : start + count, :] = keys[:, g * LANES : (g + 1) * LANES]
    values = dot_t(wv_ref[...], rows).astype(jnp.bfloat16)
    value_ref[:, 0 : values.shape[0] // heads, start : start + count] = values.reshape(
        heads, -1, count
    )


def near_kernel(
    own_ref, side_ref, wq_ref, wk_ref, wv_ref, order_ref, window_ref,
    query_ref, sums_ref, top_ref,
    key_ref, value_ref, gap_ref,
):
    nodes, width = own_ref.shape
    head_dim = width // HEADS
    per_group = LANES // head_dim
    odd = lax.rem(lax.axis_index("inner"), 2)
    side = 1 - 2 * odd
    first = odd * (nodes - NEAR)
    second = (1 - odd) * NEAR
    scale = head_dim ** (-0.5) / math.log(2.0)

    queries = dot_t(wq_ref[...], own_ref[...]).astype(jnp.bfloat16)
    part = lax.broadcasted_iota(jnp.int32, (LANES, nodes), 0) // head_dim
    for h in range(HEADS):
        g = h // per_group
        lanes = queries[g * LANES : (g + 1) * LANES]
        query_ref[h] = jnp.where(part == h % per_group, lanes, jnp.zeros_like(lanes))
    value_ref[:, head_dim:, :] = jnp.ones_like(value_ref[:, head_dim:, :])
    project_keys(own_ref[...], wk_ref, wv_ref, key_ref, value_ref, 0)
    project_keys(side_ref[pl.ds(pl.multiple_of(first, NEAR), NEAR), :], wk_ref, wv_ref, key_ref, value_ref, nodes)
    project_keys(
        side_ref[pl.ds(pl.multiple_of(second, NEAR), NEAR), :], wk_ref, wv_ref, key_ref, value_ref, nodes + NEAR
    )
    lag = lax.broadcasted_iota(jnp.int32, (nodes, nodes), 0) - lax.broadcasted_iota(
        jnp.int32, (nodes, nodes), 1
    )
    gap_ref[0:nodes] = jnp.abs(lag)
    gap_ref[nodes : nodes + NEAR] = jnp.abs(lag[0:NEAR] + (side * nodes + first))
    gap_ref[nodes + NEAR : 2 * nodes] = jnp.abs(lag[0:NEAR] + (side * nodes + second))

    def attend(h, rows):
        scores = dot(key_ref[h // per_group, 0:rows, :], query_ref[h])
        scores = jnp.where(gap_ref[0:rows] <= window_ref[h], scores, -1e30)
        top = jnp.max(scores, axis=0, keepdims=True)
        expo = jnp.exp2((scores - top) * scale).astype(jnp.bfloat16)
        sums_ref[h] = dot(value_ref[h, :, 0:rows], expo)
        top_ref[h] = jnp.broadcast_to(top, top_ref.shape[1:])

    def pair(i, carry):
        a, b = order_ref[2 * i], order_ref[2 * i + 1]
        widest = jnp.maximum(window_ref[a], window_ref[b])

        @pl.when(widest <= NEAR)
        def _():
            attend(a, nodes + NEAR)
            attend(b, nodes + NEAR)

        @pl.when(widest > NEAR)
        def _():
            attend(a, 2 * nodes)
            attend(b, 2 * nodes)

        return carry

    lax.fori_loop(0, HEADS // 2, pair, 0)


def far_kernel(
    first_ref, second_ref, even_ref, odd_ref, wk_ref, wv_ref, order_ref, window_ref,
    query_ref, sums_ref, top_ref, state_ref, w_out_ref, gain_ref, up_ref, down_ref,
    out_ref,
    key_ref, value_ref, gap_ref, attended_ref,
):
    nodes, width = even_ref.shape
    head_dim = width // HEADS
    per_group = LANES // head_dim
    total = lax.axis_size("band") * lax.axis_size("inner")
    me = lax.axis_index("band") * lax.axis_size("inner") + lax.axis_index("inner")
    odd = lax.rem(me, 2)
    far = 2 - 4 * lax.rem(me // 2, 2)
    side = 2 * odd - 1
    first = (1 - odd) * (nodes - NEAR)
    second = odd * NEAR
    scale = head_dim ** (-0.5) / math.log(2.0)
    absent = 1 << 20

    value_ref[:, head_dim:, :] = jnp.ones_like(value_ref[:, head_dim:, :])
    by_even = odd == lax.rem(me // 2 + 1, 2)
    beyond = jnp.where(by_even, first_ref[...], second_ref[...])
    beyond = jnp.where(odd == 0, jnp.concatenate([beyond[NEAR:], beyond[:NEAR]], axis=0), beyond)
    project_keys(beyond, wk_ref, wv_ref, key_ref, value_ref, 0)
    project_keys(even_ref[...], wk_ref, wv_ref, key_ref, value_ref, nodes)
    project_keys(odd_ref[...], wk_ref, wv_ref, key_ref, value_ref, 2 * nodes)
    lag = lax.broadcasted_iota(jnp.int32, (nodes, nodes), 0) - lax.broadcasted_iota(
        jnp.int32, (nodes, nodes), 1
    )

    def gap(rows, device, offset):
        inside = (me + device >= 0) & (me + device < total)
        return jnp.where(inside, jnp.abs(rows + (device * nodes + offset)), absent)

    gap_ref[0:NEAR] = gap(lag[0:NEAR], side, first)
    gap_ref[NEAR:nodes] = gap(lag[0:NEAR], side, second)
    gap_ref[nodes : 2 * nodes] = gap(lag, far, 0)
    gap_ref[2 * nodes : 3 * nodes] = gap(lag, -far, 0)

    def attend(h, rows):
        scores = dot(key_ref[h // per_group, 0:rows, :], query_ref[h])
        scores = jnp.where(gap_ref[0:rows] <= window_ref[h], scores, -1e30)
        before = top_ref[h, 0:1, :]
        top = jnp.maximum(before, jnp.max(scores, axis=0, keepdims=True))
        expo = jnp.exp2((scores - top) * scale).astype(jnp.bfloat16)
        sums = sums_ref[h] * jnp.exp2((before - top) * scale) + dot(value_ref[h, :, 0:rows], expo)
        attended_ref[h] = (sums[0:head_dim] / sums[head_dim : head_dim + 1]).astype(jnp.bfloat16)

    def pair(i, carry):
        a, b = order_ref[2 * i], order_ref[2 * i + 1]
        widest = jnp.maximum(window_ref[a], window_ref[b])

        @pl.when(widest <= NEAR)
        def _():
            attend(a, NEAR)
            attend(b, NEAR)

        @pl.when((widest > NEAR) & (widest <= nodes))
        def _():
            attend(a, nodes)
            attend(b, nodes)

        @pl.when(widest > nodes)
        def _():
            attend(a, 3 * nodes)
            attend(b, 3 * nodes)

        return carry

    lax.fori_loop(0, HEADS // 2, pair, 0)

    attended = attended_ref[...].reshape(width, nodes)
    mixed = lax.dot_general(
        attended, w_out_ref[...], (((0,), (0,)), ((), ())), preferred_element_type=jnp.float32
    )
    mid = state_ref[...] + mixed
    normed = layer_norm(mid, gain_ref[...]).astype(jnp.bfloat16)
    hidden = jax.nn.silu(dot(normed, up_ref[...])).astype(jnp.bfloat16)
    out_ref[...] = (mid + dot(hidden, down_ref[...])).astype(jnp.bfloat16)


def cost(flops, size):
    return pl.CostEstimate(flops=flops, bytes_accessed=size, transcendentals=0)


def local(
    grid_rows,
    mesh_rows,
    edge_source,
    edge_target,
    edge_count,
    w_message,
    w_merge,
    gain_attn,
    w_qkv,
    window,
    w_out,
    gain_mlp,
    w_up,
    w_down,
):
    bands = lax.axis_size("band")
    inners = lax.axis_size("inner")
    devices = bands * inners
    grid_dev = grid_rows.shape[0]
    nodes, width = mesh_rows.shape
    cap = edge_source.shape[-1]
    head_dim = width // HEADS
    pairs = inners // 2
    slots = pairs * cap
    f32, bf16, i32 = jnp.float32, jnp.bfloat16, jnp.int32

    even, even_other, odd, odd_other, own, own_other = pl.pallas_call(
        functools.partial(message_kernel, pairs),
        out_shape=[jax.ShapeDtypeStruct((slots + TILE, width), bf16)] * 6,
        in_specs=[ANY] * 2 + [VMEM] * 2 + [SMEM],
        out_specs=[ANY] * 6,
        scratch_shapes=[
            pltpu.VMEM(grid_rows.shape, bf16),
            pltpu.VMEM(w_message.shape, bf16),
            pltpu.VMEM((grid_dev, width), bf16),
            pltpu.VMEM((6, slots + TILE, width), bf16),
            pltpu.SemaphoreType.DMA((GRID_PARTS + 1,)),
            pltpu.SemaphoreType.DMA((6,)),
        ],
        compiler_params=params(MOST),
        cost_estimate=cost(2 * grid_dev * width * (width + 6 * slots), 4 << 20),
        name="messages",
    )(grid_rows, w_message, edge_source, edge_target, jnp.transpose(edge_count, (0, 2, 1, 3)))

    beside = [(g, g ^ 1) for g in range(devices)]

    def bands_trade(odd_pairs):
        route = []
        for g in range(devices):
            b = g // inners
            t = (b - odd_pairs ^ 1) + odd_pairs
            route.append((g, t * inners + g % inners if 0 <= t < bands else g ^ 1))
        return route

    even_other = lax.ppermute(even_other, NODES, beside)
    odd_other = lax.ppermute(odd_other, NODES, beside)
    own_other = lax.ppermute(own_other, NODES, beside)
    even = lax.ppermute(even, NODES, bands_trade(0))
    odd = lax.ppermute(odd, NODES, bands_trade(1))
    even_other = lax.ppermute(even_other, NODES, bands_trade(0))
    odd_other = lax.ppermute(odd_other, NODES, bands_trade(1))

    w_qkv, window, own = lax.optimization_barrier((w_qkv, window, own))
    w_query, w_key, w_value, early = pl.pallas_call(
        functools.partial(early_kernel, pairs),
        out_shape=[jax.ShapeDtypeStruct((width, width), bf16)] * 3
        + [jax.ShapeDtypeStruct((pairs, nodes, width), f32)],
        in_specs=[VMEM] * 3,
        out_specs=[VMEM] * 4,
        compiler_params=params(16),
        cost_estimate=cost(1 << 28, 4 << 20),
        name="early",
    )(w_qkv, own, own_other)
    head = jnp.arange(HEADS, dtype=i32)
    ahead = (window[None, :] > window[:, None]) | (
        (window[None, :] == window[:, None]) & (head[None, :] < head[:, None])
    )
    rank = jnp.sum(ahead.astype(i32), axis=1)
    order = jnp.sum(jnp.where(rank[None, :] == head[:, None], head[None, :], 0), axis=1).astype(i32)

    sums = pl.pallas_call(
        functools.partial(reduce_kernel, pairs),
        out_shape=[jax.ShapeDtypeStruct((nodes, width), f32)]
        + [jax.ShapeDtypeStruct((nodes, width), bf16)] * (pairs - 1),
        in_specs=[VMEM] * 5,
        out_specs=[VMEM] * pairs,
        compiler_params=params(24),
        cost_estimate=cost(2 * nodes * width * 4 * slots, 3 << 20),
        name="reduce",
    )(even, even_other, odd, odd_other, early)
    parts = [
        lax.ppermute(sums[p], NODES, [(g, g ^ (2 * p)) for g in range(devices)]) for p in range(1, pairs)
    ]

    state, normed = pl.pallas_call(
        merge_kernel,
        out_shape=[
            jax.ShapeDtypeStruct((nodes, width), f32),
            jax.ShapeDtypeStruct((nodes, width), bf16),
        ],
        in_specs=[VMEM] * (pairs + 3),
        out_specs=[VMEM] * 2,
        compiler_params=params(24),
        cost_estimate=cost(2 * nodes * width * width, 2 << 20),
        name="merge",
    )(sums[0], *parts, mesh_rows, w_merge, gain_attn.reshape(1, width))

    def chips_trade(odd_pairs):
        route = []
        for g in range(devices):
            t = (g // 2 - odd_pairs ^ 1) + odd_pairs
            route.append((g, 2 * t + g % 2 if 0 <= 2 * t < devices else g ^ 1))
        return route

    side = lax.ppermute(normed, NODES, beside)
    even = lax.ppermute(normed, NODES, chips_trade(0))
    odd = lax.ppermute(normed, NODES, chips_trade(1))

    extra = head_dim + 16
    query, near, top = pl.pallas_call(
        near_kernel,
        out_shape=[
            jax.ShapeDtypeStruct((HEADS, LANES, nodes), bf16),
            jax.ShapeDtypeStruct((HEADS, extra, nodes), f32),
            jax.ShapeDtypeStruct((HEADS, 8, nodes), f32),
        ],
        in_specs=[VMEM] * 5 + [SMEM] * 2,
        out_specs=[VMEM] * 3,
        scratch_shapes=[
            pltpu.VMEM((width // LANES, 2 * nodes, LANES), bf16),
            pltpu.VMEM((HEADS, extra, 2 * nodes), bf16),
            pltpu.VMEM((2 * nodes, nodes), i32),
        ],
        compiler_params=params(32),
        cost_estimate=cost(8 << 30, 4 << 20),
        name="near",
    )(normed, side, w_query, w_key, w_value, order, window)

    even, odd, near, top = lax.optimization_barrier((even, odd, near, top))
    first = lax.ppermute(even, NODES, beside)
    second = lax.ppermute(odd, NODES, beside)
    return pl.pallas_call(
        far_kernel,
        out_shape=jax.ShapeDtypeStruct((nodes, width), bf16),
        in_specs=[VMEM] * 6 + [SMEM] * 2 + [VMEM] * 8,
        out_specs=VMEM,
        scratch_shapes=[
            pltpu.VMEM((width // LANES, 3 * nodes, LANES), bf16),
            pltpu.VMEM((HEADS, extra, 3 * nodes), bf16),
            pltpu.VMEM((3 * nodes, nodes), i32),
            pltpu.VMEM((HEADS, head_dim, nodes), bf16),
        ],
        compiler_params=params(40),
        cost_estimate=cost(8 << 30, 8 << 20),
        name="far",
    )(
        first, second, even, odd, w_key, w_value, order, window,
        query, near, top, state, w_out, gain_mlp.reshape(1, width), w_up, w_down,
    )


def solution(mesh):
    placed = (
        P(("groups", "band", "inner"), None),
        P(("groups", "band", "inner"), None),
        P(("groups", "band"), "inner", None, None, None),
        P(("groups", "band"), "inner", None, None, None),
        P(("groups", "band"), "inner", None, None),
        P(),
        P(),
        P(),
        P(),
        P("groups"),
        P(),
        P(),
        P(),
        P(),
    )
    return jax.shard_map(
        local,
        mesh=mesh,
        in_specs=placed,
        out_specs=P(("groups", "band", "inner"), None),
        check_vma=False,
    )
```

```python
import functools
import math

import jax
import jax.numpy as jnp
from jax import lax
from jax.experimental import pallas as pl
from jax.experimental.pallas import tpu as pltpu
from jax.sharding import PartitionSpec as P

HEADS = 16
WMAX = 512
LANES = 128
NEAR = 128
TILE = 16
GRID_PARTS = 4
MOST = 56
GROUP = 4

norm_eps = 1e-05
NODES = ("band", "inner")
VMEM = pl.BlockSpec(memory_space=pltpu.VMEM)
SMEM = pl.BlockSpec(memory_space=pltpu.SMEM)
ANY = pl.BlockSpec(memory_space=pl.ANY)


def params(mib):
    return pltpu.CompilerParams(vmem_limit_bytes=mib * 1024 * 1024)


def dot(a, b):
    return jnp.dot(a, b, preferred_element_type=jnp.float32)


def dot_t(a, b):
    return lax.dot_general(a, b, (((1,), (1,)), ((), ())), preferred_element_type=jnp.float32)


def layer_norm(values, gain):
    center = values - jnp.mean(values, axis=-1, keepdims=True)
    spread = jnp.mean(center * center, axis=-1, keepdims=True)
    return center * lax.rsqrt(spread + norm_eps) * gain


def message_kernel(pair_count, grid_ref, w_ref, source_ref, target_ref, count_ref, *refs):
    out_refs, (grid_vmem, w_vmem, message_ref, out_vmem, in_sems, out_sems) = refs[:6], refs[6:]
    rows = grid_ref.shape[0]
    cap = source_ref.shape[-1]
    slots = pair_count * cap
    part = rows // GRID_PARTS
    fetches = [pltpu.make_async_copy(w_ref, w_vmem, in_sems.at[GRID_PARTS])]
    for k in range(GRID_PARTS):
        span = pl.ds(k * part, part)
        fetches.append(pltpu.make_async_copy(grid_ref.at[span], grid_vmem.at[span], in_sems.at[k]))
    for fetch in fetches:
        fetch.start()
    inner = lax.axis_index("inner")
    ahead = lax.rem(lax.axis_index("band"), 2) * 2
    blocks = [(o, inner ^ (2 * p + k)) for o in (2 - ahead, ahead, 1) for k in range(2) for p in range(pair_count)]
    sources = jnp.concatenate([source_ref[0, 0, o, pl.ds(j, 1), :] for o, j in blocks], axis=0)
    by_slot = jnp.transpose(sources.astype(jnp.float32)).astype(jnp.int32)
    slot = lax.broadcasted_iota(jnp.int32, (1, cap), 1)
    for m, (o, j) in enumerate(blocks):
        target = jnp.where(slot < count_ref[0, o, 0, j], target_ref[0, 0, o, pl.ds(j, 1), :], -1)
        tile = jnp.broadcast_to(target.astype(jnp.float32), (TILE, cap)).astype(jnp.bfloat16)
        p = m % pair_count
        out_vmem[m // pair_count, slots:, p * cap : (p + 1) * cap] = tile
    if out_vmem.shape[2] > slots:
        rest = jnp.zeros((6, TILE, out_vmem.shape[2] - slots), jnp.bfloat16)
        out_vmem[:, slots:, slots:] = rest
    fetches[0].wait()
    for k in range(GRID_PARTS):
        span = pl.ds(k * part, part)
        fetches[k + 1].wait()
        message_ref[span] = jax.nn.silu(dot(grid_vmem[span], w_vmem[...])).astype(jnp.bfloat16)
    message = message_ref[...]
    row = lax.broadcasted_iota(jnp.int32, (cap, rows), 1)
    sends = []
    for n in range(6):
        picks = jnp.concatenate(
            [
                jnp.where(row == by_slot[:, m : m + 1], 1.0, 0.0).astype(jnp.bfloat16)
                for m in range(n * pair_count, (n + 1) * pair_count)
            ],
            axis=0,
        )
        out_vmem[n, 0:slots, :] = dot(picks, message).astype(jnp.bfloat16)
        send = pltpu.make_async_copy(out_vmem.at[n], out_refs[n], out_sems.at[n])
        send.start()
        sends.append(send)
    for send in sends:
        send.wait()


def node_sums(row_refs, pair_count, nodes):
    cap = (row_refs[0].shape[0] - TILE) // pair_count
    node = lax.broadcasted_iota(jnp.int32, (nodes, cap), 0)
    targets = [r[pair_count * cap :, :].astype(jnp.float32)[0:1].astype(jnp.int32) for r in row_refs]
    for p in range(pair_count):
        span = slice(p * cap, (p + 1) * cap)
        hits = [jnp.where(node == t[:, span], 1.0, 0.0).astype(jnp.bfloat16) for t in targets]
        yield p, dot(jnp.concatenate(hits, axis=1), jnp.concatenate([r[span, :] for r in row_refs], axis=0))


def early_kernel(pair_count, w_ref, own_ref, other_ref, query_ref, key_ref, value_ref, sum_ref):
    width = w_ref.shape[0]
    head_dim = width // HEADS
    span = 3 * LANES
    row = lax.broadcasted_iota(jnp.int32, (LANES, span), 0)
    column = lax.broadcasted_iota(jnp.int32, (LANES, span), 1)
    wanted = row // head_dim * (3 * head_dim) + row % head_dim
    for c, out_ref in enumerate((query_ref, key_ref, value_ref)):
        pick = jnp.where(column == wanted + c * head_dim, 1.0, 0.0).astype(jnp.bfloat16)
        for g in range(width // LANES):
            part = dot_t(pick, w_ref[:, g * span : (g + 1) * span])
            out_ref[g * LANES : (g + 1) * LANES, :] = part.astype(jnp.bfloat16)
    for p, total in node_sums((own_ref, other_ref), pair_count, sum_ref.shape[1]):
        sum_ref[p] = total


def reduce_kernel(pair_count, *refs):
    row_refs, sum_ref, (own_ref, *part_refs) = refs[:4], refs[4], refs[5:]
    for p, total in node_sums(row_refs, pair_count, own_ref.shape[0]):
        total = total + sum_ref[p]
        if p:
            part_refs[p - 1][...] = total.astype(jnp.bfloat16)
        else:
            own_ref[...] = total


def merge_kernel(own_ref, *refs):
    part_refs, (mesh_ref, w_ref, gain_ref, state_ref, normed_ref) = refs[:-5], refs[-5:]
    total = own_ref[...]
    for part_ref in part_refs:
        total = total + part_ref[...].astype(jnp.float32)
    state = mesh_ref[...].astype(jnp.float32) + dot(total.astype(jnp.bfloat16), w_ref[...])
    state_ref[...] = state
    normed_ref[...] = layer_norm(state, gain_ref[...]).astype(jnp.bfloat16)


def project_keys(rows, wk_ref, wv_ref, key_ref, value_ref, start):
    count = rows.shape[0]
    groups = key_ref.shape[0]
    heads = value_ref.shape[0]
    keys = dot_t(rows, wk_ref[...]).astype(jnp.bfloat16)
    for g in range(groups):
        key_ref[g, start : start + count, :] = keys[:, g * LANES : (g + 1) * LANES]
    values = dot_t(wv_ref[...], rows).astype(jnp.bfloat16)
    value_ref[:, 0 : values.shape[0] // heads, start : start + count] = values.reshape(
        heads, -1, count
    )


def near_kernel(
    own_ref, side_ref, wq_ref, wk_ref, wv_ref, order_ref, window_ref,
    query_ref, sums_ref, top_ref,
    key_ref, value_ref, gap_ref,
):
    nodes, width = own_ref.shape
    head_dim = width // HEADS
    per_group = LANES // head_dim
    odd = lax.rem(lax.axis_index("inner"), 2)
    side = 1 - 2 * odd
    first = odd * (nodes - NEAR)
    second = (1 - odd) * NEAR
    scale = head_dim ** (-0.5) / math.log(2.0)

    queries = dot_t(wq_ref[...], own_ref[...]).astype(jnp.bfloat16)
    part = lax.broadcasted_iota(jnp.int32, (LANES, nodes), 0) // head_dim
    for h in range(HEADS):
        g = h // per_group
        lanes = queries[g * LANES : (g + 1) * LANES]
        query_ref[h] = jnp.where(part == h % per_group, lanes, jnp.zeros_like(lanes))
    value_ref[:, head_dim:, :] = jnp.ones_like(value_ref[:, head_dim:, :])
    project_keys(own_ref[...], wk_ref, wv_ref, key_ref, value_ref, 0)
    project_keys(side_ref[pl.ds(pl.multiple_of(first, NEAR), NEAR), :], wk_ref, wv_ref, key_ref, value_ref, nodes)
    project_keys(
        side_ref[pl.ds(pl.multiple_of(second, NEAR), NEAR), :], wk_ref, wv_ref, key_ref, value_ref, nodes + NEAR
    )
    lag = lax.broadcasted_iota(jnp.int32, (nodes, nodes), 0) - lax.broadcasted_iota(
        jnp.int32, (nodes, nodes), 1
    )
    gap_ref[0:nodes] = jnp.abs(lag)
    gap_ref[nodes : nodes + NEAR] = jnp.abs(lag[0:NEAR] + (side * nodes + first))
    gap_ref[nodes + NEAR : 2 * nodes] = jnp.abs(lag[0:NEAR] + (side * nodes + second))

    def attend(heads, rows):
        scores = [dot(key_ref[h // per_group, 0:rows, :], query_ref[h]) for h in heads]
        scores = [
            jnp.where(gap_ref[0:rows] <= window_ref[h], x, -1e30) for h, x in zip(heads, scores)
        ]
        tops = [jnp.max(x, axis=0, keepdims=True) for x in scores]
        expos = [jnp.exp2((x - top) * scale).astype(jnp.bfloat16) for x, top in zip(scores, tops)]
        for h, top, expo in zip(heads, tops, expos):
            sums_ref[h] = dot(value_ref[h, :, 0:rows], expo)
            top_ref[h] = jnp.broadcast_to(top, top_ref.shape[1:])

    def together(i, carry):
        heads = [order_ref[GROUP * i + k] for k in range(GROUP)]
        widest = functools.reduce(jnp.maximum, [window_ref[h] for h in heads])

        @pl.when(widest <= NEAR)
        def _():
            attend(heads, nodes + NEAR)

        @pl.when(widest > NEAR)
        def _():
            attend(heads, 2 * nodes)

        return carry

    lax.fori_loop(0, HEADS // GROUP, together, 0)


def far_kernel(
    first_ref, second_ref, even_ref, odd_ref, wk_ref, wv_ref, order_ref, window_ref,
    query_ref, sums_ref, top_ref, state_ref, w_out_ref, gain_ref, up_ref, down_ref,
    out_ref,
    key_ref, value_ref, gap_ref, attended_ref,
):
    nodes, width = even_ref.shape
    head_dim = width // HEADS
    per_group = LANES // head_dim
    total = lax.axis_size("band") * lax.axis_size("inner")
    me = lax.axis_index("band") * lax.axis_size("inner") + lax.axis_index("inner")
    odd = lax.rem(me, 2)
    far = 2 - 4 * lax.rem(me // 2, 2)
    side = 2 * odd - 1
    first = (1 - odd) * (nodes - NEAR)
    second = odd * NEAR
    scale = head_dim ** (-0.5) / math.log(2.0)
    absent = 1 << 20

    value_ref[:, head_dim:, :] = jnp.ones_like(value_ref[:, head_dim:, :])
    by_even = odd == lax.rem(me // 2 + 1, 2)
    beyond = jnp.where(by_even, first_ref[...], second_ref[...])
    beyond = jnp.where(odd == 0, jnp.concatenate([beyond[NEAR:], beyond[:NEAR]], axis=0), beyond)
    project_keys(beyond, wk_ref, wv_ref, key_ref, value_ref, 0)
    project_keys(even_ref[...], wk_ref, wv_ref, key_ref, value_ref, nodes)
    project_keys(odd_ref[...], wk_ref, wv_ref, key_ref, value_ref, 2 * nodes)
    lag = lax.broadcasted_iota(jnp.int32, (nodes, nodes), 0) - lax.broadcasted_iota(
        jnp.int32, (nodes, nodes), 1
    )

    def gap(rows, device, offset):
        inside = (me + device >= 0) & (me + device < total)
        return jnp.where(inside, jnp.abs(rows + (device * nodes + offset)), absent)

    gap_ref[0:NEAR] = gap(lag[0:NEAR], side, first)
    gap_ref[NEAR:nodes] = gap(lag[0:NEAR], side, second)
    gap_ref[nodes : 2 * nodes] = gap(lag, far, 0)
    gap_ref[2 * nodes : 3 * nodes] = gap(lag, -far, 0)

    def attend(heads, rows):
        scores = [dot(key_ref[h // per_group, 0:rows, :], query_ref[h]) for h in heads]
        scores = [
            jnp.where(gap_ref[0:rows] <= window_ref[h], x, -1e30) for h, x in zip(heads, scores)
        ]
        olds = [top_ref[h, 0:1, :] for h in heads]
        tops = [jnp.maximum(old, jnp.max(x, axis=0, keepdims=True)) for old, x in zip(olds, scores)]
        expos = [jnp.exp2((x - top) * scale).astype(jnp.bfloat16) for x, top in zip(scores, tops)]
        for h, old, top, expo in zip(heads, olds, tops, expos):
            sums = sums_ref[h] * jnp.exp2((old - top) * scale) + dot(value_ref[h, :, 0:rows], expo)
            attended_ref[h] = (sums[0:head_dim] / sums[head_dim : head_dim + 1]).astype(jnp.bfloat16)

    def together(i, carry):
        heads = [order_ref[GROUP * i + k] for k in range(GROUP)]
        widest = functools.reduce(jnp.maximum, [window_ref[h] for h in heads])

        @pl.when(widest <= NEAR)
        def _():
            attend(heads, NEAR)

        @pl.when((widest > NEAR) & (widest <= nodes))
        def _():
            attend(heads, nodes)

        @pl.when(widest > nodes)
        def _():
            attend(heads, 3 * nodes)

        return carry

    lax.fori_loop(0, HEADS // GROUP, together, 0)

    attended = attended_ref[...].reshape(width, nodes)
    mixed = lax.dot_general(
        attended, w_out_ref[...], (((0,), (0,)), ((), ())), preferred_element_type=jnp.float32
    )
    mid = state_ref[...] + mixed
    normed = layer_norm(mid, gain_ref[...]).astype(jnp.bfloat16)
    hidden = jax.nn.silu(dot(normed, up_ref[...])).astype(jnp.bfloat16)
    out_ref[...] = (mid + dot(hidden, down_ref[...])).astype(jnp.bfloat16)


def cost(flops, size):
    return pl.CostEstimate(flops=flops, bytes_accessed=size, transcendentals=0)


def local(
    grid_rows,
    mesh_rows,
    edge_source,
    edge_target,
    edge_count,
    w_message,
    w_merge,
    gain_attn,
    w_qkv,
    window,
    w_out,
    gain_mlp,
    w_up,
    w_down,
):
    bands = lax.axis_size("band")
    inners = lax.axis_size("inner")
    devices = bands * inners
    grid_dev = grid_rows.shape[0]
    nodes, width = mesh_rows.shape
    cap = edge_source.shape[-1]
    head_dim = width // HEADS
    pairs = inners // 2
    slots = pairs * cap
    f32, bf16, i32 = jnp.float32, jnp.bfloat16, jnp.int32

    even, even_other, odd, odd_other, own, own_other = pl.pallas_call(
        functools.partial(message_kernel, pairs),
        out_shape=[jax.ShapeDtypeStruct((slots + TILE, width), bf16)] * 6,
        in_specs=[ANY] * 2 + [VMEM] * 2 + [SMEM],
        out_specs=[ANY] * 6,
        scratch_shapes=[
            pltpu.VMEM(grid_rows.shape, bf16),
            pltpu.VMEM(w_message.shape, bf16),
            pltpu.VMEM((grid_dev, width), bf16),
            pltpu.VMEM((6, slots + TILE, width), bf16),
            pltpu.SemaphoreType.DMA((GRID_PARTS + 1,)),
            pltpu.SemaphoreType.DMA((6,)),
        ],
        compiler_params=params(MOST),
        cost_estimate=cost(2 * grid_dev * width * (width + 6 * slots), 4 << 20),
        name="messages",
    )(grid_rows, w_message, edge_source, edge_target, jnp.transpose(edge_count, (0, 2, 1, 3)))

    beside = [(g, g ^ 1) for g in range(devices)]

    def bands_trade(odd_pairs):
        route = []
        for g in range(devices):
            b = g // inners
            t = (b - odd_pairs ^ 1) + odd_pairs
            route.append((g, t * inners + g % inners if 0 <= t < bands else g ^ 1))
        return route

    even_other = lax.ppermute(even_other, NODES, beside)
    odd_other = lax.ppermute(odd_other, NODES, beside)
    own_other = lax.ppermute(own_other, NODES, beside)
    even = lax.ppermute(even, NODES, bands_trade(0))
    odd = lax.ppermute(odd, NODES, bands_trade(1))
    even_other = lax.ppermute(even_other, NODES, bands_trade(0))
    odd_other = lax.ppermute(odd_other, NODES, bands_trade(1))

    w_qkv, window, own = lax.optimization_barrier((w_qkv, window, own))
    w_query, w_key, w_value, early = pl.pallas_call(
        functools.partial(early_kernel, pairs),
        out_shape=[jax.ShapeDtypeStruct((width, width), bf16)] * 3
        + [jax.ShapeDtypeStruct((pairs, nodes, width), f32)],
        in_specs=[VMEM] * 3,
        out_specs=[VMEM] * 4,
        compiler_params=params(16),
        cost_estimate=cost(1 << 28, 4 << 20),
        name="early",
    )(w_qkv, own, own_other)
    head = jnp.arange(HEADS, dtype=i32)
    ahead = (window[None, :] > window[:, None]) | (
        (window[None, :] == window[:, None]) & (head[None, :] < head[:, None])
    )
    rank = jnp.sum(ahead.astype(i32), axis=1)
    order = jnp.sum(jnp.where(rank[None, :] == head[:, None], head[None, :], 0), axis=1).astype(i32)

    sums = pl.pallas_call(
        functools.partial(reduce_kernel, pairs),
        out_shape=[jax.ShapeDtypeStruct((nodes, width), f32)]
        + [jax.ShapeDtypeStruct((nodes, width), bf16)] * (pairs - 1),
        in_specs=[VMEM] * 5,
        out_specs=[VMEM] * pairs,
        compiler_params=params(24),
        cost_estimate=cost(2 * nodes * width * 4 * slots, 3 << 20),
        name="reduce",
    )(even, even_other, odd, odd_other, early)
    parts = [
        lax.ppermute(sums[p], NODES, [(g, g ^ (2 * p)) for g in range(devices)]) for p in range(1, pairs)
    ]

    state, normed = pl.pallas_call(
        merge_kernel,
        out_shape=[
            jax.ShapeDtypeStruct((nodes, width), f32),
            jax.ShapeDtypeStruct((nodes, width), bf16),
        ],
        in_specs=[VMEM] * (pairs + 3),
        out_specs=[VMEM] * 2,
        compiler_params=params(24),
        cost_estimate=cost(2 * nodes * width * width, 2 << 20),
        name="merge",
    )(sums[0], *parts, mesh_rows, w_merge, gain_attn.reshape(1, width))

    def chips_trade(odd_pairs):
        route = []
        for g in range(devices):
            t = (g // 2 - odd_pairs ^ 1) + odd_pairs
            route.append((g, 2 * t + g % 2 if 0 <= 2 * t < devices else g ^ 1))
        return route

    side = lax.ppermute(normed, NODES, beside)
    even = lax.ppermute(normed, NODES, chips_trade(0))
    odd = lax.ppermute(normed, NODES, chips_trade(1))

    extra = head_dim + 16
    query, near, top = pl.pallas_call(
        near_kernel,
        out_shape=[
            jax.ShapeDtypeStruct((HEADS, LANES, nodes), bf16),
            jax.ShapeDtypeStruct((HEADS, extra, nodes), f32),
            jax.ShapeDtypeStruct((HEADS, 8, nodes), f32),
        ],
        in_specs=[VMEM] * 5 + [SMEM] * 2,
        out_specs=[VMEM] * 3,
        scratch_shapes=[
            pltpu.VMEM((width // LANES, 2 * nodes, LANES), bf16),
            pltpu.VMEM((HEADS, extra, 2 * nodes), bf16),
            pltpu.VMEM((2 * nodes, nodes), i32),
        ],
        compiler_params=params(32),
        cost_estimate=cost(8 << 30, 4 << 20),
        name="near",
    )(normed, side, w_query, w_key, w_value, order, window)

    even, odd, near, top = lax.optimization_barrier((even, odd, near, top))
    first = lax.ppermute(even, NODES, beside)
    second = lax.ppermute(odd, NODES, beside)
    return pl.pallas_call(
        far_kernel,
        out_shape=jax.ShapeDtypeStruct((nodes, width), bf16),
        in_specs=[VMEM] * 6 + [SMEM] * 2 + [VMEM] * 8,
        out_specs=VMEM,
        scratch_shapes=[
            pltpu.VMEM((width // LANES, 3 * nodes, LANES), bf16),
            pltpu.VMEM((HEADS, extra, 3 * nodes), bf16),
            pltpu.VMEM((3 * nodes, nodes), i32),
            pltpu.VMEM((HEADS, head_dim, nodes), bf16),
        ],
        compiler_params=params(40),
        cost_estimate=cost(8 << 30, 8 << 20),
        name="far",
    )(
        first, second, even, odd, w_key, w_value, order, window,
        query, near, top, state, w_out, gain_mlp.reshape(1, width), w_up, w_down,
    )


def solution(mesh):
    placed = (
        P(("groups", "band", "inner"), None),
        P(("groups", "band", "inner"), None),
        P(("groups", "band"), "inner", None, None, None),
        P(("groups", "band"), "inner", None, None, None),
        P(("groups", "band"), "inner", None, None),
        P(),
        P(),
        P(),
        P(),
        P("groups"),
        P(),
        P(),
        P(),
        P(),
    )
    return jax.shard_map(
        local,
        mesh=mesh,
        in_specs=placed,
        out_specs=P(("groups", "band", "inner"), None),
        check_vma=False,
    )
```

```python
import functools
import math

import jax
import jax.numpy as jnp
from jax import lax
from jax.experimental import pallas as pl
from jax.experimental.pallas import tpu as pltpu
from jax.sharding import PartitionSpec as P

HEADS = 16
WMAX = 512
LANES = 128
NEAR = 128
TILE = 16
CAP = 128
GRID_PARTS = 4
MOST = 56
GROUP = 4

norm_eps = 1e-05
NODES = ("band", "inner")
VMEM = pl.BlockSpec(memory_space=pltpu.VMEM)
SMEM = pl.BlockSpec(memory_space=pltpu.SMEM)
ANY = pl.BlockSpec(memory_space=pl.ANY)


def params(mib):
    return pltpu.CompilerParams(vmem_limit_bytes=mib * 1024 * 1024)


def dot(a, b):
    return jnp.dot(a, b, preferred_element_type=jnp.float32)


def dot_t(a, b):
    return lax.dot_general(a, b, (((1,), (1,)), ((), ())), preferred_element_type=jnp.float32)


def layer_norm(values, gain):
    center = values - jnp.mean(values, axis=-1, keepdims=True)
    spread = jnp.mean(center * center, axis=-1, keepdims=True)
    return center * lax.rsqrt(spread + norm_eps) * gain


def band_offsets():
    ahead = lax.rem(lax.axis_index("band"), 2) * 2
    return 2 - ahead, ahead, 1


def slot_columns(source_ref, blocks):
    sources = jnp.concatenate([source_ref[0, 0, o, pl.ds(j, 1), :] for o, j in blocks], axis=0)
    return jnp.transpose(sources.astype(jnp.float32)).astype(jnp.int32)


def target_tile(target_ref, count_ref, blocks, lanes):
    cap = target_ref.shape[-1]
    slot = lax.broadcasted_iota(jnp.int32, (1, cap), 1)
    targets = [
        jnp.where(slot < count_ref[0, o, 0, j], target_ref[0, 0, o, pl.ds(j, 1), :], -1) for o, j in blocks
    ]
    targets.append(jnp.full((TILE - len(blocks), cap), -1, jnp.int32))
    tile = jnp.concatenate(targets, axis=0).astype(jnp.float32).astype(jnp.bfloat16)
    return jnp.concatenate([tile] * (lanes // cap), axis=1)


def message_kernel(pair_count, grid_ref, w_ref, source_ref, target_ref, count_ref, *refs):
    count = 4 + 2 * pair_count
    out_refs, out_vmems = refs[:count], refs[count : 2 * count]
    grid_vmem, w_vmem, message_ref, in_sems, out_sems = refs[2 * count :]
    rows = grid_ref.shape[0]
    cap = source_ref.shape[-1]
    half = w_ref.shape[1] // 2
    part = rows // GRID_PARTS
    fetches = [pltpu.make_async_copy(w_ref, w_vmem, in_sems.at[GRID_PARTS])]
    for k in range(GRID_PARTS):
        span = pl.ds(k * part, part)
        fetches.append(pltpu.make_async_copy(grid_ref.at[span], grid_vmem.at[span], in_sems.at[k]))
    for fetch in fetches:
        fetch.start()
    inner = lax.axis_index("inner")
    offsets = band_offsets()
    keys = [(t, p, k) for t in range(3) for p in range(pair_count) for k in range(2)]
    place = {(t, p, k): (offsets[t], inner ^ (2 * p + k)) for t, p, k in keys}
    by_slot = slot_columns(source_ref, [place[key] for key in keys])
    left, right = slice(0, half), slice(half, 2 * half)
    runs = [[([(t, p, k) for p in range(pair_count)], left)] for t in range(2) for k in range(2)]
    runs += [[([(t, p, k) for t in range(3)], right)] for p in range(1, pair_count) for k in range(2)]
    runs += [
        [([(2, p, k) for p in range(pair_count)], left), ([(t, 0, k) for t in range(3)], right)] for k in range(2)
    ]
    for out_vmem, parts in zip(out_vmems, runs):
        start = 0
        for chosen, _ in parts:
            start += len(chosen) * cap
            out_vmem[start : start + TILE, :] = target_tile(target_ref, count_ref, [place[key] for key in chosen], half)
            start += TILE
    fetches[0].wait()
    for k in range(GRID_PARTS):
        span = pl.ds(k * part, part)
        fetches[k + 1].wait()
        message_ref[span] = jax.nn.silu(dot(grid_vmem[span], w_vmem[...])).astype(jnp.bfloat16)
    row = lax.broadcasted_iota(jnp.int32, (cap, rows), 1)
    picks = {
        key: jnp.where(row == by_slot[:, m : m + 1], 1.0, 0.0).astype(jnp.bfloat16) for m, key in enumerate(keys)
    }
    sends = []
    for n, parts in enumerate(runs):
        start = 0
        for chosen, lanes in parts:
            taken = dot(jnp.concatenate([picks[key] for key in chosen], axis=0), message_ref[:, lanes])
            out_vmems[n][start : start + len(chosen) * cap, :] = taken.astype(jnp.bfloat16)
            start += len(chosen) * cap + TILE
        send = pltpu.make_async_copy(out_vmems[n], out_refs[n], out_sems.at[n])
        send.start()
        sends.append(send)
    for send in sends:
        send.wait()


def node_sums(arrays, nodes):
    count = arrays[0][2]
    cap = CAP
    node = lax.broadcasted_iota(jnp.int32, (nodes, cap), 0)
    targets = [
        ref[start + count * cap : start + count * cap + TILE, 0:cap].astype(jnp.float32).astype(jnp.int32)
        for ref, start, _ in arrays
    ]
    for n in range(count):
        hits = [jnp.where(node == t[n : n + 1], 1.0, 0.0).astype(jnp.bfloat16) for t in targets]
        rows = [ref[start + n * cap : start + (n + 1) * cap, :] for ref, start, _ in arrays]
        yield n, dot(jnp.concatenate(hits, axis=1), jnp.concatenate(rows, axis=0))


def early_kernel(pair_count, w_ref, own_ref, other_ref, query_ref, key_ref, value_ref, left_ref, right_ref):
    width = w_ref.shape[0]
    head_dim = width // HEADS
    span = 3 * LANES
    row = lax.broadcasted_iota(jnp.int32, (LANES, span), 0)
    column = lax.broadcasted_iota(jnp.int32, (LANES, span), 1)
    wanted = row // head_dim * (3 * head_dim) + row % head_dim
    for c, out_ref in enumerate((query_ref, key_ref, value_ref)):
        pick = jnp.where(column == wanted + c * head_dim, 1.0, 0.0).astype(jnp.bfloat16)
        for g in range(width // LANES):
            part = dot_t(pick, w_ref[:, g * span : (g + 1) * span])
            out_ref[g * LANES : (g + 1) * LANES, :] = part.astype(jnp.bfloat16)
    start = 0
    for sum_ref in (left_ref, right_ref):
        count, nodes, _ = sum_ref.shape
        for n, total in node_sums([(own_ref, start, count), (other_ref, start, count)], nodes):
            sum_ref[n] = total
        start += count * CAP + TILE


def sums_kernel(array_count, kept, *refs):
    row_refs, early_ref, out_refs = refs[:array_count], refs[array_count], refs[array_count + 1 :]
    count, nodes, _ = early_ref.shape
    for n, total in node_sums([(r, 0, count) for r in row_refs], nodes):
        total = total + early_ref[n]
        out_refs[n][...] = total if n == kept else total.astype(jnp.bfloat16)


def merge_kernel(*refs):
    *part_refs, right_ref, even_ref, odd_ref, mesh_ref, w_ref, gain_ref, state_ref, normed_ref = refs
    left = functools.reduce(jnp.add, [r[...].astype(jnp.float32) for r in part_refs])
    right = right_ref[...] + even_ref[...].astype(jnp.float32) + odd_ref[...].astype(jnp.float32)
    total = jnp.concatenate([left, right], axis=1).astype(jnp.bfloat16)
    state = mesh_ref[...].astype(jnp.float32) + dot(total, w_ref[...])
    state_ref[...] = state
    normed_ref[...] = layer_norm(state, gain_ref[...]).astype(jnp.bfloat16)


def project_keys(rows, wk_ref, wv_ref, key_ref, value_ref, start):
    count = rows.shape[0]
    groups = key_ref.shape[0]
    heads = value_ref.shape[0]
    keys = dot_t(rows, wk_ref[...]).astype(jnp.bfloat16)
    for g in range(groups):
        key_ref[g, start : start + count, :] = keys[:, g * LANES : (g + 1) * LANES]
    values = dot_t(wv_ref[...], rows).astype(jnp.bfloat16)
    value_ref[:, 0 : values.shape[0] // heads, start : start + count] = values.reshape(
        heads, -1, count
    )


def near_kernel(
    own_ref, side_ref, wq_ref, wk_ref, wv_ref, order_ref, window_ref,
    query_ref, sums_ref, top_ref,
    key_ref, value_ref, gap_ref,
):
    nodes, width = own_ref.shape
    head_dim = width // HEADS
    per_group = LANES // head_dim
    odd = lax.rem(lax.axis_index("inner"), 2)
    side = 1 - 2 * odd
    first = odd * (nodes - NEAR)
    second = (1 - odd) * NEAR
    scale = head_dim ** (-0.5) / math.log(2.0)

    queries = dot_t(wq_ref[...], own_ref[...]).astype(jnp.bfloat16)
    part = lax.broadcasted_iota(jnp.int32, (LANES, nodes), 0) // head_dim
    for h in range(HEADS):
        g = h // per_group
        lanes = queries[g * LANES : (g + 1) * LANES]
        query_ref[h] = jnp.where(part == h % per_group, lanes, jnp.zeros_like(lanes))
    value_ref[:, head_dim:, :] = jnp.ones_like(value_ref[:, head_dim:, :])
    project_keys(own_ref[...], wk_ref, wv_ref, key_ref, value_ref, 0)
    project_keys(side_ref[pl.ds(pl.multiple_of(first, NEAR), NEAR), :], wk_ref, wv_ref, key_ref, value_ref, nodes)
    project_keys(
        side_ref[pl.ds(pl.multiple_of(second, NEAR), NEAR), :], wk_ref, wv_ref, key_ref, value_ref, nodes + NEAR
    )
    lag = lax.broadcasted_iota(jnp.int32, (nodes, nodes), 0) - lax.broadcasted_iota(
        jnp.int32, (nodes, nodes), 1
    )
    gap_ref[0:nodes] = jnp.abs(lag)
    gap_ref[nodes : nodes + NEAR] = jnp.abs(lag[0:NEAR] + (side * nodes + first))
    gap_ref[nodes + NEAR : 2 * nodes] = jnp.abs(lag[0:NEAR] + (side * nodes + second))

    def attend(heads, rows):
        scores = [dot(key_ref[h // per_group, 0:rows, :], query_ref[h]) for h in heads]
        scores = [
            jnp.where(gap_ref[0:rows] <= window_ref[h], x, -1e30) for h, x in zip(heads, scores)
        ]
        tops = [jnp.max(x, axis=0, keepdims=True) for x in scores]
        expos = [jnp.exp2((x - top) * scale).astype(jnp.bfloat16) for x, top in zip(scores, tops)]
        for h, top, expo in zip(heads, tops, expos):
            sums_ref[h] = dot(value_ref[h, :, 0:rows], expo)
            top_ref[h] = jnp.broadcast_to(top, top_ref.shape[1:])

    def together(i, carry):
        heads = [order_ref[GROUP * i + k] for k in range(GROUP)]
        widest = functools.reduce(jnp.maximum, [window_ref[h] for h in heads])

        @pl.when(widest <= NEAR)
        def _():
            attend(heads, nodes + NEAR)

        @pl.when(widest > NEAR)
        def _():
            attend(heads, 2 * nodes)

        return carry

    lax.fori_loop(0, HEADS // GROUP, together, 0)


def far_kernel(
    first_ref, second_ref, even_ref, odd_ref, wk_ref, wv_ref, order_ref, window_ref,
    query_ref, sums_ref, top_ref, state_ref, w_out_ref, gain_ref, up_ref, down_ref,
    out_ref,
    key_ref, value_ref, gap_ref, attended_ref,
):
    nodes, width = even_ref.shape
    head_dim = width // HEADS
    per_group = LANES // head_dim
    total = lax.axis_size("band") * lax.axis_size("inner")
    me = lax.axis_index("band") * lax.axis_size("inner") + lax.axis_index("inner")
    odd = lax.rem(me, 2)
    far = 2 - 4 * lax.rem(me // 2, 2)
    side = 2 * odd - 1
    first = (1 - odd) * (nodes - NEAR)
    second = odd * NEAR
    scale = head_dim ** (-0.5) / math.log(2.0)
    absent = 1 << 20

    value_ref[:, head_dim:, :] = jnp.ones_like(value_ref[:, head_dim:, :])
    by_even = odd == lax.rem(me // 2 + 1, 2)
    beyond = jnp.where(by_even, first_ref[...], second_ref[...])
    beyond = jnp.where(odd == 0, jnp.concatenate([beyond[NEAR:], beyond[:NEAR]], axis=0), beyond)
    project_keys(beyond, wk_ref, wv_ref, key_ref, value_ref, 0)
    project_keys(even_ref[...], wk_ref, wv_ref, key_ref, value_ref, nodes)
    project_keys(odd_ref[...], wk_ref, wv_ref, key_ref, value_ref, 2 * nodes)
    lag = lax.broadcasted_iota(jnp.int32, (nodes, nodes), 0) - lax.broadcasted_iota(
        jnp.int32, (nodes, nodes), 1
    )

    def gap(rows, device, offset):
        inside = (me + device >= 0) & (me + device < total)
        return jnp.where(inside, jnp.abs(rows + (device * nodes + offset)), absent)

    gap_ref[0:NEAR] = gap(lag[0:NEAR], side, first)
    gap_ref[NEAR:nodes] = gap(lag[0:NEAR], side, second)
    gap_ref[nodes : 2 * nodes] = gap(lag, far, 0)
    gap_ref[2 * nodes : 3 * nodes] = gap(lag, -far, 0)

    def attend(heads, rows):
        scores = [dot(key_ref[h // per_group, 0:rows, :], query_ref[h]) for h in heads]
        scores = [
            jnp.where(gap_ref[0:rows] <= window_ref[h], x, -1e30) for h, x in zip(heads, scores)
        ]
        olds = [top_ref[h, 0:1, :] for h in heads]
        tops = [jnp.maximum(old, jnp.max(x, axis=0, keepdims=True)) for old, x in zip(olds, scores)]
        expos = [jnp.exp2((x - top) * scale).astype(jnp.bfloat16) for x, top in zip(scores, tops)]
        for h, old, top, expo in zip(heads, olds, tops, expos):
            sums = sums_ref[h] * jnp.exp2((old - top) * scale) + dot(value_ref[h, :, 0:rows], expo)
            attended_ref[h] = (sums[0:head_dim] / sums[head_dim : head_dim + 1]).astype(jnp.bfloat16)

    def together(i, carry):
        heads = [order_ref[GROUP * i + k] for k in range(GROUP)]
        widest = functools.reduce(jnp.maximum, [window_ref[h] for h in heads])

        @pl.when(widest <= NEAR)
        def _():
            attend(heads, NEAR)

        @pl.when((widest > NEAR) & (widest <= nodes))
        def _():
            attend(heads, nodes)

        @pl.when(widest > nodes)
        def _():
            attend(heads, 3 * nodes)

        return carry

    lax.fori_loop(0, HEADS // GROUP, together, 0)

    attended = attended_ref[...].reshape(width, nodes)
    mixed = lax.dot_general(
        attended, w_out_ref[...], (((0,), (0,)), ((), ())), preferred_element_type=jnp.float32
    )
    mid = state_ref[...] + mixed
    normed = layer_norm(mid, gain_ref[...]).astype(jnp.bfloat16)
    hidden = jax.nn.silu(dot(normed, up_ref[...])).astype(jnp.bfloat16)
    out_ref[...] = (mid + dot(hidden, down_ref[...])).astype(jnp.bfloat16)


def cost(flops, size):
    return pl.CostEstimate(flops=flops, bytes_accessed=size, transcendentals=0)


def local(
    grid_rows,
    mesh_rows,
    edge_source,
    edge_target,
    edge_count,
    w_message,
    w_merge,
    gain_attn,
    w_qkv,
    window,
    w_out,
    gain_mlp,
    w_up,
    w_down,
):
    bands = lax.axis_size("band")
    inners = lax.axis_size("inner")
    devices = bands * inners
    grid_dev = grid_rows.shape[0]
    nodes, width = mesh_rows.shape
    cap = edge_source.shape[-1]
    head_dim = width // HEADS
    pairs = inners // 2
    half = width // 2
    f32, bf16, i32 = jnp.float32, jnp.bfloat16, jnp.int32
    edges = (edge_source, edge_target, jnp.transpose(edge_count, (0, 2, 1, 3)))

    def rows_of(*blocks):
        return jax.ShapeDtypeStruct((sum(n * cap + TILE for n in blocks), half), bf16)

    outgoing = [rows_of(pairs)] * 4 + [rows_of(3)] * (2 * pairs - 2) + [rows_of(pairs, 3)] * 2
    even, even_other, odd, odd_other, *cross, here, here_other = pl.pallas_call(
        functools.partial(message_kernel, pairs),
        out_shape=outgoing,
        in_specs=[ANY] * 2 + [VMEM] * 2 + [SMEM],
        out_specs=[ANY] * len(outgoing),
        scratch_shapes=[pltpu.VMEM(a.shape, bf16) for a in outgoing]
        + [
            pltpu.VMEM(grid_rows.shape, bf16),
            pltpu.VMEM(w_message.shape, bf16),
            pltpu.VMEM((grid_dev, width), bf16),
            pltpu.SemaphoreType.DMA((GRID_PARTS + 1,)),
            pltpu.SemaphoreType.DMA((len(outgoing),)),
        ],
        compiler_params=params(MOST),
        cost_estimate=cost(2 * grid_dev * width * (width + 3 * inners * cap), 4 << 20),
        name="messages",
    )(grid_rows, w_message, *edges)
    beside = [(g, g ^ 1) for g in range(devices)]

    def bands_trade(odd_pairs):
        route = []
        for g in range(devices):
            b = g // inners
            t = (b - odd_pairs ^ 1) + odd_pairs
            route.append((g, t * inners + g % inners if 0 <= t < bands else g ^ 1))
        return route

    def chip_trade(p):
        return [(g, g ^ (2 * p)) for g in range(devices)]

    even_other = lax.ppermute(even_other, NODES, beside)
    cross_other = [lax.ppermute(c, NODES, beside) for c in cross[1::2]]
    odd_other = lax.ppermute(odd_other, NODES, beside)
    cross = [lax.ppermute(c, NODES, chip_trade(p + 1)) for p, c in enumerate(cross[0::2])]
    even = lax.ppermute(even, NODES, bands_trade(0))
    odd = lax.ppermute(odd, NODES, bands_trade(1))
    cross_other = [lax.ppermute(c, NODES, chip_trade(p + 1)) for p, c in enumerate(cross_other)]
    even_other = lax.ppermute(even_other, NODES, bands_trade(0))
    odd_other = lax.ppermute(odd_other, NODES, bands_trade(1))
    here_other = lax.ppermute(here_other, NODES, beside)

    w_qkv, window, here = lax.optimization_barrier((w_qkv, window, here))
    w_query, w_key, w_value, early_left, early_right = pl.pallas_call(
        functools.partial(early_kernel, pairs),
        out_shape=[jax.ShapeDtypeStruct((width, width), bf16)] * 3
        + [jax.ShapeDtypeStruct((n, nodes, half), f32) for n in (pairs, 3)],
        in_specs=[VMEM] * 3,
        out_specs=[VMEM] * 5,
        compiler_params=params(24),
        cost_estimate=cost(1 << 28, 4 << 20),
        name="early",
    )(w_qkv, here, here_other)
    head = jnp.arange(HEADS, dtype=i32)
    ahead = (window[None, :] > window[:, None]) | (
        (window[None, :] == window[:, None]) & (head[None, :] < head[:, None])
    )
    rank = jnp.sum(ahead.astype(i32), axis=1)
    order = jnp.sum(jnp.where(rank[None, :] == head[:, None], head[None, :], 0), axis=1).astype(i32)

    def sums(arrays, early, kept, name):
        count = early.shape[0]
        return pl.pallas_call(
            functools.partial(sums_kernel, len(arrays), kept),
            out_shape=[jax.ShapeDtypeStruct((nodes, half), f32 if n == kept else bf16) for n in range(count)],
            in_specs=[VMEM] * (len(arrays) + 1),
            out_specs=[VMEM] * count,
            compiler_params=params(24),
            cost_estimate=cost(2 * nodes * half * len(arrays) * count * cap, 2 << 20),
            name=name,
        )(*arrays, early)

    left, *parts = sums([even, even_other, odd, odd_other], early_left, 0, "left")
    parts = [lax.ppermute(part, NODES, chip_trade(p + 1)) for p, part in enumerate(parts)]
    to_even, to_odd, right = sums([*cross, *cross_other], early_right, 2, "right")
    from_even = lax.ppermute(to_even, NODES, bands_trade(0))
    from_odd = lax.ppermute(to_odd, NODES, bands_trade(1))

    state, normed = pl.pallas_call(
        merge_kernel,
        out_shape=[
            jax.ShapeDtypeStruct((nodes, width), f32),
            jax.ShapeDtypeStruct((nodes, width), bf16),
        ],
        in_specs=[VMEM] * (pairs + 6),
        out_specs=[VMEM] * 2,
        compiler_params=params(24),
        cost_estimate=cost(2 * nodes * width * width, 2 << 20),
        name="merge",
    )(left, *parts, right, from_even, from_odd, mesh_rows, w_merge, gain_attn.reshape(1, width))

    def chips_trade(odd_pairs):
        route = []
        for g in range(devices):
            t = (g // 2 - odd_pairs ^ 1) + odd_pairs
            route.append((g, 2 * t + g % 2 if 0 <= 2 * t < devices else g ^ 1))
        return route

    side = lax.ppermute(normed, NODES, beside)
    even = lax.ppermute(normed, NODES, chips_trade(0))
    odd = lax.ppermute(normed, NODES, chips_trade(1))

    extra = head_dim + 16
    query, near, top = pl.pallas_call(
        near_kernel,
        out_shape=[
            jax.ShapeDtypeStruct((HEADS, LANES, nodes), bf16),
            jax.ShapeDtypeStruct((HEADS, extra, nodes), f32),
            jax.ShapeDtypeStruct((HEADS, 8, nodes), f32),
        ],
        in_specs=[VMEM] * 5 + [SMEM] * 2,
        out_specs=[VMEM] * 3,
        scratch_shapes=[
            pltpu.VMEM((width // LANES, 2 * nodes, LANES), bf16),
            pltpu.VMEM((HEADS, extra, 2 * nodes), bf16),
            pltpu.VMEM((2 * nodes, nodes), i32),
        ],
        compiler_params=params(32),
        cost_estimate=cost(8 << 30, 4 << 20),
        name="near",
    )(normed, side, w_query, w_key, w_value, order, window)

    even, odd, near, top = lax.optimization_barrier((even, odd, near, top))
    first = lax.ppermute(even, NODES, beside)
    second = lax.ppermute(odd, NODES, beside)
    return pl.pallas_call(
        far_kernel,
        out_shape=jax.ShapeDtypeStruct((nodes, width), bf16),
        in_specs=[VMEM] * 6 + [SMEM] * 2 + [VMEM] * 8,
        out_specs=VMEM,
        scratch_shapes=[
            pltpu.VMEM((width // LANES, 3 * nodes, LANES), bf16),
            pltpu.VMEM((HEADS, extra, 3 * nodes), bf16),
            pltpu.VMEM((3 * nodes, nodes), i32),
            pltpu.VMEM((HEADS, head_dim, nodes), bf16),
        ],
        compiler_params=params(40),
        cost_estimate=cost(8 << 30, 8 << 20),
        name="far",
    )(
        first, second, even, odd, w_key, w_value, order, window,
        query, near, top, state, w_out, gain_mlp.reshape(1, width), w_up, w_down,
    )


def solution(mesh):
    placed = (
        P(("groups", "band", "inner"), None),
        P(("groups", "band", "inner"), None),
        P(("groups", "band"), "inner", None, None, None),
        P(("groups", "band"), "inner", None, None, None),
        P(("groups", "band"), "inner", None, None),
        P(),
        P(),
        P(),
        P(),
        P("groups"),
        P(),
        P(),
        P(),
        P(),
    )
    return jax.shard_map(
        local,
        mesh=mesh,
        in_specs=placed,
        out_specs=P(("groups", "band", "inner"), None),
        check_vma=False,
    )
```

```python
import functools
import math

import jax
import jax.numpy as jnp
from jax import lax
from jax.experimental import pallas as pl
from jax.experimental.pallas import tpu as pltpu
from jax.sharding import PartitionSpec as P

HEADS = 16
WMAX = 512
LANES = 128
NEAR = 128
TILE = 16
CAP = 128
GRID_PARTS = 4
MOST = 56
GROUP = 4

norm_eps = 1e-05
NODES = ("band", "inner")
VMEM = pl.BlockSpec(memory_space=pltpu.VMEM)
SMEM = pl.BlockSpec(memory_space=pltpu.SMEM)
ANY = pl.BlockSpec(memory_space=pl.ANY)


def params(mib):
    return pltpu.CompilerParams(vmem_limit_bytes=mib * 1024 * 1024)


def dot(a, b):
    return jnp.dot(a, b, preferred_element_type=jnp.float32)


def dot_t(a, b):
    return lax.dot_general(a, b, (((1,), (1,)), ((), ())), preferred_element_type=jnp.float32)


def layer_norm(values, gain):
    center = values - jnp.mean(values, axis=-1, keepdims=True)
    spread = jnp.mean(center * center, axis=-1, keepdims=True)
    return center * lax.rsqrt(spread + norm_eps) * gain


def band_offsets():
    ahead = lax.rem(lax.axis_index("band"), 2) * 2
    return 2 - ahead, ahead, 1


def slot_columns(source_ref, blocks):
    sources = jnp.concatenate([source_ref[0, 0, o, pl.ds(j, 1), :] for o, j in blocks], axis=0)
    return jnp.transpose(sources.astype(jnp.float32)).astype(jnp.int32)


def target_tile(target_ref, count_ref, blocks, lanes):
    cap = target_ref.shape[-1]
    slot = lax.broadcasted_iota(jnp.int32, (1, cap), 1)
    targets = [
        jnp.where(slot < count_ref[0, o, 0, j], target_ref[0, 0, o, pl.ds(j, 1), :], -1) for o, j in blocks
    ]
    targets.append(jnp.full((TILE - len(blocks), cap), -1, jnp.int32))
    tile = jnp.concatenate(targets, axis=0).astype(jnp.float32).astype(jnp.bfloat16)
    return jnp.concatenate([tile] * (lanes // cap), axis=1)


def message_kernel(pair_count, grid_ref, w_ref, source_ref, target_ref, count_ref, *refs):
    count = 4 + 2 * pair_count
    out_refs, out_vmems = refs[:count], refs[count : 2 * count]
    grid_vmem, w_vmem, message_ref, in_sems, out_sems = refs[2 * count :]
    rows = grid_ref.shape[0]
    cap = source_ref.shape[-1]
    half = w_ref.shape[1] // 2
    part = rows // GRID_PARTS
    fetches = [pltpu.make_async_copy(w_ref, w_vmem, in_sems.at[GRID_PARTS])]
    for k in range(GRID_PARTS):
        span = pl.ds(k * part, part)
        fetches.append(pltpu.make_async_copy(grid_ref.at[span], grid_vmem.at[span], in_sems.at[k]))
    for fetch in fetches:
        fetch.start()
    inner = lax.axis_index("inner")
    offsets = band_offsets()
    keys = [(t, p, k) for t in range(3) for p in range(pair_count) for k in range(2)]
    place = {(t, p, k): (offsets[t], inner ^ (2 * p + k)) for t, p, k in keys}
    by_slot = slot_columns(source_ref, [place[key] for key in keys])
    left, right = slice(0, half), slice(half, 2 * half)
    runs = [[([(t, p, k) for p in range(pair_count)], left)] for t in range(2) for k in range(2)]
    runs += [[([(t, p, k) for t in range(3)], right)] for p in range(1, pair_count) for k in range(2)]
    runs += [
        [([(2, p, k) for p in range(pair_count)], left), ([(t, 0, k) for t in range(3)], right)] for k in range(2)
    ]
    for out_vmem, parts in zip(out_vmems, runs):
        start = 0
        for chosen, _ in parts:
            start += len(chosen) * cap
            out_vmem[start : start + TILE, :] = target_tile(target_ref, count_ref, [place[key] for key in chosen], half)
            start += TILE
    fetches[0].wait()
    for k in range(GRID_PARTS):
        span = pl.ds(k * part, part)
        fetches[k + 1].wait()
        message_ref[span] = jax.nn.silu(dot(grid_vmem[span], w_vmem[...])).astype(jnp.bfloat16)
    row = lax.broadcasted_iota(jnp.int32, (cap, rows), 1)
    picks = {
        key: jnp.where(row == by_slot[:, m : m + 1], 1.0, 0.0).astype(jnp.bfloat16) for m, key in enumerate(keys)
    }
    sends = []
    for n, parts in enumerate(runs):
        start = 0
        for chosen, lanes in parts:
            taken = dot(jnp.concatenate([picks[key] for key in chosen], axis=0), message_ref[:, lanes])
            out_vmems[n][start : start + len(chosen) * cap, :] = taken.astype(jnp.bfloat16)
            start += len(chosen) * cap + TILE
        send = pltpu.make_async_copy(out_vmems[n], out_refs[n], out_sems.at[n])
        send.start()
        sends.append(send)
    for send in sends:
        send.wait()


def node_sums(arrays, nodes):
    count = arrays[0][2]
    cap = CAP
    node = lax.broadcasted_iota(jnp.int32, (nodes, cap), 0)
    targets = [
        ref[start + count * cap : start + count * cap + TILE, 0:cap].astype(jnp.float32).astype(jnp.int32)
        for ref, start, _ in arrays
    ]
    for n in range(count):
        hits = [jnp.where(node == t[n : n + 1], 1.0, 0.0).astype(jnp.bfloat16) for t in targets]
        rows = [ref[start + n * cap : start + (n + 1) * cap, :] for ref, start, _ in arrays]
        yield n, dot(jnp.concatenate(hits, axis=1), jnp.concatenate(rows, axis=0))


def early_kernel(pair_count, w_ref, own_ref, other_ref, query_ref, key_ref, value_ref, left_ref, right_ref):
    width = w_ref.shape[0]
    head_dim = width // HEADS
    span = 3 * LANES
    row = lax.broadcasted_iota(jnp.int32, (LANES, span), 0)
    column = lax.broadcasted_iota(jnp.int32, (LANES, span), 1)
    wanted = row // head_dim * (3 * head_dim) + row % head_dim
    for c, out_ref in enumerate((query_ref, key_ref, value_ref)):
        pick = jnp.where(column == wanted + c * head_dim, 1.0, 0.0).astype(jnp.bfloat16)
        for g in range(width // LANES):
            part = dot_t(pick, w_ref[:, g * span : (g + 1) * span])
            out_ref[g * LANES : (g + 1) * LANES, :] = part.astype(jnp.bfloat16)
    start = 0
    for sum_ref in (left_ref, right_ref):
        count, nodes, _ = sum_ref.shape
        for n, total in node_sums([(own_ref, start, count), (other_ref, start, count)], nodes):
            sum_ref[n] = total
        start += count * CAP + TILE


def sums_kernel(array_count, kept, *refs):
    row_refs, early_ref, out_refs = refs[:array_count], refs[array_count], refs[array_count + 1 :]
    count, nodes, _ = early_ref.shape
    for n, total in node_sums([(r, 0, count) for r in row_refs], nodes):
        total = total + early_ref[n]
        out_refs[n][...] = total if n == kept else total.astype(jnp.bfloat16)


def merge_kernel(*refs):
    *part_refs, right_ref, even_ref, odd_ref, mesh_ref, w_ref, gain_ref, state_ref, normed_ref, top_ref, bottom_ref = refs
    left = functools.reduce(jnp.add, [r[...].astype(jnp.float32) for r in part_refs])
    right = right_ref[...] + even_ref[...].astype(jnp.float32) + odd_ref[...].astype(jnp.float32)
    total = jnp.concatenate([left, right], axis=1).astype(jnp.bfloat16)
    state = mesh_ref[...].astype(jnp.float32) + dot(total, w_ref[...])
    state_ref[...] = state
    normed = layer_norm(state, gain_ref[...]).astype(jnp.bfloat16)
    normed_ref[...] = normed
    top_ref[...] = normed[:NEAR]
    bottom_ref[...] = normed[NEAR:]


def project_keys(rows, wk_ref, wv_ref, key_ref, value_ref, start):
    count = rows.shape[0]
    groups = key_ref.shape[0]
    heads = value_ref.shape[0]
    keys = dot_t(rows, wk_ref[...]).astype(jnp.bfloat16)
    for g in range(groups):
        key_ref[g, start : start + count, :] = keys[:, g * LANES : (g + 1) * LANES]
    values = dot_t(wv_ref[...], rows).astype(jnp.bfloat16)
    value_ref[:, 0 : values.shape[0] // heads, start : start + count] = values.reshape(
        heads, -1, count
    )


def near_kernel(
    own_ref, side_ref, wq_ref, wk_ref, wv_ref, order_ref, window_ref,
    query_ref, sums_ref, top_ref,
    key_ref, value_ref, gap_ref,
):
    nodes, width = own_ref.shape
    head_dim = width // HEADS
    per_group = LANES // head_dim
    odd = lax.rem(lax.axis_index("inner"), 2)
    side = 1 - 2 * odd
    first = odd * (nodes - NEAR)
    second = (1 - odd) * NEAR
    scale = head_dim ** (-0.5) / math.log(2.0)

    queries = dot_t(wq_ref[...], own_ref[...]).astype(jnp.bfloat16)
    part = lax.broadcasted_iota(jnp.int32, (LANES, nodes), 0) // head_dim
    for h in range(HEADS):
        g = h // per_group
        lanes = queries[g * LANES : (g + 1) * LANES]
        query_ref[h] = jnp.where(part == h % per_group, lanes, jnp.zeros_like(lanes))
    value_ref[:, head_dim:, :] = jnp.ones_like(value_ref[:, head_dim:, :])
    project_keys(own_ref[...], wk_ref, wv_ref, key_ref, value_ref, 0)
    project_keys(side_ref[pl.ds(pl.multiple_of(first, NEAR), NEAR), :], wk_ref, wv_ref, key_ref, value_ref, nodes)
    project_keys(
        side_ref[pl.ds(pl.multiple_of(second, NEAR), NEAR), :], wk_ref, wv_ref, key_ref, value_ref, nodes + NEAR
    )
    lag = lax.broadcasted_iota(jnp.int32, (nodes, nodes), 0) - lax.broadcasted_iota(
        jnp.int32, (nodes, nodes), 1
    )
    gap_ref[0:nodes] = jnp.abs(lag)
    gap_ref[nodes : nodes + NEAR] = jnp.abs(lag[0:NEAR] + (side * nodes + first))
    gap_ref[nodes + NEAR : 2 * nodes] = jnp.abs(lag[0:NEAR] + (side * nodes + second))

    def attend(heads, rows):
        scores = [dot(key_ref[h // per_group, 0:rows, :], query_ref[h]) for h in heads]
        scores = [
            jnp.where(gap_ref[0:rows] <= window_ref[h], x, -1e30) for h, x in zip(heads, scores)
        ]
        tops = [jnp.max(x, axis=0, keepdims=True) for x in scores]
        expos = [jnp.exp2((x - top) * scale).astype(jnp.bfloat16) for x, top in zip(scores, tops)]
        for h, top, expo in zip(heads, tops, expos):
            sums_ref[h] = dot(value_ref[h, :, 0:rows], expo)
            top_ref[h] = jnp.broadcast_to(top, top_ref.shape[1:])

    def together(i, carry):
        heads = [order_ref[GROUP * i + k] for k in range(GROUP)]
        widest = functools.reduce(jnp.maximum, [window_ref[h] for h in heads])

        @pl.when(widest <= NEAR)
        def _():
            attend(heads, nodes + NEAR)

        @pl.when(widest > NEAR)
        def _():
            attend(heads, 2 * nodes)

        return carry

    lax.fori_loop(0, HEADS // GROUP, together, 0)


def more_attention(
    by_pair, other_top, other_bottom, block_top, block_bottom, wk_ref, wv_ref, order_ref, window_ref,
    query_ref, sums_ref, top_ref, key_ref, value_ref, gap_ref, store,
):
    cap = block_top.shape[0]
    nodes = 2 * cap
    head_dim = wv_ref.shape[0] // HEADS
    per_group = LANES // head_dim
    total = lax.axis_size("band") * lax.axis_size("inner")
    me = lax.axis_index("band") * lax.axis_size("inner") + lax.axis_index("inner")
    odd = lax.rem(me, 2)
    chip_odd = lax.rem(me // 2, 2)
    ahead = (1 - 2 * chip_odd) * (1 if by_pair else -1)
    closer = odd == (ahead + 1) // 2
    scale = head_dim ** (-0.5) / math.log(2.0)

    value_ref[:, head_dim:, :] = jnp.ones_like(value_ref[:, head_dim:, :])
    lag = lax.broadcasted_iota(jnp.int32, (nodes, nodes), 0) - lax.broadcasted_iota(
        jnp.int32, (nodes, nodes), 1
    )

    def gap(rows, device, offset):
        inside = (me + device >= 0) & (me + device < total)
        return jnp.where(inside, jnp.abs(rows + (device * nodes + offset)), 1 << 20)

    @pl.when(closer)
    def _():
        top, bottom = other_top[...], other_bottom[...]
        project_keys(jnp.where(odd == 1, top, bottom), wk_ref, wv_ref, key_ref, value_ref, 0)
        project_keys(jnp.where(odd == 1, bottom, top), wk_ref, wv_ref, key_ref, value_ref, cap)
        gap_ref[0:cap] = gap(lag[0:cap], ahead, (1 - odd) * cap)
        gap_ref[cap:nodes] = gap(lag[0:cap], ahead, odd * cap)

    project_keys(block_top[...], wk_ref, wv_ref, key_ref, value_ref, nodes)
    project_keys(block_bottom[...], wk_ref, wv_ref, key_ref, value_ref, nodes + cap)
    gap_ref[nodes : 2 * nodes] = gap(lag, 2 * ahead, 0)

    def attend(heads, start, stop):
        olds = [top_ref[h, 0:1, :] for h in heads]
        if start == stop:
            for h, old in zip(heads, olds):
                store(h, sums_ref[h], old)
            return
        scores = [dot(key_ref[h // per_group, start:stop, :], query_ref[h]) for h in heads]
        scores = [
            jnp.where(gap_ref[start:stop] <= window_ref[h], x, -1e30) for h, x in zip(heads, scores)
        ]
        tops = [jnp.maximum(old, jnp.max(x, axis=0, keepdims=True)) for old, x in zip(olds, scores)]
        expos = [jnp.exp2((x - top) * scale).astype(jnp.bfloat16) for x, top in zip(scores, tops)]
        for h, old, top, expo in zip(heads, olds, tops, expos):
            sums = sums_ref[h] * jnp.exp2((old - top) * scale) + dot(value_ref[h, :, start:stop], expo)
            store(h, sums, top)

    def together(i, carry):
        heads = [order_ref[GROUP * i + k] for k in range(GROUP)]
        widest = functools.reduce(jnp.maximum, [window_ref[h] for h in heads])
        cases = (
            (closer & (widest <= cap), 0, cap),
            (closer & (widest > cap) & (widest <= nodes), 0, nodes),
            (closer & (widest > nodes), 0, 2 * nodes),
            (jnp.logical_not(closer) & (widest > nodes), nodes, 2 * nodes),
            (jnp.logical_not(closer) & (widest <= nodes), 0, 0),
        )
        for case, start, stop in cases:
            pl.when(case)(functools.partial(attend, heads, start, stop))
        return carry

    lax.fori_loop(0, HEADS // GROUP, together, 0)


def mid_kernel(*refs):
    operands, (sums_out, top_out), scratch = refs[:11], refs[11:13], refs[13:]

    def store(h, sums, top):
        sums_out[h] = sums
        top_out[h] = jnp.broadcast_to(top, top_out.shape[1:])

    more_attention(True, *operands, *scratch, store)


def far_kernel(*refs):
    operands, rest = refs[:11], refs[11:]
    state_ref, w_out_ref, gain_ref, up_ref, down_ref, out_ref, attended_ref, *scratch = rest
    nodes, width = out_ref.shape
    head_dim = width // HEADS

    def store(h, sums, top):
        attended_ref[h] = (sums[0:head_dim] / sums[head_dim : head_dim + 1]).astype(jnp.bfloat16)

    more_attention(False, *operands, *scratch, store)
    attended = attended_ref[...].reshape(width, nodes)
    mixed = lax.dot_general(
        attended, w_out_ref[...], (((0,), (0,)), ((), ())), preferred_element_type=jnp.float32
    )
    mid = state_ref[...] + mixed
    normed = layer_norm(mid, gain_ref[...]).astype(jnp.bfloat16)
    hidden = jax.nn.silu(dot(normed, up_ref[...])).astype(jnp.bfloat16)
    out_ref[...] = (mid + dot(hidden, down_ref[...])).astype(jnp.bfloat16)


def cost(flops, size):
    return pl.CostEstimate(flops=flops, bytes_accessed=size, transcendentals=0)


def local(
    grid_rows,
    mesh_rows,
    edge_source,
    edge_target,
    edge_count,
    w_message,
    w_merge,
    gain_attn,
    w_qkv,
    window,
    w_out,
    gain_mlp,
    w_up,
    w_down,
):
    bands = lax.axis_size("band")
    inners = lax.axis_size("inner")
    devices = bands * inners
    grid_dev = grid_rows.shape[0]
    nodes, width = mesh_rows.shape
    cap = edge_source.shape[-1]
    head_dim = width // HEADS
    pairs = inners // 2
    half = width // 2
    f32, bf16, i32 = jnp.float32, jnp.bfloat16, jnp.int32
    edges = (edge_source, edge_target, jnp.transpose(edge_count, (0, 2, 1, 3)))

    def rows_of(*blocks):
        return jax.ShapeDtypeStruct((sum(n * cap + TILE for n in blocks), half), bf16)

    outgoing = [rows_of(pairs)] * 4 + [rows_of(3)] * (2 * pairs - 2) + [rows_of(pairs, 3)] * 2
    even, even_other, odd, odd_other, *cross, here, here_other = pl.pallas_call(
        functools.partial(message_kernel, pairs),
        out_shape=outgoing,
        in_specs=[ANY] * 2 + [VMEM] * 2 + [SMEM],
        out_specs=[ANY] * len(outgoing),
        scratch_shapes=[pltpu.VMEM(a.shape, bf16) for a in outgoing]
        + [
            pltpu.VMEM(grid_rows.shape, bf16),
            pltpu.VMEM(w_message.shape, bf16),
            pltpu.VMEM((grid_dev, width), bf16),
            pltpu.SemaphoreType.DMA((GRID_PARTS + 1,)),
            pltpu.SemaphoreType.DMA((len(outgoing),)),
        ],
        compiler_params=params(MOST),
        cost_estimate=cost(2 * grid_dev * width * (width + 3 * inners * cap), 4 << 20),
        name="messages",
    )(grid_rows, w_message, *edges)
    beside = [(g, g ^ 1) for g in range(devices)]

    def bands_trade(odd_pairs):
        route = []
        for g in range(devices):
            b = g // inners
            t = (b - odd_pairs ^ 1) + odd_pairs
            route.append((g, t * inners + g % inners if 0 <= t < bands else g ^ 1))
        return route

    def chip_trade(p):
        return [(g, g ^ (2 * p)) for g in range(devices)]

    even_other = lax.ppermute(even_other, NODES, beside)
    cross_other = [lax.ppermute(c, NODES, beside) for c in cross[1::2]]
    odd_other = lax.ppermute(odd_other, NODES, beside)
    cross = [lax.ppermute(c, NODES, chip_trade(p + 1)) for p, c in enumerate(cross[0::2])]
    even = lax.ppermute(even, NODES, bands_trade(0))
    odd = lax.ppermute(odd, NODES, bands_trade(1))
    cross_other = [lax.ppermute(c, NODES, chip_trade(p + 1)) for p, c in enumerate(cross_other)]
    even_other = lax.ppermute(even_other, NODES, bands_trade(0))
    odd_other = lax.ppermute(odd_other, NODES, bands_trade(1))
    here_other = lax.ppermute(here_other, NODES, beside)

    w_qkv, window, here = lax.optimization_barrier((w_qkv, window, here))
    w_query, w_key, w_value, early_left, early_right = pl.pallas_call(
        functools.partial(early_kernel, pairs),
        out_shape=[jax.ShapeDtypeStruct((width, width), bf16)] * 3
        + [jax.ShapeDtypeStruct((n, nodes, half), f32) for n in (pairs, 3)],
        in_specs=[VMEM] * 3,
        out_specs=[VMEM] * 5,
        compiler_params=params(24),
        cost_estimate=cost(1 << 28, 4 << 20),
        name="early",
    )(w_qkv, here, here_other)
    head = jnp.arange(HEADS, dtype=i32)
    ahead = (window[None, :] > window[:, None]) | (
        (window[None, :] == window[:, None]) & (head[None, :] < head[:, None])
    )
    rank = jnp.sum(ahead.astype(i32), axis=1)
    order = jnp.sum(jnp.where(rank[None, :] == head[:, None], head[None, :], 0), axis=1).astype(i32)

    def sums(arrays, early, kept, name):
        count = early.shape[0]
        return pl.pallas_call(
            functools.partial(sums_kernel, len(arrays), kept),
            out_shape=[jax.ShapeDtypeStruct((nodes, half), f32 if n == kept else bf16) for n in range(count)],
            in_specs=[VMEM] * (len(arrays) + 1),
            out_specs=[VMEM] * count,
            compiler_params=params(24),
            cost_estimate=cost(2 * nodes * half * len(arrays) * count * cap, 2 << 20),
            name=name,
        )(*arrays, early)

    left, *parts = sums([even, even_other, odd, odd_other], early_left, 0, "left")
    parts = [lax.ppermute(part, NODES, chip_trade(p + 1)) for p, part in enumerate(parts)]
    to_even, to_odd, right = sums([*cross, *cross_other], early_right, 2, "right")
    from_even = lax.ppermute(to_even, NODES, bands_trade(0))
    from_odd = lax.ppermute(to_odd, NODES, bands_trade(1))

    state, normed, top_rows, bottom_rows = pl.pallas_call(
        merge_kernel,
        out_shape=[jax.ShapeDtypeStruct((nodes, width), f32)]
        + [jax.ShapeDtypeStruct((n, width), bf16) for n in (nodes, NEAR, nodes - NEAR)],
        in_specs=[VMEM] * (pairs + 6),
        out_specs=[VMEM] * 4,
        compiler_params=params(24),
        cost_estimate=cost(2 * nodes * width * width, 2 << 20),
        name="merge",
    )(left, *parts, right, from_even, from_odd, mesh_rows, w_merge, gain_attn.reshape(1, width))

    def chips_trade(odd_pairs):
        route = []
        for g in range(devices):
            t = (g // 2 - odd_pairs ^ 1) + odd_pairs
            route.append((g, 2 * t + g % 2 if 0 <= 2 * t < devices else g ^ 1))
        return route

    side = lax.ppermute(normed, NODES, beside)
    pair_top = lax.ppermute(top_rows, NODES, chips_trade(0))
    pair_bottom = lax.ppermute(bottom_rows, NODES, chips_trade(0))

    extra = head_dim + 16
    query, near, top = pl.pallas_call(
        near_kernel,
        out_shape=[
            jax.ShapeDtypeStruct((HEADS, LANES, nodes), bf16),
            jax.ShapeDtypeStruct((HEADS, extra, nodes), f32),
            jax.ShapeDtypeStruct((HEADS, 8, nodes), f32),
        ],
        in_specs=[VMEM] * 5 + [SMEM] * 2,
        out_specs=[VMEM] * 3,
        scratch_shapes=[
            pltpu.VMEM((width // LANES, 2 * nodes, LANES), bf16),
            pltpu.VMEM((HEADS, extra, 2 * nodes), bf16),
            pltpu.VMEM((2 * nodes, nodes), i32),
        ],
        compiler_params=params(32),
        cost_estimate=cost(8 << 30, 4 << 20),
        name="near",
    )(normed, side, w_query, w_key, w_value, order, window)

    top_rows, bottom_rows, pair_top, pair_bottom, near, top = lax.optimization_barrier(
        (top_rows, bottom_rows, pair_top, pair_bottom, near, top)
    )
    other_top = lax.ppermute(top_rows, NODES, chips_trade(1))
    if pairs == 2:
        route = []
        for g in range(devices):
            x = g // 2 % 2
            t = g + inners * (1 - 2 * x)
            route.append((g, t if 0 <= t < devices else g ^ 2))
        other_bottom = lax.ppermute(pair_bottom, NODES, route)
    else:
        other_bottom = lax.ppermute(bottom_rows, NODES, chips_trade(1))
    beside_top = lax.ppermute(pair_top, NODES, beside)
    beside_bottom = lax.ppermute(pair_bottom, NODES, beside)

    weights = (w_key, w_value, order, window)
    scratch = [
        pltpu.VMEM((width // LANES, 2 * nodes, LANES), bf16),
        pltpu.VMEM((HEADS, extra, 2 * nodes), bf16),
        pltpu.VMEM((2 * nodes, nodes), i32),
    ]
    near, top = pl.pallas_call(
        mid_kernel,
        out_shape=[
            jax.ShapeDtypeStruct((HEADS, extra, nodes), f32),
            jax.ShapeDtypeStruct((HEADS, 8, nodes), f32),
        ],
        in_specs=[VMEM] * 6 + [SMEM] * 2 + [VMEM] * 3,
        out_specs=[VMEM] * 2,
        scratch_shapes=scratch,
        compiler_params=params(32),
        cost_estimate=cost(4 << 30, 4 << 20),
        name="mid",
    )(beside_top, beside_bottom, pair_top, pair_bottom, *weights, query, near, top)

    other_top, other_bottom, near, top = lax.optimization_barrier((other_top, other_bottom, near, top))
    beside_top = lax.ppermute(other_top, NODES, beside)
    beside_bottom = lax.ppermute(other_bottom, NODES, beside)
    return pl.pallas_call(
        far_kernel,
        out_shape=jax.ShapeDtypeStruct((nodes, width), bf16),
        in_specs=[VMEM] * 6 + [SMEM] * 2 + [VMEM] * 8,
        out_specs=VMEM,
        scratch_shapes=[pltpu.VMEM((HEADS, head_dim, nodes), bf16)] + scratch,
        compiler_params=params(40),
        cost_estimate=cost(8 << 30, 8 << 20),
        name="far",
    )(
        beside_top, beside_bottom, other_top, other_bottom, *weights,
        query, near, top, state, w_out, gain_mlp.reshape(1, width), w_up, w_down,
    )


def solution(mesh):
    placed = (
        P(("groups", "band", "inner"), None),
        P(("groups", "band", "inner"), None),
        P(("groups", "band"), "inner", None, None, None),
        P(("groups", "band"), "inner", None, None, None),
        P(("groups", "band"), "inner", None, None),
        P(),
        P(),
        P(),
        P(),
        P("groups"),
        P(),
        P(),
        P(),
        P(),
    )
    return jax.shard_map(
        local,
        mesh=mesh,
        in_specs=placed,
        out_specs=P(("groups", "band", "inner"), None),
        check_vma=False,
    )
```

```python
import functools
import math

import jax
import jax.numpy as jnp
from jax import lax
from jax.experimental import pallas as pl
from jax.experimental.pallas import tpu as pltpu
from jax.sharding import PartitionSpec as P

HEADS = 16
WMAX = 512
LANES = 128
NEAR = 128
TILE = 16
CAP = 128
GRID_PARTS = 4
MOST = 56
GROUP = 4

norm_eps = 1e-05
NODES = ("band", "inner")
VMEM = pl.BlockSpec(memory_space=pltpu.VMEM)
SMEM = pl.BlockSpec(memory_space=pltpu.SMEM)
ANY = pl.BlockSpec(memory_space=pl.ANY)


def params(mib):
    return pltpu.CompilerParams(vmem_limit_bytes=mib * 1024 * 1024)


def dot(a, b):
    return jnp.dot(a, b, preferred_element_type=jnp.float32)


def dot_t(a, b):
    return lax.dot_general(a, b, (((1,), (1,)), ((), ())), preferred_element_type=jnp.float32)


def layer_norm(values, gain):
    center = values - jnp.mean(values, axis=-1, keepdims=True)
    spread = jnp.mean(center * center, axis=-1, keepdims=True)
    return center * lax.rsqrt(spread + norm_eps) * gain


def band_offsets():
    ahead = lax.rem(lax.axis_index("band"), 2) * 2
    return 2 - ahead, ahead, 1


def slot_columns(source_ref, blocks):
    sources = jnp.concatenate([source_ref[0, 0, o, pl.ds(j, 1), :] for o, j in blocks], axis=0)
    return jnp.transpose(sources.astype(jnp.float32)).astype(jnp.int32)


def target_tile(target_ref, count_ref, blocks, lanes):
    cap = target_ref.shape[-1]
    slot = lax.broadcasted_iota(jnp.int32, (1, cap), 1)
    targets = [
        jnp.where(slot < count_ref[0, o, 0, j], target_ref[0, 0, o, pl.ds(j, 1), :], -1) for o, j in blocks
    ]
    targets.append(jnp.full((TILE - len(blocks), cap), -1, jnp.int32))
    tile = jnp.concatenate(targets, axis=0).astype(jnp.float32).astype(jnp.bfloat16)
    return jnp.concatenate([tile] * (lanes // cap), axis=1)


def message_kernel(pair_count, grid_ref, w_ref, source_ref, target_ref, count_ref, *refs):
    count = 4 + 2 * pair_count
    out_refs, out_vmems = refs[:count], refs[count : 2 * count]
    grid_vmem, w_vmem, message_ref, in_sems, out_sems = refs[2 * count :]
    rows = grid_ref.shape[0]
    cap = source_ref.shape[-1]
    half = w_ref.shape[1] // 2
    part = rows // GRID_PARTS
    fetches = [pltpu.make_async_copy(w_ref, w_vmem, in_sems.at[GRID_PARTS])]
    for k in range(GRID_PARTS):
        span = pl.ds(k * part, part)
        fetches.append(pltpu.make_async_copy(grid_ref.at[span], grid_vmem.at[span], in_sems.at[k]))
    for fetch in fetches:
        fetch.start()
    inner = lax.axis_index("inner")
    offsets = band_offsets()
    keys = [(t, p, k) for t in range(3) for p in range(pair_count) for k in range(2)]
    place = {(t, p, k): (offsets[t], inner ^ (2 * p + k)) for t, p, k in keys}
    by_slot = slot_columns(source_ref, [place[key] for key in keys])
    left, right = slice(0, half), slice(half, 2 * half)
    runs = [[([(t, p, k) for p in range(pair_count)], left)] for t in range(2) for k in range(2)]
    runs += [[([(t, p, k) for t in range(3)], right)] for p in range(1, pair_count) for k in range(2)]
    runs += [
        [([(2, p, k) for p in range(pair_count)], left), ([(t, 0, k) for t in range(3)], right)] for k in range(2)
    ]
    for out_vmem, parts in zip(out_vmems, runs):
        start = 0
        for chosen, _ in parts:
            start += len(chosen) * cap
            out_vmem[start : start + TILE, :] = target_tile(target_ref, count_ref, [place[key] for key in chosen], half)
            start += TILE
    fetches[0].wait()
    for k in range(GRID_PARTS):
        span = pl.ds(k * part, part)
        fetches[k + 1].wait()
        message_ref[span] = jax.nn.silu(dot(grid_vmem[span], w_vmem[...])).astype(jnp.bfloat16)
    row = lax.broadcasted_iota(jnp.int32, (cap, rows), 1)
    picks = {
        key: jnp.where(row == by_slot[:, m : m + 1], 1.0, 0.0).astype(jnp.bfloat16) for m, key in enumerate(keys)
    }
    sends = []
    for n in reversed(range(count)):
        start = 0
        for chosen, lanes in runs[n]:
            taken = dot(jnp.concatenate([picks[key] for key in chosen], axis=0), message_ref[:, lanes])
            out_vmems[n][start : start + len(chosen) * cap, :] = taken.astype(jnp.bfloat16)
            start += len(chosen) * cap + TILE
        send = pltpu.make_async_copy(out_vmems[n], out_refs[n], out_sems.at[n])
        send.start()
        sends.append(send)
    for send in sends:
        send.wait()


def node_sums(arrays, nodes):
    count = arrays[0][2]
    cap = CAP
    node = lax.broadcasted_iota(jnp.int32, (nodes, cap), 0)
    targets = [
        ref[start + count * cap : start + count * cap + TILE, 0:cap].astype(jnp.float32).astype(jnp.int32)
        for ref, start, _ in arrays
    ]
    for n in range(count):
        hits = [jnp.where(node == t[n : n + 1], 1.0, 0.0).astype(jnp.bfloat16) for t in targets]
        rows = [ref[start + n * cap : start + (n + 1) * cap, :] for ref, start, _ in arrays]
        yield n, dot(jnp.concatenate(hits, axis=1), jnp.concatenate(rows, axis=0))


def early_kernel(pair_count, w_ref, own_ref, other_ref, query_ref, key_ref, value_ref, left_ref, right_ref):
    width = w_ref.shape[0]
    head_dim = width // HEADS
    span = 3 * LANES
    def pick(c, along):
        shape = (LANES, span) if along else (span, LANES)
        to = lax.broadcasted_iota(jnp.int32, shape, 1 - along)
        column = lax.broadcasted_iota(jnp.int32, shape, along)
        wanted = to // head_dim * (3 * head_dim) + to % head_dim + c * head_dim
        return jnp.where(column == wanted, 1.0, 0.0).astype(jnp.bfloat16)

    for g in range(width // LANES):
        columns = w_ref[:, g * span : (g + 1) * span]
        part = slice(g * LANES, (g + 1) * LANES)
        query_ref[part, :] = dot_t(pick(0, 1), columns).astype(jnp.bfloat16)
        key_ref[:, part] = dot(columns, pick(1, 0)).astype(jnp.bfloat16)
        value_ref[part, :] = dot_t(pick(2, 1), columns).astype(jnp.bfloat16)
    start = 0
    for sum_ref in (left_ref, right_ref):
        count, nodes, _ = sum_ref.shape
        for n, total in node_sums([(own_ref, start, count), (other_ref, start, count)], nodes):
            sum_ref[n] = total
        start += count * CAP + TILE


def sums_kernel(array_count, kept, *refs):
    row_refs, early_ref, out_refs = refs[:array_count], refs[array_count], refs[array_count + 1 :]
    count, nodes, _ = early_ref.shape
    for n, total in node_sums([(r, 0, count) for r in row_refs], nodes):
        total = total + early_ref[n]
        out_refs[n][...] = total if n == kept else total.astype(jnp.bfloat16)


def merge_kernel(*refs):
    *part_refs, right_ref, even_ref, odd_ref, mesh_ref, w_ref, gain_ref, state_ref, normed_ref = refs
    left = functools.reduce(jnp.add, [r[...].astype(jnp.float32) for r in part_refs])
    right = right_ref[...] + even_ref[...].astype(jnp.float32) + odd_ref[...].astype(jnp.float32)
    total = jnp.concatenate([left, right], axis=1).astype(jnp.bfloat16)
    state = mesh_ref[...].astype(jnp.float32) + dot(total, w_ref[...])
    state_ref[...] = state
    normed_ref[...] = layer_norm(state, gain_ref[...]).astype(jnp.bfloat16)


def project_keys(rows, wk_ref, wv_ref, key_ref, value_ref, start):
    count = rows.shape[0]
    groups = key_ref.shape[0]
    heads = value_ref.shape[0]
    keys = dot(rows, wk_ref[...]).astype(jnp.bfloat16)
    for g in range(groups):
        key_ref[g, start : start + count, :] = keys[:, g * LANES : (g + 1) * LANES]
    values = dot_t(wv_ref[...], rows).astype(jnp.bfloat16)
    value_ref[:, 0 : values.shape[0] // heads, start : start + count] = values.reshape(
        heads, -1, count
    )


def near_kernel(
    own_ref, side_ref, wq_ref, wk_ref, wv_ref, order_ref, window_ref,
    query_ref, sums_ref, top_ref,
    key_ref, value_ref, gap_ref,
):
    nodes, width = own_ref.shape
    head_dim = width // HEADS
    per_group = LANES // head_dim
    odd = lax.rem(lax.axis_index("inner"), 2)
    side = 1 - 2 * odd
    first = odd * (nodes - NEAR)
    second = (1 - odd) * NEAR
    scale = head_dim ** (-0.5) / math.log(2.0)

    queries = dot_t(wq_ref[...], own_ref[...]).astype(jnp.bfloat16)
    part = lax.broadcasted_iota(jnp.int32, (LANES, nodes), 0) // head_dim
    for h in range(HEADS):
        g = h // per_group
        lanes = queries[g * LANES : (g + 1) * LANES]
        query_ref[h] = jnp.where(part == h % per_group, lanes, jnp.zeros_like(lanes))
    value_ref[:, head_dim:, :] = jnp.ones_like(value_ref[:, head_dim:, :])
    project_keys(own_ref[...], wk_ref, wv_ref, key_ref, value_ref, 0)
    project_keys(side_ref[pl.ds(pl.multiple_of(first, NEAR), NEAR), :], wk_ref, wv_ref, key_ref, value_ref, nodes)
    project_keys(
        side_ref[pl.ds(pl.multiple_of(second, NEAR), NEAR), :], wk_ref, wv_ref, key_ref, value_ref, nodes + NEAR
    )
    lag = lax.broadcasted_iota(jnp.int32, (nodes, nodes), 0) - lax.broadcasted_iota(
        jnp.int32, (nodes, nodes), 1
    )
    gap_ref[0:nodes] = jnp.abs(lag)
    gap_ref[nodes : nodes + NEAR] = jnp.abs(lag[0:NEAR] + (side * nodes + first))
    gap_ref[nodes + NEAR : 2 * nodes] = jnp.abs(lag[0:NEAR] + (side * nodes + second))

    def attend(heads, rows):
        scores = [dot(key_ref[h // per_group, 0:rows, :], query_ref[h]) for h in heads]
        scores = [
            jnp.where(gap_ref[0:rows] <= window_ref[h], x, -1e30) for h, x in zip(heads, scores)
        ]
        tops = [jnp.max(x, axis=0, keepdims=True) for x in scores]
        expos = [jnp.exp2((x - top) * scale).astype(jnp.bfloat16) for x, top in zip(scores, tops)]
        for h, top, expo in zip(heads, tops, expos):
            sums_ref[h] = dot(value_ref[h, :, 0:rows], expo)
            top_ref[h] = jnp.broadcast_to(top, top_ref.shape[1:])

    def together(i, carry):
        heads = [order_ref[GROUP * i + k] for k in range(GROUP)]
        widest = functools.reduce(jnp.maximum, [window_ref[h] for h in heads])

        @pl.when(widest <= NEAR)
        def _():
            attend(heads, nodes + NEAR)

        @pl.when(widest > NEAR)
        def _():
            attend(heads, 2 * nodes)

        return carry

    lax.fori_loop(0, HEADS // GROUP, together, 0)


def outer_kernel(even_ref, odd_ref, wk_ref, wv_ref, key_ref, value_ref):
    nodes, width = even_ref.shape
    head_dim = width // HEADS
    value_ref[:, head_dim:, :] = jnp.ones_like(value_ref[:, head_dim:, :])
    project_keys(even_ref[...], wk_ref, wv_ref, key_ref, value_ref, 0)
    project_keys(odd_ref[...], wk_ref, wv_ref, key_ref, value_ref, nodes)


def far_kernel(
    first_ref, second_ref, far_key_ref, far_value_ref, wk_ref, wv_ref, order_ref, window_ref,
    query_ref, sums_ref, top_ref, state_ref, w_out_ref, gain_ref, up_ref, down_ref,
    out_ref,
    key_ref, value_ref, gap_ref, attended_ref,
):
    nodes, width = first_ref.shape
    head_dim = width // HEADS
    per_group = LANES // head_dim
    total = lax.axis_size("band") * lax.axis_size("inner")
    me = lax.axis_index("band") * lax.axis_size("inner") + lax.axis_index("inner")
    odd = lax.rem(me, 2)
    far = 2 - 4 * lax.rem(me // 2, 2)
    side = 2 * odd - 1
    first = (1 - odd) * (nodes - NEAR)
    second = odd * NEAR
    scale = head_dim ** (-0.5) / math.log(2.0)
    absent = 1 << 20

    value_ref[:, head_dim:, :] = jnp.ones_like(value_ref[:, head_dim:, :])
    by_even = odd == lax.rem(me // 2 + 1, 2)
    beyond = jnp.where(by_even, first_ref[...], second_ref[...])
    beyond = jnp.where(odd == 0, jnp.concatenate([beyond[NEAR:], beyond[:NEAR]], axis=0), beyond)
    project_keys(beyond, wk_ref, wv_ref, key_ref, value_ref, 0)
    lag = lax.broadcasted_iota(jnp.int32, (nodes, nodes), 0) - lax.broadcasted_iota(
        jnp.int32, (nodes, nodes), 1
    )

    def gap(rows, device, offset):
        inside = (me + device >= 0) & (me + device < total)
        return jnp.where(inside, jnp.abs(rows + (device * nodes + offset)), absent)

    gap_ref[0:NEAR] = gap(lag[0:NEAR], side, first)
    gap_ref[NEAR:nodes] = gap(lag[0:NEAR], side, second)
    gap_ref[nodes : 2 * nodes] = gap(lag, far, 0)
    gap_ref[2 * nodes : 3 * nodes] = gap(lag, -far, 0)

    def attend(heads, rows):
        close = min(rows, nodes)
        scores = [dot(key_ref[h // per_group, 0:close, :], query_ref[h]) for h in heads]
        if rows > close:
            scores = [
                jnp.concatenate([x, dot(far_key_ref[h // per_group], query_ref[h])], axis=0)
                for h, x in zip(heads, scores)
            ]
        scores = [
            jnp.where(gap_ref[0:rows] <= window_ref[h], x, -1e30) for h, x in zip(heads, scores)
        ]
        olds = [top_ref[h, 0:1, :] for h in heads]
        tops = [jnp.maximum(old, jnp.max(x, axis=0, keepdims=True)) for old, x in zip(olds, scores)]
        expos = [jnp.exp2((x - top) * scale).astype(jnp.bfloat16) for x, top in zip(scores, tops)]
        for h, old, top, expo in zip(heads, olds, tops, expos):
            sums = sums_ref[h] * jnp.exp2((old - top) * scale)
            sums += dot(value_ref[h, :, 0:close], expo[0:close])
            if rows > close:
                sums += dot(far_value_ref[h], expo[close:])
            attended_ref[h] = (sums[0:head_dim] / sums[head_dim : head_dim + 1]).astype(jnp.bfloat16)

    def together(i, carry):
        heads = [order_ref[GROUP * i + k] for k in range(GROUP)]
        widest = functools.reduce(jnp.maximum, [window_ref[h] for h in heads])

        @pl.when(widest <= NEAR)
        def _():
            attend(heads, NEAR)

        @pl.when((widest > NEAR) & (widest <= nodes))
        def _():
            attend(heads, nodes)

        @pl.when(widest > nodes)
        def _():
            attend(heads, 3 * nodes)

        return carry

    lax.fori_loop(0, HEADS // GROUP, together, 0)

    attended = attended_ref[...].reshape(width, nodes)
    mixed = lax.dot_general(
        attended, w_out_ref[...], (((0,), (0,)), ((), ())), preferred_element_type=jnp.float32
    )
    mid = state_ref[...] + mixed
    normed = layer_norm(mid, gain_ref[...]).astype(jnp.bfloat16)
    hidden = jax.nn.silu(dot(normed, up_ref[...])).astype(jnp.bfloat16)
    out_ref[...] = (mid + dot(hidden, down_ref[...])).astype(jnp.bfloat16)


def cost(flops, size):
    return pl.CostEstimate(flops=flops, bytes_accessed=size, transcendentals=0)


def local(
    grid_rows,
    mesh_rows,
    edge_source,
    edge_target,
    edge_count,
    w_message,
    w_merge,
    gain_attn,
    w_qkv,
    window,
    w_out,
    gain_mlp,
    w_up,
    w_down,
):
    bands = lax.axis_size("band")
    inners = lax.axis_size("inner")
    devices = bands * inners
    grid_dev = grid_rows.shape[0]
    nodes, width = mesh_rows.shape
    cap = edge_source.shape[-1]
    head_dim = width // HEADS
    pairs = inners // 2
    half = width // 2
    f32, bf16, i32 = jnp.float32, jnp.bfloat16, jnp.int32
    edges = (edge_source, edge_target, jnp.transpose(edge_count, (0, 2, 1, 3)))

    def rows_of(*blocks):
        return jax.ShapeDtypeStruct((sum(n * cap + TILE for n in blocks), half), bf16)

    outgoing = [rows_of(pairs)] * 4 + [rows_of(3)] * (2 * pairs - 2) + [rows_of(pairs, 3)] * 2
    even, even_other, odd, odd_other, *cross, here, here_other = pl.pallas_call(
        functools.partial(message_kernel, pairs),
        out_shape=outgoing,
        in_specs=[ANY] * 2 + [VMEM] * 2 + [SMEM],
        out_specs=[ANY] * len(outgoing),
        scratch_shapes=[pltpu.VMEM(a.shape, bf16) for a in outgoing]
        + [
            pltpu.VMEM(grid_rows.shape, bf16),
            pltpu.VMEM(w_message.shape, bf16),
            pltpu.VMEM((grid_dev, width), bf16),
            pltpu.SemaphoreType.DMA((GRID_PARTS + 1,)),
            pltpu.SemaphoreType.DMA((len(outgoing),)),
        ],
        compiler_params=params(MOST),
        cost_estimate=cost(2 * grid_dev * width * (width + 3 * inners * cap), 4 << 20),
        name="messages",
    )(grid_rows, w_message, *edges)
    beside = [(g, g ^ 1) for g in range(devices)]

    def bands_trade(odd_pairs, k=0):
        route = []
        for g in range(devices):
            b = g // inners
            t = (b - odd_pairs ^ 1) + odd_pairs
            route.append((g, t * inners + (g % inners ^ k) if 0 <= t < bands else g ^ 1))
        return route

    def chip_trade(p, k=0):
        return [(g, g ^ (2 * p + k)) for g in range(devices)]

    cross = [lax.ppermute(c, NODES, chip_trade(n // 2 + 1, n % 2)) for n, c in enumerate(cross)]
    even = lax.ppermute(even, NODES, bands_trade(0))
    odd = lax.ppermute(odd, NODES, bands_trade(1))
    even_other = lax.ppermute(even_other, NODES, bands_trade(0, 1))
    odd_other = lax.ppermute(odd_other, NODES, bands_trade(1, 1))
    here_other = lax.ppermute(here_other, NODES, beside)

    w_qkv, window, here = lax.optimization_barrier((w_qkv, window, here))
    w_query, w_key, w_value, early_left, early_right = pl.pallas_call(
        functools.partial(early_kernel, pairs),
        out_shape=[jax.ShapeDtypeStruct((width, width), bf16)] * 3
        + [jax.ShapeDtypeStruct((n, nodes, half), f32) for n in (pairs, 3)],
        in_specs=[VMEM] * 3,
        out_specs=[VMEM] * 5,
        compiler_params=params(24),
        cost_estimate=cost(1 << 28, 4 << 20),
        name="early",
    )(w_qkv, here, here_other)
    head = jnp.arange(HEADS, dtype=i32)
    ahead = (window[None, :] > window[:, None]) | (
        (window[None, :] == window[:, None]) & (head[None, :] < head[:, None])
    )
    rank = jnp.sum(ahead.astype(i32), axis=1)
    order = jnp.sum(jnp.where(rank[None, :] == head[:, None], head[None, :], 0), axis=1).astype(i32)

    def sums(arrays, early, kept, name):
        count = early.shape[0]
        return pl.pallas_call(
            functools.partial(sums_kernel, len(arrays), kept),
            out_shape=[jax.ShapeDtypeStruct((nodes, half), f32 if n == kept else bf16) for n in range(count)],
            in_specs=[VMEM] * (len(arrays) + 1),
            out_specs=[VMEM] * count,
            compiler_params=params(24),
            cost_estimate=cost(2 * nodes * half * len(arrays) * count * cap, 2 << 20),
            name=name,
        )(*arrays, early)

    left, *parts = sums([even, even_other, odd, odd_other], early_left, 0, "left")
    parts = [lax.ppermute(part, NODES, chip_trade(p + 1)) for p, part in enumerate(parts)]
    to_even, to_odd, right = sums(cross, early_right, 2, "right")
    from_even = lax.ppermute(to_even, NODES, bands_trade(0))
    from_odd = lax.ppermute(to_odd, NODES, bands_trade(1))

    state, normed = pl.pallas_call(
        merge_kernel,
        out_shape=[
            jax.ShapeDtypeStruct((nodes, width), f32),
            jax.ShapeDtypeStruct((nodes, width), bf16),
        ],
        in_specs=[VMEM] * (pairs + 6),
        out_specs=[VMEM] * 2,
        compiler_params=params(24),
        cost_estimate=cost(2 * nodes * width * width, 2 << 20),
        name="merge",
    )(left, *parts, right, from_even, from_odd, mesh_rows, w_merge, gain_attn.reshape(1, width))

    def chips_trade(odd_pairs):
        route = []
        for g in range(devices):
            t = (g // 2 - odd_pairs ^ 1) + odd_pairs
            route.append((g, 2 * t + g % 2 if 0 <= 2 * t < devices else g ^ 1))
        return route

    side = lax.ppermute(normed, NODES, beside)
    even = lax.ppermute(normed, NODES, chips_trade(0))
    odd = lax.ppermute(normed, NODES, chips_trade(1))

    extra = head_dim + 16
    query, near, top = pl.pallas_call(
        near_kernel,
        out_shape=[
            jax.ShapeDtypeStruct((HEADS, LANES, nodes), bf16),
            jax.ShapeDtypeStruct((HEADS, extra, nodes), f32),
            jax.ShapeDtypeStruct((HEADS, 8, nodes), f32),
        ],
        in_specs=[VMEM] * 5 + [SMEM] * 2,
        out_specs=[VMEM] * 3,
        scratch_shapes=[
            pltpu.VMEM((width // LANES, 2 * nodes, LANES), bf16),
            pltpu.VMEM((HEADS, extra, 2 * nodes), bf16),
            pltpu.VMEM((2 * nodes, nodes), i32),
        ],
        compiler_params=params(32),
        cost_estimate=cost(8 << 30, 4 << 20),
        name="near",
    )(normed, side, w_query, w_key, w_value, order, window)

    even, odd, near, top = lax.optimization_barrier((even, odd, near, top))
    first = lax.ppermute(even, NODES, beside)
    second = lax.ppermute(odd, NODES, beside)
    keys, values = pl.pallas_call(
        outer_kernel,
        out_shape=[
            jax.ShapeDtypeStruct((width // LANES, 2 * nodes, LANES), bf16),
            jax.ShapeDtypeStruct((HEADS, extra, 2 * nodes), bf16),
        ],
        in_specs=[VMEM] * 4,
        out_specs=[VMEM] * 2,
        compiler_params=params(16),
        cost_estimate=cost(8 * nodes * width * width, 3 << 20),
        name="outer",
    )(even, odd, w_key, w_value)

    return pl.pallas_call(
        far_kernel,
        out_shape=jax.ShapeDtypeStruct((nodes, width), bf16),
        in_specs=[VMEM] * 6 + [SMEM] * 2 + [VMEM] * 8,
        out_specs=VMEM,
        scratch_shapes=[
            pltpu.VMEM((width // LANES, nodes, LANES), bf16),
            pltpu.VMEM((HEADS, extra, nodes), bf16),
            pltpu.VMEM((3 * nodes, nodes), i32),
            pltpu.VMEM((HEADS, head_dim, nodes), bf16),
        ],
        compiler_params=params(40),
        cost_estimate=cost(8 << 30, 8 << 20),
        name="far",
    )(
        first, second, keys, values, w_key, w_value, order, window,
        query, near, top, state, w_out, gain_mlp.reshape(1, width), w_up, w_down,
    )


def solution(mesh):
    placed = (
        P(("groups", "band", "inner"), None),
        P(("groups", "band", "inner"), None),
        P(("groups", "band"), "inner", None, None, None),
        P(("groups", "band"), "inner", None, None, None),
        P(("groups", "band"), "inner", None, None),
        P(),
        P(),
        P(),
        P(),
        P("groups"),
        P(),
        P(),
        P(),
        P(),
    )
    return jax.shard_map(
        local,
        mesh=mesh,
        in_specs=placed,
        out_specs=P(("groups", "band", "inner"), None),
        check_vma=False,
    )
```

```python
import functools
import math

import jax
import jax.numpy as jnp
from jax import lax
from jax.experimental import pallas as pl
from jax.experimental.pallas import tpu as pltpu
from jax.sharding import PartitionSpec as P

HEADS = 16
WMAX = 512
LANES = 128
NEAR = 128
TILE = 16
CAP = 128
GRID_PARTS = 4
MOST = 56
GROUP = 4

norm_eps = 1e-05
NODES = ("band", "inner")
VMEM = pl.BlockSpec(memory_space=pltpu.VMEM)
SMEM = pl.BlockSpec(memory_space=pltpu.SMEM)
ANY = pl.BlockSpec(memory_space=pl.ANY)


def params(mib):
    return pltpu.CompilerParams(vmem_limit_bytes=mib * 1024 * 1024)


def dot(a, b):
    return jnp.dot(a, b, preferred_element_type=jnp.float32)


def dot_t(a, b):
    return lax.dot_general(a, b, (((1,), (1,)), ((), ())), preferred_element_type=jnp.float32)


def silu(values):
    half = 0.5 * values
    return half + half * jnp.tanh(half)


def layer_norm(values, gain):
    center = values - jnp.mean(values, axis=-1, keepdims=True)
    spread = jnp.mean(center * center, axis=-1, keepdims=True)
    return center * lax.rsqrt(spread + norm_eps) * gain


def band_offsets():
    ahead = lax.rem(lax.axis_index("band"), 2) * 2
    return 2 - ahead, ahead, 1


def slot_columns(source_ref, blocks):
    sources = jnp.concatenate([source_ref[0, 0, o, pl.ds(j, 1), :] for o, j in blocks], axis=0)
    return jnp.transpose(sources.astype(jnp.float32)).astype(jnp.int32)


def target_tile(target_ref, count_ref, blocks, lanes):
    cap = target_ref.shape[-1]
    slot = lax.broadcasted_iota(jnp.int32, (1, cap), 1)
    targets = [
        jnp.where(slot < count_ref[0, o, 0, j], target_ref[0, 0, o, pl.ds(j, 1), :], -1) for o, j in blocks
    ]
    targets.append(jnp.full((TILE - len(blocks), cap), -1, jnp.int32))
    tile = jnp.concatenate(targets, axis=0).astype(jnp.float32).astype(jnp.bfloat16)
    return jnp.concatenate([tile] * (lanes // cap), axis=1)


def message_kernel(pair_count, grid_ref, w_ref, source_ref, target_ref, count_ref, *refs):
    count = 4 + 2 * pair_count
    out_refs, out_vmems = refs[:count], refs[count : 2 * count]
    grid_vmem, w_vmem, message_ref, in_sems, out_sems = refs[2 * count :]
    rows = grid_ref.shape[0]
    cap = source_ref.shape[-1]
    half = w_ref.shape[1] // 2
    part = rows // GRID_PARTS
    fetches = [pltpu.make_async_copy(w_ref, w_vmem, in_sems.at[GRID_PARTS])]
    for k in range(GRID_PARTS):
        span = pl.ds(k * part, part)
        fetches.append(pltpu.make_async_copy(grid_ref.at[span], grid_vmem.at[span], in_sems.at[k]))
    for fetch in fetches:
        fetch.start()
    inner = lax.axis_index("inner")
    offsets = band_offsets()
    keys = [(t, p, k) for t in range(3) for p in range(pair_count) for k in range(2)]
    place = {(t, p, k): (offsets[t], inner ^ (2 * p + k)) for t, p, k in keys}
    by_slot = slot_columns(source_ref, [place[key] for key in keys])
    left, right = slice(0, half), slice(half, 2 * half)
    runs = [[([(t, p, k) for p in range(pair_count)], left)] for t in range(2) for k in range(2)]
    runs += [[([(t, p, k) for t in range(3)], right)] for p in range(1, pair_count) for k in range(2)]
    runs += [
        [([(2, p, k) for p in range(pair_count)], left), ([(t, 0, k) for t in range(3)], right)] for k in range(2)
    ]
    for out_vmem, parts in zip(out_vmems, runs):
        start = 0
        for chosen, _ in parts:
            start += len(chosen) * cap
            out_vmem[start : start + TILE, :] = target_tile(target_ref, count_ref, [place[key] for key in chosen], half)
            start += TILE
    fetches[0].wait()
    for k in range(GRID_PARTS):
        span = pl.ds(k * part, part)
        fetches[k + 1].wait()
        message_ref[span] = silu(dot(grid_vmem[span], w_vmem[...])).astype(jnp.bfloat16)
    row = lax.broadcasted_iota(jnp.int32, (cap, rows), 1)
    picks = {
        key: jnp.where(row == by_slot[:, m : m + 1], 1.0, 0.0).astype(jnp.bfloat16) for m, key in enumerate(keys)
    }
    sends = []
    for n in reversed(range(count)):
        start = 0
        for chosen, lanes in runs[n]:
            taken = dot(jnp.concatenate([picks[key] for key in chosen], axis=0), message_ref[:, lanes])
            out_vmems[n][start : start + len(chosen) * cap, :] = taken.astype(jnp.bfloat16)
            start += len(chosen) * cap + TILE
        send = pltpu.make_async_copy(out_vmems[n], out_refs[n], out_sems.at[n])
        send.start()
        sends.append(send)
    for send in sends:
        send.wait()


def node_sums(arrays, nodes):
    count = arrays[0][2]
    cap = CAP
    node = lax.broadcasted_iota(jnp.int32, (nodes, cap), 0)
    targets = [
        ref[start + count * cap : start + count * cap + TILE, 0:cap].astype(jnp.float32).astype(jnp.int32)
        for ref, start, _ in arrays
    ]
    for n in range(count):
        hits = [jnp.where(node == t[n : n + 1], 1.0, 0.0).astype(jnp.bfloat16) for t in targets]
        rows = [ref[start + n * cap : start + (n + 1) * cap, :] for ref, start, _ in arrays]
        yield n, dot(jnp.concatenate(hits, axis=1), jnp.concatenate(rows, axis=0))


def early_kernel(pair_count, w_ref, own_ref, other_ref, query_ref, key_ref, value_ref, left_ref, right_ref):
    width = w_ref.shape[0]
    head_dim = width // HEADS
    span = 3 * LANES
    def pick(c, along):
        shape = (LANES, span) if along else (span, LANES)
        to = lax.broadcasted_iota(jnp.int32, shape, 1 - along)
        column = lax.broadcasted_iota(jnp.int32, shape, along)
        wanted = to // head_dim * (3 * head_dim) + to % head_dim + c * head_dim
        return jnp.where(column == wanted, 1.0, 0.0).astype(jnp.bfloat16)

    for g in range(width // LANES):
        columns = w_ref[:, g * span : (g + 1) * span]
        part = slice(g * LANES, (g + 1) * LANES)
        query_ref[part, :] = dot_t(pick(0, 1), columns).astype(jnp.bfloat16)
        key_ref[:, part] = dot(columns, pick(1, 0)).astype(jnp.bfloat16)
        value_ref[part, :] = dot_t(pick(2, 1), columns).astype(jnp.bfloat16)
    start = 0
    for sum_ref in (left_ref, right_ref):
        count, nodes, _ = sum_ref.shape
        for n, total in node_sums([(own_ref, start, count), (other_ref, start, count)], nodes):
            sum_ref[n] = total
        start += count * CAP + TILE


def sums_kernel(array_count, kept, *refs):
    row_refs, early_ref, out_refs = refs[:array_count], refs[array_count], refs[array_count + 1 :]
    count, nodes, _ = early_ref.shape
    for n, total in node_sums([(r, 0, count) for r in row_refs], nodes):
        total = total + early_ref[n]
        out_refs[n][...] = total if n == kept else total.astype(jnp.bfloat16)


def merge_kernel(*refs):
    *part_refs, right_ref, even_ref, odd_ref, mesh_ref, w_ref, gain_ref, state_ref, normed_ref = refs
    left = functools.reduce(jnp.add, [r[...].astype(jnp.float32) for r in part_refs])
    right = right_ref[...] + even_ref[...].astype(jnp.float32) + odd_ref[...].astype(jnp.float32)
    total = jnp.concatenate([left, right], axis=1).astype(jnp.bfloat16)
    state = mesh_ref[...].astype(jnp.float32) + dot(total, w_ref[...])
    state_ref[...] = state
    normed_ref[...] = layer_norm(state, gain_ref[...]).astype(jnp.bfloat16)


def project_keys(rows, wk_ref, wv_ref, key_ref, value_ref, start):
    count = rows.shape[0]
    groups = key_ref.shape[0]
    heads = value_ref.shape[0]
    keys = dot(rows, wk_ref[...]).astype(jnp.bfloat16)
    for g in range(groups):
        key_ref[g, start : start + count, :] = keys[:, g * LANES : (g + 1) * LANES]
    values = dot_t(wv_ref[...], rows).astype(jnp.bfloat16)
    value_ref[:, 0 : values.shape[0] // heads, start : start + count] = values.reshape(
        heads, -1, count
    )


def near_kernel(
    own_ref, side_ref, wq_ref, wk_ref, wv_ref, order_ref, window_ref,
    query_ref, sums_ref, top_ref,
    key_ref, value_ref, gap_ref,
):
    nodes, width = own_ref.shape
    head_dim = width // HEADS
    per_group = LANES // head_dim
    odd = lax.rem(lax.axis_index("inner"), 2)
    side = 1 - 2 * odd
    first = odd * (nodes - NEAR)
    second = (1 - odd) * NEAR
    scale = head_dim ** (-0.5) / math.log(2.0)

    queries = dot_t(wq_ref[...], own_ref[...]).astype(jnp.bfloat16)
    part = lax.broadcasted_iota(jnp.int32, (LANES, nodes), 0) // head_dim
    for h in range(HEADS):
        g = h // per_group
        lanes = queries[g * LANES : (g + 1) * LANES]
        query_ref[h] = jnp.where(part == h % per_group, lanes, jnp.zeros_like(lanes))
    value_ref[:, head_dim:, :] = jnp.ones_like(value_ref[:, head_dim:, :])
    project_keys(own_ref[...], wk_ref, wv_ref, key_ref, value_ref, 0)
    project_keys(side_ref[pl.ds(pl.multiple_of(first, NEAR), NEAR), :], wk_ref, wv_ref, key_ref, value_ref, nodes)
    project_keys(
        side_ref[pl.ds(pl.multiple_of(second, NEAR), NEAR), :], wk_ref, wv_ref, key_ref, value_ref, nodes + NEAR
    )
    lag = lax.broadcasted_iota(jnp.int32, (nodes, nodes), 0) - lax.broadcasted_iota(
        jnp.int32, (nodes, nodes), 1
    )
    gap_ref[0:nodes] = jnp.abs(lag)
    gap_ref[nodes : nodes + NEAR] = jnp.abs(lag[0:NEAR] + (side * nodes + first))
    gap_ref[nodes + NEAR : 2 * nodes] = jnp.abs(lag[0:NEAR] + (side * nodes + second))

    def attend(heads, rows):
        scores = [dot(key_ref[h // per_group, 0:rows, :], query_ref[h]) for h in heads]
        scores = [
            jnp.where(gap_ref[0:rows] <= window_ref[h], x, -1e30) for h, x in zip(heads, scores)
        ]
        tops = [jnp.max(x, axis=0, keepdims=True) for x in scores]
        expos = [jnp.exp2((x - top) * scale).astype(jnp.bfloat16) for x, top in zip(scores, tops)]
        for h, top, expo in zip(heads, tops, expos):
            sums_ref[h] = dot(value_ref[h, :, 0:rows], expo)
            top_ref[h] = jnp.broadcast_to(top, top_ref.shape[1:])

    def together(i, carry):
        heads = [order_ref[GROUP * i + k] for k in range(GROUP)]
        widest = functools.reduce(jnp.maximum, [window_ref[h] for h in heads])

        @pl.when(widest <= NEAR)
        def _():
            attend(heads, nodes + NEAR)

        @pl.when(widest > NEAR)
        def _():
            attend(heads, 2 * nodes)

        return carry

    lax.fori_loop(0, HEADS // GROUP, together, 0)


def gaps(device, start, rows, nodes):
    total = lax.axis_size("band") * lax.axis_size("inner")
    there = lax.axis_index("band") * lax.axis_size("inner") + lax.axis_index("inner") + device
    lag = lax.broadcasted_iota(jnp.int32, (rows, nodes), 0) - lax.broadcasted_iota(jnp.int32, (rows, nodes), 1)
    return jnp.where((there >= 0) & (there < total), jnp.abs(lag + (device * nodes + start)), 1 << 20)


def extend(heads, keys, values, gap_ref, window_ref, query_ref, sums_ref, top_ref, scale):
    scores = [dot(k, query_ref[h]) for h, k in zip(heads, keys)]
    scores = [jnp.where(gap_ref[...] <= window_ref[h], x, -1e30) for h, x in zip(heads, scores)]
    olds = [top_ref[h, 0:1, :] for h in heads]
    tops = [jnp.maximum(old, jnp.max(x, axis=0, keepdims=True)) for old, x in zip(olds, scores)]
    expos = [jnp.exp2((x - top) * scale).astype(jnp.bfloat16) for x, top in zip(scores, tops)]
    for h, v, old, top, expo in zip(heads, values, olds, tops, expos):
        yield h, sums_ref[h] * jnp.exp2((old - top) * scale) + dot(v, expo), top


def outer_kernel(
    even_ref, odd_ref, wk_ref, wv_ref, order_ref, window_ref, query_ref, sums_ref, top_ref,
    sums_out, top_out,
    key_ref, value_ref, gap_ref,
):
    nodes, width = even_ref.shape
    head_dim = width // HEADS
    per_group = LANES // head_dim
    far = 2 - 4 * lax.rem(lax.axis_index("inner") // 2, 2)
    scale = head_dim ** (-0.5) / math.log(2.0)
    value_ref[:, head_dim:, :] = jnp.ones_like(value_ref[:, head_dim:, :])
    project_keys(even_ref[...], wk_ref, wv_ref, key_ref, value_ref, 0)
    project_keys(odd_ref[...], wk_ref, wv_ref, key_ref, value_ref, nodes)
    gap_ref[0:nodes] = gaps(far, 0, nodes, nodes)
    gap_ref[nodes:] = gaps(-far, 0, nodes, nodes)

    def together(i, carry):
        heads = [order_ref[GROUP * i + k] for k in range(GROUP)]
        widest = functools.reduce(jnp.maximum, [window_ref[h] for h in heads])

        @pl.when(widest > nodes)
        def _():
            keys, values = [key_ref[h // per_group] for h in heads], [value_ref[h] for h in heads]
            for h, sums, top in extend(
                heads, keys, values, gap_ref, window_ref, query_ref, sums_ref, top_ref, scale
            ):
                sums_out[h] = sums
                top_out[h] = jnp.broadcast_to(top, top_out.shape[1:])

        @pl.when(widest <= nodes)
        def _():
            for h in heads:
                sums_out[h] = sums_ref[h]
                top_out[h] = top_ref[h]

        return carry

    lax.fori_loop(0, HEADS // GROUP, together, 0)


def far_kernel(
    first_ref, second_ref, wk_ref, wv_ref, window_ref, query_ref, sums_ref, top_ref,
    state_ref, w_out_ref, gain_ref, up_ref, down_ref,
    out_ref,
    key_ref, value_ref, gap_ref, attended_ref,
):
    nodes, width = first_ref.shape
    head_dim = width // HEADS
    per_group = LANES // head_dim
    inner = lax.axis_index("inner")
    odd = lax.rem(inner, 2)
    scale = head_dim ** (-0.5) / math.log(2.0)
    value_ref[:, head_dim:, :] = jnp.ones_like(value_ref[:, head_dim:, :])
    by_even = odd == lax.rem(inner // 2 + 1, 2)
    project_keys(jnp.where(by_even, first_ref[...], second_ref[...]), wk_ref, wv_ref, key_ref, value_ref, 0)
    gap_ref[...] = gaps(2 * odd - 1, 0, nodes, nodes)
    for i in range(HEADS // GROUP):
        heads = range(GROUP * i, GROUP * (i + 1))
        keys, values = [key_ref[h // per_group] for h in heads], [value_ref[h] for h in heads]
        for h, sums, _ in extend(
            heads, keys, values, gap_ref, window_ref, query_ref, sums_ref, top_ref, scale
        ):
            attended_ref[h] = (sums[0:head_dim] / sums[head_dim : head_dim + 1]).astype(jnp.bfloat16)

    attended = attended_ref[...].reshape(width, nodes)
    mixed = lax.dot_general(
        attended, w_out_ref[...], (((0,), (0,)), ((), ())), preferred_element_type=jnp.float32
    )
    mid = state_ref[...] + mixed
    normed = layer_norm(mid, gain_ref[...]).astype(jnp.bfloat16)
    total = mid
    chunk = math.gcd(up_ref.shape[1], 512)
    for start in range(0, up_ref.shape[1], chunk):
        hidden = silu(dot(normed, up_ref[:, start : start + chunk])).astype(jnp.bfloat16)
        total = total + dot(hidden, down_ref[start : start + chunk, :])
    out_ref[...] = total.astype(jnp.bfloat16)


def cost(flops, size):
    return pl.CostEstimate(flops=flops, bytes_accessed=size, transcendentals=0)


def local(
    grid_rows,
    mesh_rows,
    edge_source,
    edge_target,
    edge_count,
    w_message,
    w_merge,
    gain_attn,
    w_qkv,
    window,
    w_out,
    gain_mlp,
    w_up,
    w_down,
):
    bands = lax.axis_size("band")
    inners = lax.axis_size("inner")
    devices = bands * inners
    grid_dev = grid_rows.shape[0]
    nodes, width = mesh_rows.shape
    cap = edge_source.shape[-1]
    head_dim = width // HEADS
    pairs = inners // 2
    half = width // 2
    f32, bf16, i32 = jnp.float32, jnp.bfloat16, jnp.int32
    edges = (edge_source, edge_target, jnp.transpose(edge_count, (0, 2, 1, 3)))

    def rows_of(*blocks):
        return jax.ShapeDtypeStruct((sum(n * cap + TILE for n in blocks), half), bf16)

    outgoing = [rows_of(pairs)] * 4 + [rows_of(3)] * (2 * pairs - 2) + [rows_of(pairs, 3)] * 2
    even, even_other, odd, odd_other, *cross, here, here_other = pl.pallas_call(
        functools.partial(message_kernel, pairs),
        out_shape=outgoing,
        in_specs=[ANY] * 2 + [VMEM] * 2 + [SMEM],
        out_specs=[ANY] * len(outgoing),
        scratch_shapes=[pltpu.VMEM(a.shape, bf16) for a in outgoing]
        + [
            pltpu.VMEM(grid_rows.shape, bf16),
            pltpu.VMEM(w_message.shape, bf16),
            pltpu.VMEM((grid_dev, width), bf16),
            pltpu.SemaphoreType.DMA((GRID_PARTS + 1,)),
            pltpu.SemaphoreType.DMA((len(outgoing),)),
        ],
        compiler_params=params(MOST),
        cost_estimate=cost(2 * grid_dev * width * (width + 3 * inners * cap), 4 << 20),
        name="messages",
    )(grid_rows, w_message, *edges)
    beside = [(g, g ^ 1) for g in range(devices)]

    def bands_trade(odd_pairs, k=0):
        route = []
        for g in range(devices):
            b = g // inners
            t = (b - odd_pairs ^ 1) + odd_pairs
            route.append((g, t * inners + (g % inners ^ k) if 0 <= t < bands else g ^ 1))
        return route

    def chip_trade(p, k=0):
        return [(g, g ^ (2 * p + k)) for g in range(devices)]

    here_other = lax.ppermute(here_other, NODES, beside)
    cross[0::2] = [lax.ppermute(c, NODES, chip_trade(p + 1)) for p, c in enumerate(cross[0::2])]
    even = lax.ppermute(even, NODES, bands_trade(0))
    odd = lax.ppermute(odd, NODES, bands_trade(1))
    here_other, even_other, odd_other, *cross[1::2] = lax.optimization_barrier(
        (here_other, even_other, odd_other, *cross[1::2])
    )
    cross[1::2] = [lax.ppermute(c, NODES, chip_trade(p + 1, 1)) for p, c in enumerate(cross[1::2])]
    even_other = lax.ppermute(even_other, NODES, bands_trade(0, 1))
    odd_other = lax.ppermute(odd_other, NODES, bands_trade(1, 1))

    w_qkv, window, here = lax.optimization_barrier((w_qkv, window, here))
    w_query, w_key, w_value, early_left, early_right = pl.pallas_call(
        functools.partial(early_kernel, pairs),
        out_shape=[jax.ShapeDtypeStruct((width, width), bf16)] * 3
        + [jax.ShapeDtypeStruct((n, nodes, half), f32) for n in (pairs, 3)],
        in_specs=[VMEM] * 3,
        out_specs=[VMEM] * 5,
        compiler_params=params(24),
        cost_estimate=cost(1 << 28, 4 << 20),
        name="early",
    )(w_qkv, here, here_other)
    head = jnp.arange(HEADS, dtype=i32)
    ahead = (window[None, :] > window[:, None]) | (
        (window[None, :] == window[:, None]) & (head[None, :] < head[:, None])
    )
    rank = jnp.sum(ahead.astype(i32), axis=1)
    order = jnp.sum(jnp.where(rank[None, :] == head[:, None], head[None, :], 0), axis=1).astype(i32)

    def sums(arrays, early, kept, name):
        count = early.shape[0]
        return pl.pallas_call(
            functools.partial(sums_kernel, len(arrays), kept),
            out_shape=[jax.ShapeDtypeStruct((nodes, half), f32 if n == kept else bf16) for n in range(count)],
            in_specs=[VMEM] * (len(arrays) + 1),
            out_specs=[VMEM] * count,
            compiler_params=params(24),
            cost_estimate=cost(2 * nodes * half * len(arrays) * count * cap, 2 << 20),
            name=name,
        )(*arrays, early)

    left, *parts = sums([even, even_other, odd, odd_other], early_left, 0, "left")
    parts = [lax.ppermute(part, NODES, chip_trade(p + 1)) for p, part in enumerate(parts)]
    to_even, to_odd, right = sums(cross, early_right, 2, "right")
    from_even = lax.ppermute(to_even, NODES, bands_trade(0))
    from_odd = lax.ppermute(to_odd, NODES, bands_trade(1))

    state, normed = pl.pallas_call(
        merge_kernel,
        out_shape=[
            jax.ShapeDtypeStruct((nodes, width), f32),
            jax.ShapeDtypeStruct((nodes, width), bf16),
        ],
        in_specs=[VMEM] * (pairs + 6),
        out_specs=[VMEM] * 2,
        compiler_params=params(24),
        cost_estimate=cost(2 * nodes * width * width, 2 << 20),
        name="merge",
    )(left, *parts, right, from_even, from_odd, mesh_rows, w_merge, gain_attn.reshape(1, width))

    def chips_trade(odd_pairs):
        route = []
        for g in range(devices):
            t = (g // 2 - odd_pairs ^ 1) + odd_pairs
            route.append((g, 2 * t + g % 2 if 0 <= 2 * t < devices else g ^ 1))
        return route

    side = lax.ppermute(normed, NODES, beside)
    even = lax.ppermute(normed, NODES, chips_trade(0))
    odd = lax.ppermute(normed, NODES, chips_trade(1))

    extra = head_dim + 16
    query, near, top = pl.pallas_call(
        near_kernel,
        out_shape=[
            jax.ShapeDtypeStruct((HEADS, LANES, nodes), bf16),
            jax.ShapeDtypeStruct((HEADS, extra, nodes), f32),
            jax.ShapeDtypeStruct((HEADS, 8, nodes), f32),
        ],
        in_specs=[VMEM] * 5 + [SMEM] * 2,
        out_specs=[VMEM] * 3,
        scratch_shapes=[
            pltpu.VMEM((width // LANES, 2 * nodes, LANES), bf16),
            pltpu.VMEM((HEADS, extra, 2 * nodes), bf16),
            pltpu.VMEM((2 * nodes, nodes), i32),
        ],
        compiler_params=params(32),
        cost_estimate=cost(8 << 30, 4 << 20),
        name="near",
    )(normed, side, w_query, w_key, w_value, order, window)

    even, odd, near, top = lax.optimization_barrier((even, odd, near, top))
    first = lax.ppermute(even, NODES, beside)
    second = lax.ppermute(odd, NODES, beside)
    near, top = pl.pallas_call(
        outer_kernel,
        out_shape=[
            jax.ShapeDtypeStruct((HEADS, extra, nodes), f32),
            jax.ShapeDtypeStruct((HEADS, 8, nodes), f32),
        ],
        in_specs=[VMEM] * 4 + [SMEM] * 2 + [VMEM] * 3,
        out_specs=[VMEM] * 2,
        scratch_shapes=[
            pltpu.VMEM((width // LANES, 2 * nodes, LANES), bf16),
            pltpu.VMEM((HEADS, extra, 2 * nodes), bf16),
            pltpu.VMEM((2 * nodes, nodes), i32),
        ],
        compiler_params=params(24),
        cost_estimate=cost(16 * nodes * width * width, 3 << 20),
        name="outer",
    )(even, odd, w_key, w_value, order, window, query, near, top)

    return pl.pallas_call(
        far_kernel,
        out_shape=jax.ShapeDtypeStruct((nodes, width), bf16),
        in_specs=[VMEM] * 4 + [SMEM] + [VMEM] * 8,
        out_specs=VMEM,
        scratch_shapes=[
            pltpu.VMEM((width // LANES, nodes, LANES), bf16),
            pltpu.VMEM((HEADS, extra, nodes), bf16),
            pltpu.VMEM((nodes, nodes), i32),
            pltpu.VMEM((HEADS, head_dim, nodes), bf16),
        ],
        compiler_params=params(40),
        cost_estimate=cost(8 << 30, 8 << 20),
        name="far",
    )(
        first, second, w_key, w_value, window,
        query, near, top, state, w_out, gain_mlp.reshape(1, width), w_up, w_down,
    )


def solution(mesh):
    placed = (
        P(("groups", "band", "inner"), None),
        P(("groups", "band", "inner"), None),
        P(("groups", "band"), "inner", None, None, None),
        P(("groups", "band"), "inner", None, None, None),
        P(("groups", "band"), "inner", None, None),
        P(),
        P(),
        P(),
        P(),
        P("groups"),
        P(),
        P(),
        P(),
        P(),
    )
    return jax.shard_map(
        local,
        mesh=mesh,
        in_specs=placed,
        out_specs=P(("groups", "band", "inner"), None),
        check_vma=False,
    )
```

```python
import functools
import math

import jax
import jax.numpy as jnp
from jax import lax
from jax.experimental import pallas as pl
from jax.experimental.pallas import tpu as pltpu
from jax.sharding import PartitionSpec as P

HEADS = 16
WMAX = 512
LANES = 128
NEAR = 128
TILE = 16
CAP = 128
GRID_PARTS = 2
MOST = 56
GROUP = 4

norm_eps = 1e-05
NODES = ("band", "inner")
VMEM = pl.BlockSpec(memory_space=pltpu.VMEM)
SMEM = pl.BlockSpec(memory_space=pltpu.SMEM)
ANY = pl.BlockSpec(memory_space=pl.ANY)


def params(mib):
    return pltpu.CompilerParams(vmem_limit_bytes=mib * 1024 * 1024)


def dot(a, b):
    return jnp.dot(a, b, preferred_element_type=jnp.float32)


def dot_t(a, b):
    return lax.dot_general(a, b, (((1,), (1,)), ((), ())), preferred_element_type=jnp.float32)


def silu(values):
    half = 0.5 * values
    return half + half * jnp.tanh(half)


def layer_norm(values, gain):
    center = values - jnp.mean(values, axis=-1, keepdims=True)
    spread = jnp.mean(center * center, axis=-1, keepdims=True)
    return center * lax.rsqrt(spread + norm_eps) * gain


def band_offsets():
    ahead = lax.rem(lax.axis_index("band"), 2) * 2
    return 2 - ahead, ahead, 1


def slot_columns(source_ref, blocks):
    sources = jnp.concatenate([source_ref[0, 0, o, pl.ds(j, 1), :] for o, j in blocks], axis=0)
    return jnp.transpose(sources.astype(jnp.float32)).astype(jnp.int32)


def target_tile(target_ref, count_ref, blocks, lanes):
    cap = target_ref.shape[-1]
    slot = lax.broadcasted_iota(jnp.int32, (1, cap), 1)
    targets = [
        jnp.where(slot < count_ref[0, o, 0, j], target_ref[0, 0, o, pl.ds(j, 1), :], -1) for o, j in blocks
    ]
    targets.append(jnp.full((TILE - len(blocks), cap), -1, jnp.int32))
    tile = jnp.concatenate(targets, axis=0).astype(jnp.float32).astype(jnp.bfloat16)
    return jnp.concatenate([tile] * (lanes // cap), axis=1)


def message_kernel(pair_count, grid_ref, w_ref, source_ref, target_ref, count_ref, *refs):
    count = 4 + 2 * pair_count
    out_refs, out_vmems = refs[:count], refs[count : 2 * count]
    grid_vmem, w_vmem, message_ref, pick_ref, in_sems, out_sems = refs[2 * count :]
    rows = grid_ref.shape[0]
    cap = source_ref.shape[-1]
    half = w_ref.shape[1] // 2
    part = rows // GRID_PARTS
    fetches = [pltpu.make_async_copy(w_ref, w_vmem, in_sems.at[GRID_PARTS])]
    for k in range(GRID_PARTS):
        span = pl.ds(k * part, part)
        fetches.append(pltpu.make_async_copy(grid_ref.at[span], grid_vmem.at[span], in_sems.at[k]))
    for fetch in fetches:
        fetch.start()
    inner = lax.axis_index("inner")
    offsets = band_offsets()
    keys = [(t, p, k) for k in range(2) for t in range(3) for p in range(pair_count)]
    place = {(t, p, k): (offsets[t], inner ^ (2 * p + k)) for t, p, k in keys}
    by_slot = slot_columns(source_ref, [place[key] for key in keys])
    left, right = slice(0, half), slice(half, 2 * half)
    runs = [[([(t, p, k) for p in range(pair_count)], left)] for t in range(2) for k in range(2)]
    runs += [[([(t, p, k) for t in range(3)], right)] for p in range(1, pair_count) for k in range(2)]
    runs += [
        [([(2, p, k) for p in range(pair_count)], left), ([(t, 0, k) for t in range(3)], right)] for k in range(2)
    ]
    for out_vmem, parts in zip(out_vmems, runs):
        start = 0
        for chosen, _ in parts:
            start += len(chosen) * cap
            out_vmem[start : start + TILE, :] = target_tile(target_ref, count_ref, [place[key] for key in chosen], half)
            start += TILE
    row = lax.broadcasted_iota(jnp.int32, (cap, rows), 1)
    for m in range(len(keys)):
        pick_ref[m * cap : (m + 1) * cap, :] = jnp.where(row == by_slot[:, m : m + 1], 1.0, 0.0).astype(jnp.bfloat16)
    fetches[0].wait()
    for k in range(GRID_PARTS):
        span = pl.ds(k * part, part)
        fetches[k + 1].wait()
        message_ref[span] = silu(dot(grid_vmem[span], w_vmem[...])).astype(jnp.bfloat16)
    sends = []
    per_core = len(keys) // 2
    for k in range(2):
        first = k * per_core
        taken = dot(pick_ref[first * cap : (first + per_core) * cap, :], message_ref[...]).astype(jnp.bfloat16)
        for n in range(count):
            start = 0
            if runs[n][0][0][0][2] != k:
                continue
            for chosen, lanes in runs[n]:
                for key in chosen:
                    m = keys.index(key) - first
                    out_vmems[n][start : start + cap, :] = taken[m * cap : (m + 1) * cap, lanes]
                    start += cap
                start += TILE
            send = pltpu.make_async_copy(out_vmems[n], out_refs[n], out_sems.at[n])
            send.start()
            sends.append(send)
    for send in sends:
        send.wait()


def node_sums(arrays, nodes):
    count = arrays[0][2]
    cap = CAP
    node = lax.broadcasted_iota(jnp.int32, (nodes, cap), 0)
    targets = [
        ref[start + count * cap : start + count * cap + TILE, 0:cap].astype(jnp.float32).astype(jnp.int32)
        for ref, start, _ in arrays
    ]
    for n in range(count):
        hits = [jnp.where(node == t[n : n + 1], 1.0, 0.0).astype(jnp.bfloat16) for t in targets]
        rows = [ref[start + n * cap : start + (n + 1) * cap, :] for ref, start, _ in arrays]
        yield n, dot(jnp.concatenate(hits, axis=1), jnp.concatenate(rows, axis=0))


def early_kernel(pair_count, w_ref, own_ref, other_ref, query_ref, key_ref, value_ref, left_ref, right_ref):
    width = w_ref.shape[0]
    head_dim = width // HEADS
    span = 3 * LANES
    def pick(c, along):
        shape = (LANES, span) if along else (span, LANES)
        to = lax.broadcasted_iota(jnp.int32, shape, 1 - along)
        column = lax.broadcasted_iota(jnp.int32, shape, along)
        wanted = to // head_dim * (3 * head_dim) + to % head_dim + c * head_dim
        return jnp.where(column == wanted, 1.0, 0.0).astype(jnp.bfloat16)

    for g in range(width // LANES):
        columns = w_ref[:, g * span : (g + 1) * span]
        part = slice(g * LANES, (g + 1) * LANES)
        query_ref[part, :] = dot_t(pick(0, 1), columns).astype(jnp.bfloat16)
        key_ref[:, part] = dot(columns, pick(1, 0)).astype(jnp.bfloat16)
        value_ref[part, :] = dot_t(pick(2, 1), columns).astype(jnp.bfloat16)
    start = 0
    for sum_ref in (left_ref, right_ref):
        count, nodes, _ = sum_ref.shape
        for n, total in node_sums([(own_ref, start, count), (other_ref, start, count)], nodes):
            sum_ref[n] = total
        start += count * CAP + TILE


def sums_kernel(array_count, kept, *refs):
    row_refs, early_ref, out_refs = refs[:array_count], refs[array_count], refs[array_count + 1 :]
    count, nodes, _ = early_ref.shape
    for n, total in node_sums([(r, 0, count) for r in row_refs], nodes):
        total = total + early_ref[n]
        out_refs[n][...] = total if n == kept else total.astype(jnp.bfloat16)


def merge_kernel(*refs):
    *part_refs, right_ref, even_ref, odd_ref, mesh_ref, w_ref, gain_ref, state_ref, normed_ref = refs
    left = functools.reduce(jnp.add, [r[...].astype(jnp.float32) for r in part_refs])
    right = right_ref[...] + even_ref[...].astype(jnp.float32) + odd_ref[...].astype(jnp.float32)
    total = jnp.concatenate([left, right], axis=1).astype(jnp.bfloat16)
    state = mesh_ref[...].astype(jnp.float32) + dot(total, w_ref[...])
    state_ref[...] = state
    normed_ref[...] = layer_norm(state, gain_ref[...]).astype(jnp.bfloat16)


def project_keys(rows, wk_ref, wv_ref, key_ref, value_ref, start):
    count = rows.shape[0]
    groups = key_ref.shape[0]
    heads = value_ref.shape[0]
    keys = dot(rows, wk_ref[...]).astype(jnp.bfloat16)
    for g in range(groups):
        key_ref[g, start : start + count, :] = keys[:, g * LANES : (g + 1) * LANES]
    values = dot_t(wv_ref[...], rows).astype(jnp.bfloat16)
    value_ref[:, 0 : values.shape[0] // heads, start : start + count] = values.reshape(
        heads, -1, count
    )


def near_kernel(
    own_ref, side_ref, wq_ref, wk_ref, wv_ref, order_ref, window_ref,
    query_ref, sums_ref, top_ref,
    key_ref, value_ref, gap_ref,
):
    nodes, width = own_ref.shape
    head_dim = width // HEADS
    per_group = LANES // head_dim
    odd = lax.rem(lax.axis_index("inner"), 2)
    side = 1 - 2 * odd
    first = odd * (nodes - NEAR)
    second = (1 - odd) * NEAR
    scale = head_dim ** (-0.5) / math.log(2.0)

    queries = dot_t(wq_ref[...], own_ref[...]).astype(jnp.bfloat16)
    part = lax.broadcasted_iota(jnp.int32, (LANES, nodes), 0) // head_dim
    for h in range(HEADS):
        g = h // per_group
        lanes = queries[g * LANES : (g + 1) * LANES]
        query_ref[h] = jnp.where(part == h % per_group, lanes, jnp.zeros_like(lanes))
    value_ref[:, head_dim:, :] = jnp.ones_like(value_ref[:, head_dim:, :])
    project_keys(own_ref[...], wk_ref, wv_ref, key_ref, value_ref, 0)
    project_keys(side_ref[pl.ds(pl.multiple_of(first, NEAR), NEAR), :], wk_ref, wv_ref, key_ref, value_ref, nodes)
    project_keys(
        side_ref[pl.ds(pl.multiple_of(second, NEAR), NEAR), :], wk_ref, wv_ref, key_ref, value_ref, nodes + NEAR
    )
    lag = lax.broadcasted_iota(jnp.int32, (nodes, nodes), 0) - lax.broadcasted_iota(
        jnp.int32, (nodes, nodes), 1
    )
    gap_ref[0:nodes] = jnp.abs(lag)
    gap_ref[nodes : nodes + NEAR] = jnp.abs(lag[0:NEAR] + (side * nodes + first))
    gap_ref[nodes + NEAR : 2 * nodes] = jnp.abs(lag[0:NEAR] + (side * nodes + second))

    def attend(heads, rows):
        scores = [dot(key_ref[h // per_group, 0:rows, :], query_ref[h]) for h in heads]
        scores = [
            jnp.where(gap_ref[0:rows] <= window_ref[h], x, -1e30) for h, x in zip(heads, scores)
        ]
        tops = [jnp.max(x, axis=0, keepdims=True) for x in scores]
        expos = [jnp.exp2((x - top) * scale).astype(jnp.bfloat16) for x, top in zip(scores, tops)]
        for h, top, expo in zip(heads, tops, expos):
            sums_ref[h] = dot(value_ref[h, :, 0:rows], expo)
            top_ref[h] = jnp.broadcast_to(top, top_ref.shape[1:])

    def together(i, carry):
        heads = [order_ref[GROUP * i + k] for k in range(GROUP)]
        widest = functools.reduce(jnp.maximum, [window_ref[h] for h in heads])

        @pl.when(widest <= NEAR)
        def _():
            attend(heads, nodes + NEAR)

        @pl.when(widest > NEAR)
        def _():
            attend(heads, 2 * nodes)

        return carry

    lax.fori_loop(0, HEADS // GROUP, together, 0)


def gaps(device, start, rows, nodes):
    total = lax.axis_size("band") * lax.axis_size("inner")
    there = lax.axis_index("band") * lax.axis_size("inner") + lax.axis_index("inner") + device
    lag = lax.broadcasted_iota(jnp.int32, (rows, nodes), 0) - lax.broadcasted_iota(jnp.int32, (rows, nodes), 1)
    return jnp.where((there >= 0) & (there < total), jnp.abs(lag + (device * nodes + start)), 1 << 20)


def extend(heads, keys, values, gap_ref, window_ref, query_ref, sums_ref, top_ref, scale):
    scores = [dot(k, query_ref[h]) for h, k in zip(heads, keys)]
    scores = [jnp.where(gap_ref[...] <= window_ref[h], x, -1e30) for h, x in zip(heads, scores)]
    olds = [top_ref[h, 0:1, :] for h in heads]
    tops = [jnp.maximum(old, jnp.max(x, axis=0, keepdims=True)) for old, x in zip(olds, scores)]
    expos = [jnp.exp2((x - top) * scale).astype(jnp.bfloat16) for x, top in zip(scores, tops)]
    for h, v, old, top, expo in zip(heads, values, olds, tops, expos):
        yield h, sums_ref[h] * jnp.exp2((old - top) * scale) + dot(v, expo), top


def next_node(odd, block, wk_ref, wv_ref, window_ref, query_ref, sums_ref, top_ref, key_ref, value_ref, gap_ref, store):
    nodes = block.shape[0]
    head_dim = wv_ref.shape[0] // HEADS
    per_group = LANES // head_dim
    scale = head_dim ** (-0.5) / math.log(2.0)
    value_ref[:, head_dim:, :] = jnp.ones_like(value_ref[:, head_dim:, :])
    project_keys(block, wk_ref, wv_ref, key_ref, value_ref, 0)
    gap_ref[...] = gaps(2 * odd - 1, 0, nodes, nodes)
    for i in range(HEADS // GROUP):
        heads = range(GROUP * i, GROUP * (i + 1))
        keys, values = [key_ref[h // per_group] for h in heads], [value_ref[h] for h in heads]
        for h, sums, top in extend(
            heads, keys, values, gap_ref, window_ref, query_ref, sums_ref, top_ref, scale
        ):
            store(h, sums, top)


def next_but_one(ahead, block, wk_ref, wv_ref, order_ref, window_ref, query_ref, sums_ref, top_ref,
                 sums_out, top_out, key_ref, value_ref, gap_ref):
    nodes = block.shape[0]
    head_dim = wv_ref.shape[0] // HEADS
    per_group = LANES // head_dim
    scale = head_dim ** (-0.5) / math.log(2.0)
    value_ref[:, head_dim:, :] = jnp.ones_like(value_ref[:, head_dim:, :])
    project_keys(block, wk_ref, wv_ref, key_ref, value_ref, 0)
    gap_ref[...] = gaps(2 * ahead, 0, nodes, nodes)

    def together(i, carry):
        heads = [order_ref[GROUP * i + k] for k in range(GROUP)]
        widest = functools.reduce(jnp.maximum, [window_ref[h] for h in heads])

        @pl.when(widest > nodes)
        def _():
            keys, values = [key_ref[h // per_group] for h in heads], [value_ref[h] for h in heads]
            for h, sums, top in extend(
                heads, keys, values, gap_ref, window_ref, query_ref, sums_ref, top_ref, scale
            ):
                sums_out[h] = sums
                top_out[h] = jnp.broadcast_to(top, top_out.shape[1:])

        @pl.when(widest <= nodes)
        def _():
            for h in heads:
                sums_out[h] = sums_ref[h]
                top_out[h] = top_ref[h]

        return carry

    lax.fori_loop(0, HEADS // GROUP, together, 0)


def chip_side():
    inner = lax.axis_index("inner")
    ahead = 1 - 2 * lax.rem(inner // 2, 2)
    return ahead, lax.rem(inner, 2) == (ahead + 1) // 2


def mid_kernel(
    beside_ref, block_ref, wk_ref, wv_ref, order_ref, window_ref, query_ref, sums_ref, top_ref,
    sums_out, top_out,
    key_ref, value_ref, gap_ref,
):
    ahead, close = chip_side()
    scratch = (key_ref, value_ref, gap_ref)
    next_but_one(ahead, block_ref[...], wk_ref, wv_ref, order_ref, window_ref, query_ref, sums_ref, top_ref,
                 sums_out, top_out, *scratch)

    def store(h, sums, top):
        sums_out[h] = sums
        top_out[h] = jnp.broadcast_to(top, top_out.shape[1:])

    @pl.when(close)
    def _():
        odd = lax.rem(lax.axis_index("inner"), 2)
        next_node(odd, beside_ref[...], wk_ref, wv_ref, window_ref, query_ref, sums_out, top_out, *scratch, store)


def outer_kernel(
    block_ref, wk_ref, wv_ref, order_ref, window_ref, query_ref, sums_ref, top_ref,
    sums_out, top_out,
    key_ref, value_ref, gap_ref,
):
    ahead, _ = chip_side()
    next_but_one(-ahead, block_ref[...], wk_ref, wv_ref, order_ref, window_ref, query_ref, sums_ref, top_ref,
                 sums_out, top_out, key_ref, value_ref, gap_ref)


def far_kernel(
    beside_ref, wk_ref, wv_ref, window_ref, query_ref, sums_ref, top_ref,
    state_ref, w_out_ref, gain_ref, up_ref, down_ref,
    out_ref,
    key_ref, value_ref, gap_ref, attended_ref,
):
    nodes, width = beside_ref.shape
    head_dim = width // HEADS
    _, close = chip_side()

    def store(h, sums, top):
        attended_ref[h] = (sums[0:head_dim] / sums[head_dim : head_dim + 1]).astype(jnp.bfloat16)

    @pl.when(jnp.logical_not(close))
    def _():
        odd = lax.rem(lax.axis_index("inner"), 2)
        next_node(odd, beside_ref[...], wk_ref, wv_ref, window_ref, query_ref, sums_ref, top_ref,
                  key_ref, value_ref, gap_ref, store)

    @pl.when(close)
    def _():
        for h in range(HEADS):
            store(h, sums_ref[h], None)

    attended = attended_ref[...].reshape(width, nodes)
    mixed = lax.dot_general(
        attended, w_out_ref[...], (((0,), (0,)), ((), ())), preferred_element_type=jnp.float32
    )
    mid = state_ref[...] + mixed
    normed = layer_norm(mid, gain_ref[...]).astype(jnp.bfloat16)
    total = mid
    chunk = math.gcd(up_ref.shape[1], 512)
    for start in range(0, up_ref.shape[1], chunk):
        hidden = silu(dot(normed, up_ref[:, start : start + chunk])).astype(jnp.bfloat16)
        total = total + dot(hidden, down_ref[start : start + chunk, :])
    out_ref[...] = total.astype(jnp.bfloat16)


def cost(flops, size):
    return pl.CostEstimate(flops=flops, bytes_accessed=size, transcendentals=0)


def local(
    grid_rows,
    mesh_rows,
    edge_source,
    edge_target,
    edge_count,
    w_message,
    w_merge,
    gain_attn,
    w_qkv,
    window,
    w_out,
    gain_mlp,
    w_up,
    w_down,
):
    bands = lax.axis_size("band")
    inners = lax.axis_size("inner")
    devices = bands * inners
    grid_dev = grid_rows.shape[0]
    nodes, width = mesh_rows.shape
    cap = edge_source.shape[-1]
    head_dim = width // HEADS
    pairs = inners // 2
    half = width // 2
    f32, bf16, i32 = jnp.float32, jnp.bfloat16, jnp.int32
    edges = (edge_source, edge_target, jnp.transpose(edge_count, (0, 2, 1, 3)))

    def rows_of(*blocks):
        return jax.ShapeDtypeStruct((sum(n * cap + TILE for n in blocks), half), bf16)

    outgoing = [rows_of(pairs)] * 4 + [rows_of(3)] * (2 * pairs - 2) + [rows_of(pairs, 3)] * 2
    even, even_other, odd, odd_other, *cross, here, here_other = pl.pallas_call(
        functools.partial(message_kernel, pairs),
        out_shape=outgoing,
        in_specs=[ANY] * 2 + [VMEM] * 2 + [SMEM],
        out_specs=[ANY] * len(outgoing),
        scratch_shapes=[pltpu.VMEM(a.shape, bf16) for a in outgoing]
        + [
            pltpu.VMEM(grid_rows.shape, bf16),
            pltpu.VMEM(w_message.shape, bf16),
            pltpu.VMEM((grid_dev, width), bf16),
            pltpu.VMEM((3 * inners * cap, grid_dev), bf16),
            pltpu.SemaphoreType.DMA((GRID_PARTS + 1,)),
            pltpu.SemaphoreType.DMA((len(outgoing),)),
        ],
        compiler_params=params(MOST),
        cost_estimate=cost(2 * grid_dev * width * (width + 3 * inners * cap), 4 << 20),
        name="messages",
    )(grid_rows, w_message, *edges)
    beside = [(g, g ^ 1) for g in range(devices)]

    def bands_trade(odd_pairs, k=0):
        route = []
        for g in range(devices):
            b = g // inners
            t = (b - odd_pairs ^ 1) + odd_pairs
            route.append((g, t * inners + (g % inners ^ k) if 0 <= t < bands else g ^ 1))
        return route

    def chip_trade(p, k=0):
        return [(g, g ^ (2 * p + k)) for g in range(devices)]

    here_other = lax.ppermute(here_other, NODES, beside)
    cross[0::2] = [lax.ppermute(c, NODES, chip_trade(p + 1)) for p, c in enumerate(cross[0::2])]
    even = lax.ppermute(even, NODES, bands_trade(0))
    odd = lax.ppermute(odd, NODES, bands_trade(1))
    here_other, even_other, odd_other, *cross[1::2] = lax.optimization_barrier(
        (here_other, even_other, odd_other, *cross[1::2])
    )
    cross[1::2] = [lax.ppermute(c, NODES, chip_trade(p + 1, 1)) for p, c in enumerate(cross[1::2])]
    even_other = lax.ppermute(even_other, NODES, bands_trade(0, 1))
    odd_other = lax.ppermute(odd_other, NODES, bands_trade(1, 1))

    w_qkv, window, here = lax.optimization_barrier((w_qkv, window, here))
    w_query, w_key, w_value, early_left, early_right = pl.pallas_call(
        functools.partial(early_kernel, pairs),
        out_shape=[jax.ShapeDtypeStruct((width, width), bf16)] * 3
        + [jax.ShapeDtypeStruct((n, nodes, half), f32) for n in (pairs, 3)],
        in_specs=[VMEM] * 3,
        out_specs=[VMEM] * 5,
        compiler_params=params(24),
        cost_estimate=cost(1 << 28, 4 << 20),
        name="early",
    )(w_qkv, here, here_other)
    head = jnp.arange(HEADS, dtype=i32)
    ahead = (window[None, :] > window[:, None]) | (
        (window[None, :] == window[:, None]) & (head[None, :] < head[:, None])
    )
    rank = jnp.sum(ahead.astype(i32), axis=1)
    order = jnp.sum(jnp.where(rank[None, :] == head[:, None], head[None, :], 0), axis=1).astype(i32)

    def sums(arrays, early, kept, name):
        count = early.shape[0]
        return pl.pallas_call(
            functools.partial(sums_kernel, len(arrays), kept),
            out_shape=[jax.ShapeDtypeStruct((nodes, half), f32 if n == kept else bf16) for n in range(count)],
            in_specs=[VMEM] * (len(arrays) + 1),
            out_specs=[VMEM] * count,
            compiler_params=params(24),
            cost_estimate=cost(2 * nodes * half * len(arrays) * count * cap, 2 << 20),
            name=name,
        )(*arrays, early)

    left, *parts = sums([even, even_other, odd, odd_other], early_left, 0, "left")
    parts = [lax.ppermute(part, NODES, chip_trade(p + 1)) for p, part in enumerate(parts)]
    to_even, to_odd, right = sums(cross, early_right, 2, "right")
    from_even = lax.ppermute(to_even, NODES, bands_trade(0))
    from_odd = lax.ppermute(to_odd, NODES, bands_trade(1))

    state, normed = pl.pallas_call(
        merge_kernel,
        out_shape=[
            jax.ShapeDtypeStruct((nodes, width), f32),
            jax.ShapeDtypeStruct((nodes, width), bf16),
        ],
        in_specs=[VMEM] * (pairs + 6),
        out_specs=[VMEM] * 2,
        compiler_params=params(24),
        cost_estimate=cost(2 * nodes * width * width, 2 << 20),
        name="merge",
    )(left, *parts, right, from_even, from_odd, mesh_rows, w_merge, gain_attn.reshape(1, width))

    def chips_trade(odd_pairs):
        route = []
        for g in range(devices):
            t = (g // 2 - odd_pairs ^ 1) + odd_pairs
            route.append((g, 2 * t + g % 2 if 0 <= 2 * t < devices else g ^ 1))
        return route

    side = lax.ppermute(normed, NODES, beside)
    even = lax.ppermute(normed, NODES, chips_trade(0))

    extra = head_dim + 16
    query, near, top = pl.pallas_call(
        near_kernel,
        out_shape=[
            jax.ShapeDtypeStruct((HEADS, LANES, nodes), bf16),
            jax.ShapeDtypeStruct((HEADS, extra, nodes), f32),
            jax.ShapeDtypeStruct((HEADS, 8, nodes), f32),
        ],
        in_specs=[VMEM] * 5 + [SMEM] * 2,
        out_specs=[VMEM] * 3,
        scratch_shapes=[
            pltpu.VMEM((width // LANES, 2 * nodes, LANES), bf16),
            pltpu.VMEM((HEADS, extra, 2 * nodes), bf16),
            pltpu.VMEM((2 * nodes, nodes), i32),
        ],
        compiler_params=params(32),
        cost_estimate=cost(8 << 30, 4 << 20),
        name="near",
    )(normed, side, w_query, w_key, w_value, order, window)

    normed, even, near, top = lax.optimization_barrier((normed, even, near, top))
    odd = lax.ppermute(normed, NODES, chips_trade(1))
    first = lax.ppermute(even, NODES, beside)
    weights = (w_key, w_value, order, window)
    sums_shape = [
        jax.ShapeDtypeStruct((HEADS, extra, nodes), f32),
        jax.ShapeDtypeStruct((HEADS, 8, nodes), f32),
    ]
    scratch = [
        pltpu.VMEM((width // LANES, nodes, LANES), bf16),
        pltpu.VMEM((HEADS, extra, nodes), bf16),
        pltpu.VMEM((nodes, nodes), i32),
    ]
    near, top = pl.pallas_call(
        mid_kernel,
        out_shape=sums_shape,
        in_specs=[VMEM] * 4 + [SMEM] * 2 + [VMEM] * 3,
        out_specs=[VMEM] * 2,
        scratch_shapes=scratch,
        compiler_params=params(24),
        cost_estimate=cost(16 * nodes * width * width, 3 << 20),
        name="mid",
    )(first, even, *weights, query, near, top)

    odd, near, top = lax.optimization_barrier((odd, near, top))
    second = lax.ppermute(odd, NODES, beside)
    near, top = pl.pallas_call(
        outer_kernel,
        out_shape=sums_shape,
        in_specs=[VMEM] * 3 + [SMEM] * 2 + [VMEM] * 3,
        out_specs=[VMEM] * 2,
        scratch_shapes=scratch,
        compiler_params=params(24),
        cost_estimate=cost(8 * nodes * width * width, 3 << 20),
        name="outer",
    )(odd, *weights, query, near, top)

    return pl.pallas_call(
        far_kernel,
        out_shape=jax.ShapeDtypeStruct((nodes, width), bf16),
        in_specs=[VMEM] * 3 + [SMEM] + [VMEM] * 8,
        out_specs=VMEM,
        scratch_shapes=scratch + [pltpu.VMEM((HEADS, head_dim, nodes), bf16)],
        compiler_params=params(40),
        cost_estimate=cost(8 << 30, 8 << 20),
        name="far",
    )(
        second, w_key, w_value, window,
        query, near, top, state, w_out, gain_mlp.reshape(1, width), w_up, w_down,
    )


def solution(mesh):
    placed = (
        P(("groups", "band", "inner"), None),
        P(("groups", "band", "inner"), None),
        P(("groups", "band"), "inner", None, None, None),
        P(("groups", "band"), "inner", None, None, None),
        P(("groups", "band"), "inner", None, None),
        P(),
        P(),
        P(),
        P(),
        P("groups"),
        P(),
        P(),
        P(),
        P(),
    )
    return jax.shard_map(
        local,
        mesh=mesh,
        in_specs=placed,
        out_specs=P(("groups", "band", "inner"), None),
        check_vma=False,
    )
```

```python
import functools
import math

import jax
import jax.numpy as jnp
from jax import lax
from jax.experimental import pallas as pl
from jax.experimental.pallas import tpu as pltpu
from jax.sharding import PartitionSpec as P

HEADS = 16
WMAX = 512
LANES = 128
NEAR = 128
TILE = 16
CAP = 128
GRID_PARTS = 2
MOST = 56
GROUP = 4

norm_eps = 1e-05
NODES = ("band", "inner")
VMEM = pl.BlockSpec(memory_space=pltpu.VMEM)
SMEM = pl.BlockSpec(memory_space=pltpu.SMEM)
ANY = pl.BlockSpec(memory_space=pl.ANY)


def params(mib):
    return pltpu.CompilerParams(vmem_limit_bytes=mib * 1024 * 1024)


def dot(a, b):
    return jnp.dot(a, b, preferred_element_type=jnp.float32)


def dot_t(a, b):
    return lax.dot_general(a, b, (((1,), (1,)), ((), ())), preferred_element_type=jnp.float32)


def silu(values):
    half = 0.5 * values
    return half + half * jnp.tanh(half)


def layer_norm(values, gain):
    center = values - jnp.mean(values, axis=-1, keepdims=True)
    spread = jnp.mean(center * center, axis=-1, keepdims=True)
    return center * lax.rsqrt(spread + norm_eps) * gain


def band_offsets():
    ahead = lax.rem(lax.axis_index("band"), 2) * 2
    return 2 - ahead, ahead, 1


def slot_columns(source_ref, blocks):
    sources = jnp.concatenate([source_ref[0, 0, o, pl.ds(j, 1), :] for o, j in blocks], axis=0)
    return jnp.transpose(sources.astype(jnp.float32)).astype(jnp.int32)


def target_tile(target_ref, count_ref, blocks, lanes):
    cap = target_ref.shape[-1]
    slot = lax.broadcasted_iota(jnp.int32, (1, cap), 1)
    targets = [
        jnp.where(slot < count_ref[0, o, 0, j], target_ref[0, 0, o, pl.ds(j, 1), :], -1) for o, j in blocks
    ]
    targets.append(jnp.full((TILE - len(blocks), cap), -1, jnp.int32))
    tile = jnp.concatenate(targets, axis=0).astype(jnp.float32).astype(jnp.bfloat16)
    return jnp.concatenate([tile] * (lanes // cap), axis=1)


def message_kernel(pair_count, grid_ref, w_ref, source_ref, target_ref, count_ref, *refs):
    count = 4 + 2 * pair_count
    out_refs, out_vmems = refs[:count], refs[count : 2 * count]
    grid_vmem, w_vmem, message_ref, pick_ref, in_sems, out_sems = refs[2 * count :]
    rows = grid_ref.shape[0]
    cap = source_ref.shape[-1]
    half = w_ref.shape[1] // 2
    part = rows // GRID_PARTS
    fetches = [pltpu.make_async_copy(w_ref, w_vmem, in_sems.at[GRID_PARTS])]
    for k in range(GRID_PARTS):
        span = pl.ds(k * part, part)
        fetches.append(pltpu.make_async_copy(grid_ref.at[span], grid_vmem.at[span], in_sems.at[k]))
    for fetch in fetches:
        fetch.start()
    inner = lax.axis_index("inner")
    offsets = band_offsets()
    keys = [(t, p, k) for k in range(2) for t in range(3) for p in range(pair_count)]
    place = {(t, p, k): (offsets[t], inner ^ (2 * p + k)) for t, p, k in keys}
    by_slot = slot_columns(source_ref, [place[key] for key in keys])
    left, right = slice(0, half), slice(half, 2 * half)
    runs = [[([(t, p, k) for p in range(pair_count)], left)] for t in range(2) for k in range(2)]
    runs += [[([(t, p, k) for t in range(3)], right)] for p in range(1, pair_count) for k in range(2)]
    runs += [
        [([(2, p, k) for p in range(pair_count)], left), ([(t, 0, k) for t in range(3)], right)] for k in range(2)
    ]
    for out_vmem, parts in zip(out_vmems, runs):
        start = 0
        for chosen, _ in parts:
            start += len(chosen) * cap
            out_vmem[start : start + TILE, :] = target_tile(target_ref, count_ref, [place[key] for key in chosen], half)
            start += TILE
    row = lax.broadcasted_iota(jnp.int32, (cap, rows), 1)
    for m in range(len(keys)):
        pick_ref[m * cap : (m + 1) * cap, :] = jnp.where(row == by_slot[:, m : m + 1], 1.0, 0.0).astype(jnp.bfloat16)
    fetches[0].wait()
    for k in range(GRID_PARTS):
        span = pl.ds(k * part, part)
        fetches[k + 1].wait()
        message_ref[span] = silu(dot(grid_vmem[span], w_vmem[...])).astype(jnp.bfloat16)
    sends = []
    per_core = len(keys) // 2
    for k in range(2):
        first = k * per_core
        taken = dot(pick_ref[first * cap : (first + per_core) * cap, :], message_ref[...]).astype(jnp.bfloat16)
        for n in range(count):
            start = 0
            if runs[n][0][0][0][2] != k:
                continue
            for chosen, lanes in runs[n]:
                for key in chosen:
                    m = keys.index(key) - first
                    out_vmems[n][start : start + cap, :] = taken[m * cap : (m + 1) * cap, lanes]
                    start += cap
                start += TILE
            send = pltpu.make_async_copy(out_vmems[n], out_refs[n], out_sems.at[n])
            send.start()
            sends.append(send)
    for send in sends:
        send.wait()


def node_sums(arrays, nodes):
    count = arrays[0][2]
    cap = CAP
    node = lax.broadcasted_iota(jnp.int32, (nodes, cap), 0)
    targets = [
        ref[start + count * cap : start + count * cap + TILE, 0:cap].astype(jnp.float32).astype(jnp.int32)
        for ref, start, _ in arrays
    ]
    for n in range(count):
        hits = [jnp.where(node == t[n : n + 1], 1.0, 0.0).astype(jnp.bfloat16) for t in targets]
        rows = [ref[start + n * cap : start + (n + 1) * cap, :] for ref, start, _ in arrays]
        yield n, dot(jnp.concatenate(hits, axis=1), jnp.concatenate(rows, axis=0))


def early_kernel(pair_count, w_ref, own_ref, other_ref, order_ref, query_ref, key_ref, value_ref, left_ref, right_ref):
    width = w_ref.shape[0]
    head_dim = width // HEADS
    span = 3 * LANES
    def pick(c, along):
        shape = (LANES, span) if along else (span, LANES)
        to = lax.broadcasted_iota(jnp.int32, shape, 1 - along)
        column = lax.broadcasted_iota(jnp.int32, shape, along)
        wanted = to // head_dim * (3 * head_dim) + to % head_dim + c * head_dim
        return jnp.where(column == wanted, 1.0, 0.0).astype(jnp.bfloat16)

    for g in range(width // LANES):
        columns = w_ref[:, g * span : (g + 1) * span]
        part = slice(g * LANES, (g + 1) * LANES)
        query_ref[part, :] = dot_t(pick(0, 1), columns).astype(jnp.bfloat16)
        key_ref[:, part] = dot(columns, pick(1, 0)).astype(jnp.bfloat16)
        value_ref[part, :] = dot_t(pick(2, 1), columns).astype(jnp.bfloat16)
    start = 0
    for sum_ref in (left_ref, right_ref):
        count, nodes, _ = sum_ref.shape
        for n, total in node_sums([(own_ref, start, count), (other_ref, start, count)], nodes):
            sum_ref[n] = total
        start += count * CAP + TILE


def sums_kernel(array_count, kept, *refs):
    row_refs, early_ref, out_refs = refs[:array_count], refs[array_count], refs[array_count + 1 :]
    count, nodes, _ = early_ref.shape
    for n, total in node_sums([(r, 0, count) for r in row_refs], nodes):
        total = total + early_ref[n]
        out_refs[n][...] = total if n == kept else total.astype(jnp.bfloat16)


def merge_kernel(*refs):
    *part_refs, right_ref, even_ref, odd_ref, mesh_ref, w_ref, gain_ref, state_ref, normed_ref = refs
    left = functools.reduce(jnp.add, [r[...].astype(jnp.float32) for r in part_refs])
    right = right_ref[...] + even_ref[...].astype(jnp.float32) + odd_ref[...].astype(jnp.float32)
    total = jnp.concatenate([left, right], axis=1).astype(jnp.bfloat16)
    state = mesh_ref[...].astype(jnp.float32) + dot(total, w_ref[...])
    state_ref[...] = state
    normed_ref[...] = layer_norm(state, gain_ref[...]).astype(jnp.bfloat16)


def project_keys(rows, wk_ref, wv_ref, key_ref, value_ref, start):
    count = rows.shape[0]
    groups = key_ref.shape[0]
    heads = value_ref.shape[0]
    keys = dot(rows, wk_ref[...]).astype(jnp.bfloat16)
    for g in range(groups):
        key_ref[g, start : start + count, :] = keys[:, g * LANES : (g + 1) * LANES]
    values = dot_t(wv_ref[...], rows).astype(jnp.bfloat16)
    value_ref[:, 0 : values.shape[0] // heads, start : start + count] = values.reshape(
        heads, -1, count
    )


def near_kernel(
    own_ref, side_ref, wq_ref, wk_ref, wv_ref, order_ref, window_ref,
    query_ref, sums_ref, top_ref,
    key_ref, value_ref, gap_ref,
):
    nodes, width = own_ref.shape
    head_dim = width // HEADS
    per_group = LANES // head_dim
    odd = lax.rem(lax.axis_index("inner"), 2)
    side = 1 - 2 * odd
    first = odd * (nodes - NEAR)
    second = (1 - odd) * NEAR
    scale = head_dim ** (-0.5) / math.log(2.0)

    queries = dot_t(wq_ref[...], own_ref[...]).astype(jnp.bfloat16)
    part = lax.broadcasted_iota(jnp.int32, (LANES, nodes), 0) // head_dim
    for h in range(HEADS):
        g = h // per_group
        lanes = queries[g * LANES : (g + 1) * LANES]
        query_ref[h] = jnp.where(part == h % per_group, lanes, jnp.zeros_like(lanes))
    value_ref[:, head_dim:, :] = jnp.ones_like(value_ref[:, head_dim:, :])
    project_keys(own_ref[...], wk_ref, wv_ref, key_ref, value_ref, 0)
    project_keys(side_ref[pl.ds(pl.multiple_of(first, NEAR), NEAR), :], wk_ref, wv_ref, key_ref, value_ref, nodes)
    project_keys(
        side_ref[pl.ds(pl.multiple_of(second, NEAR), NEAR), :], wk_ref, wv_ref, key_ref, value_ref, nodes + NEAR
    )
    lag = lax.broadcasted_iota(jnp.int32, (nodes, nodes), 0) - lax.broadcasted_iota(
        jnp.int32, (nodes, nodes), 1
    )
    gap_ref[0:nodes] = jnp.abs(lag)
    gap_ref[nodes : nodes + NEAR] = jnp.abs(lag[0:NEAR] + (side * nodes + first))
    gap_ref[nodes + NEAR : 2 * nodes] = jnp.abs(lag[0:NEAR] + (side * nodes + second))

    def attend(heads, rows):
        scores = [dot(key_ref[h // per_group, 0:rows, :], query_ref[h]) for h in heads]
        scores = [
            jnp.where(gap_ref[0:rows] <= window_ref[h], x, -1e30) for h, x in zip(heads, scores)
        ]
        tops = [jnp.max(x, axis=0, keepdims=True) for x in scores]
        expos = [jnp.exp2((x - top) * scale).astype(jnp.bfloat16) for x, top in zip(scores, tops)]
        for h, top, expo in zip(heads, tops, expos):
            sums_ref[h] = dot(value_ref[h, :, 0:rows], expo)
            top_ref[h] = jnp.broadcast_to(top, top_ref.shape[1:])

    def together(i, carry):
        heads = [order_ref[GROUP * i + k] for k in range(GROUP)]
        widest = functools.reduce(jnp.maximum, [window_ref[h] for h in heads])

        @pl.when(widest <= NEAR)
        def _():
            attend(heads, nodes + NEAR)

        @pl.when(widest > NEAR)
        def _():
            attend(heads, 2 * nodes)

        return carry

    lax.fori_loop(0, HEADS // GROUP, together, 0)


def gaps(device, start, rows, nodes):
    total = lax.axis_size("band") * lax.axis_size("inner")
    there = lax.axis_index("band") * lax.axis_size("inner") + lax.axis_index("inner") + device
    lag = lax.broadcasted_iota(jnp.int32, (rows, nodes), 0) - lax.broadcasted_iota(jnp.int32, (rows, nodes), 1)
    return jnp.where((there >= 0) & (there < total), jnp.abs(lag + (device * nodes + start)), 1 << 20)


def extend(heads, keys, values, gap_ref, window_ref, query_ref, sums_ref, top_ref, scale):
    scores = [dot(k, query_ref[h]) for h, k in zip(heads, keys)]
    scores = [jnp.where(gap_ref[...] <= window_ref[h], x, -1e30) for h, x in zip(heads, scores)]
    olds = [top_ref[h, 0:1, :] for h in heads]
    tops = [jnp.maximum(old, jnp.max(x, axis=0, keepdims=True)) for old, x in zip(olds, scores)]
    expos = [jnp.exp2((x - top) * scale).astype(jnp.bfloat16) for x, top in zip(scores, tops)]
    for h, v, old, top, expo in zip(heads, values, olds, tops, expos):
        yield h, sums_ref[h] * jnp.exp2((old - top) * scale) + dot(v, expo), top


def outer_kernel(
    even_ref, odd_ref, wk_ref, wv_ref, order_ref, window_ref, query_ref, sums_ref, top_ref,
    sums_out, top_out,
    key_ref, value_ref, gap_ref,
):
    nodes, width = even_ref.shape
    head_dim = width // HEADS
    per_group = LANES // head_dim
    far = 2 - 4 * lax.rem(lax.axis_index("inner") // 2, 2)
    scale = head_dim ** (-0.5) / math.log(2.0)
    value_ref[:, head_dim:, :] = jnp.ones_like(value_ref[:, head_dim:, :])
    project_keys(even_ref[...], wk_ref, wv_ref, key_ref, value_ref, 0)
    project_keys(odd_ref[...], wk_ref, wv_ref, key_ref, value_ref, nodes)
    gap_ref[0:nodes] = gaps(far, 0, nodes, nodes)
    gap_ref[nodes:] = gaps(-far, 0, nodes, nodes)

    def together(i, carry):
        heads = [order_ref[GROUP * i + k] for k in range(GROUP)]
        widest = functools.reduce(jnp.maximum, [window_ref[h] for h in heads])

        @pl.when(widest > nodes)
        def _():
            keys, values = [key_ref[h // per_group] for h in heads], [value_ref[h] for h in heads]
            for h, sums, top in extend(
                heads, keys, values, gap_ref, window_ref, query_ref, sums_ref, top_ref, scale
            ):
                sums_out[h] = sums
                top_out[h] = jnp.broadcast_to(top, top_out.shape[1:])

        @pl.when(widest <= nodes)
        def _():
            for h in heads:
                sums_out[h] = sums_ref[h]
                top_out[h] = top_ref[h]

        return carry

    lax.fori_loop(0, HEADS // GROUP, together, 0)


def far_kernel(
    first_ref, second_ref, wk_ref, wv_ref, window_ref, query_ref, sums_ref, top_ref,
    state_ref, w_out_ref, gain_ref, up_ref, down_ref,
    out_ref,
    key_ref, value_ref, gap_ref, attended_ref,
):
    nodes, width = first_ref.shape
    head_dim = width // HEADS
    per_group = LANES // head_dim
    inner = lax.axis_index("inner")
    odd = lax.rem(inner, 2)
    scale = head_dim ** (-0.5) / math.log(2.0)
    value_ref[:, head_dim:, :] = jnp.ones_like(value_ref[:, head_dim:, :])
    by_even = odd == lax.rem(inner // 2 + 1, 2)
    project_keys(jnp.where(by_even, first_ref[...], second_ref[...]), wk_ref, wv_ref, key_ref, value_ref, 0)
    gap_ref[...] = gaps(2 * odd - 1, 0, nodes, nodes)
    for i in range(HEADS // GROUP):
        heads = range(GROUP * i, GROUP * (i + 1))
        keys, values = [key_ref[h // per_group] for h in heads], [value_ref[h] for h in heads]
        for h, sums, _ in extend(
            heads, keys, values, gap_ref, window_ref, query_ref, sums_ref, top_ref, scale
        ):
            attended_ref[h] = (sums[0:head_dim] / sums[head_dim : head_dim + 1]).astype(jnp.bfloat16)

    attended = attended_ref[...].reshape(width, nodes)
    chunk = math.gcd(up_ref.shape[1], 512)
    for first in range(0, nodes, NEAR):
        rows = slice(first, first + NEAR)
        mixed = lax.dot_general(
            attended[:, rows], w_out_ref[...], (((0,), (0,)), ((), ())), preferred_element_type=jnp.float32
        )
        total = state_ref[rows] + mixed
        normed = layer_norm(total, gain_ref[...]).astype(jnp.bfloat16)
        for start in range(0, up_ref.shape[1], chunk):
            hidden = silu(dot(normed, up_ref[:, start : start + chunk])).astype(jnp.bfloat16)
            total = total + dot(hidden, down_ref[start : start + chunk, :])
        out_ref[rows] = total.astype(jnp.bfloat16)


def cost(flops, size):
    return pl.CostEstimate(flops=flops, bytes_accessed=size, transcendentals=0)


def local(
    grid_rows,
    mesh_rows,
    edge_source,
    edge_target,
    edge_count,
    w_message,
    w_merge,
    gain_attn,
    w_qkv,
    window,
    w_out,
    gain_mlp,
    w_up,
    w_down,
):
    bands = lax.axis_size("band")
    inners = lax.axis_size("inner")
    devices = bands * inners
    grid_dev = grid_rows.shape[0]
    nodes, width = mesh_rows.shape
    cap = edge_source.shape[-1]
    head_dim = width // HEADS
    pairs = inners // 2
    half = width // 2
    f32, bf16, i32 = jnp.float32, jnp.bfloat16, jnp.int32
    edges = (edge_source, edge_target, jnp.transpose(edge_count, (0, 2, 1, 3)))

    def rows_of(*blocks):
        return jax.ShapeDtypeStruct((sum(n * cap + TILE for n in blocks), half), bf16)

    outgoing = [rows_of(pairs)] * 4 + [rows_of(3)] * (2 * pairs - 2) + [rows_of(pairs, 3)] * 2
    even, even_other, odd, odd_other, *cross, here, here_other = pl.pallas_call(
        functools.partial(message_kernel, pairs),
        out_shape=outgoing,
        in_specs=[ANY] * 2 + [VMEM] * 2 + [SMEM],
        out_specs=[ANY] * len(outgoing),
        scratch_shapes=[pltpu.VMEM(a.shape, bf16) for a in outgoing]
        + [
            pltpu.VMEM(grid_rows.shape, bf16),
            pltpu.VMEM(w_message.shape, bf16),
            pltpu.VMEM((grid_dev, width), bf16),
            pltpu.VMEM((3 * inners * cap, grid_dev), bf16),
            pltpu.SemaphoreType.DMA((GRID_PARTS + 1,)),
            pltpu.SemaphoreType.DMA((len(outgoing),)),
        ],
        compiler_params=params(MOST),
        cost_estimate=cost(2 * grid_dev * width * (width + 3 * inners * cap), 4 << 20),
        name="messages",
    )(grid_rows, w_message, *edges)
    beside = [(g, g ^ 1) for g in range(devices)]

    def bands_trade(odd_pairs, k=0):
        route = []
        for g in range(devices):
            b = g // inners
            t = (b - odd_pairs ^ 1) + odd_pairs
            route.append((g, t * inners + (g % inners ^ k) if 0 <= t < bands else g ^ 1))
        return route

    def chip_trade(p, k=0):
        return [(g, g ^ (2 * p + k)) for g in range(devices)]

    here_other = lax.ppermute(here_other, NODES, beside)
    cross[0::2] = [lax.ppermute(c, NODES, chip_trade(p + 1)) for p, c in enumerate(cross[0::2])]
    even = lax.ppermute(even, NODES, bands_trade(0))
    odd = lax.ppermute(odd, NODES, bands_trade(1))
    here_other, even_other, odd_other, *cross[1::2] = lax.optimization_barrier(
        (here_other, even_other, odd_other, *cross[1::2])
    )
    cross[1::2] = [lax.ppermute(c, NODES, chip_trade(p + 1, 1)) for p, c in enumerate(cross[1::2])]
    even_other = lax.ppermute(even_other, NODES, bands_trade(0, 1))
    odd_other = lax.ppermute(odd_other, NODES, bands_trade(1, 1))

    w_qkv, window, here = lax.optimization_barrier((w_qkv, window, here))
    head = jnp.arange(HEADS, dtype=i32)
    ahead = (window[None, :] > window[:, None]) | (
        (window[None, :] == window[:, None]) & (head[None, :] < head[:, None])
    )
    rank = jnp.sum(ahead.astype(i32), axis=1)
    order = jnp.sum(jnp.where(rank[None, :] == head[:, None], head[None, :], 0), axis=1).astype(i32)
    w_query, w_key, w_value, early_left, early_right = pl.pallas_call(
        functools.partial(early_kernel, pairs),
        out_shape=[jax.ShapeDtypeStruct((width, width), bf16)] * 3
        + [jax.ShapeDtypeStruct((n, nodes, half), f32) for n in (pairs, 3)],
        in_specs=[VMEM] * 3 + [SMEM],
        out_specs=[VMEM] * 5,
        compiler_params=params(24),
        cost_estimate=cost(1 << 28, 4 << 20),
        name="early",
    )(w_qkv, here, here_other, order)
    def sums(arrays, early, kept, name):
        count = early.shape[0]
        return pl.pallas_call(
            functools.partial(sums_kernel, len(arrays), kept),
            out_shape=[jax.ShapeDtypeStruct((nodes, half), f32 if n == kept else bf16) for n in range(count)],
            in_specs=[VMEM] * (len(arrays) + 1),
            out_specs=[VMEM] * count,
            compiler_params=params(24),
            cost_estimate=cost(2 * nodes * half * len(arrays) * count * cap, 2 << 20),
            name=name,
        )(*arrays, early)

    left, *parts = sums([even, even_other, odd, odd_other], early_left, 0, "left")
    parts = [lax.ppermute(part, NODES, chip_trade(p + 1)) for p, part in enumerate(parts)]
    to_even, to_odd, right = sums(cross, early_right, 2, "right")
    from_even = lax.ppermute(to_even, NODES, bands_trade(0))
    from_odd = lax.ppermute(to_odd, NODES, bands_trade(1))

    state, normed = pl.pallas_call(
        merge_kernel,
        out_shape=[
            jax.ShapeDtypeStruct((nodes, width), f32),
            jax.ShapeDtypeStruct((nodes, width), bf16),
        ],
        in_specs=[VMEM] * (pairs + 6),
        out_specs=[VMEM] * 2,
        compiler_params=params(24),
        cost_estimate=cost(2 * nodes * width * width, 2 << 20),
        name="merge",
    )(left, *parts, right, from_even, from_odd, mesh_rows, w_merge, gain_attn.reshape(1, width))

    def chips_trade(odd_pairs):
        route = []
        for g in range(devices):
            t = (g // 2 - odd_pairs ^ 1) + odd_pairs
            route.append((g, 2 * t + g % 2 if 0 <= 2 * t < devices else g ^ 1))
        return route

    side = lax.ppermute(normed, NODES, beside)
    even = lax.ppermute(normed, NODES, chips_trade(0))
    odd = lax.ppermute(normed, NODES, chips_trade(1))

    extra = head_dim + 16
    query, near, top = pl.pallas_call(
        near_kernel,
        out_shape=[
            jax.ShapeDtypeStruct((HEADS, LANES, nodes), bf16),
            jax.ShapeDtypeStruct((HEADS, extra, nodes), f32),
            jax.ShapeDtypeStruct((HEADS, 8, nodes), f32),
        ],
        in_specs=[VMEM] * 5 + [SMEM] * 2,
        out_specs=[VMEM] * 3,
        scratch_shapes=[
            pltpu.VMEM((width // LANES, 2 * nodes, LANES), bf16),
            pltpu.VMEM((HEADS, extra, 2 * nodes), bf16),
            pltpu.VMEM((2 * nodes, nodes), i32),
        ],
        compiler_params=params(32),
        cost_estimate=cost(8 << 30, 4 << 20),
        name="near",
    )(normed, side, w_query, w_key, w_value, order, window)

    even, odd, near, top = lax.optimization_barrier((even, odd, near, top))
    first = lax.ppermute(even, NODES, beside)
    second = lax.ppermute(odd, NODES, beside)
    near, top = pl.pallas_call(
        outer_kernel,
        out_shape=[
            jax.ShapeDtypeStruct((HEADS, extra, nodes), f32),
            jax.ShapeDtypeStruct((HEADS, 8, nodes), f32),
        ],
        in_specs=[VMEM] * 4 + [SMEM] * 2 + [VMEM] * 3,
        out_specs=[VMEM] * 2,
        scratch_shapes=[
            pltpu.VMEM((width // LANES, 2 * nodes, LANES), bf16),
            pltpu.VMEM((HEADS, extra, 2 * nodes), bf16),
            pltpu.VMEM((2 * nodes, nodes), i32),
        ],
        compiler_params=params(24),
        cost_estimate=cost(16 * nodes * width * width, 3 << 20),
        name="outer",
    )(even, odd, w_key, w_value, order, window, query, near, top)

    return pl.pallas_call(
        far_kernel,
        out_shape=jax.ShapeDtypeStruct((nodes, width), bf16),
        in_specs=[VMEM] * 4 + [SMEM] + [VMEM] * 8,
        out_specs=VMEM,
        scratch_shapes=[
            pltpu.VMEM((width // LANES, nodes, LANES), bf16),
            pltpu.VMEM((HEADS, extra, nodes), bf16),
            pltpu.VMEM((nodes, nodes), i32),
            pltpu.VMEM((HEADS, head_dim, nodes), bf16),
        ],
        compiler_params=params(40),
        cost_estimate=cost(8 << 30, 8 << 20),
        name="far",
    )(
        first, second, w_key, w_value, window,
        query, near, top, state, w_out, gain_mlp.reshape(1, width), w_up, w_down,
    )


def solution(mesh):
    placed = (
        P(("groups", "band", "inner"), None),
        P(("groups", "band", "inner"), None),
        P(("groups", "band"), "inner", None, None, None),
        P(("groups", "band"), "inner", None, None, None),
        P(("groups", "band"), "inner", None, None),
        P(),
        P(),
        P(),
        P(),
        P("groups"),
        P(),
        P(),
        P(),
        P(),
    )
    return jax.shard_map(
        local,
        mesh=mesh,
        in_specs=placed,
        out_specs=P(("groups", "band", "inner"), None),
        check_vma=False,
    )
```

```python
import functools
import math

import jax
import jax.numpy as jnp
from jax import lax
from jax.experimental import pallas as pl
from jax.experimental.pallas import tpu as pltpu
from jax.sharding import PartitionSpec as P

HEADS = 16
WMAX = 512
LANES = 128
NEAR = 128
TILE = 16
CAP = 128
GRID_PARTS = 2
MOST = 56
GROUP = 4

norm_eps = 1e-05
NODES = ("band", "inner")
VMEM = pl.BlockSpec(memory_space=pltpu.VMEM)
SMEM = pl.BlockSpec(memory_space=pltpu.SMEM)
ANY = pl.BlockSpec(memory_space=pl.ANY)


def params(mib):
    return pltpu.CompilerParams(vmem_limit_bytes=mib * 1024 * 1024)


def dot(a, b):
    return jnp.dot(a, b, preferred_element_type=jnp.float32)


def dot_t(a, b):
    return lax.dot_general(a, b, (((1,), (1,)), ((), ())), preferred_element_type=jnp.float32)


def silu(values):
    half = 0.5 * values
    return half + half * jnp.tanh(half)


def layer_norm(values, gain):
    center = values - jnp.mean(values, axis=-1, keepdims=True)
    spread = jnp.mean(center * center, axis=-1, keepdims=True)
    return center * lax.rsqrt(spread + norm_eps) * gain


def band_offsets():
    ahead = lax.rem(lax.axis_index("band"), 2) * 2
    return 2 - ahead, ahead, 1


def slot_columns(source_ref, blocks):
    sources = jnp.concatenate([source_ref[0, 0, o, pl.ds(j, 1), :] for o, j in blocks], axis=0)
    return jnp.transpose(sources.astype(jnp.float32)).astype(jnp.int32)


def target_tile(target_ref, count_ref, blocks, lanes):
    cap = target_ref.shape[-1]
    slot = lax.broadcasted_iota(jnp.int32, (1, cap), 1)
    targets = [
        jnp.where(slot < count_ref[0, o, 0, j], target_ref[0, 0, o, pl.ds(j, 1), :], -1) for o, j in blocks
    ]
    targets.append(jnp.full((TILE - len(blocks), cap), -1, jnp.int32))
    tile = jnp.concatenate(targets, axis=0).astype(jnp.float32).astype(jnp.bfloat16)
    return jnp.concatenate([tile] * (lanes // cap), axis=1)


def message_kernel(pair_count, grid_ref, w_ref, source_ref, target_ref, count_ref, *refs):
    count = 4 + 2 * pair_count
    out_refs, out_vmems = refs[:count], refs[count : 2 * count]
    grid_vmem, w_vmem, message_ref, pick_ref, in_sems, out_sems = refs[2 * count :]
    rows = grid_ref.shape[0]
    cap = source_ref.shape[-1]
    half = w_ref.shape[1] // 2
    part = rows // GRID_PARTS
    fetches = [pltpu.make_async_copy(w_ref, w_vmem, in_sems.at[GRID_PARTS])]
    for k in range(GRID_PARTS):
        span = pl.ds(k * part, part)
        fetches.append(pltpu.make_async_copy(grid_ref.at[span], grid_vmem.at[span], in_sems.at[k]))
    for fetch in fetches:
        fetch.start()
    inner = lax.axis_index("inner")
    offsets = band_offsets()
    keys = [(t, p, k) for k in range(2) for t in range(3) for p in range(pair_count)]
    place = {(t, p, k): (offsets[t], inner ^ (2 * p + k)) for t, p, k in keys}
    by_slot = slot_columns(source_ref, [place[key] for key in keys])
    left, right = slice(0, half), slice(half, 2 * half)
    runs = [[([(t, p, k) for p in range(pair_count)], left)] for t in range(2) for k in range(2)]
    runs += [[([(t, p, k) for t in range(3)], right)] for p in range(1, pair_count) for k in range(2)]
    runs += [
        [([(2, p, k) for p in range(pair_count)], left), ([(t, 0, k) for t in range(3)], right)] for k in range(2)
    ]
    for out_vmem, parts in zip(out_vmems, runs):
        start = 0
        for chosen, _ in parts:
            start += len(chosen) * cap
            out_vmem[start : start + TILE, :] = target_tile(target_ref, count_ref, [place[key] for key in chosen], half)
            start += TILE
    row = lax.broadcasted_iota(jnp.int32, (cap, rows), 1)
    for m in range(len(keys)):
        pick_ref[m * cap : (m + 1) * cap, :] = jnp.where(row == by_slot[:, m : m + 1], 1.0, 0.0).astype(jnp.bfloat16)
    fetches[0].wait()
    for k in range(GRID_PARTS):
        span = pl.ds(k * part, part)
        fetches[k + 1].wait()
        message_ref[span] = silu(dot(grid_vmem[span], w_vmem[...])).astype(jnp.bfloat16)
    sends = []
    per_core = len(keys) // 2
    for k in range(2):
        first = k * per_core
        taken = dot(pick_ref[first * cap : (first + per_core) * cap, :], message_ref[...]).astype(jnp.bfloat16)
        for n in range(count):
            start = 0
            if runs[n][0][0][0][2] != k:
                continue
            for chosen, lanes in runs[n]:
                for key in chosen:
                    m = keys.index(key) - first
                    out_vmems[n][start : start + cap, :] = taken[m * cap : (m + 1) * cap, lanes]
                    start += cap
                start += TILE
            send = pltpu.make_async_copy(out_vmems[n], out_refs[n], out_sems.at[n])
            send.start()
            sends.append(send)
    for send in sends:
        send.wait()


def node_sums(arrays, nodes):
    count = arrays[0][2]
    cap = CAP
    node = lax.broadcasted_iota(jnp.int32, (nodes, cap), 0)
    targets = [
        ref[start + count * cap : start + count * cap + TILE, 0:cap].astype(jnp.float32).astype(jnp.int32)
        for ref, start, _ in arrays
    ]
    for n in range(count):
        hits = [jnp.where(node == t[n : n + 1], 1.0, 0.0).astype(jnp.bfloat16) for t in targets]
        rows = [ref[start + n * cap : start + (n + 1) * cap, :] for ref, start, _ in arrays]
        yield n, dot(jnp.concatenate(hits, axis=1), jnp.concatenate(rows, axis=0))


def early_kernel(pair_count, w_ref, own_ref, other_ref, order_ref, query_ref, key_ref, value_ref, left_ref, right_ref):
    width = w_ref.shape[0]
    head_dim = width // HEADS
    span = 3 * LANES
    def pick(c, along):
        shape = (LANES, span) if along else (span, LANES)
        to = lax.broadcasted_iota(jnp.int32, shape, 1 - along)
        column = lax.broadcasted_iota(jnp.int32, shape, along)
        wanted = to // head_dim * (3 * head_dim) + to % head_dim + c * head_dim
        return jnp.where(column == wanted, 1.0, 0.0).astype(jnp.bfloat16)

    for g in range(width // LANES):
        columns = w_ref[:, g * span : (g + 1) * span]
        part = slice(g * LANES, (g + 1) * LANES)
        query_ref[part, :] = dot_t(pick(0, 1), columns).astype(jnp.bfloat16)
        key_ref[:, part] = dot(columns, pick(1, 0)).astype(jnp.bfloat16)
        value_ref[part, :] = dot_t(pick(2, 1), columns).astype(jnp.bfloat16)
    start = 0
    for sum_ref in (left_ref, right_ref):
        count, nodes, _ = sum_ref.shape
        for n, total in node_sums([(own_ref, start, count), (other_ref, start, count)], nodes):
            sum_ref[n] = total
        start += count * CAP + TILE


def sums_kernel(array_count, kept, *refs):
    row_refs, early_ref, out_refs = refs[:array_count], refs[array_count], refs[array_count + 1 :]
    count, nodes, _ = early_ref.shape
    for n, total in node_sums([(r, 0, count) for r in row_refs], nodes):
        total = total + early_ref[n]
        out_refs[n][...] = total if n == kept else total.astype(jnp.bfloat16)


def merge_kernel(*refs):
    *part_refs, right_ref, even_ref, odd_ref, mesh_ref, w_ref, gain_ref, state_ref, normed_ref = refs
    left = functools.reduce(jnp.add, [r[...].astype(jnp.float32) for r in part_refs])
    right = right_ref[...] + even_ref[...].astype(jnp.float32) + odd_ref[...].astype(jnp.float32)
    total = jnp.concatenate([left, right], axis=1).astype(jnp.bfloat16)
    state = mesh_ref[...].astype(jnp.float32) + dot(total, w_ref[...])
    state_ref[...] = state
    normed_ref[...] = layer_norm(state, gain_ref[...]).astype(jnp.bfloat16)


def project_keys(rows, wk_ref, wv_ref, key_ref, value_ref, start):
    count = rows.shape[0]
    groups = key_ref.shape[0]
    heads = value_ref.shape[0]
    keys = dot(rows, wk_ref[...]).astype(jnp.bfloat16)
    for g in range(groups):
        key_ref[g, start : start + count, :] = keys[:, g * LANES : (g + 1) * LANES]
    values = dot_t(wv_ref[...], rows).astype(jnp.bfloat16)
    value_ref[:, 0 : values.shape[0] // heads, start : start + count] = values.reshape(
        heads, -1, count
    )


def near_kernel(
    own_ref, side_ref, wq_ref, wk_ref, wv_ref, order_ref, window_ref,
    query_ref, sums_ref, top_ref,
    key_ref, value_ref, gap_ref,
):
    nodes, width = own_ref.shape
    head_dim = width // HEADS
    per_group = LANES // head_dim
    odd = lax.rem(lax.axis_index("inner"), 2)
    side = 1 - 2 * odd
    first = odd * (nodes - NEAR)
    second = (1 - odd) * NEAR
    scale = head_dim ** (-0.5) / math.log(2.0)

    queries = dot_t(wq_ref[...], own_ref[...]).astype(jnp.bfloat16)
    part = lax.broadcasted_iota(jnp.int32, (LANES, nodes), 0) // head_dim
    for h in range(HEADS):
        g = h // per_group
        lanes = queries[g * LANES : (g + 1) * LANES]
        query_ref[h] = jnp.where(part == h % per_group, lanes, jnp.zeros_like(lanes))
    value_ref[:, head_dim:, :] = jnp.ones_like(value_ref[:, head_dim:, :])
    project_keys(own_ref[...], wk_ref, wv_ref, key_ref, value_ref, 0)
    project_keys(side_ref[pl.ds(pl.multiple_of(first, NEAR), NEAR), :], wk_ref, wv_ref, key_ref, value_ref, nodes)
    project_keys(
        side_ref[pl.ds(pl.multiple_of(second, NEAR), NEAR), :], wk_ref, wv_ref, key_ref, value_ref, nodes + NEAR
    )
    lag = lax.broadcasted_iota(jnp.int32, (nodes, nodes), 0) - lax.broadcasted_iota(
        jnp.int32, (nodes, nodes), 1
    )
    gap_ref[0:nodes] = jnp.abs(lag)
    gap_ref[nodes : nodes + NEAR] = jnp.abs(lag[0:NEAR] + (side * nodes + first))
    gap_ref[nodes + NEAR : 2 * nodes] = jnp.abs(lag[0:NEAR] + (side * nodes + second))

    def attend(heads, rows):
        scores = [dot(key_ref[h // per_group, 0:rows, :], query_ref[h]) for h in heads]
        scores = [
            jnp.where(gap_ref[0:rows] <= window_ref[h], x, -1e30) for h, x in zip(heads, scores)
        ]
        tops = [jnp.max(x, axis=0, keepdims=True) for x in scores]
        expos = [jnp.exp2((x - top) * scale).astype(jnp.bfloat16) for x, top in zip(scores, tops)]
        for h, top, expo in zip(heads, tops, expos):
            sums_ref[h] = dot(value_ref[h, :, 0:rows], expo)
            top_ref[h] = jnp.broadcast_to(top, top_ref.shape[1:])

    def together(i, carry):
        heads = [order_ref[GROUP * i + k] for k in range(GROUP)]
        widest = functools.reduce(jnp.maximum, [window_ref[h] for h in heads])

        @pl.when(widest <= NEAR)
        def _():
            attend(heads, nodes + NEAR)

        @pl.when(widest > NEAR)
        def _():
            attend(heads, 2 * nodes)

        return carry

    lax.fori_loop(0, HEADS // GROUP, together, 0)


def gaps(device, start, rows, nodes):
    total = lax.axis_size("band") * lax.axis_size("inner")
    there = lax.axis_index("band") * lax.axis_size("inner") + lax.axis_index("inner") + device
    lag = lax.broadcasted_iota(jnp.int32, (rows, nodes), 0) - lax.broadcasted_iota(jnp.int32, (rows, nodes), 1)
    return jnp.where((there >= 0) & (there < total), jnp.abs(lag + (device * nodes + start)), 1 << 20)


def extend(heads, keys, values, gap_ref, window_ref, query_ref, sums_ref, top_ref, scale):
    scores = [dot(k, query_ref[h]) for h, k in zip(heads, keys)]
    scores = [jnp.where(gap_ref[...] <= window_ref[h], x, -1e30) for h, x in zip(heads, scores)]
    olds = [top_ref[h, 0:1, :] for h in heads]
    tops = [jnp.maximum(old, jnp.max(x, axis=0, keepdims=True)) for old, x in zip(olds, scores)]
    expos = [jnp.exp2((x - top) * scale).astype(jnp.bfloat16) for x, top in zip(scores, tops)]
    for h, v, old, top, expo in zip(heads, values, olds, tops, expos):
        yield h, sums_ref[h] * jnp.exp2((old - top) * scale) + dot(v, expo), top


def outer_kernel(
    even_ref, odd_ref, wk_ref, wv_ref, order_ref, window_ref, query_ref, sums_ref, top_ref,
    sums_out, top_out,
    key_ref, value_ref, gap_ref,
):
    nodes, width = even_ref.shape
    head_dim = width // HEADS
    per_group = LANES // head_dim
    far = 2 - 4 * lax.rem(lax.axis_index("inner") // 2, 2)
    scale = head_dim ** (-0.5) / math.log(2.0)
    value_ref[:, head_dim:, :] = jnp.ones_like(value_ref[:, head_dim:, :])
    project_keys(even_ref[...], wk_ref, wv_ref, key_ref, value_ref, 0)
    project_keys(odd_ref[...], wk_ref, wv_ref, key_ref, value_ref, nodes)
    gap_ref[0:nodes] = gaps(far, 0, nodes, nodes)
    gap_ref[nodes:] = gaps(-far, 0, nodes, nodes)

    def together(i, carry):
        heads = [order_ref[GROUP * i + k] for k in range(GROUP)]
        widest = functools.reduce(jnp.maximum, [window_ref[h] for h in heads])

        @pl.when(widest > nodes)
        def _():
            keys, values = [key_ref[h // per_group] for h in heads], [value_ref[h] for h in heads]
            for h, sums, top in extend(
                heads, keys, values, gap_ref, window_ref, query_ref, sums_ref, top_ref, scale
            ):
                sums_out[h] = sums
                top_out[h] = jnp.broadcast_to(top, top_out.shape[1:])

        @pl.when(widest <= nodes)
        def _():
            for h in heads:
                sums_out[h] = sums_ref[h]
                top_out[h] = top_ref[h]

        return carry

    lax.fori_loop(0, HEADS // GROUP, together, 0)


def far_kernel(
    first_ref, second_ref, wk_ref, wv_ref, window_ref, query_ref, sums_ref, top_ref,
    state_ref, w_out_ref, gain_ref, up_ref, down_ref,
    out_ref,
    key_ref, value_ref, gap_ref, attended_ref,
):
    nodes, width = first_ref.shape
    head_dim = width // HEADS
    per_group = LANES // head_dim
    inner = lax.axis_index("inner")
    odd = lax.rem(inner, 2)
    scale = head_dim ** (-0.5) / math.log(2.0)
    value_ref[:, head_dim:, :] = jnp.ones_like(value_ref[:, head_dim:, :])
    by_even = odd == lax.rem(inner // 2 + 1, 2)
    project_keys(jnp.where(by_even, first_ref[...], second_ref[...]), wk_ref, wv_ref, key_ref, value_ref, 0)
    gap_ref[...] = gaps(2 * odd - 1, 0, nodes, nodes)
    for i in range(HEADS // GROUP):
        heads = range(GROUP * i, GROUP * (i + 1))
        keys, values = [key_ref[h // per_group] for h in heads], [value_ref[h] for h in heads]
        for h, sums, _ in extend(
            heads, keys, values, gap_ref, window_ref, query_ref, sums_ref, top_ref, scale
        ):
            attended_ref[h] = (sums[0:head_dim] / sums[head_dim : head_dim + 1]).astype(jnp.bfloat16)

    attended = attended_ref[...].reshape(width, nodes)
    mixed = lax.dot_general(
        attended, w_out_ref[...], (((0,), (0,)), ((), ())), preferred_element_type=jnp.float32
    )
    total = state_ref[...] + mixed
    normed = layer_norm(total, gain_ref[...]).astype(jnp.bfloat16)
    chunk = math.gcd(up_ref.shape[1], 512)
    for start in range(0, up_ref.shape[1], chunk):
        hidden = silu(dot(normed, up_ref[:, start : start + chunk])).astype(jnp.bfloat16)
        total = total + dot(hidden, down_ref[start : start + chunk, :])
    out_ref[...] = total.astype(jnp.bfloat16)


def cost(flops, size):
    return pl.CostEstimate(flops=flops, bytes_accessed=size, transcendentals=0)


def local(
    grid_rows,
    mesh_rows,
    edge_source,
    edge_target,
    edge_count,
    w_message,
    w_merge,
    gain_attn,
    w_qkv,
    window,
    w_out,
    gain_mlp,
    w_up,
    w_down,
):
    bands = lax.axis_size("band")
    inners = lax.axis_size("inner")
    devices = bands * inners
    grid_dev = grid_rows.shape[0]
    nodes, width = mesh_rows.shape
    cap = edge_source.shape[-1]
    head_dim = width // HEADS
    pairs = inners // 2
    half = width // 2
    f32, bf16, i32 = jnp.float32, jnp.bfloat16, jnp.int32
    edges = (edge_source, edge_target, jnp.transpose(edge_count, (0, 2, 1, 3)))

    def rows_of(*blocks):
        return jax.ShapeDtypeStruct((sum(n * cap + TILE for n in blocks), half), bf16)

    outgoing = [rows_of(pairs)] * 4 + [rows_of(3)] * (2 * pairs - 2) + [rows_of(pairs, 3)] * 2
    even, even_other, odd, odd_other, *cross, here, here_other = pl.pallas_call(
        functools.partial(message_kernel, pairs),
        out_shape=outgoing,
        in_specs=[ANY] * 2 + [VMEM] * 2 + [SMEM],
        out_specs=[ANY] * len(outgoing),
        scratch_shapes=[pltpu.VMEM(a.shape, bf16) for a in outgoing]
        + [
            pltpu.VMEM(grid_rows.shape, bf16),
            pltpu.VMEM(w_message.shape, bf16),
            pltpu.VMEM((grid_dev, width), bf16),
            pltpu.VMEM((3 * inners * cap, grid_dev), bf16),
            pltpu.SemaphoreType.DMA((GRID_PARTS + 1,)),
            pltpu.SemaphoreType.DMA((len(outgoing),)),
        ],
        compiler_params=params(MOST),
        cost_estimate=cost(2 * grid_dev * width * (width + 3 * inners * cap), 4 << 20),
        name="messages",
    )(grid_rows, w_message, *edges)
    beside = [(g, g ^ 1) for g in range(devices)]

    def bands_trade(odd_pairs, k=0):
        route = []
        for g in range(devices):
            b = g // inners
            t = (b - odd_pairs ^ 1) + odd_pairs
            route.append((g, t * inners + (g % inners ^ k) if 0 <= t < bands else g ^ 1))
        return route

    def chip_trade(p, k=0):
        return [(g, g ^ (2 * p + k)) for g in range(devices)]

    here_other = lax.ppermute(here_other, NODES, beside)
    cross[0::2] = [lax.ppermute(c, NODES, chip_trade(p + 1)) for p, c in enumerate(cross[0::2])]
    even = lax.ppermute(even, NODES, bands_trade(0))
    odd = lax.ppermute(odd, NODES, bands_trade(1))
    here_other, even_other, odd_other, *cross[1::2] = lax.optimization_barrier(
        (here_other, even_other, odd_other, *cross[1::2])
    )
    cross[1::2] = [lax.ppermute(c, NODES, chip_trade(p + 1, 1)) for p, c in enumerate(cross[1::2])]
    even_other = lax.ppermute(even_other, NODES, bands_trade(0, 1))
    odd_other = lax.ppermute(odd_other, NODES, bands_trade(1, 1))

    w_qkv, window, here = lax.optimization_barrier((w_qkv, window, here))
    head = jnp.arange(HEADS, dtype=i32)
    ahead = (window[None, :] > window[:, None]) | (
        (window[None, :] == window[:, None]) & (head[None, :] < head[:, None])
    )
    rank = jnp.sum(ahead.astype(i32), axis=1)
    order = jnp.sum(jnp.where(rank[None, :] == head[:, None], head[None, :], 0), axis=1).astype(i32)
    w_query, w_key, w_value, early_left, early_right = pl.pallas_call(
        functools.partial(early_kernel, pairs),
        out_shape=[jax.ShapeDtypeStruct((width, width), bf16)] * 3
        + [jax.ShapeDtypeStruct((n, nodes, half), f32) for n in (pairs, 3)],
        in_specs=[VMEM] * 3 + [SMEM],
        out_specs=[VMEM] * 5,
        compiler_params=params(24),
        cost_estimate=cost(1 << 28, 4 << 20),
        name="early",
    )(w_qkv, here, here_other, order)
    def sums(arrays, early, kept, name):
        count = early.shape[0]
        return pl.pallas_call(
            functools.partial(sums_kernel, len(arrays), kept),
            out_shape=[jax.ShapeDtypeStruct((nodes, half), f32 if n == kept else bf16) for n in range(count)],
            in_specs=[VMEM] * (len(arrays) + 1),
            out_specs=[VMEM] * count,
            compiler_params=params(24),
            cost_estimate=cost(2 * nodes * half * len(arrays) * count * cap, 2 << 20),
            name=name,
        )(*arrays, early)

    left, *parts = sums([even, even_other, odd, odd_other], early_left, 0, "left")
    parts = [lax.ppermute(part, NODES, chip_trade(p + 1)) for p, part in enumerate(parts)]
    to_even, to_odd, right = sums(cross, early_right, 2, "right")
    from_even = lax.ppermute(to_even, NODES, bands_trade(0))
    from_odd = lax.ppermute(to_odd, NODES, bands_trade(1))

    state, normed = pl.pallas_call(
        merge_kernel,
        out_shape=[
            jax.ShapeDtypeStruct((nodes, width), f32),
            jax.ShapeDtypeStruct((nodes, width), bf16),
        ],
        in_specs=[VMEM] * (pairs + 6),
        out_specs=[VMEM] * 2,
        compiler_params=params(24),
        cost_estimate=cost(2 * nodes * width * width, 2 << 20),
        name="merge",
    )(left, *parts, right, from_even, from_odd, mesh_rows, w_merge, gain_attn.reshape(1, width))

    def chips_trade(odd_pairs):
        route = []
        for g in range(devices):
            t = (g // 2 - odd_pairs ^ 1) + odd_pairs
            route.append((g, 2 * t + g % 2 if 0 <= 2 * t < devices else g ^ 1))
        return route

    side = lax.ppermute(normed, NODES, beside)
    even = lax.ppermute(normed, NODES, chips_trade(0))
    odd = lax.ppermute(normed, NODES, chips_trade(1))

    extra = head_dim + 16
    query, near, top = pl.pallas_call(
        near_kernel,
        out_shape=[
            jax.ShapeDtypeStruct((HEADS, LANES, nodes), bf16),
            jax.ShapeDtypeStruct((HEADS, extra, nodes), f32),
            jax.ShapeDtypeStruct((HEADS, 8, nodes), f32),
        ],
        in_specs=[VMEM] * 5 + [SMEM] * 2,
        out_specs=[VMEM] * 3,
        scratch_shapes=[
            pltpu.VMEM((width // LANES, 2 * nodes, LANES), bf16),
            pltpu.VMEM((HEADS, extra, 2 * nodes), bf16),
            pltpu.VMEM((2 * nodes, nodes), i32),
        ],
        compiler_params=params(32),
        cost_estimate=cost(8 << 30, 4 << 20),
        name="near",
    )(normed, side, w_query, w_key, w_value, order, window)

    even, odd, near, top = lax.optimization_barrier((even, odd, near, top))
    first = lax.ppermute(even, NODES, beside)
    second = lax.ppermute(odd, NODES, beside)
    near, top = pl.pallas_call(
        outer_kernel,
        out_shape=[
            jax.ShapeDtypeStruct((HEADS, extra, nodes), f32),
            jax.ShapeDtypeStruct((HEADS, 8, nodes), f32),
        ],
        in_specs=[VMEM] * 4 + [SMEM] * 2 + [VMEM] * 3,
        out_specs=[VMEM] * 2,
        scratch_shapes=[
            pltpu.VMEM((width // LANES, 2 * nodes, LANES), bf16),
            pltpu.VMEM((HEADS, extra, 2 * nodes), bf16),
            pltpu.VMEM((2 * nodes, nodes), i32),
        ],
        compiler_params=params(24),
        cost_estimate=cost(16 * nodes * width * width, 3 << 20),
        name="outer",
    )(even, odd, w_key, w_value, order, window, query, near, top)

    return pl.pallas_call(
        far_kernel,
        out_shape=jax.ShapeDtypeStruct((nodes, width), bf16),
        in_specs=[VMEM] * 4 + [SMEM] + [VMEM] * 8,
        out_specs=VMEM,
        scratch_shapes=[
            pltpu.VMEM((width // LANES, nodes, LANES), bf16),
            pltpu.VMEM((HEADS, extra, nodes), bf16),
            pltpu.VMEM((nodes, nodes), i32),
            pltpu.VMEM((HEADS, head_dim, nodes), bf16),
        ],
        compiler_params=params(40),
        cost_estimate=cost(8 << 30, 8 << 20),
        name="far",
    )(
        first, second, w_key, w_value, window,
        query, near, top, state, w_out, gain_mlp.reshape(1, width), w_up, w_down,
    )


def solution(mesh):
    placed = (
        P(("groups", "band", "inner"), None),
        P(("groups", "band", "inner"), None),
        P(("groups", "band"), "inner", None, None, None),
        P(("groups", "band"), "inner", None, None, None),
        P(("groups", "band"), "inner", None, None),
        P(),
        P(),
        P(),
        P(),
        P("groups"),
        P(),
        P(),
        P(),
        P(),
    )
    return jax.shard_map(
        local,
        mesh=mesh,
        in_specs=placed,
        out_specs=P(("groups", "band", "inner"), None),
        check_vma=False,
    )
```

```python
import functools
import math

import jax
import jax.numpy as jnp
from jax import lax
from jax.experimental import pallas as pl
from jax.experimental.pallas import tpu as pltpu
from jax.sharding import PartitionSpec as P

HEADS = 16
WMAX = 512
LANES = 128
NEAR = 128
TILE = 16
CAP = 128
GRID_PARTS = 8
CHUNKS = 2
MOST = 56
GROUP = 4

norm_eps = 1e-05
NODES = ("band", "inner")
VMEM = pl.BlockSpec(memory_space=pltpu.VMEM)
SMEM = pl.BlockSpec(memory_space=pltpu.SMEM)
ANY = pl.BlockSpec(memory_space=pl.ANY)


def params(mib):
    return pltpu.CompilerParams(vmem_limit_bytes=mib * 1024 * 1024)


def dot(a, b):
    return jnp.dot(a, b, preferred_element_type=jnp.float32)


def dot_t(a, b):
    return lax.dot_general(a, b, (((1,), (1,)), ((), ())), preferred_element_type=jnp.float32)


def silu(values):
    half = 0.5 * values
    return half + half * jnp.tanh(half)


def layer_norm(values, gain):
    center = values - jnp.mean(values, axis=-1, keepdims=True)
    spread = jnp.mean(center * center, axis=-1, keepdims=True)
    return center * lax.rsqrt(spread + norm_eps) * gain


def band_offsets():
    ahead = lax.rem(lax.axis_index("band"), 2) * 2
    return 2 - ahead, ahead, 1


def slot_columns(source_ref, blocks):
    sources = jnp.concatenate([source_ref[0, 0, o, pl.ds(j, 1), :] for o, j in blocks], axis=0)
    return jnp.transpose(sources.astype(jnp.float32)).astype(jnp.int32)


def target_tile(target_ref, count_ref, blocks, lanes):
    cap = target_ref.shape[-1]
    slot = lax.broadcasted_iota(jnp.int32, (1, cap), 1)
    targets = [
        jnp.where(slot < count_ref[0, o, 0, j], target_ref[0, 0, o, pl.ds(j, 1), :], -1) for o, j in blocks
    ]
    targets.append(jnp.full((TILE - len(blocks), cap), -1, jnp.int32))
    tile = jnp.concatenate(targets, axis=0).astype(jnp.float32).astype(jnp.bfloat16)
    return jnp.concatenate([tile] * (lanes // cap), axis=1)


def message_kernel(pair_count, grid_ref, w_ref, source_ref, target_ref, count_ref, *refs):
    count = 4 + 2 * pair_count
    out_refs, out_vmems = refs[:count], refs[count : 2 * count]
    grid_vmem, w_vmem, message_ref, pick_ref, in_sems, out_sems = refs[2 * count :]
    rows = grid_ref.shape[0]
    cap = source_ref.shape[-1]
    half = w_ref.shape[1] // 2
    fetches = []
    for source, target in ((w_ref, w_vmem), (grid_ref, grid_vmem)):
        part = source.shape[0] // GRID_PARTS
        for n in range(GRID_PARTS):
            span = pl.ds(n * part, part)
            fetches.append(pltpu.make_async_copy(source.at[span], target.at[span], in_sems.at[len(fetches)]))
    for fetch in fetches:
        fetch.start()
    inner = lax.axis_index("inner")
    offsets = band_offsets()
    keys = [(t, p, k) for k in range(2) for t in range(3) for p in range(pair_count)]
    place = {(t, p, k): (offsets[t], inner ^ (2 * p + k)) for t, p, k in keys}
    by_slot = slot_columns(source_ref, [place[key] for key in keys])
    left, right = slice(0, half), slice(half, 2 * half)
    runs = [[([(t, p, k) for p in range(pair_count)], left)] for t in range(2) for k in range(2)]
    runs += [[([(t, p, k) for t in range(3)], right)] for p in range(1, pair_count) for k in range(2)]
    runs += [
        [([(2, p, k) for p in range(pair_count)], left), ([(t, 0, k) for t in range(3)], right)] for k in range(2)
    ]
    for out_vmem, parts in zip(out_vmems, runs):
        start = 0
        for chosen, _ in parts:
            start += len(chosen) * cap
            out_vmem[start : start + TILE, :] = target_tile(target_ref, count_ref, [place[key] for key in chosen], half)
            start += TILE
    row = lax.broadcasted_iota(jnp.int32, (cap, rows), 1)
    for m in range(len(keys)):
        pick_ref[m * cap : (m + 1) * cap, :] = jnp.where(row == by_slot[:, m : m + 1], 1.0, 0.0).astype(jnp.bfloat16)
    for fetch in fetches[:GRID_PARTS]:
        fetch.wait()
    for n in range(CHUNKS):
        for fetch in fetches[GRID_PARTS * (CHUNKS + n) // CHUNKS : GRID_PARTS * (CHUNKS + n + 1) // CHUNKS]:
            fetch.wait()
        span = pl.ds(n * (rows // CHUNKS), rows // CHUNKS)
        message_ref[span] = silu(dot(grid_vmem[span], w_vmem[...])).astype(jnp.bfloat16)
    sends = []
    per_core = len(keys) // 2
    for k in range(2):
        first = k * per_core
        taken = dot(pick_ref[first * cap : (first + per_core) * cap, :], message_ref[...]).astype(jnp.bfloat16)
        for n in range(count):
            start = 0
            if runs[n][0][0][0][2] != k:
                continue
            for chosen, lanes in runs[n]:
                for key in chosen:
                    m = keys.index(key) - first
                    out_vmems[n][start : start + cap, :] = taken[m * cap : (m + 1) * cap, lanes]
                    start += cap
                start += TILE
            send = pltpu.make_async_copy(out_vmems[n], out_refs[n], out_sems.at[n])
            send.start()
            sends.append(send)
    for send in sends:
        send.wait()


def node_sums(arrays, nodes):
    count = arrays[0][2]
    cap = CAP
    node = lax.broadcasted_iota(jnp.int32, (nodes, cap), 0)
    targets = [
        ref[start + count * cap : start + count * cap + TILE, 0:cap].astype(jnp.float32).astype(jnp.int32)
        for ref, start, _ in arrays
    ]
    for n in range(count):
        hits = [jnp.where(node == t[n : n + 1], 1.0, 0.0).astype(jnp.bfloat16) for t in targets]
        rows = [ref[start + n * cap : start + (n + 1) * cap, :] for ref, start, _ in arrays]
        yield n, dot(jnp.concatenate(hits, axis=1), jnp.concatenate(rows, axis=0))


def early_kernel(pair_count, w_ref, own_ref, other_ref, order_ref, query_ref, key_ref, value_ref, left_ref, right_ref):
    width = w_ref.shape[0]
    head_dim = width // HEADS
    span = 3 * LANES
    def pick(c, along):
        shape = (LANES, span) if along else (span, LANES)
        to = lax.broadcasted_iota(jnp.int32, shape, 1 - along)
        column = lax.broadcasted_iota(jnp.int32, shape, along)
        wanted = to // head_dim * (3 * head_dim) + to % head_dim + c * head_dim
        return jnp.where(column == wanted, 1.0, 0.0).astype(jnp.bfloat16)

    for g in range(width // LANES):
        columns = w_ref[:, g * span : (g + 1) * span]
        part = slice(g * LANES, (g + 1) * LANES)
        query_ref[part, :] = dot_t(pick(0, 1), columns).astype(jnp.bfloat16)
        key_ref[:, part] = dot(columns, pick(1, 0)).astype(jnp.bfloat16)
        value_ref[part, :] = dot_t(pick(2, 1), columns).astype(jnp.bfloat16)
    start = 0
    for sum_ref in (left_ref, right_ref):
        count, nodes, _ = sum_ref.shape
        for n, total in node_sums([(own_ref, start, count), (other_ref, start, count)], nodes):
            sum_ref[n] = total
        start += count * CAP + TILE


def sums_kernel(array_count, kept, *refs):
    row_refs, early_ref, out_refs = refs[:array_count], refs[array_count], refs[array_count + 1 :]
    count, nodes, _ = early_ref.shape
    for n, total in node_sums([(r, 0, count) for r in row_refs], nodes):
        total = total + early_ref[n]
        out_refs[n][...] = total if n == kept else total.astype(jnp.bfloat16)


def merge_kernel(*refs):
    *part_refs, right_ref, even_ref, odd_ref, mesh_ref, w_ref, gain_ref, state_ref, normed_ref = refs
    left = functools.reduce(jnp.add, [r[...].astype(jnp.float32) for r in part_refs])
    right = right_ref[...] + even_ref[...].astype(jnp.float32) + odd_ref[...].astype(jnp.float32)
    total = jnp.concatenate([left, right], axis=1).astype(jnp.bfloat16)
    state = mesh_ref[...].astype(jnp.float32) + dot(total, w_ref[...])
    state_ref[...] = state
    normed_ref[...] = layer_norm(state, gain_ref[...]).astype(jnp.bfloat16)


def project_keys(rows, wk_ref, wv_ref, key_ref, value_ref, start):
    count = rows.shape[0]
    groups = key_ref.shape[0]
    heads = value_ref.shape[0]
    keys = dot(rows, wk_ref[...]).astype(jnp.bfloat16)
    for g in range(groups):
        key_ref[g, start : start + count, :] = keys[:, g * LANES : (g + 1) * LANES]
    values = dot_t(wv_ref[...], rows).astype(jnp.bfloat16)
    value_ref[:, 0 : values.shape[0] // heads, start : start + count] = values.reshape(
        heads, -1, count
    )


def near_kernel(
    own_ref, side_ref, wq_ref, wk_ref, wv_ref, order_ref, window_ref,
    query_ref, sums_ref, top_ref,
    key_ref, value_ref, gap_ref,
):
    nodes, width = own_ref.shape
    head_dim = width // HEADS
    per_group = LANES // head_dim
    odd = lax.rem(lax.axis_index("inner"), 2)
    side = 1 - 2 * odd
    first = odd * (nodes - NEAR)
    second = (1 - odd) * NEAR
    scale = head_dim ** (-0.5) / math.log(2.0)

    queries = dot_t(wq_ref[...], own_ref[...]).astype(jnp.bfloat16)
    part = lax.broadcasted_iota(jnp.int32, (LANES, nodes), 0) // head_dim
    for h in range(HEADS):
        g = h // per_group
        lanes = queries[g * LANES : (g + 1) * LANES]
        query_ref[h] = jnp.where(part == h % per_group, lanes, jnp.zeros_like(lanes))
    value_ref[:, head_dim:, :] = jnp.ones_like(value_ref[:, head_dim:, :])
    project_keys(own_ref[...], wk_ref, wv_ref, key_ref, value_ref, 0)
    project_keys(side_ref[pl.ds(pl.multiple_of(first, NEAR), NEAR), :], wk_ref, wv_ref, key_ref, value_ref, nodes)
    project_keys(
        side_ref[pl.ds(pl.multiple_of(second, NEAR), NEAR), :], wk_ref, wv_ref, key_ref, value_ref, nodes + NEAR
    )
    lag = lax.broadcasted_iota(jnp.int32, (nodes, nodes), 0) - lax.broadcasted_iota(
        jnp.int32, (nodes, nodes), 1
    )
    gap_ref[0:nodes] = jnp.abs(lag)
    gap_ref[nodes : nodes + NEAR] = jnp.abs(lag[0:NEAR] + (side * nodes + first))
    gap_ref[nodes + NEAR : 2 * nodes] = jnp.abs(lag[0:NEAR] + (side * nodes + second))

    def attend(heads, rows):
        scores = [dot(key_ref[h // per_group, 0:rows, :], query_ref[h]) for h in heads]
        scores = [
            jnp.where(gap_ref[0:rows] <= window_ref[h], x, -1e30) for h, x in zip(heads, scores)
        ]
        tops = [jnp.max(x, axis=0, keepdims=True) for x in scores]
        expos = [jnp.exp2((x - top) * scale).astype(jnp.bfloat16) for x, top in zip(scores, tops)]
        for h, top, expo in zip(heads, tops, expos):
            sums_ref[h] = dot(value_ref[h, :, 0:rows], expo)
            top_ref[h] = jnp.broadcast_to(top, top_ref.shape[1:])

    def together(i, carry):
        heads = [order_ref[GROUP * i + k] for k in range(GROUP)]
        widest = functools.reduce(jnp.maximum, [window_ref[h] for h in heads])

        @pl.when(widest <= NEAR)
        def _():
            attend(heads, nodes + NEAR)

        @pl.when(widest > NEAR)
        def _():
            attend(heads, 2 * nodes)

        return carry

    lax.fori_loop(0, HEADS // GROUP, together, 0)


def gaps(device, start, rows, nodes):
    total = lax.axis_size("band") * lax.axis_size("inner")
    there = lax.axis_index("band") * lax.axis_size("inner") + lax.axis_index("inner") + device
    lag = lax.broadcasted_iota(jnp.int32, (rows, nodes), 0) - lax.broadcasted_iota(jnp.int32, (rows, nodes), 1)
    return jnp.where((there >= 0) & (there < total), jnp.abs(lag + (device * nodes + start)), 1 << 20)


def extend(heads, keys, values, gap_ref, window_ref, query_ref, sums_ref, top_ref, scale):
    scores = [dot(k, query_ref[h]) for h, k in zip(heads, keys)]
    scores = [jnp.where(gap_ref[...] <= window_ref[h], x, -1e30) for h, x in zip(heads, scores)]
    olds = [top_ref[h, 0:1, :] for h in heads]
    tops = [jnp.maximum(old, jnp.max(x, axis=0, keepdims=True)) for old, x in zip(olds, scores)]
    expos = [jnp.exp2((x - top) * scale).astype(jnp.bfloat16) for x, top in zip(scores, tops)]
    for h, v, old, top, expo in zip(heads, values, olds, tops, expos):
        yield h, sums_ref[h] * jnp.exp2((old - top) * scale) + dot(v, expo), top


def outer_kernel(
    even_ref, odd_ref, wk_ref, wv_ref, order_ref, window_ref, query_ref, sums_ref, top_ref,
    sums_out, top_out,
    key_ref, value_ref, gap_ref,
):
    nodes, width = even_ref.shape
    head_dim = width // HEADS
    per_group = LANES // head_dim
    far = 2 - 4 * lax.rem(lax.axis_index("inner") // 2, 2)
    scale = head_dim ** (-0.5) / math.log(2.0)
    value_ref[:, head_dim:, :] = jnp.ones_like(value_ref[:, head_dim:, :])
    project_keys(jnp.concatenate([even_ref[...], odd_ref[...]], axis=0), wk_ref, wv_ref, key_ref, value_ref, 0)
    gap_ref[0:nodes] = gaps(far, 0, nodes, nodes)
    gap_ref[nodes:] = gaps(-far, 0, nodes, nodes)

    def wide(n):
        return window_ref[order_ref[n]] > nodes

    def reach(first, last):
        heads = [order_ref[n] for n in range(first, last)]
        keys, values = [key_ref[h // per_group] for h in heads], [value_ref[h] for h in heads]
        for h, sums, top in extend(
            heads, keys, values, gap_ref, window_ref, query_ref, sums_ref, top_ref, scale
        ):
            sums_out[h] = sums
            top_out[h] = jnp.broadcast_to(top, top_out.shape[1:])

    def leave(first, last):
        for n in range(first, last):
            h = order_ref[n]
            sums_out[h] = sums_ref[h]
            top_out[h] = top_ref[h]

    @pl.when(wide(GROUP))
    def _():
        reach(0, 2 * GROUP)

    @pl.when(jnp.logical_not(wide(GROUP)))
    def _():
        reach(0, GROUP)
        leave(GROUP, 2 * GROUP)

    for first in range(2 * GROUP, HEADS, GROUP):
        pl.when(wide(first))(functools.partial(reach, first, first + GROUP))
        pl.when(jnp.logical_not(wide(first)))(functools.partial(leave, first, first + GROUP))


def turn_kernel(up_ref, down_ref, w_out_ref, gain_ref, state_ref, up_t, down_t, w_out_t, gain_t, state_t):
    side = 2 * LANES
    one = lax.broadcasted_iota(jnp.int32, (side, side), 0) == lax.broadcasted_iota(jnp.int32, (side, side), 1)
    unit = jnp.where(one, 1.0, 0.0).astype(jnp.bfloat16)
    for ref, turned in ((up_ref, up_t), (down_ref, down_t), (w_out_ref, w_out_t)):
        for start in range(0, ref.shape[1], side):
            turned[start : start + side, :] = dot_t(unit, ref[:, start : start + side]).astype(jnp.bfloat16)
    gain_t[...] = jnp.transpose(jnp.broadcast_to(gain_ref[...], (LANES, gain_ref.shape[1])))
    state_t[...] = jnp.transpose(state_ref[...])


def far_kernel(
    first_ref, second_ref, wk_ref, wv_ref, window_ref, query_ref, sums_ref, top_ref,
    up_t, down_t, w_out_t, gain_t, state_t,
    out_ref,
    key_ref, value_ref, gap_ref, attended_ref,
):
    nodes, width = first_ref.shape
    head_dim = width // HEADS
    per_group = LANES // head_dim
    inner = lax.axis_index("inner")
    odd = lax.rem(inner, 2)
    scale = head_dim ** (-0.5) / math.log(2.0)
    value_ref[:, head_dim:, :] = jnp.ones_like(value_ref[:, head_dim:, :])
    by_even = odd == lax.rem(inner // 2 + 1, 2)
    project_keys(jnp.where(by_even, first_ref[...], second_ref[...]), wk_ref, wv_ref, key_ref, value_ref, 0)
    gap_ref[...] = gaps(2 * odd - 1, 0, nodes, nodes)
    for i in range(HEADS // GROUP):
        heads = range(GROUP * i, GROUP * (i + 1))
        keys, values = [key_ref[h // per_group] for h in heads], [value_ref[h] for h in heads]
        for h, sums, _ in extend(
            heads, keys, values, gap_ref, window_ref, query_ref, sums_ref, top_ref, scale
        ):
            attended_ref[h] = (sums[0:head_dim] / sums[head_dim : head_dim + 1]).astype(jnp.bfloat16)

    total = state_t[...] + dot(w_out_t[...], attended_ref[...].reshape(width, nodes))
    center = total - jnp.mean(total, axis=0, keepdims=True)
    spread = jnp.mean(center * center, axis=0, keepdims=True)
    gain = jnp.concatenate([gain_t[...]] * (nodes // LANES), axis=1)
    normed = (center * lax.rsqrt(spread + norm_eps) * gain).astype(jnp.bfloat16)
    chunk = math.gcd(up_t.shape[0], 512)
    for start in range(0, up_t.shape[0], chunk):
        hidden = silu(dot(up_t[start : start + chunk, :], normed)).astype(jnp.bfloat16)
        total = total + dot(down_t[:, start : start + chunk], hidden)
    out_ref[...] = jnp.transpose(total).astype(jnp.bfloat16)


def cost(flops, size):
    return pl.CostEstimate(flops=flops, bytes_accessed=size, transcendentals=0)


def local(
    grid_rows,
    mesh_rows,
    edge_source,
    edge_target,
    edge_count,
    w_message,
    w_merge,
    gain_attn,
    w_qkv,
    window,
    w_out,
    gain_mlp,
    w_up,
    w_down,
):
    bands = lax.axis_size("band")
    inners = lax.axis_size("inner")
    devices = bands * inners
    grid_dev = grid_rows.shape[0]
    nodes, width = mesh_rows.shape
    cap = edge_source.shape[-1]
    head_dim = width // HEADS
    pairs = inners // 2
    half = width // 2
    f32, bf16, i32 = jnp.float32, jnp.bfloat16, jnp.int32
    edges = (edge_source, edge_target, jnp.transpose(edge_count, (0, 2, 1, 3)))

    def rows_of(*blocks):
        return jax.ShapeDtypeStruct((sum(n * cap + TILE for n in blocks), half), bf16)

    outgoing = [rows_of(pairs)] * 4 + [rows_of(3)] * (2 * pairs - 2) + [rows_of(pairs, 3)] * 2
    even, even_other, odd, odd_other, *cross, here, here_other = pl.pallas_call(
        functools.partial(message_kernel, pairs),
        out_shape=outgoing,
        in_specs=[ANY] * 2 + [VMEM] * 2 + [SMEM],
        out_specs=[ANY] * len(outgoing),
        scratch_shapes=[pltpu.VMEM(a.shape, bf16) for a in outgoing]
        + [
            pltpu.VMEM(grid_rows.shape, bf16),
            pltpu.VMEM(w_message.shape, bf16),
            pltpu.VMEM((grid_dev, width), bf16),
            pltpu.VMEM((3 * inners * cap, grid_dev), bf16),
            pltpu.SemaphoreType.DMA((2 * GRID_PARTS,)),
            pltpu.SemaphoreType.DMA((len(outgoing),)),
        ],
        compiler_params=params(MOST),
        cost_estimate=cost(2 * grid_dev * width * (width + 3 * inners * cap), 4 << 20),
        name="messages",
    )(grid_rows, w_message, *edges)
    beside = [(g, g ^ 1) for g in range(devices)]

    def bands_trade(odd_pairs, k=0):
        route = []
        for g in range(devices):
            b = g // inners
            t = (b - odd_pairs ^ 1) + odd_pairs
            route.append((g, t * inners + (g % inners ^ k) if 0 <= t < bands else g ^ 1))
        return route

    def chip_trade(p, k=0):
        return [(g, g ^ (2 * p + k)) for g in range(devices)]

    here_other = lax.ppermute(here_other, NODES, beside)
    cross[0::2] = [lax.ppermute(c, NODES, chip_trade(p + 1)) for p, c in enumerate(cross[0::2])]
    even = lax.ppermute(even, NODES, bands_trade(0))
    odd = lax.ppermute(odd, NODES, bands_trade(1))
    here_other, even_other, odd_other, *cross[1::2] = lax.optimization_barrier(
        (here_other, even_other, odd_other, *cross[1::2])
    )
    cross[1::2] = [lax.ppermute(c, NODES, chip_trade(p + 1, 1)) for p, c in enumerate(cross[1::2])]
    even_other = lax.ppermute(even_other, NODES, bands_trade(0, 1))
    odd_other = lax.ppermute(odd_other, NODES, bands_trade(1, 1))

    w_qkv, window, here = lax.optimization_barrier((w_qkv, window, here))
    head = jnp.arange(HEADS, dtype=i32)
    ahead = (window[None, :] > window[:, None]) | (
        (window[None, :] == window[:, None]) & (head[None, :] < head[:, None])
    )
    rank = jnp.sum(ahead.astype(i32), axis=1)
    order = jnp.sum(jnp.where(rank[None, :] == head[:, None], head[None, :], 0), axis=1).astype(i32)
    w_query, w_key, w_value, early_left, early_right = pl.pallas_call(
        functools.partial(early_kernel, pairs),
        out_shape=[jax.ShapeDtypeStruct((width, width), bf16)] * 3
        + [jax.ShapeDtypeStruct((n, nodes, half), f32) for n in (pairs, 3)],
        in_specs=[VMEM] * 3 + [SMEM],
        out_specs=[VMEM] * 5,
        compiler_params=params(24),
        cost_estimate=cost(1 << 28, 4 << 20),
        name="early",
    )(w_qkv, here, here_other, order)
    def sums(arrays, early, kept, name):
        count = early.shape[0]
        return pl.pallas_call(
            functools.partial(sums_kernel, len(arrays), kept),
            out_shape=[jax.ShapeDtypeStruct((nodes, half), f32 if n == kept else bf16) for n in range(count)],
            in_specs=[VMEM] * (len(arrays) + 1),
            out_specs=[VMEM] * count,
            compiler_params=params(24),
            cost_estimate=cost(2 * nodes * half * len(arrays) * count * cap, 2 << 20),
            name=name,
        )(*arrays, early)

    left, *parts = sums([even, even_other, odd, odd_other], early_left, 0, "left")
    parts = [lax.ppermute(part, NODES, chip_trade(p + 1)) for p, part in enumerate(parts)]
    to_even, to_odd, right = sums(cross, early_right, 2, "right")
    from_even = lax.ppermute(to_even, NODES, bands_trade(0))
    from_odd = lax.ppermute(to_odd, NODES, bands_trade(1))

    state, normed = pl.pallas_call(
        merge_kernel,
        out_shape=[
            jax.ShapeDtypeStruct((nodes, width), f32),
            jax.ShapeDtypeStruct((nodes, width), bf16),
        ],
        in_specs=[VMEM] * (pairs + 6),
        out_specs=[VMEM] * 2,
        compiler_params=params(24),
        cost_estimate=cost(2 * nodes * width * width, 2 << 20),
        name="merge",
    )(left, *parts, right, from_even, from_odd, mesh_rows, w_merge, gain_attn.reshape(1, width))

    def chips_trade(odd_pairs):
        route = []
        for g in range(devices):
            t = (g // 2 - odd_pairs ^ 1) + odd_pairs
            route.append((g, 2 * t + g % 2 if 0 <= 2 * t < devices else g ^ 1))
        return route

    side = lax.ppermute(normed, NODES, beside)
    even = lax.ppermute(normed, NODES, chips_trade(0))
    odd = lax.ppermute(normed, NODES, chips_trade(1))

    extra = head_dim + 16
    query, near, top = pl.pallas_call(
        near_kernel,
        out_shape=[
            jax.ShapeDtypeStruct((HEADS, LANES, nodes), bf16),
            jax.ShapeDtypeStruct((HEADS, extra, nodes), f32),
            jax.ShapeDtypeStruct((HEADS, 8, nodes), f32),
        ],
        in_specs=[VMEM] * 5 + [SMEM] * 2,
        out_specs=[VMEM] * 3,
        scratch_shapes=[
            pltpu.VMEM((width // LANES, 2 * nodes, LANES), bf16),
            pltpu.VMEM((HEADS, extra, 2 * nodes), bf16),
            pltpu.VMEM((2 * nodes, nodes), i32),
        ],
        compiler_params=params(32),
        cost_estimate=cost(8 << 30, 4 << 20),
        name="near",
    )(normed, side, w_query, w_key, w_value, order, window)

    w_up, w_down, w_out, state, near, top = lax.optimization_barrier((w_up, w_down, w_out, state, near, top))
    turned = pl.pallas_call(
        turn_kernel,
        out_shape=[jax.ShapeDtypeStruct(w.shape[::-1], bf16) for w in (w_up, w_down, w_out)]
        + [jax.ShapeDtypeStruct((width, LANES), f32), jax.ShapeDtypeStruct((width, nodes), f32)],
        in_specs=[VMEM] * 5,
        out_specs=[VMEM] * 5,
        compiler_params=params(24),
        cost_estimate=cost(4 << 30, 10 << 20),
        name="turn",
    )(w_up, w_down, w_out, gain_mlp.reshape(1, width), state)
    even, odd, near, top, *turned = lax.optimization_barrier((even, odd, near, top, *turned))
    first = lax.ppermute(even, NODES, beside)
    second = lax.ppermute(odd, NODES, beside)
    near, top = pl.pallas_call(
        outer_kernel,
        out_shape=[
            jax.ShapeDtypeStruct((HEADS, extra, nodes), f32),
            jax.ShapeDtypeStruct((HEADS, 8, nodes), f32),
        ],
        in_specs=[VMEM] * 4 + [SMEM] * 2 + [VMEM] * 3,
        out_specs=[VMEM] * 2,
        scratch_shapes=[
            pltpu.VMEM((width // LANES, 2 * nodes, LANES), bf16),
            pltpu.VMEM((HEADS, extra, 2 * nodes), bf16),
            pltpu.VMEM((2 * nodes, nodes), i32),
        ],
        compiler_params=params(24),
        cost_estimate=cost(16 * nodes * width * width, 3 << 20),
        name="outer",
    )(even, odd, w_key, w_value, order, window, query, near, top)

    return pl.pallas_call(
        far_kernel,
        out_shape=jax.ShapeDtypeStruct((nodes, width), bf16),
        in_specs=[VMEM] * 4 + [SMEM] + [VMEM] * 8,
        out_specs=VMEM,
        scratch_shapes=[
            pltpu.VMEM((width // LANES, nodes, LANES), bf16),
            pltpu.VMEM((HEADS, extra, nodes), bf16),
            pltpu.VMEM((nodes, nodes), i32),
            pltpu.VMEM((HEADS, head_dim, nodes), bf16),
        ],
        compiler_params=params(40),
        cost_estimate=cost(8 << 30, 8 << 20),
        name="far",
    )(
        first, second, w_key, w_value, window,
        query, near, top, *turned,
    )


def solution(mesh):
    placed = (
        P(("groups", "band", "inner"), None),
        P(("groups", "band", "inner"), None),
        P(("groups", "band"), "inner", None, None, None),
        P(("groups", "band"), "inner", None, None, None),
        P(("groups", "band"), "inner", None, None),
        P(),
        P(),
        P(),
        P(),
        P("groups"),
        P(),
        P(),
        P(),
        P(),
    )
    return jax.shard_map(
        local,
        mesh=mesh,
        in_specs=placed,
        out_specs=P(("groups", "band", "inner"), None),
        check_vma=False,
    )
```

```python
import functools
import math

import jax
import jax.numpy as jnp
from jax import lax
from jax.experimental import pallas as pl
from jax.experimental.pallas import tpu as pltpu
from jax.sharding import PartitionSpec as P

HEADS = 16
WMAX = 512
LANES = 128
NEAR = 128
TILE = 16
CAP = 128
GRID_PARTS = 2
MOST = 56
GROUP = 4

norm_eps = 1e-05
NODES = ("band", "inner")
VMEM = pl.BlockSpec(memory_space=pltpu.VMEM)
SMEM = pl.BlockSpec(memory_space=pltpu.SMEM)
ANY = pl.BlockSpec(memory_space=pl.ANY)


def params(mib):
    return pltpu.CompilerParams(vmem_limit_bytes=mib * 1024 * 1024)


def dot(a, b):
    return jnp.dot(a, b, preferred_element_type=jnp.float32)


def dot_t(a, b):
    return lax.dot_general(a, b, (((1,), (1,)), ((), ())), preferred_element_type=jnp.float32)


def silu(values):
    half = 0.5 * values
    return half + half * jnp.tanh(half)


def layer_norm(values, gain):
    center = values - jnp.mean(values, axis=-1, keepdims=True)
    spread = jnp.mean(center * center, axis=-1, keepdims=True)
    return center * lax.rsqrt(spread + norm_eps) * gain


def band_offsets():
    ahead = lax.rem(lax.axis_index("band"), 2) * 2
    return 2 - ahead, ahead, 1


def slot_columns(source_ref, blocks):
    sources = jnp.concatenate([source_ref[0, 0, o, pl.ds(j, 1), :] for o, j in blocks], axis=0)
    return jnp.transpose(sources.astype(jnp.float32)).astype(jnp.int32)


def target_tile(target_ref, count_ref, blocks, lanes):
    cap = target_ref.shape[-1]
    slot = lax.broadcasted_iota(jnp.int32, (1, cap), 1)
    targets = [
        jnp.where(slot < count_ref[0, o, 0, j], target_ref[0, 0, o, pl.ds(j, 1), :], -1) for o, j in blocks
    ]
    targets.append(jnp.full((TILE - len(blocks), cap), -1, jnp.int32))
    tile = jnp.concatenate(targets, axis=0).astype(jnp.float32).astype(jnp.bfloat16)
    return jnp.concatenate([tile] * (lanes // cap), axis=1)


def message_kernel(pair_count, grid_ref, w_ref, source_in, target_in, count_in, *refs):
    count = 4 + 2 * pair_count
    out_refs, out_vmems = refs[:count], refs[count : 2 * count]
    source_ref, target_ref, count_ref, grid_vmem, w_vmem, message_ref, pick_ref, in_sems, edge_sems, out_sems = refs[2 * count :]
    rows = grid_ref.shape[0]
    cap = source_ref.shape[-1]
    half = w_ref.shape[1] // 2
    part = rows // GRID_PARTS
    fetches = [pltpu.make_async_copy(w_ref, w_vmem, in_sems.at[GRID_PARTS])]
    for k in range(GRID_PARTS):
        span = pl.ds(k * part, part)
        fetches.append(pltpu.make_async_copy(grid_ref.at[span], grid_vmem.at[span], in_sems.at[k]))
    edges = ((source_in, source_ref), (target_in, target_ref), (count_in, count_ref))
    edge_fetches = [pltpu.make_async_copy(a, b, edge_sems.at[n]) for n, (a, b) in enumerate(edges)]
    for fetch in edge_fetches + fetches:
        fetch.start()
    for fetch in edge_fetches:
        fetch.wait()
    inner = lax.axis_index("inner")
    offsets = band_offsets()
    keys = [(t, p, k) for k in range(2) for t in range(3) for p in range(pair_count)]
    place = {(t, p, k): (offsets[t], inner ^ (2 * p + k)) for t, p, k in keys}
    by_slot = slot_columns(source_ref, [place[key] for key in keys])
    left, right = slice(0, half), slice(half, 2 * half)
    runs = [[([(t, p, k) for p in range(pair_count)], left)] for t in range(2) for k in range(2)]
    runs += [[([(t, p, k) for t in range(3)], right)] for p in range(1, pair_count) for k in range(2)]
    runs += [
        [([(2, p, k) for p in range(pair_count)], left), ([(t, 0, k) for t in range(3)], right)] for k in range(2)
    ]
    for out_vmem, parts in zip(out_vmems, runs):
        start = 0
        for chosen, _ in parts:
            start += len(chosen) * cap
            out_vmem[start : start + TILE, :] = target_tile(target_ref, count_ref, [place[key] for key in chosen], half)
            start += TILE
    row = lax.broadcasted_iota(jnp.int32, (cap, rows), 1)
    for m in range(len(keys)):
        pick_ref[m * cap : (m + 1) * cap, :] = jnp.where(row == by_slot[:, m : m + 1], 1.0, 0.0).astype(jnp.bfloat16)
    fetches[0].wait()
    for k in range(GRID_PARTS):
        span = pl.ds(k * part, part)
        fetches[k + 1].wait()
        message_ref[span] = silu(dot(grid_vmem[span], w_vmem[...])).astype(jnp.bfloat16)
    sends = []
    per_core = len(keys) // 2
    for k in range(2):
        first = k * per_core
        taken = dot(pick_ref[first * cap : (first + per_core) * cap, :], message_ref[...]).astype(jnp.bfloat16)
        for n in range(count):
            start = 0
            if runs[n][0][0][0][2] != k:
                continue
            for chosen, lanes in runs[n]:
                for key in chosen:
                    m = keys.index(key) - first
                    out_vmems[n][start : start + cap, :] = taken[m * cap : (m + 1) * cap, lanes]
                    start += cap
                start += TILE
            send = pltpu.make_async_copy(out_vmems[n], out_refs[n], out_sems.at[n])
            send.start()
            sends.append(send)
    for send in sends:
        send.wait()


def node_sums(arrays, nodes):
    count = arrays[0][2]
    cap = CAP
    node = lax.broadcasted_iota(jnp.int32, (nodes, cap), 0)
    targets = [
        ref[start + count * cap : start + count * cap + TILE, 0:cap].astype(jnp.float32).astype(jnp.int32)
        for ref, start, _ in arrays
    ]
    for n in range(count):
        hits = [jnp.where(node == t[n : n + 1], 1.0, 0.0).astype(jnp.bfloat16) for t in targets]
        rows = [ref[start + n * cap : start + (n + 1) * cap, :] for ref, start, _ in arrays]
        yield n, dot(jnp.concatenate(hits, axis=1), jnp.concatenate(rows, axis=0))


def early_kernel(pair_count, w_ref, own_ref, other_ref, plan_ref, query_ref, key_ref, value_ref, left_ref, right_ref):
    width = w_ref.shape[0]
    head_dim = width // HEADS
    span = 3 * LANES
    def pick(c, along):
        shape = (LANES, span) if along else (span, LANES)
        to = lax.broadcasted_iota(jnp.int32, shape, 1 - along)
        column = lax.broadcasted_iota(jnp.int32, shape, along)
        wanted = to // head_dim * (3 * head_dim) + to % head_dim + c * head_dim
        return jnp.where(column == wanted, 1.0, 0.0).astype(jnp.bfloat16)

    for g in range(width // LANES):
        columns = w_ref[:, g * span : (g + 1) * span]
        part = slice(g * LANES, (g + 1) * LANES)
        query_ref[part, :] = dot_t(pick(0, 1), columns).astype(jnp.bfloat16)
        key_ref[:, part] = dot(columns, pick(1, 0)).astype(jnp.bfloat16)
        value_ref[part, :] = dot_t(pick(2, 1), columns).astype(jnp.bfloat16)
    start = 0
    for sum_ref in (left_ref, right_ref):
        count, nodes, _ = sum_ref.shape
        for n, total in node_sums([(own_ref, start, count), (other_ref, start, count)], nodes):
            sum_ref[n] = total
        start += count * CAP + TILE


def sums_kernel(array_count, kept, *refs):
    row_refs, early_ref, out_refs = refs[:array_count], refs[array_count], refs[array_count + 1 :]
    count, nodes, _ = early_ref.shape
    for n, total in node_sums([(r, 0, count) for r in row_refs], nodes):
        total = total + early_ref[n]
        out_refs[n][...] = total if n == kept else total.astype(jnp.bfloat16)


def merge_kernel(*refs):
    *part_refs, right_ref, even_ref, odd_ref, mesh_ref, w_ref, gain_ref, state_ref, normed_ref = refs
    left = functools.reduce(jnp.add, [r[...].astype(jnp.float32) for r in part_refs])
    right = right_ref[...] + even_ref[...].astype(jnp.float32) + odd_ref[...].astype(jnp.float32)
    total = jnp.concatenate([left, right], axis=1).astype(jnp.bfloat16)
    state = mesh_ref[...].astype(jnp.float32) + dot(total, w_ref[...])
    state_ref[...] = state
    normed_ref[...] = layer_norm(state, gain_ref[...]).astype(jnp.bfloat16)


def project_keys(rows, wk_ref, wv_ref, key_ref, value_ref, start):
    count = rows.shape[0]
    groups = key_ref.shape[0]
    heads = value_ref.shape[0]
    keys = dot(rows, wk_ref[...]).astype(jnp.bfloat16)
    for g in range(groups):
        key_ref[g, start : start + count, :] = keys[:, g * LANES : (g + 1) * LANES]
    values = dot_t(wv_ref[...], rows).astype(jnp.bfloat16)
    value_ref[:, 0 : values.shape[0] // heads, start : start + count] = values.reshape(
        heads, -1, count
    )


def near_kernel(
    own_ref, side_ref, wq_ref, wk_ref, wv_ref, plan_ref,
    query_ref, sums_ref, top_ref,
    key_ref, value_ref, gap_ref,
):
    nodes, width = own_ref.shape
    head_dim = width // HEADS
    per_group = LANES // head_dim
    odd = lax.rem(lax.axis_index("inner"), 2)
    side = 1 - 2 * odd
    first = odd * (nodes - NEAR)
    second = (1 - odd) * NEAR
    scale = head_dim ** (-0.5) / math.log(2.0)

    queries = dot_t(wq_ref[...], own_ref[...]).astype(jnp.bfloat16)
    part = lax.broadcasted_iota(jnp.int32, (LANES, nodes), 0) // head_dim
    for h in range(HEADS):
        g = h // per_group
        lanes = queries[g * LANES : (g + 1) * LANES]
        query_ref[h] = jnp.where(part == h % per_group, lanes, jnp.zeros_like(lanes))
    value_ref[:, head_dim:, :] = jnp.ones_like(value_ref[:, head_dim:, :])
    project_keys(own_ref[...], wk_ref, wv_ref, key_ref, value_ref, 0)
    project_keys(side_ref[pl.ds(pl.multiple_of(first, NEAR), NEAR), :], wk_ref, wv_ref, key_ref, value_ref, nodes)
    project_keys(
        side_ref[pl.ds(pl.multiple_of(second, NEAR), NEAR), :], wk_ref, wv_ref, key_ref, value_ref, nodes + NEAR
    )
    lag = lax.broadcasted_iota(jnp.int32, (nodes, nodes), 0) - lax.broadcasted_iota(
        jnp.int32, (nodes, nodes), 1
    )
    gap_ref[0:nodes] = jnp.abs(lag)
    gap_ref[nodes : nodes + NEAR] = jnp.abs(lag[0:NEAR] + (side * nodes + first))
    gap_ref[nodes + NEAR : 2 * nodes] = jnp.abs(lag[0:NEAR] + (side * nodes + second))

    def attend(heads, windows, rows):
        scores = [dot(key_ref[h // per_group, 0:rows, :], query_ref[h]) for h in heads]
        scores = [
            jnp.where(gap_ref[0:rows] <= w, x, -1e30) for w, x in zip(windows, scores)
        ]
        tops = [jnp.max(x, axis=0, keepdims=True) for x in scores]
        expos = [jnp.exp2((x - top) * scale).astype(jnp.bfloat16) for x, top in zip(scores, tops)]
        for h, w, top, expo in zip(heads, windows, tops, expos):
            sums_ref[h] = dot(value_ref[h, :, 0:rows], expo)
            top_ref[h, 0:1] = top
            top_ref[h, 1:2] = jnp.full((1, nodes), w.astype(jnp.float32))

    def together(i, carry):
        heads = [plan_ref[0, GROUP * i + k] for k in range(GROUP)]
        windows = [plan_ref[1, GROUP * i + k] for k in range(GROUP)]
        widest = windows[0]

        @pl.when(widest <= NEAR)
        def _():
            attend(heads, windows, nodes + NEAR)

        @pl.when(widest > NEAR)
        def _():
            attend(heads, windows, 2 * nodes)

        return carry

    lax.fori_loop(0, HEADS // GROUP, together, 0)


def gaps(device, start, rows, nodes):
    total = lax.axis_size("band") * lax.axis_size("inner")
    there = lax.axis_index("band") * lax.axis_size("inner") + lax.axis_index("inner") + device
    lag = lax.broadcasted_iota(jnp.int32, (rows, nodes), 0) - lax.broadcasted_iota(jnp.int32, (rows, nodes), 1)
    gap = jnp.where((there >= 0) & (there < total), jnp.abs(lag + (device * nodes + start)), 1 << 20)
    return gap.astype(jnp.float32)


def extend(heads, keys, values, gap_ref, query_ref, sums_ref, top_ref, scale):
    scores = [dot(k, query_ref[h]) for h, k in zip(heads, keys)]
    scores = [jnp.where(gap_ref[...] <= top_ref[h, 1:2, :], x, -1e30) for h, x in zip(heads, scores)]
    olds = [top_ref[h, 0:1, :] for h in heads]
    tops = [jnp.maximum(old, jnp.max(x, axis=0, keepdims=True)) for old, x in zip(olds, scores)]
    expos = [jnp.exp2((x - top) * scale).astype(jnp.bfloat16) for x, top in zip(scores, tops)]
    for h, v, old, top, expo in zip(heads, values, olds, tops, expos):
        yield h, sums_ref[h] * jnp.exp2((old - top) * scale) + dot(v, expo), top


def outer_kernel(
    even_ref, odd_ref, wk_ref, wv_ref, plan_ref, query_ref, sums_ref, top_ref,
    sums_out, top_out,
    key_ref, value_ref, gap_ref,
):
    nodes, width = even_ref.shape
    head_dim = width // HEADS
    per_group = LANES // head_dim
    far = 2 - 4 * lax.rem(lax.axis_index("inner") // 2, 2)
    scale = head_dim ** (-0.5) / math.log(2.0)
    value_ref[:, head_dim:, :] = jnp.ones_like(value_ref[:, head_dim:, :])
    project_keys(jnp.concatenate([even_ref[...], odd_ref[...]], axis=0), wk_ref, wv_ref, key_ref, value_ref, 0)
    gap_ref[0:nodes] = gaps(far, 0, nodes, nodes)
    gap_ref[nodes:] = gaps(-far, 0, nodes, nodes)

    def wide(n):
        return plan_ref[1, n] > nodes

    def reach(first, last):
        heads = [plan_ref[0, n] for n in range(first, last)]
        keys, values = [key_ref[h // per_group] for h in heads], [value_ref[h] for h in heads]
        for h, sums, top in extend(
            heads, keys, values, gap_ref, query_ref, sums_ref, top_ref, scale
        ):
            sums_out[h] = sums
            top_out[h, 0:1] = top
            top_out[h, 1:2] = top_ref[h, 1:2]

    def leave(first, last):
        for n in range(first, last):
            h = plan_ref[0, n]
            sums_out[h] = sums_ref[h]
            top_out[h, 0:2] = top_ref[h, 0:2]

    @pl.when(wide(GROUP))
    def _():
        reach(0, 2 * GROUP)

    @pl.when(jnp.logical_not(wide(GROUP)))
    def _():
        reach(0, GROUP)
        leave(GROUP, 2 * GROUP)

    for first in range(2 * GROUP, HEADS, GROUP):
        pl.when(wide(first))(functools.partial(reach, first, first + GROUP))
        pl.when(jnp.logical_not(wide(first)))(functools.partial(leave, first, first + GROUP))


def far_kernel(
    first_ref, second_ref, wk_ref, wv_ref, query_ref, sums_ref, top_ref,
    state_ref, w_out_ref, gain_ref, up_ref, down_ref,
    out_ref,
    key_ref, value_ref, gap_ref, attended_ref,
):
    nodes, width = first_ref.shape
    head_dim = width // HEADS
    per_group = LANES // head_dim
    inner = lax.axis_index("inner")
    odd = lax.rem(inner, 2)
    scale = head_dim ** (-0.5) / math.log(2.0)
    value_ref[:, head_dim:, :] = jnp.ones_like(value_ref[:, head_dim:, :])
    by_even = odd == lax.rem(inner // 2 + 1, 2)
    project_keys(jnp.where(by_even, first_ref[...], second_ref[...]), wk_ref, wv_ref, key_ref, value_ref, 0)
    gap_ref[...] = gaps(2 * odd - 1, 0, nodes, nodes)
    for i in range(HEADS // GROUP):
        heads = range(GROUP * i, GROUP * (i + 1))
        keys, values = [key_ref[h // per_group] for h in heads], [value_ref[h] for h in heads]
        for h, sums, _ in extend(
            heads, keys, values, gap_ref, query_ref, sums_ref, top_ref, scale
        ):
            attended_ref[h] = (sums[0:head_dim] / sums[head_dim : head_dim + 1]).astype(jnp.bfloat16)

    attended = attended_ref[...].reshape(width, nodes)
    mixed = lax.dot_general(
        attended, w_out_ref[...], (((0,), (0,)), ((), ())), preferred_element_type=jnp.float32
    )
    total = state_ref[...] + mixed
    normed = layer_norm(total, gain_ref[...]).astype(jnp.bfloat16)
    chunk = math.gcd(up_ref.shape[1], 512)
    for start in range(0, up_ref.shape[1], chunk):
        hidden = silu(dot(normed, up_ref[:, start : start + chunk])).astype(jnp.bfloat16)
        total = total + dot(hidden, down_ref[start : start + chunk, :])
    out_ref[...] = total.astype(jnp.bfloat16)


def cost(flops, size):
    return pl.CostEstimate(flops=flops, bytes_accessed=size, transcendentals=0)


def local(
    grid_rows,
    mesh_rows,
    edge_source,
    edge_target,
    edge_count,
    w_message,
    w_merge,
    gain_attn,
    w_qkv,
    window,
    w_out,
    gain_mlp,
    w_up,
    w_down,
):
    bands = lax.axis_size("band")
    inners = lax.axis_size("inner")
    devices = bands * inners
    grid_dev = grid_rows.shape[0]
    nodes, width = mesh_rows.shape
    cap = edge_source.shape[-1]
    head_dim = width // HEADS
    pairs = inners // 2
    half = width // 2
    f32, bf16, i32 = jnp.float32, jnp.bfloat16, jnp.int32
    edges = (edge_source, edge_target, jnp.transpose(edge_count, (0, 2, 1, 3)))

    def rows_of(*blocks):
        return jax.ShapeDtypeStruct((sum(n * cap + TILE for n in blocks), half), bf16)

    outgoing = [rows_of(pairs)] * 4 + [rows_of(3)] * (2 * pairs - 2) + [rows_of(pairs, 3)] * 2
    even, even_other, odd, odd_other, *cross, here, here_other = pl.pallas_call(
        functools.partial(message_kernel, pairs),
        out_shape=outgoing,
        in_specs=[ANY] * 5,
        out_specs=[ANY] * len(outgoing),
        scratch_shapes=[pltpu.VMEM(a.shape, bf16) for a in outgoing]
        + [
            pltpu.VMEM(edges[0].shape, i32),
            pltpu.VMEM(edges[1].shape, i32),
            pltpu.SMEM(edges[2].shape, i32),
            pltpu.VMEM(grid_rows.shape, bf16),
            pltpu.VMEM(w_message.shape, bf16),
            pltpu.VMEM((grid_dev, width), bf16),
            pltpu.VMEM((3 * inners * cap, grid_dev), bf16),
            pltpu.SemaphoreType.DMA((GRID_PARTS + 1,)),
            pltpu.SemaphoreType.DMA((3,)),
            pltpu.SemaphoreType.DMA((len(outgoing),)),
        ],
        compiler_params=params(MOST),
        cost_estimate=cost(2 * grid_dev * width * (width + 3 * inners * cap), 4 << 20),
        name="messages",
    )(grid_rows, w_message, *edges)
    beside = [(g, g ^ 1) for g in range(devices)]

    def bands_trade(odd_pairs, k=0):
        route = []
        for g in range(devices):
            b = g // inners
            t = (b - odd_pairs ^ 1) + odd_pairs
            route.append((g, t * inners + (g % inners ^ k) if 0 <= t < bands else g ^ 1))
        return route

    def chip_trade(p, k=0):
        return [(g, g ^ (2 * p + k)) for g in range(devices)]

    here_other = lax.ppermute(here_other, NODES, beside)
    cross[0::2] = [lax.ppermute(c, NODES, chip_trade(p + 1)) for p, c in enumerate(cross[0::2])]
    even = lax.ppermute(even, NODES, bands_trade(0))
    odd = lax.ppermute(odd, NODES, bands_trade(1))
    here_other, even_other, odd_other, *cross[1::2] = lax.optimization_barrier(
        (here_other, even_other, odd_other, *cross[1::2])
    )
    cross[1::2] = [lax.ppermute(c, NODES, chip_trade(p + 1, 1)) for p, c in enumerate(cross[1::2])]
    even_other = lax.ppermute(even_other, NODES, bands_trade(0, 1))
    odd_other = lax.ppermute(odd_other, NODES, bands_trade(1, 1))

    w_qkv, window, here = lax.optimization_barrier((w_qkv, window, here))
    head = jnp.arange(HEADS, dtype=i32)
    ahead = (window[None, :] > window[:, None]) | (
        (window[None, :] == window[:, None]) & (head[None, :] < head[:, None])
    )
    rank = jnp.sum(ahead.astype(i32), axis=1)
    sorted_to = rank[None, :] == head[:, None]
    plan = jnp.sum(jnp.where(sorted_to[None], jnp.stack([head, window])[:, None, :], 0), axis=2).astype(i32)
    w_query, w_key, w_value, early_left, early_right = pl.pallas_call(
        functools.partial(early_kernel, pairs),
        out_shape=[jax.ShapeDtypeStruct((width, width), bf16)] * 3
        + [jax.ShapeDtypeStruct((n, nodes, half), f32) for n in (pairs, 3)],
        in_specs=[VMEM] * 3 + [ANY],
        out_specs=[VMEM] * 5,
        compiler_params=params(24),
        cost_estimate=cost(1 << 28, 4 << 20),
        name="early",
    )(w_qkv, here, here_other, plan)
    def sums(arrays, early, kept, name):
        count = early.shape[0]
        return pl.pallas_call(
            functools.partial(sums_kernel, len(arrays), kept),
            out_shape=[jax.ShapeDtypeStruct((nodes, half), f32 if n == kept else bf16) for n in range(count)],
            in_specs=[VMEM] * (len(arrays) + 1),
            out_specs=[VMEM] * count,
            compiler_params=params(24),
            cost_estimate=cost(2 * nodes * half * len(arrays) * count * cap, 2 << 20),
            name=name,
        )(*arrays, early)

    left, *parts = sums([even, even_other, odd, odd_other], early_left, 0, "left")
    parts = [lax.ppermute(part, NODES, chip_trade(p + 1)) for p, part in enumerate(parts)]
    to_even, to_odd, right = sums(cross, early_right, 2, "right")
    from_even = lax.ppermute(to_even, NODES, bands_trade(0))
    from_odd = lax.ppermute(to_odd, NODES, bands_trade(1))

    state, normed = pl.pallas_call(
        merge_kernel,
        out_shape=[
            jax.ShapeDtypeStruct((nodes, width), f32),
            jax.ShapeDtypeStruct((nodes, width), bf16),
        ],
        in_specs=[VMEM] * (pairs + 6),
        out_specs=[VMEM] * 2,
        compiler_params=params(24),
        cost_estimate=cost(2 * nodes * width * width, 2 << 20),
        name="merge",
    )(left, *parts, right, from_even, from_odd, mesh_rows, w_merge, gain_attn.reshape(1, width))

    def chips_trade(odd_pairs):
        route = []
        for g in range(devices):
            t = (g // 2 - odd_pairs ^ 1) + odd_pairs
            route.append((g, 2 * t + g % 2 if 0 <= 2 * t < devices else g ^ 1))
        return route

    side = lax.ppermute(normed, NODES, beside)
    even = lax.ppermute(normed, NODES, chips_trade(0))
    side, normed = lax.optimization_barrier((side, normed))
    odd = lax.ppermute(normed, NODES, chips_trade(1))

    extra = head_dim + 16
    query, near, top = pl.pallas_call(
        near_kernel,
        out_shape=[
            jax.ShapeDtypeStruct((HEADS, LANES, nodes), bf16),
            jax.ShapeDtypeStruct((HEADS, extra, nodes), f32),
            jax.ShapeDtypeStruct((HEADS, 8, nodes), f32),
        ],
        in_specs=[VMEM] * 5 + [SMEM],
        out_specs=[VMEM] * 3,
        scratch_shapes=[
            pltpu.VMEM((width // LANES, 2 * nodes, LANES), bf16),
            pltpu.VMEM((HEADS, extra, 2 * nodes), bf16),
            pltpu.VMEM((2 * nodes, nodes), i32),
        ],
        compiler_params=params(32),
        cost_estimate=cost(8 << 30, 4 << 20),
        name="near",
    )(normed, side, w_query, w_key, w_value, plan)

    even, odd, near, top = lax.optimization_barrier((even, odd, near, top))
    first = lax.ppermute(even, NODES, beside)
    second = lax.ppermute(odd, NODES, beside)
    near, top = pl.pallas_call(
        outer_kernel,
        out_shape=[
            jax.ShapeDtypeStruct((HEADS, extra, nodes), f32),
            jax.ShapeDtypeStruct((HEADS, 8, nodes), f32),
        ],
        in_specs=[VMEM] * 4 + [SMEM] + [VMEM] * 3,
        out_specs=[VMEM] * 2,
        scratch_shapes=[
            pltpu.VMEM((width // LANES, 2 * nodes, LANES), bf16),
            pltpu.VMEM((HEADS, extra, 2 * nodes), bf16),
            pltpu.VMEM((2 * nodes, nodes), f32),
        ],
        compiler_params=params(24),
        cost_estimate=cost(16 * nodes * width * width, 3 << 20),
        name="outer",
    )(even, odd, w_key, w_value, plan, query, near, top)

    return pl.pallas_call(
        far_kernel,
        out_shape=jax.ShapeDtypeStruct((nodes, width), bf16),
        in_specs=[VMEM] * 12,
        out_specs=VMEM,
        scratch_shapes=[
            pltpu.VMEM((width // LANES, nodes, LANES), bf16),
            pltpu.VMEM((HEADS, extra, nodes), bf16),
            pltpu.VMEM((nodes, nodes), f32),
            pltpu.VMEM((HEADS, head_dim, nodes), bf16),
        ],
        compiler_params=params(40),
        cost_estimate=cost(8 << 30, 8 << 20),
        name="far",
    )(
        first, second, w_key, w_value,
        query, near, top, state, w_out, gain_mlp.reshape(1, width), w_up, w_down,
    )


def solution(mesh):
    placed = (
        P(("groups", "band", "inner"), None),
        P(("groups", "band", "inner"), None),
        P(("groups", "band"), "inner", None, None, None),
        P(("groups", "band"), "inner", None, None, None),
        P(("groups", "band"), "inner", None, None),
        P(),
        P(),
        P(),
        P(),
        P("groups"),
        P(),
        P(),
        P(),
        P(),
    )
    return jax.shard_map(
        local,
        mesh=mesh,
        in_specs=placed,
        out_specs=P(("groups", "band", "inner"), None),
        check_vma=False,
    )
```

```python
import functools
import math

import jax
import jax.numpy as jnp
from jax import lax
from jax.experimental import pallas as pl
from jax.experimental.pallas import tpu as pltpu
from jax.sharding import PartitionSpec as P

HEADS = 16
WMAX = 512
LANES = 128
NEAR = 128
TILE = 16
CAP = 128
GRID_PARTS = 2
MOST = 56
GROUP = 4

norm_eps = 1e-05
NODES = ("band", "inner")
VMEM = pl.BlockSpec(memory_space=pltpu.VMEM)
SMEM = pl.BlockSpec(memory_space=pltpu.SMEM)
ANY = pl.BlockSpec(memory_space=pl.ANY)


def params(mib):
    return pltpu.CompilerParams(vmem_limit_bytes=mib * 1024 * 1024)


def dot(a, b):
    return jnp.dot(a, b, preferred_element_type=jnp.float32)


def dot_t(a, b):
    return lax.dot_general(a, b, (((1,), (1,)), ((), ())), preferred_element_type=jnp.float32)


def silu(values):
    half = 0.5 * values
    return half + half * jnp.tanh(half)


def layer_norm(values, gain):
    center = values - jnp.mean(values, axis=-1, keepdims=True)
    spread = jnp.mean(center * center, axis=-1, keepdims=True)
    return center * lax.rsqrt(spread + norm_eps) * gain


def band_offsets():
    ahead = lax.rem(lax.axis_index("band"), 2) * 2
    return 2 - ahead, ahead, 1


def slot_columns(source_ref, blocks):
    sources = jnp.concatenate([source_ref[0, 0, o, pl.ds(j, 1), :] for o, j in blocks], axis=0)
    return jnp.transpose(sources.astype(jnp.float32)).astype(jnp.int32)


def target_tile(target_ref, count_ref, blocks, lanes):
    cap = target_ref.shape[-1]
    slot = lax.broadcasted_iota(jnp.int32, (1, cap), 1)
    targets = [
        jnp.where(slot < count_ref[0, o, 0, j], target_ref[0, 0, o, pl.ds(j, 1), :], -1) for o, j in blocks
    ]
    targets.append(jnp.full((TILE - len(blocks), cap), -1, jnp.int32))
    tile = jnp.concatenate(targets, axis=0).astype(jnp.float32).astype(jnp.bfloat16)
    return jnp.concatenate([tile] * (lanes // cap), axis=1)


def message_kernel(pair_count, grid_ref, w_ref, source_in, target_in, count_in, *refs):
    count = 4 + 2 * pair_count
    out_refs, out_vmems = refs[:count], refs[count : 2 * count]
    source_ref, target_ref, count_ref, grid_vmem, w_vmem, message_ref, pick_ref, in_sems, edge_sems, out_sems = refs[2 * count :]
    rows = grid_ref.shape[0]
    cap = source_ref.shape[-1]
    half = w_ref.shape[1] // 2
    part = rows // GRID_PARTS
    fetches = [pltpu.make_async_copy(w_ref, w_vmem, in_sems.at[GRID_PARTS])]
    for k in range(GRID_PARTS):
        span = pl.ds(k * part, part)
        fetches.append(pltpu.make_async_copy(grid_ref.at[span], grid_vmem.at[span], in_sems.at[k]))
    edges = ((source_in, source_ref), (target_in, target_ref), (count_in, count_ref))
    edge_fetches = [pltpu.make_async_copy(a, b, edge_sems.at[n]) for n, (a, b) in enumerate(edges)]
    for fetch in edge_fetches + fetches:
        fetch.start()
    for fetch in edge_fetches:
        fetch.wait()
    inner = lax.axis_index("inner")
    offsets = band_offsets()
    keys = [(t, p, k) for k in range(2) for t in range(3) for p in range(pair_count)]
    place = {(t, p, k): (offsets[t], inner ^ (2 * p + k)) for t, p, k in keys}
    by_slot = slot_columns(source_ref, [place[key] for key in keys])
    left, right = slice(0, half), slice(half, 2 * half)
    runs = [[([(t, p, k) for p in range(pair_count)], left)] for t in range(2) for k in range(2)]
    runs += [[([(t, p, k) for t in range(3)], right)] for p in range(1, pair_count) for k in range(2)]
    runs += [
        [([(2, p, k) for p in range(pair_count)], left), ([(t, 0, k) for t in range(3)], right)] for k in range(2)
    ]
    for out_vmem, parts in zip(out_vmems, runs):
        start = 0
        for chosen, _ in parts:
            start += len(chosen) * cap
            out_vmem[start : start + TILE, :] = target_tile(target_ref, count_ref, [place[key] for key in chosen], half)
            start += TILE
    row = lax.broadcasted_iota(jnp.int32, (cap, rows), 1)
    for m in range(len(keys)):
        pick_ref[m * cap : (m + 1) * cap, :] = jnp.where(row == by_slot[:, m : m + 1], 1.0, 0.0).astype(jnp.bfloat16)
    fetches[0].wait()
    for k in range(GRID_PARTS):
        span = pl.ds(k * part, part)
        fetches[k + 1].wait()
        message_ref[span] = silu(dot(grid_vmem[span], w_vmem[...])).astype(jnp.bfloat16)
    sends = []
    per_core = len(keys) // 2
    for k in range(2):
        first = k * per_core
        taken = dot(pick_ref[first * cap : (first + per_core) * cap, :], message_ref[...]).astype(jnp.bfloat16)
        for n in reversed(range(count)):
            start = 0
            if runs[n][0][0][0][2] != k:
                continue
            for chosen, lanes in runs[n]:
                for key in chosen:
                    m = keys.index(key) - first
                    out_vmems[n][start : start + cap, :] = taken[m * cap : (m + 1) * cap, lanes]
                    start += cap
                start += TILE
            send = pltpu.make_async_copy(out_vmems[n], out_refs[n], out_sems.at[n])
            send.start()
            sends.append(send)
    for send in sends:
        send.wait()


def node_sums(arrays, nodes):
    count = arrays[0][2]
    cap = CAP
    node = lax.broadcasted_iota(jnp.int32, (nodes, cap), 0)
    targets = [
        ref[start + count * cap : start + count * cap + TILE, 0:cap].astype(jnp.float32).astype(jnp.int32)
        for ref, start, _ in arrays
    ]
    for n in range(count):
        hits = [jnp.where(node == t[n : n + 1], 1.0, 0.0).astype(jnp.bfloat16) for t in targets]
        rows = [ref[start + n * cap : start + (n + 1) * cap, :] for ref, start, _ in arrays]
        yield n, dot(jnp.concatenate(hits, axis=1), jnp.concatenate(rows, axis=0))


def early_kernel(pair_count, w_ref, own_ref, other_ref, plan_ref, query_ref, key_ref, value_ref, left_ref, right_ref):
    width = w_ref.shape[0]
    head_dim = width // HEADS
    span = 3 * LANES
    def pick(c, along):
        shape = (LANES, span) if along else (span, LANES)
        to = lax.broadcasted_iota(jnp.int32, shape, 1 - along)
        column = lax.broadcasted_iota(jnp.int32, shape, along)
        wanted = to // head_dim * (3 * head_dim) + to % head_dim + c * head_dim
        return jnp.where(column == wanted, 1.0, 0.0).astype(jnp.bfloat16)

    for g in range(width // LANES):
        columns = w_ref[:, g * span : (g + 1) * span]
        part = slice(g * LANES, (g + 1) * LANES)
        query_ref[part, :] = dot_t(pick(0, 1), columns).astype(jnp.bfloat16)
        key_ref[:, part] = dot(columns, pick(1, 0)).astype(jnp.bfloat16)
        value_ref[part, :] = dot_t(pick(2, 1), columns).astype(jnp.bfloat16)
    start = 0
    for sum_ref in (left_ref, right_ref):
        count, nodes, _ = sum_ref.shape
        for n, total in node_sums([(own_ref, start, count), (other_ref, start, count)], nodes):
            sum_ref[n] = total
        start += count * CAP + TILE


def sums_kernel(array_count, kept, *refs):
    row_refs, early_ref, out_refs = refs[:array_count], refs[array_count], refs[array_count + 1 :]
    count, nodes, _ = early_ref.shape
    for n, total in node_sums([(r, 0, count) for r in row_refs], nodes):
        total = total + early_ref[n]
        out_refs[n][...] = total if n == kept else total.astype(jnp.bfloat16)


def merge_kernel(*refs):
    *part_refs, right_ref, even_ref, odd_ref, mesh_ref, w_ref, gain_ref, state_ref, normed_ref = refs
    left = functools.reduce(jnp.add, [r[...].astype(jnp.float32) for r in part_refs])
    right = right_ref[...] + even_ref[...].astype(jnp.float32) + odd_ref[...].astype(jnp.float32)
    total = jnp.concatenate([left, right], axis=1).astype(jnp.bfloat16)
    state = mesh_ref[...].astype(jnp.float32) + dot(total, w_ref[...])
    state_ref[...] = state
    normed_ref[...] = layer_norm(state, gain_ref[...]).astype(jnp.bfloat16)


def project_keys(rows, wk_ref, wv_ref, key_ref, value_ref, start):
    count = rows.shape[0]
    groups = key_ref.shape[0]
    heads = value_ref.shape[0]
    keys = dot(rows, wk_ref[...]).astype(jnp.bfloat16)
    for g in range(groups):
        key_ref[g, start : start + count, :] = keys[:, g * LANES : (g + 1) * LANES]
    values = dot_t(wv_ref[...], rows).astype(jnp.bfloat16)
    value_ref[:, 0 : values.shape[0] // heads, start : start + count] = values.reshape(
        heads, -1, count
    )


def near_kernel(
    own_ref, side_ref, wq_ref, wk_ref, wv_ref, plan_ref,
    query_ref, sums_ref, top_ref,
    key_ref, value_ref, gap_ref,
):
    nodes, width = own_ref.shape
    head_dim = width // HEADS
    per_group = LANES // head_dim
    odd = lax.rem(lax.axis_index("inner"), 2)
    side = 1 - 2 * odd
    first = odd * (nodes - NEAR)
    second = (1 - odd) * NEAR
    scale = head_dim ** (-0.5) / math.log(2.0)

    queries = dot_t(wq_ref[...], own_ref[...]).astype(jnp.bfloat16)
    part = lax.broadcasted_iota(jnp.int32, (LANES, nodes), 0) // head_dim
    for h in range(HEADS):
        g = h // per_group
        lanes = queries[g * LANES : (g + 1) * LANES]
        query_ref[h] = jnp.where(part == h % per_group, lanes, jnp.zeros_like(lanes))
    value_ref[:, head_dim:, :] = jnp.ones_like(value_ref[:, head_dim:, :])
    project_keys(own_ref[...], wk_ref, wv_ref, key_ref, value_ref, 0)
    project_keys(side_ref[pl.ds(pl.multiple_of(first, NEAR), NEAR), :], wk_ref, wv_ref, key_ref, value_ref, nodes)
    project_keys(
        side_ref[pl.ds(pl.multiple_of(second, NEAR), NEAR), :], wk_ref, wv_ref, key_ref, value_ref, nodes + NEAR
    )
    lag = lax.broadcasted_iota(jnp.int32, (nodes, nodes), 0) - lax.broadcasted_iota(
        jnp.int32, (nodes, nodes), 1
    )
    gap_ref[0:nodes] = jnp.abs(lag)
    gap_ref[nodes : nodes + NEAR] = jnp.abs(lag[0:NEAR] + (side * nodes + first))
    gap_ref[nodes + NEAR : 2 * nodes] = jnp.abs(lag[0:NEAR] + (side * nodes + second))

    def attend(heads, windows, rows):
        scores = [dot(key_ref[h // per_group, 0:rows, :], query_ref[h]) for h in heads]
        scores = [
            jnp.where(gap_ref[0:rows] <= w, x, -1e30) for w, x in zip(windows, scores)
        ]
        tops = [jnp.max(x, axis=0, keepdims=True) for x in scores]
        expos = [jnp.exp2((x - top) * scale).astype(jnp.bfloat16) for x, top in zip(scores, tops)]
        for h, w, top, expo in zip(heads, windows, tops, expos):
            sums_ref[h] = dot(value_ref[h, :, 0:rows], expo)
            top_ref[h, 0:1] = top
            top_ref[h, 1:2] = jnp.full((1, nodes), w.astype(jnp.float32))

    def together(i, carry):
        heads = [plan_ref[0, GROUP * i + k] for k in range(GROUP)]
        windows = [plan_ref[1, GROUP * i + k] for k in range(GROUP)]
        widest = windows[0]

        @pl.when(widest <= NEAR)
        def _():
            attend(heads, windows, nodes + NEAR)

        @pl.when(widest > NEAR)
        def _():
            attend(heads, windows, 2 * nodes)

        return carry

    lax.fori_loop(0, HEADS // GROUP, together, 0)


def gaps(device, start, rows, nodes):
    total = lax.axis_size("band") * lax.axis_size("inner")
    there = lax.axis_index("band") * lax.axis_size("inner") + lax.axis_index("inner") + device
    lag = lax.broadcasted_iota(jnp.int32, (rows, nodes), 0) - lax.broadcasted_iota(jnp.int32, (rows, nodes), 1)
    gap = jnp.where((there >= 0) & (there < total), jnp.abs(lag + (device * nodes + start)), 1 << 20)
    return gap.astype(jnp.float32)


def extend(heads, keys, values, gap_ref, query_ref, sums_ref, top_ref, scale):
    scores = [dot(k, query_ref[h]) for h, k in zip(heads, keys)]
    scores = [jnp.where(gap_ref[...] <= top_ref[h, 1:2, :], x, -1e30) for h, x in zip(heads, scores)]
    olds = [top_ref[h, 0:1, :] for h in heads]
    tops = [jnp.maximum(old, jnp.max(x, axis=0, keepdims=True)) for old, x in zip(olds, scores)]
    expos = [jnp.exp2((x - top) * scale).astype(jnp.bfloat16) for x, top in zip(scores, tops)]
    for h, v, old, top, expo in zip(heads, values, olds, tops, expos):
        yield h, sums_ref[h] * jnp.exp2((old - top) * scale) + dot(v, expo), top


def outer_kernel(
    even_ref, odd_ref, wk_ref, wv_ref, plan_in, query_ref, sums_ref, top_ref,
    sums_out, top_out,
    key_ref, value_ref, gap_ref, plan_ref, sem,
):
    fetch = pltpu.make_async_copy(plan_in, plan_ref, sem)
    fetch.start()
    nodes, width = even_ref.shape
    head_dim = width // HEADS
    per_group = LANES // head_dim
    far = 2 - 4 * lax.rem(lax.axis_index("inner") // 2, 2)
    scale = head_dim ** (-0.5) / math.log(2.0)
    value_ref[:, head_dim:, :] = jnp.ones_like(value_ref[:, head_dim:, :])
    project_keys(jnp.concatenate([even_ref[...], odd_ref[...]], axis=0), wk_ref, wv_ref, key_ref, value_ref, 0)
    gap_ref[0:nodes] = gaps(far, 0, nodes, nodes)
    gap_ref[nodes:] = gaps(-far, 0, nodes, nodes)

    fetch.wait()

    def wide(n):
        return plan_ref[1, n] > nodes

    def reach(first, last):
        heads = [plan_ref[0, n] for n in range(first, last)]
        keys, values = [key_ref[h // per_group] for h in heads], [value_ref[h] for h in heads]
        for h, sums, top in extend(
            heads, keys, values, gap_ref, query_ref, sums_ref, top_ref, scale
        ):
            sums_out[h] = sums
            top_out[h, 0:1] = top
            top_out[h, 1:2] = top_ref[h, 1:2]

    def leave(first, last):
        for n in range(first, last):
            h = plan_ref[0, n]
            sums_out[h] = sums_ref[h]
            top_out[h, 0:2] = top_ref[h, 0:2]

    @pl.when(wide(GROUP))
    def _():
        reach(0, 2 * GROUP)

    @pl.when(jnp.logical_not(wide(GROUP)))
    def _():
        reach(0, GROUP)
        leave(GROUP, 2 * GROUP)

    for first in range(2 * GROUP, HEADS, GROUP):
        pl.when(wide(first))(functools.partial(reach, first, first + GROUP))
        pl.when(jnp.logical_not(wide(first)))(functools.partial(leave, first, first + GROUP))


def far_kernel(
    first_ref, second_ref, wk_ref, wv_ref, query_ref, sums_ref, top_ref,
    state_ref, w_out_ref, gain_ref, up_ref, down_ref,
    out_ref,
    key_ref, value_ref, gap_ref, attended_ref,
):
    nodes, width = first_ref.shape
    head_dim = width // HEADS
    per_group = LANES // head_dim
    inner = lax.axis_index("inner")
    odd = lax.rem(inner, 2)
    scale = head_dim ** (-0.5) / math.log(2.0)
    value_ref[:, head_dim:, :] = jnp.ones_like(value_ref[:, head_dim:, :])
    by_even = odd == lax.rem(inner // 2 + 1, 2)
    project_keys(jnp.where(by_even, first_ref[...], second_ref[...]), wk_ref, wv_ref, key_ref, value_ref, 0)
    gap_ref[...] = gaps(2 * odd - 1, 0, nodes, nodes)
    for i in range(HEADS // GROUP):
        heads = range(GROUP * i, GROUP * (i + 1))
        keys, values = [key_ref[h // per_group] for h in heads], [value_ref[h] for h in heads]
        for h, sums, _ in extend(
            heads, keys, values, gap_ref, query_ref, sums_ref, top_ref, scale
        ):
            attended_ref[h] = (sums[0:head_dim] / sums[head_dim : head_dim + 1]).astype(jnp.bfloat16)

    attended = attended_ref[...].reshape(width, nodes)
    mixed = lax.dot_general(
        attended, w_out_ref[...], (((0,), (0,)), ((), ())), preferred_element_type=jnp.float32
    )
    total = state_ref[...] + mixed
    normed = layer_norm(total, gain_ref[...]).astype(jnp.bfloat16)
    chunk = math.gcd(up_ref.shape[1], 512)
    for start in range(0, up_ref.shape[1], chunk):
        hidden = silu(dot(normed, up_ref[:, start : start + chunk])).astype(jnp.bfloat16)
        total = total + dot(hidden, down_ref[start : start + chunk, :])
    out_ref[...] = total.astype(jnp.bfloat16)


def cost(flops, size):
    return pl.CostEstimate(flops=flops, bytes_accessed=size, transcendentals=0)


def local(
    grid_rows,
    mesh_rows,
    edge_source,
    edge_target,
    edge_count,
    w_message,
    w_merge,
    gain_attn,
    w_qkv,
    window,
    w_out,
    gain_mlp,
    w_up,
    w_down,
):
    bands = lax.axis_size("band")
    inners = lax.axis_size("inner")
    devices = bands * inners
    grid_dev = grid_rows.shape[0]
    nodes, width = mesh_rows.shape
    cap = edge_source.shape[-1]
    head_dim = width // HEADS
    pairs = inners // 2
    half = width // 2
    f32, bf16, i32 = jnp.float32, jnp.bfloat16, jnp.int32
    edges = (edge_source, edge_target, jnp.transpose(edge_count, (0, 2, 1, 3)))

    def rows_of(*blocks):
        return jax.ShapeDtypeStruct((sum(n * cap + TILE for n in blocks), half), bf16)

    outgoing = [rows_of(pairs)] * 4 + [rows_of(3)] * (2 * pairs - 2) + [rows_of(pairs, 3)] * 2
    even, even_other, odd, odd_other, *cross, here, here_other = pl.pallas_call(
        functools.partial(message_kernel, pairs),
        out_shape=outgoing,
        in_specs=[ANY] * 5,
        out_specs=[ANY] * len(outgoing),
        scratch_shapes=[pltpu.VMEM(a.shape, bf16) for a in outgoing]
        + [
            pltpu.VMEM(edges[0].shape, i32),
            pltpu.VMEM(edges[1].shape, i32),
            pltpu.SMEM(edges[2].shape, i32),
            pltpu.VMEM(grid_rows.shape, bf16),
            pltpu.VMEM(w_message.shape, bf16),
            pltpu.VMEM((grid_dev, width), bf16),
            pltpu.VMEM((3 * inners * cap, grid_dev), bf16),
            pltpu.SemaphoreType.DMA((GRID_PARTS + 1,)),
            pltpu.SemaphoreType.DMA((3,)),
            pltpu.SemaphoreType.DMA((len(outgoing),)),
        ],
        compiler_params=params(MOST),
        cost_estimate=cost(2 * grid_dev * width * (width + 3 * inners * cap), 4 << 20),
        name="messages",
    )(grid_rows, w_message, *edges)
    beside = [(g, g ^ 1) for g in range(devices)]

    def bands_trade(odd_pairs, k=0):
        route = []
        for g in range(devices):
            b = g // inners
            t = (b - odd_pairs ^ 1) + odd_pairs
            route.append((g, t * inners + (g % inners ^ k) if 0 <= t < bands else g ^ 1))
        return route

    def chip_trade(p, k=0):
        return [(g, g ^ (2 * p + k)) for g in range(devices)]

    here_other = lax.ppermute(here_other, NODES, beside)
    cross[0::2] = [lax.ppermute(c, NODES, chip_trade(p + 1)) for p, c in enumerate(cross[0::2])]
    even = lax.ppermute(even, NODES, bands_trade(0))
    odd = lax.ppermute(odd, NODES, bands_trade(1))
    here_other, even_other, odd_other, *cross[1::2] = lax.optimization_barrier(
        (here_other, even_other, odd_other, *cross[1::2])
    )
    cross[1::2] = [lax.ppermute(c, NODES, chip_trade(p + 1, 1)) for p, c in enumerate(cross[1::2])]
    even_other = lax.ppermute(even_other, NODES, bands_trade(0, 1))
    odd_other = lax.ppermute(odd_other, NODES, bands_trade(1, 1))

    w_qkv, window, here = lax.optimization_barrier((w_qkv, window, here))
    head = jnp.arange(HEADS, dtype=i32)
    ahead = (window[None, :] > window[:, None]) | (
        (window[None, :] == window[:, None]) & (head[None, :] < head[:, None])
    )
    rank = jnp.sum(ahead.astype(i32), axis=1)
    sorted_to = rank[None, :] == head[:, None]
    plan = jnp.sum(jnp.where(sorted_to[None], jnp.stack([head, window])[:, None, :], 0), axis=2).astype(i32)
    w_query, w_key, w_value, early_left, early_right = pl.pallas_call(
        functools.partial(early_kernel, pairs),
        out_shape=[jax.ShapeDtypeStruct((width, width), bf16)] * 3
        + [jax.ShapeDtypeStruct((n, nodes, half), f32) for n in (pairs, 3)],
        in_specs=[VMEM] * 3 + [ANY],
        out_specs=[VMEM] * 5,
        compiler_params=params(24),
        cost_estimate=cost(1 << 28, 4 << 20),
        name="early",
    )(w_qkv, here, here_other, plan)
    def sums(arrays, early, kept, name):
        count = early.shape[0]
        return pl.pallas_call(
            functools.partial(sums_kernel, len(arrays), kept),
            out_shape=[jax.ShapeDtypeStruct((nodes, half), f32 if n == kept else bf16) for n in range(count)],
            in_specs=[VMEM] * (len(arrays) + 1),
            out_specs=[VMEM] * count,
            compiler_params=params(24),
            cost_estimate=cost(2 * nodes * half * len(arrays) * count * cap, 2 << 20),
            name=name,
        )(*arrays, early)

    left, *parts = sums([even, even_other, odd, odd_other], early_left, 0, "left")
    parts = [lax.ppermute(part, NODES, chip_trade(p + 1)) for p, part in enumerate(parts)]
    to_even, to_odd, right = sums(cross, early_right, 2, "right")
    from_even = lax.ppermute(to_even, NODES, bands_trade(0))
    from_odd = lax.ppermute(to_odd, NODES, bands_trade(1))

    state, normed = pl.pallas_call(
        merge_kernel,
        out_shape=[
            jax.ShapeDtypeStruct((nodes, width), f32),
            jax.ShapeDtypeStruct((nodes, width), bf16),
        ],
        in_specs=[VMEM] * (pairs + 6),
        out_specs=[VMEM] * 2,
        compiler_params=params(24),
        cost_estimate=cost(2 * nodes * width * width, 2 << 20),
        name="merge",
    )(left, *parts, right, from_even, from_odd, mesh_rows, w_merge, gain_attn.reshape(1, width))

    def chips_trade(odd_pairs):
        route = []
        for g in range(devices):
            t = (g // 2 - odd_pairs ^ 1) + odd_pairs
            route.append((g, 2 * t + g % 2 if 0 <= 2 * t < devices else g ^ 1))
        return route

    side = lax.ppermute(normed, NODES, beside)
    even = lax.ppermute(normed, NODES, chips_trade(0))
    side, normed = lax.optimization_barrier((side, normed))
    odd = lax.ppermute(normed, NODES, chips_trade(1))

    extra = head_dim + 16
    query, near, top = pl.pallas_call(
        near_kernel,
        out_shape=[
            jax.ShapeDtypeStruct((HEADS, LANES, nodes), bf16),
            jax.ShapeDtypeStruct((HEADS, extra, nodes), f32),
            jax.ShapeDtypeStruct((HEADS, 8, nodes), f32),
        ],
        in_specs=[VMEM] * 5 + [SMEM],
        out_specs=[VMEM] * 3,
        scratch_shapes=[
            pltpu.VMEM((width // LANES, 2 * nodes, LANES), bf16),
            pltpu.VMEM((HEADS, extra, 2 * nodes), bf16),
            pltpu.VMEM((2 * nodes, nodes), i32),
        ],
        compiler_params=params(32),
        cost_estimate=cost(8 << 30, 4 << 20),
        name="near",
    )(normed, side, w_query, w_key, w_value, plan)

    even, odd, near, top = lax.optimization_barrier((even, odd, near, top))
    first = lax.ppermute(even, NODES, beside)
    second = lax.ppermute(odd, NODES, beside)
    near, top = pl.pallas_call(
        outer_kernel,
        out_shape=[
            jax.ShapeDtypeStruct((HEADS, extra, nodes), f32),
            jax.ShapeDtypeStruct((HEADS, 8, nodes), f32),
        ],
        in_specs=[VMEM] * 4 + [ANY] + [VMEM] * 3,
        out_specs=[VMEM] * 2,
        scratch_shapes=[
            pltpu.VMEM((width // LANES, 2 * nodes, LANES), bf16),
            pltpu.VMEM((HEADS, extra, 2 * nodes), bf16),
            pltpu.VMEM((2 * nodes, nodes), f32),
            pltpu.SMEM((2, HEADS), i32),
            pltpu.SemaphoreType.DMA(()),
        ],
        compiler_params=params(24),
        cost_estimate=cost(16 * nodes * width * width, 3 << 20),
        name="outer",
    )(even, odd, w_key, w_value, plan, query, near, top)

    return pl.pallas_call(
        far_kernel,
        out_shape=jax.ShapeDtypeStruct((nodes, width), bf16),
        in_specs=[VMEM] * 12,
        out_specs=VMEM,
        scratch_shapes=[
            pltpu.VMEM((width // LANES, nodes, LANES), bf16),
            pltpu.VMEM((HEADS, extra, nodes), bf16),
            pltpu.VMEM((nodes, nodes), f32),
            pltpu.VMEM((HEADS, head_dim, nodes), bf16),
        ],
        compiler_params=params(40),
        cost_estimate=cost(8 << 30, 8 << 20),
        name="far",
    )(
        first, second, w_key, w_value,
        query, near, top, state, w_out, gain_mlp.reshape(1, width), w_up, w_down,
    )


def solution(mesh):
    placed = (
        P(("groups", "band", "inner"), None),
        P(("groups", "band", "inner"), None),
        P(("groups", "band"), "inner", None, None, None),
        P(("groups", "band"), "inner", None, None, None),
        P(("groups", "band"), "inner", None, None),
        P(),
        P(),
        P(),
        P(),
        P("groups"),
        P(),
        P(),
        P(),
        P(),
    )
    return jax.shard_map(
        local,
        mesh=mesh,
        in_specs=placed,
        out_specs=P(("groups", "band", "inner"), None),
        check_vma=False,
    )
```

```python
import functools
import math

import jax
import jax.numpy as jnp
from jax import lax
from jax.experimental import pallas as pl
from jax.experimental.pallas import tpu as pltpu
from jax.sharding import PartitionSpec as P

HEADS = 16
WMAX = 512
LANES = 128
NEAR = 128
TILE = 16
CAP = 128
GRID_PARTS = 2
MOST = 56
GROUP = 4

norm_eps = 1e-05
NODES = ("band", "inner")
VMEM = pl.BlockSpec(memory_space=pltpu.VMEM)
SMEM = pl.BlockSpec(memory_space=pltpu.SMEM)
ANY = pl.BlockSpec(memory_space=pl.ANY)


def params(mib):
    return pltpu.CompilerParams(vmem_limit_bytes=mib * 1024 * 1024)


def dot(a, b):
    return jnp.dot(a, b, preferred_element_type=jnp.float32)


def dot_t(a, b):
    return lax.dot_general(a, b, (((1,), (1,)), ((), ())), preferred_element_type=jnp.float32)


def silu(values):
    half = 0.5 * values
    return half + half * jnp.tanh(half)


def layer_norm(values, gain):
    center = values - jnp.mean(values, axis=-1, keepdims=True)
    spread = jnp.mean(center * center, axis=-1, keepdims=True)
    return center * lax.rsqrt(spread + norm_eps) * gain


def band_offsets():
    ahead = lax.rem(lax.axis_index("band"), 2) * 2
    return 2 - ahead, ahead, 1


def slot_columns(source_ref, blocks):
    sources = jnp.concatenate([source_ref[0, 0, o, pl.ds(j, 1), :] for o, j in blocks], axis=0)
    return jnp.transpose(sources.astype(jnp.float32)).astype(jnp.int32)


def target_tile(target_ref, count_ref, blocks, lanes):
    cap = target_ref.shape[-1]
    slot = lax.broadcasted_iota(jnp.int32, (1, cap), 1)
    targets = [
        jnp.where(slot < count_ref[0, o, 0, j], target_ref[0, 0, o, pl.ds(j, 1), :], -1) for o, j in blocks
    ]
    targets.append(jnp.full((TILE - len(blocks), cap), -1, jnp.int32))
    tile = jnp.concatenate(targets, axis=0).astype(jnp.float32).astype(jnp.bfloat16)
    return jnp.concatenate([tile] * (lanes // cap), axis=1)


def message_kernel(pair_count, grid_ref, w_ref, source_in, target_in, count_in, *refs):
    count = 4 + 2 * pair_count
    out_refs, out_vmems = refs[:count], refs[count : 2 * count]
    source_ref, target_ref, count_ref, grid_vmem, w_vmem, message_ref, pick_ref, in_sems, edge_sems, out_sems = refs[2 * count :]
    rows = grid_ref.shape[0]
    cap = source_ref.shape[-1]
    half = w_ref.shape[1] // 2
    part = rows // GRID_PARTS
    fetches = [pltpu.make_async_copy(w_ref, w_vmem, in_sems.at[GRID_PARTS])]
    for k in range(GRID_PARTS):
        span = pl.ds(k * part, part)
        fetches.append(pltpu.make_async_copy(grid_ref.at[span], grid_vmem.at[span], in_sems.at[k]))
    edges = ((source_in, source_ref), (target_in, target_ref), (count_in, count_ref))
    edge_fetches = [pltpu.make_async_copy(a, b, edge_sems.at[n]) for n, (a, b) in enumerate(edges)]
    for fetch in edge_fetches + fetches:
        fetch.start()
    for fetch in edge_fetches:
        fetch.wait()
    inner = lax.axis_index("inner")
    offsets = band_offsets()
    keys = [(t, p, k) for k in range(2) for t in range(3) for p in range(pair_count)]
    place = {(t, p, k): (offsets[t], inner ^ (2 * p + k)) for t, p, k in keys}
    by_slot = slot_columns(source_ref, [place[key] for key in keys])
    left, right = slice(0, half), slice(half, 2 * half)
    runs = [[([(t, p, k) for p in range(pair_count)], left)] for t in range(2) for k in range(2)]
    runs += [[([(t, p, k) for t in range(3)], right)] for p in range(1, pair_count) for k in range(2)]
    runs += [
        [([(2, p, k) for p in range(pair_count)], left), ([(t, 0, k) for t in range(3)], right)] for k in range(2)
    ]
    for out_vmem, parts in zip(out_vmems, runs):
        start = 0
        for chosen, _ in parts:
            start += len(chosen) * cap
            out_vmem[start : start + TILE, :] = target_tile(target_ref, count_ref, [place[key] for key in chosen], half)
            start += TILE
    row = lax.broadcasted_iota(jnp.int32, (cap, rows), 1)
    for m in range(len(keys)):
        pick_ref[m * cap : (m + 1) * cap, :] = jnp.where(row == by_slot[:, m : m + 1], 1.0, 0.0).astype(jnp.bfloat16)
    fetches[0].wait()
    for k in range(GRID_PARTS):
        span = pl.ds(k * part, part)
        fetches[k + 1].wait()
        message_ref[span] = silu(dot(grid_vmem[span], w_vmem[...])).astype(jnp.bfloat16)
    sends = []
    per_core = len(keys) // 2
    for k in range(2):
        first = k * per_core
        taken = dot(pick_ref[first * cap : (first + per_core) * cap, :], message_ref[...]).astype(jnp.bfloat16)
        for n in reversed(range(count)):
            start = 0
            if runs[n][0][0][0][2] != k:
                continue
            for chosen, lanes in runs[n]:
                for key in chosen:
                    m = keys.index(key) - first
                    out_vmems[n][start : start + cap, :] = taken[m * cap : (m + 1) * cap, lanes]
                    start += cap
                start += TILE
            send = pltpu.make_async_copy(out_vmems[n], out_refs[n], out_sems.at[n])
            send.start()
            sends.append(send)
    for send in sends:
        send.wait()


def node_sums(arrays, nodes):
    count = arrays[0][2]
    cap = CAP
    node = lax.broadcasted_iota(jnp.int32, (nodes, cap), 0)
    targets = [
        ref[start + count * cap : start + count * cap + TILE, 0:cap].astype(jnp.float32).astype(jnp.int32)
        for ref, start, _ in arrays
    ]
    for n in range(count):
        hits = [jnp.where(node == t[n : n + 1], 1.0, 0.0).astype(jnp.bfloat16) for t in targets]
        rows = [ref[start + n * cap : start + (n + 1) * cap, :] for ref, start, _ in arrays]
        yield n, dot(jnp.concatenate(hits, axis=1), jnp.concatenate(rows, axis=0))


def early_kernel(pair_count, w_ref, own_ref, other_ref, plan_ref, query_ref, key_ref, value_ref, left_ref, right_ref):
    width = w_ref.shape[0]
    head_dim = width // HEADS
    span = 3 * LANES
    def pick(c, along):
        shape = (LANES, span) if along else (span, LANES)
        to = lax.broadcasted_iota(jnp.int32, shape, 1 - along)
        column = lax.broadcasted_iota(jnp.int32, shape, along)
        wanted = to // head_dim * (3 * head_dim) + to % head_dim + c * head_dim
        return jnp.where(column == wanted, 1.0, 0.0).astype(jnp.bfloat16)

    for g in range(width // LANES):
        columns = w_ref[:, g * span : (g + 1) * span]
        part = slice(g * LANES, (g + 1) * LANES)
        query_ref[part, :] = dot_t(pick(0, 1), columns).astype(jnp.bfloat16)
        key_ref[:, part] = dot(columns, pick(1, 0)).astype(jnp.bfloat16)
        value_ref[part, :] = dot_t(pick(2, 1), columns).astype(jnp.bfloat16)
    start = 0
    for sum_ref in (left_ref, right_ref):
        count, nodes, _ = sum_ref.shape
        for n, total in node_sums([(own_ref, start, count), (other_ref, start, count)], nodes):
            sum_ref[n] = total
        start += count * CAP + TILE


def sums_kernel(array_count, kept, *refs):
    row_refs, early_ref, out_refs = refs[:array_count], refs[array_count], refs[array_count + 1 :]
    count, nodes, _ = early_ref.shape
    for n, total in node_sums([(r, 0, count) for r in row_refs], nodes):
        total = total + early_ref[n]
        out_refs[n][...] = total if n == kept else total.astype(jnp.bfloat16)


def merge_kernel(*refs):
    *part_refs, right_ref, even_ref, odd_ref, mesh_ref, w_ref, gain_ref, state_ref, normed_ref = refs
    left = functools.reduce(jnp.add, [r[...].astype(jnp.float32) for r in part_refs])
    right = right_ref[...] + even_ref[...].astype(jnp.float32) + odd_ref[...].astype(jnp.float32)
    total = jnp.concatenate([left, right], axis=1).astype(jnp.bfloat16)
    state = mesh_ref[...].astype(jnp.float32) + dot(total, w_ref[...])
    state_ref[...] = state
    normed_ref[...] = layer_norm(state, gain_ref[...]).astype(jnp.bfloat16)


def project_keys(rows, wk_ref, wv_ref, key_ref, value_ref, start):
    count = rows.shape[0]
    groups = key_ref.shape[0]
    heads = value_ref.shape[0]
    keys = dot(rows, wk_ref[...]).astype(jnp.bfloat16)
    for g in range(groups):
        key_ref[g, start : start + count, :] = keys[:, g * LANES : (g + 1) * LANES]
    values = dot_t(wv_ref[...], rows).astype(jnp.bfloat16)
    value_ref[:, 0 : values.shape[0] // heads, start : start + count] = values.reshape(
        heads, -1, count
    )


def near_kernel(
    own_ref, side_ref, wq_ref, wk_ref, wv_ref, plan_ref,
    query_ref, sums_ref, top_ref,
    key_ref, value_ref, gap_ref,
):
    nodes, width = own_ref.shape
    head_dim = width // HEADS
    per_group = LANES // head_dim
    odd = lax.rem(lax.axis_index("inner"), 2)
    side = 1 - 2 * odd
    first = odd * (nodes - NEAR)
    second = (1 - odd) * NEAR
    scale = head_dim ** (-0.5) / math.log(2.0)

    queries = dot_t(wq_ref[...], own_ref[...]).astype(jnp.bfloat16)
    part = lax.broadcasted_iota(jnp.int32, (LANES, nodes), 0) // head_dim
    for h in range(HEADS):
        g = h // per_group
        lanes = queries[g * LANES : (g + 1) * LANES]
        query_ref[h] = jnp.where(part == h % per_group, lanes, jnp.zeros_like(lanes))
    value_ref[:, head_dim:, :] = jnp.ones_like(value_ref[:, head_dim:, :])
    project_keys(own_ref[...], wk_ref, wv_ref, key_ref, value_ref, 0)
    project_keys(side_ref[pl.ds(pl.multiple_of(first, NEAR), NEAR), :], wk_ref, wv_ref, key_ref, value_ref, nodes)
    project_keys(
        side_ref[pl.ds(pl.multiple_of(second, NEAR), NEAR), :], wk_ref, wv_ref, key_ref, value_ref, nodes + NEAR
    )
    lag = lax.broadcasted_iota(jnp.int32, (nodes, nodes), 0) - lax.broadcasted_iota(
        jnp.int32, (nodes, nodes), 1
    )
    gap_ref[0:nodes] = jnp.abs(lag)
    gap_ref[nodes : nodes + NEAR] = jnp.abs(lag[0:NEAR] + (side * nodes + first))
    gap_ref[nodes + NEAR : 2 * nodes] = jnp.abs(lag[0:NEAR] + (side * nodes + second))

    def attend(heads, windows, rows):
        scores = [dot(key_ref[h // per_group, 0:rows, :], query_ref[h]) for h in heads]
        scores = [
            jnp.where(gap_ref[0:rows] <= w, x, -1e30) for w, x in zip(windows, scores)
        ]
        tops = [jnp.max(x, axis=0, keepdims=True) for x in scores]
        expos = [jnp.exp2((x - top) * scale).astype(jnp.bfloat16) for x, top in zip(scores, tops)]
        for h, w, top, expo in zip(heads, windows, tops, expos):
            sums_ref[h] = dot(value_ref[h, :, 0:rows], expo)
            top_ref[h, 0:1] = top
            top_ref[h, 1:2] = jnp.full((1, nodes), w.astype(jnp.float32))

    def together(i, carry):
        heads = [plan_ref[0, GROUP * i + k] for k in range(GROUP)]
        windows = [plan_ref[1, GROUP * i + k] for k in range(GROUP)]
        widest = windows[0]

        @pl.when(widest <= NEAR)
        def _():
            attend(heads, windows, nodes + NEAR)

        @pl.when(widest > NEAR)
        def _():
            attend(heads, windows, 2 * nodes)

        return carry

    lax.fori_loop(0, HEADS // GROUP, together, 0)


def gaps(device, start, rows, nodes):
    total = lax.axis_size("band") * lax.axis_size("inner")
    there = lax.axis_index("band") * lax.axis_size("inner") + lax.axis_index("inner") + device
    lag = lax.broadcasted_iota(jnp.int32, (rows, nodes), 0) - lax.broadcasted_iota(jnp.int32, (rows, nodes), 1)
    gap = jnp.where((there >= 0) & (there < total), jnp.abs(lag + (device * nodes + start)), 1 << 20)
    return gap.astype(jnp.float32)


def extend(heads, keys, values, gap_ref, query_ref, sums_ref, top_ref, scale):
    scores = [dot(k, query_ref[h]) for h, k in zip(heads, keys)]
    scores = [jnp.where(gap_ref[...] <= top_ref[h, 1:2, :], x, -1e30) for h, x in zip(heads, scores)]
    olds = [top_ref[h, 0:1, :] for h in heads]
    tops = [jnp.maximum(old, jnp.max(x, axis=0, keepdims=True)) for old, x in zip(olds, scores)]
    expos = [jnp.exp2((x - top) * scale).astype(jnp.bfloat16) for x, top in zip(scores, tops)]
    for h, v, old, top, expo in zip(heads, values, olds, tops, expos):
        yield h, sums_ref[h] * jnp.exp2((old - top) * scale) + dot(v, expo), top


def outer_kernel(
    by_pair, block_ref, wk_ref, wv_ref, plan_in, query_ref, sums_ref, top_ref,
    sums_out, top_out,
    key_ref, value_ref, gap_ref, plan_ref, sem,
):
    fetch = pltpu.make_async_copy(plan_in, plan_ref, sem)
    fetch.start()
    nodes, width = block_ref.shape
    head_dim = width // HEADS
    per_group = LANES // head_dim
    far = 2 - 4 * lax.rem(lax.axis_index("inner") // 2, 2)
    scale = head_dim ** (-0.5) / math.log(2.0)
    value_ref[:, head_dim:, :] = jnp.ones_like(value_ref[:, head_dim:, :])
    project_keys(block_ref[...], wk_ref, wv_ref, key_ref, value_ref, 0)
    gap_ref[...] = gaps(far if by_pair else -far, 0, nodes, nodes)
    fetch.wait()

    def wide(n):
        return plan_ref[1, n] > nodes

    def reach(first, last):
        heads = [plan_ref[0, n] for n in range(first, last)]
        keys, values = [key_ref[h // per_group] for h in heads], [value_ref[h] for h in heads]
        for h, sums, top in extend(
            heads, keys, values, gap_ref, query_ref, sums_ref, top_ref, scale
        ):
            sums_out[h] = sums
            top_out[h, 0:1] = top
            top_out[h, 1:2] = top_ref[h, 1:2]

    def leave(first, last):
        for n in range(first, last):
            h = plan_ref[0, n]
            sums_out[h] = sums_ref[h]
            top_out[h, 0:2] = top_ref[h, 0:2]

    @pl.when(wide(GROUP))
    def _():
        reach(0, 2 * GROUP)

    @pl.when(jnp.logical_not(wide(GROUP)))
    def _():
        reach(0, GROUP)
        leave(GROUP, 2 * GROUP)

    for first in range(2 * GROUP, HEADS, GROUP):
        pl.when(wide(first))(functools.partial(reach, first, first + GROUP))
        pl.when(jnp.logical_not(wide(first)))(functools.partial(leave, first, first + GROUP))


def far_kernel(
    first_ref, second_ref, wk_ref, wv_ref, query_ref, sums_ref, top_ref,
    state_ref, w_out_ref, gain_ref, up_ref, down_ref,
    out_ref,
    key_ref, value_ref, gap_ref, attended_ref,
):
    nodes, width = first_ref.shape
    head_dim = width // HEADS
    per_group = LANES // head_dim
    inner = lax.axis_index("inner")
    odd = lax.rem(inner, 2)
    scale = head_dim ** (-0.5) / math.log(2.0)
    value_ref[:, head_dim:, :] = jnp.ones_like(value_ref[:, head_dim:, :])
    by_even = odd == lax.rem(inner // 2 + 1, 2)
    project_keys(jnp.where(by_even, first_ref[...], second_ref[...]), wk_ref, wv_ref, key_ref, value_ref, 0)
    gap_ref[...] = gaps(2 * odd - 1, 0, nodes, nodes)
    for i in range(HEADS // GROUP):
        heads = range(GROUP * i, GROUP * (i + 1))
        keys, values = [key_ref[h // per_group] for h in heads], [value_ref[h] for h in heads]
        for h, sums, _ in extend(
            heads, keys, values, gap_ref, query_ref, sums_ref, top_ref, scale
        ):
            attended_ref[h] = (sums[0:head_dim] / sums[head_dim : head_dim + 1]).astype(jnp.bfloat16)

    attended = attended_ref[...].reshape(width, nodes)
    mixed = lax.dot_general(
        attended, w_out_ref[...], (((0,), (0,)), ((), ())), preferred_element_type=jnp.float32
    )
    total = state_ref[...] + mixed
    normed = layer_norm(total, gain_ref[...]).astype(jnp.bfloat16)
    chunk = math.gcd(up_ref.shape[1], 512)
    for start in range(0, up_ref.shape[1], chunk):
        hidden = silu(dot(normed, up_ref[:, start : start + chunk])).astype(jnp.bfloat16)
        total = total + dot(hidden, down_ref[start : start + chunk, :])
    out_ref[...] = total.astype(jnp.bfloat16)


def cost(flops, size):
    return pl.CostEstimate(flops=flops, bytes_accessed=size, transcendentals=0)


def local(
    grid_rows,
    mesh_rows,
    edge_source,
    edge_target,
    edge_count,
    w_message,
    w_merge,
    gain_attn,
    w_qkv,
    window,
    w_out,
    gain_mlp,
    w_up,
    w_down,
):
    bands = lax.axis_size("band")
    inners = lax.axis_size("inner")
    devices = bands * inners
    grid_dev = grid_rows.shape[0]
    nodes, width = mesh_rows.shape
    cap = edge_source.shape[-1]
    head_dim = width // HEADS
    pairs = inners // 2
    half = width // 2
    f32, bf16, i32 = jnp.float32, jnp.bfloat16, jnp.int32
    edges = (edge_source, edge_target, jnp.transpose(edge_count, (0, 2, 1, 3)))

    def rows_of(*blocks):
        return jax.ShapeDtypeStruct((sum(n * cap + TILE for n in blocks), half), bf16)

    outgoing = [rows_of(pairs)] * 4 + [rows_of(3)] * (2 * pairs - 2) + [rows_of(pairs, 3)] * 2
    even, even_other, odd, odd_other, *cross, here, here_other = pl.pallas_call(
        functools.partial(message_kernel, pairs),
        out_shape=outgoing,
        in_specs=[ANY] * 5,
        out_specs=[ANY] * len(outgoing),
        scratch_shapes=[pltpu.VMEM(a.shape, bf16) for a in outgoing]
        + [
            pltpu.VMEM(edges[0].shape, i32),
            pltpu.VMEM(edges[1].shape, i32),
            pltpu.SMEM(edges[2].shape, i32),
            pltpu.VMEM(grid_rows.shape, bf16),
            pltpu.VMEM(w_message.shape, bf16),
            pltpu.VMEM((grid_dev, width), bf16),
            pltpu.VMEM((3 * inners * cap, grid_dev), bf16),
            pltpu.SemaphoreType.DMA((GRID_PARTS + 1,)),
            pltpu.SemaphoreType.DMA((3,)),
            pltpu.SemaphoreType.DMA((len(outgoing),)),
        ],
        compiler_params=params(MOST),
        cost_estimate=cost(2 * grid_dev * width * (width + 3 * inners * cap), 4 << 20),
        name="messages",
    )(grid_rows, w_message, *edges)
    beside = [(g, g ^ 1) for g in range(devices)]

    def bands_trade(odd_pairs, k=0):
        route = []
        for g in range(devices):
            b = g // inners
            t = (b - odd_pairs ^ 1) + odd_pairs
            route.append((g, t * inners + (g % inners ^ k) if 0 <= t < bands else g ^ 1))
        return route

    def chip_trade(p, k=0):
        return [(g, g ^ (2 * p + k)) for g in range(devices)]

    here_other = lax.ppermute(here_other, NODES, beside)
    cross[0::2] = [lax.ppermute(c, NODES, chip_trade(p + 1)) for p, c in enumerate(cross[0::2])]
    even = lax.ppermute(even, NODES, bands_trade(0))
    odd = lax.ppermute(odd, NODES, bands_trade(1))
    here_other, even_other, odd_other, *cross[1::2] = lax.optimization_barrier(
        (here_other, even_other, odd_other, *cross[1::2])
    )
    cross[1::2] = [lax.ppermute(c, NODES, chip_trade(p + 1, 1)) for p, c in enumerate(cross[1::2])]
    even_other = lax.ppermute(even_other, NODES, bands_trade(0, 1))
    odd_other = lax.ppermute(odd_other, NODES, bands_trade(1, 1))

    w_qkv, window, here = lax.optimization_barrier((w_qkv, window, here))
    head = jnp.arange(HEADS, dtype=i32)
    ahead = (window[None, :] > window[:, None]) | (
        (window[None, :] == window[:, None]) & (head[None, :] < head[:, None])
    )
    rank = jnp.sum(ahead.astype(i32), axis=1)
    sorted_to = rank[None, :] == head[:, None]
    plan = jnp.sum(jnp.where(sorted_to[None], jnp.stack([head, window])[:, None, :], 0), axis=2).astype(i32)
    w_query, w_key, w_value, early_left, early_right = pl.pallas_call(
        functools.partial(early_kernel, pairs),
        out_shape=[jax.ShapeDtypeStruct((width, width), bf16)] * 3
        + [jax.ShapeDtypeStruct((n, nodes, half), f32) for n in (pairs, 3)],
        in_specs=[VMEM] * 3 + [ANY],
        out_specs=[VMEM] * 5,
        compiler_params=params(24),
        cost_estimate=cost(1 << 28, 4 << 20),
        name="early",
    )(w_qkv, here, here_other, plan)
    def sums(arrays, early, kept, name):
        count = early.shape[0]
        return pl.pallas_call(
            functools.partial(sums_kernel, len(arrays), kept),
            out_shape=[jax.ShapeDtypeStruct((nodes, half), f32 if n == kept else bf16) for n in range(count)],
            in_specs=[VMEM] * (len(arrays) + 1),
            out_specs=[VMEM] * count,
            compiler_params=params(24),
            cost_estimate=cost(2 * nodes * half * len(arrays) * count * cap, 2 << 20),
            name=name,
        )(*arrays, early)

    left, *parts = sums([even, even_other, odd, odd_other], early_left, 0, "left")
    parts = [lax.ppermute(part, NODES, chip_trade(p + 1)) for p, part in enumerate(parts)]
    to_even, to_odd, right = sums(cross, early_right, 2, "right")
    from_even = lax.ppermute(to_even, NODES, bands_trade(0))
    from_odd = lax.ppermute(to_odd, NODES, bands_trade(1))

    state, normed = pl.pallas_call(
        merge_kernel,
        out_shape=[
            jax.ShapeDtypeStruct((nodes, width), f32),
            jax.ShapeDtypeStruct((nodes, width), bf16),
        ],
        in_specs=[VMEM] * (pairs + 6),
        out_specs=[VMEM] * 2,
        compiler_params=params(24),
        cost_estimate=cost(2 * nodes * width * width, 2 << 20),
        name="merge",
    )(left, *parts, right, from_even, from_odd, mesh_rows, w_merge, gain_attn.reshape(1, width))

    def chips_trade(odd_pairs):
        route = []
        for g in range(devices):
            t = (g // 2 - odd_pairs ^ 1) + odd_pairs
            route.append((g, 2 * t + g % 2 if 0 <= 2 * t < devices else g ^ 1))
        return route

    side = lax.ppermute(normed, NODES, beside)
    even = lax.ppermute(normed, NODES, chips_trade(0))
    side, normed = lax.optimization_barrier((side, normed))
    odd = lax.ppermute(normed, NODES, chips_trade(1))

    extra = head_dim + 16
    query, near, top = pl.pallas_call(
        near_kernel,
        out_shape=[
            jax.ShapeDtypeStruct((HEADS, LANES, nodes), bf16),
            jax.ShapeDtypeStruct((HEADS, extra, nodes), f32),
            jax.ShapeDtypeStruct((HEADS, 8, nodes), f32),
        ],
        in_specs=[VMEM] * 5 + [SMEM],
        out_specs=[VMEM] * 3,
        scratch_shapes=[
            pltpu.VMEM((width // LANES, 2 * nodes, LANES), bf16),
            pltpu.VMEM((HEADS, extra, 2 * nodes), bf16),
            pltpu.VMEM((2 * nodes, nodes), i32),
        ],
        compiler_params=params(32),
        cost_estimate=cost(8 << 30, 4 << 20),
        name="near",
    )(normed, side, w_query, w_key, w_value, plan)

    def outer(by_pair, block, near, top):
        return pl.pallas_call(
            functools.partial(outer_kernel, by_pair),
            out_shape=[
                jax.ShapeDtypeStruct((HEADS, extra, nodes), f32),
                jax.ShapeDtypeStruct((HEADS, 8, nodes), f32),
            ],
            in_specs=[VMEM] * 3 + [ANY] + [VMEM] * 3,
            out_specs=[VMEM] * 2,
            scratch_shapes=[
                pltpu.VMEM((width // LANES, nodes, LANES), bf16),
                pltpu.VMEM((HEADS, extra, nodes), bf16),
                pltpu.VMEM((nodes, nodes), f32),
                pltpu.SMEM((2, HEADS), i32),
                pltpu.SemaphoreType.DMA(()),
            ],
            compiler_params=params(24),
            cost_estimate=cost(8 * nodes * width * width, 3 << 20),
            name="pair" if by_pair else "other",
        )(block, w_key, w_value, plan, query, near, top)

    odd, near, top = lax.optimization_barrier((odd, near, top))
    second = lax.ppermute(odd, NODES, beside)
    near, top = outer(False, odd, near, top)
    even, near, top = lax.optimization_barrier((even, near, top))
    first = lax.ppermute(even, NODES, beside)
    near, top = outer(True, even, near, top)

    return pl.pallas_call(
        far_kernel,
        out_shape=jax.ShapeDtypeStruct((nodes, width), bf16),
        in_specs=[VMEM] * 12,
        out_specs=VMEM,
        scratch_shapes=[
            pltpu.VMEM((width // LANES, nodes, LANES), bf16),
            pltpu.VMEM((HEADS, extra, nodes), bf16),
            pltpu.VMEM((nodes, nodes), f32),
            pltpu.VMEM((HEADS, head_dim, nodes), bf16),
        ],
        compiler_params=params(40),
        cost_estimate=cost(8 << 30, 8 << 20),
        name="far",
    )(
        first, second, w_key, w_value,
        query, near, top, state, w_out, gain_mlp.reshape(1, width), w_up, w_down,
    )


def solution(mesh):
    placed = (
        P(("groups", "band", "inner"), None),
        P(("groups", "band", "inner"), None),
        P(("groups", "band"), "inner", None, None, None),
        P(("groups", "band"), "inner", None, None, None),
        P(("groups", "band"), "inner", None, None),
        P(),
        P(),
        P(),
        P(),
        P("groups"),
        P(),
        P(),
        P(),
        P(),
    )
    return jax.shard_map(
        local,
        mesh=mesh,
        in_specs=placed,
        out_specs=P(("groups", "band", "inner"), None),
        check_vma=False,
    )
```

```python
import functools
import math

import jax
import jax.numpy as jnp
from jax import lax
from jax.experimental import pallas as pl
from jax.experimental.pallas import tpu as pltpu
from jax.sharding import PartitionSpec as P

HEADS = 16
WMAX = 512
LANES = 128
NEAR = 128
TILE = 16
CAP = 128
GRID_PARTS = 2
MOST = 56
GROUP = 4

norm_eps = 1e-05
NODES = ("band", "inner")
VMEM = pl.BlockSpec(memory_space=pltpu.VMEM)
SMEM = pl.BlockSpec(memory_space=pltpu.SMEM)
ANY = pl.BlockSpec(memory_space=pl.ANY)


def params(mib):
    return pltpu.CompilerParams(vmem_limit_bytes=mib * 1024 * 1024)


def dot(a, b):
    return jnp.dot(a, b, preferred_element_type=jnp.float32)


def dot_t(a, b):
    return lax.dot_general(a, b, (((1,), (1,)), ((), ())), preferred_element_type=jnp.float32)


def silu(values):
    half = 0.5 * values
    return half + half * jnp.tanh(half)


def layer_norm(values, gain):
    center = values - jnp.mean(values, axis=-1, keepdims=True)
    spread = jnp.mean(center * center, axis=-1, keepdims=True)
    return center * lax.rsqrt(spread + norm_eps) * gain


def band_offsets():
    ahead = lax.rem(lax.axis_index("band"), 2) * 2
    return 2 - ahead, ahead, 1


def slot_columns(source_ref, blocks):
    sources = jnp.concatenate([source_ref[0, 0, o, pl.ds(j, 1), :] for o, j in blocks], axis=0)
    return jnp.transpose(sources.astype(jnp.float32)).astype(jnp.int32)


def target_tile(target_ref, count_ref, blocks, lanes):
    cap = target_ref.shape[-1]
    slot = lax.broadcasted_iota(jnp.int32, (1, cap), 1)
    targets = [
        jnp.where(slot < count_ref[0, o, 0, j], target_ref[0, 0, o, pl.ds(j, 1), :], -1) for o, j in blocks
    ]
    targets.append(jnp.full((TILE - len(blocks), cap), -1, jnp.int32))
    tile = jnp.concatenate(targets, axis=0).astype(jnp.float32).astype(jnp.bfloat16)
    return jnp.concatenate([tile] * (lanes // cap), axis=1)


def message_kernel(pair_count, grid_ref, w_ref, source_in, target_in, count_in, *refs):
    count = 4 + 2 * pair_count
    out_refs, out_vmems = refs[:count], refs[count : 2 * count]
    source_ref, target_ref, count_ref, grid_vmem, w_vmem, message_ref, pick_ref, in_sems, edge_sems, out_sems = refs[2 * count :]
    rows = grid_ref.shape[0]
    cap = source_ref.shape[-1]
    half = w_ref.shape[1] // 2
    part = rows // GRID_PARTS
    fetches = [pltpu.make_async_copy(w_ref, w_vmem, in_sems.at[GRID_PARTS])]
    for k in range(GRID_PARTS):
        span = pl.ds(k * part, part)
        fetches.append(pltpu.make_async_copy(grid_ref.at[span], grid_vmem.at[span], in_sems.at[k]))
    edges = ((source_in, source_ref), (target_in, target_ref), (count_in, count_ref))
    edge_fetches = [pltpu.make_async_copy(a, b, edge_sems.at[n]) for n, (a, b) in enumerate(edges)]
    for fetch in edge_fetches + fetches:
        fetch.start()
    for fetch in edge_fetches:
        fetch.wait()
    inner = lax.axis_index("inner")
    offsets = band_offsets()
    keys = [(t, p, k) for k in range(2) for t in range(3) for p in range(pair_count)]
    place = {(t, p, k): (offsets[t], inner ^ (2 * p + k)) for t, p, k in keys}
    by_slot = slot_columns(source_ref, [place[key] for key in keys])
    left, right = slice(0, half), slice(half, 2 * half)
    runs = [[([(t, p, k) for p in range(pair_count)], left)] for t in range(2) for k in range(2)]
    runs += [[([(t, p, k) for t in range(3)], right)] for p in range(1, pair_count) for k in range(2)]
    runs += [
        [([(2, p, k) for p in range(pair_count)], left), ([(t, 0, k) for t in range(3)], right)] for k in range(2)
    ]
    for out_vmem, parts in zip(out_vmems, runs):
        start = 0
        for chosen, _ in parts:
            start += len(chosen) * cap
            out_vmem[start : start + TILE, :] = target_tile(target_ref, count_ref, [place[key] for key in chosen], half)
            start += TILE
    row = lax.broadcasted_iota(jnp.int32, (cap, rows), 1)
    for m in range(len(keys)):
        pick_ref[m * cap : (m + 1) * cap, :] = jnp.where(row == by_slot[:, m : m + 1], 1.0, 0.0).astype(jnp.bfloat16)
    fetches[0].wait()
    for k in range(GRID_PARTS):
        span = pl.ds(k * part, part)
        fetches[k + 1].wait()
        message_ref[span] = silu(dot(grid_vmem[span], w_vmem[...])).astype(jnp.bfloat16)
    sends = []
    per_core = len(keys) // 2
    for k in range(2):
        first = k * per_core
        taken = dot(pick_ref[first * cap : (first + per_core) * cap, :], message_ref[...]).astype(jnp.bfloat16)
        for n in reversed(range(count)):
            start = 0
            if runs[n][0][0][0][2] != k:
                continue
            for chosen, lanes in runs[n]:
                for key in chosen:
                    m = keys.index(key) - first
                    out_vmems[n][start : start + cap, :] = taken[m * cap : (m + 1) * cap, lanes]
                    start += cap
                start += TILE
            send = pltpu.make_async_copy(out_vmems[n], out_refs[n], out_sems.at[n])
            send.start()
            sends.append(send)
    for send in sends:
        send.wait()


def node_sums(arrays, nodes):
    count = arrays[0][2]
    cap = CAP
    node = lax.broadcasted_iota(jnp.int32, (nodes, cap), 0)
    targets = [
        ref[start + count * cap : start + count * cap + TILE, 0:cap].astype(jnp.float32).astype(jnp.int32)
        for ref, start, _ in arrays
    ]
    for n in range(count):
        hits = [jnp.where(node == t[n : n + 1], 1.0, 0.0).astype(jnp.bfloat16) for t in targets]
        rows = [ref[start + n * cap : start + (n + 1) * cap, :] for ref, start, _ in arrays]
        yield n, dot(jnp.concatenate(hits, axis=1), jnp.concatenate(rows, axis=0))


def early_kernel(pair_count, w_ref, own_ref, other_ref, plan_ref, query_ref, key_ref, value_ref, left_ref, right_ref):
    width = w_ref.shape[0]
    head_dim = width // HEADS
    span = 3 * LANES
    def pick(c, along):
        shape = (LANES, span) if along else (span, LANES)
        to = lax.broadcasted_iota(jnp.int32, shape, 1 - along)
        column = lax.broadcasted_iota(jnp.int32, shape, along)
        wanted = to // head_dim * (3 * head_dim) + to % head_dim + c * head_dim
        return jnp.where(column == wanted, 1.0, 0.0).astype(jnp.bfloat16)

    for g in range(width // LANES):
        columns = w_ref[:, g * span : (g + 1) * span]
        part = slice(g * LANES, (g + 1) * LANES)
        query_ref[part, :] = dot_t(pick(0, 1), columns).astype(jnp.bfloat16)
        key_ref[:, part] = dot(columns, pick(1, 0)).astype(jnp.bfloat16)
        value_ref[part, :] = dot_t(pick(2, 1), columns).astype(jnp.bfloat16)
    start = 0
    for sum_ref in (left_ref, right_ref):
        count, nodes, _ = sum_ref.shape
        for n, total in node_sums([(own_ref, start, count), (other_ref, start, count)], nodes):
            sum_ref[n] = total
        start += count * CAP + TILE


def sums_kernel(array_count, kept, *refs):
    row_refs, early_ref, out_refs = refs[:array_count], refs[array_count], refs[array_count + 1 :]
    count, nodes, _ = early_ref.shape
    for n, total in node_sums([(r, 0, count) for r in row_refs], nodes):
        total = total + early_ref[n]
        out_refs[n][...] = total if n == kept else total.astype(jnp.bfloat16)


def merge_kernel(*refs):
    *part_refs, right_ref, even_ref, odd_ref, mesh_ref, w_ref, gain_ref, state_ref, normed_ref = refs
    left = functools.reduce(jnp.add, [r[...].astype(jnp.float32) for r in part_refs])
    right = right_ref[...] + even_ref[...].astype(jnp.float32) + odd_ref[...].astype(jnp.float32)
    total = jnp.concatenate([left, right], axis=1).astype(jnp.bfloat16)
    state = mesh_ref[...].astype(jnp.float32) + dot(total, w_ref[...])
    state_ref[...] = state
    normed_ref[...] = layer_norm(state, gain_ref[...]).astype(jnp.bfloat16)


def project_keys(rows, wk_ref, wv_ref, key_ref, value_ref, start):
    count = rows.shape[0]
    groups = key_ref.shape[0]
    heads = value_ref.shape[0]
    keys = dot(rows, wk_ref[...]).astype(jnp.bfloat16)
    for g in range(groups):
        key_ref[g, start : start + count, :] = keys[:, g * LANES : (g + 1) * LANES]
    values = dot_t(wv_ref[...], rows).astype(jnp.bfloat16)
    value_ref[:, 0 : values.shape[0] // heads, start : start + count] = values.reshape(
        heads, -1, count
    )


def near_kernel(
    own_ref, side_ref, wq_ref, wk_ref, wv_ref, plan_ref,
    query_ref, sums_ref, top_ref,
    key_ref, value_ref, gap_ref,
):
    nodes, width = own_ref.shape
    head_dim = width // HEADS
    per_group = LANES // head_dim
    odd = lax.rem(lax.axis_index("inner"), 2)
    side = 1 - 2 * odd
    first = odd * (nodes - NEAR)
    second = (1 - odd) * NEAR
    scale = head_dim ** (-0.5) / math.log(2.0)

    queries = dot_t(wq_ref[...], own_ref[...]).astype(jnp.bfloat16)
    part = lax.broadcasted_iota(jnp.int32, (LANES, nodes), 0) // head_dim
    for h in range(HEADS):
        g = h // per_group
        lanes = queries[g * LANES : (g + 1) * LANES]
        query_ref[h] = jnp.where(part == h % per_group, lanes, jnp.zeros_like(lanes))
    value_ref[:, head_dim:, :] = jnp.ones_like(value_ref[:, head_dim:, :])
    project_keys(own_ref[...], wk_ref, wv_ref, key_ref, value_ref, 0)
    project_keys(side_ref[pl.ds(pl.multiple_of(first, NEAR), NEAR), :], wk_ref, wv_ref, key_ref, value_ref, nodes)
    project_keys(
        side_ref[pl.ds(pl.multiple_of(second, NEAR), NEAR), :], wk_ref, wv_ref, key_ref, value_ref, nodes + NEAR
    )
    lag = lax.broadcasted_iota(jnp.int32, (nodes, nodes), 0) - lax.broadcasted_iota(
        jnp.int32, (nodes, nodes), 1
    )
    gap_ref[0:nodes] = jnp.abs(lag)
    gap_ref[nodes : nodes + NEAR] = jnp.abs(lag[0:NEAR] + (side * nodes + first))
    gap_ref[nodes + NEAR : 2 * nodes] = jnp.abs(lag[0:NEAR] + (side * nodes + second))

    def attend(heads, windows, rows):
        scores = [dot(key_ref[h // per_group, 0:rows, :], query_ref[h]) for h in heads]
        scores = [
            jnp.where(gap_ref[0:rows] <= w, x, -1e30) for w, x in zip(windows, scores)
        ]
        tops = [jnp.max(x, axis=0, keepdims=True) for x in scores]
        expos = [jnp.exp2((x - top) * scale).astype(jnp.bfloat16) for x, top in zip(scores, tops)]
        for h, w, top, expo in zip(heads, windows, tops, expos):
            sums_ref[h] = dot(value_ref[h, :, 0:rows], expo)
            top_ref[h, 0:1] = top
            top_ref[h, 1:2] = jnp.full((1, nodes), w.astype(jnp.float32))

    def together(i, carry):
        heads = [plan_ref[0, GROUP * i + k] for k in range(GROUP)]
        windows = [plan_ref[1, GROUP * i + k] for k in range(GROUP)]
        widest = windows[0]

        @pl.when(widest <= NEAR)
        def _():
            attend(heads, windows, nodes + NEAR)

        @pl.when(widest > NEAR)
        def _():
            attend(heads, windows, 2 * nodes)

        return carry

    lax.fori_loop(0, HEADS // GROUP, together, 0)


def gaps(device, start, rows, nodes):
    total = lax.axis_size("band") * lax.axis_size("inner")
    there = lax.axis_index("band") * lax.axis_size("inner") + lax.axis_index("inner") + device
    lag = lax.broadcasted_iota(jnp.int32, (rows, nodes), 0) - lax.broadcasted_iota(jnp.int32, (rows, nodes), 1)
    gap = jnp.where((there >= 0) & (there < total), jnp.abs(lag + (device * nodes + start)), 1 << 20)
    return gap.astype(jnp.float32)


def extend(heads, keys, values, gap_ref, query_ref, sums_ref, top_ref, scale):
    scores = [dot(k, query_ref[h]) for h, k in zip(heads, keys)]
    scores = [jnp.where(gap_ref[...] <= top_ref[h, 1:2, :], x, -1e30) for h, x in zip(heads, scores)]
    olds = [top_ref[h, 0:1, :] for h in heads]
    tops = [jnp.maximum(old, jnp.max(x, axis=0, keepdims=True)) for old, x in zip(olds, scores)]
    expos = [jnp.exp2((x - top) * scale).astype(jnp.bfloat16) for x, top in zip(scores, tops)]
    for h, v, old, top, expo in zip(heads, values, olds, tops, expos):
        yield h, sums_ref[h] * jnp.exp2((old - top) * scale) + dot(v, expo), top


def outer_kernel(
    by_pair, block_ref, wk_ref, wv_ref, plan_in, query_ref, sums_ref, top_ref,
    sums_out, top_out,
    key_ref, value_ref, gap_ref, plan_ref, sem,
):
    fetch = pltpu.make_async_copy(plan_in, plan_ref, sem)
    fetch.start()
    nodes, width = block_ref.shape
    head_dim = width // HEADS
    per_group = LANES // head_dim
    far = 2 - 4 * lax.rem(lax.axis_index("inner") // 2, 2)
    scale = head_dim ** (-0.5) / math.log(2.0)
    value_ref[:, head_dim:, :] = jnp.ones_like(value_ref[:, head_dim:, :])
    project_keys(block_ref[...], wk_ref, wv_ref, key_ref, value_ref, 0)
    gap_ref[...] = gaps(far if by_pair else -far, 0, nodes, nodes)
    fetch.wait()

    def wide(n):
        return plan_ref[1, n] > nodes

    def reach(first, last):
        heads = [plan_ref[0, n] for n in range(first, last)]
        keys, values = [key_ref[h // per_group] for h in heads], [value_ref[h] for h in heads]
        for h, sums, top in extend(
            heads, keys, values, gap_ref, query_ref, sums_ref, top_ref, scale
        ):
            sums_out[h] = sums
            top_out[h, 0:1] = top
            top_out[h, 1:2] = top_ref[h, 1:2]

    def leave(first, last):
        for n in range(first, last):
            h = plan_ref[0, n]
            sums_out[h] = sums_ref[h]
            top_out[h, 0:2] = top_ref[h, 0:2]

    @pl.when(wide(GROUP))
    def _():
        reach(0, 2 * GROUP)

    @pl.when(jnp.logical_not(wide(GROUP)))
    def _():
        reach(0, GROUP)
        leave(GROUP, 2 * GROUP)

    for first in range(2 * GROUP, HEADS, GROUP):
        pl.when(wide(first))(functools.partial(reach, first, first + GROUP))
        pl.when(jnp.logical_not(wide(first)))(functools.partial(leave, first, first + GROUP))


def far_kernel(
    first_ref, second_ref, wk_ref, wv_ref, query_ref, sums_ref, top_ref,
    state_ref, w_out_ref, gain_ref, up_ref, down_ref,
    out_ref,
    key_ref, value_ref, gap_ref, attended_ref,
):
    nodes, width = first_ref.shape
    head_dim = width // HEADS
    per_group = LANES // head_dim
    inner = lax.axis_index("inner")
    odd = lax.rem(inner, 2)
    scale = head_dim ** (-0.5) / math.log(2.0)
    value_ref[:, head_dim:, :] = jnp.ones_like(value_ref[:, head_dim:, :])
    by_even = odd == lax.rem(inner // 2 + 1, 2)
    project_keys(jnp.where(by_even, first_ref[...], second_ref[...]), wk_ref, wv_ref, key_ref, value_ref, 0)
    gap_ref[...] = gaps(2 * odd - 1, 0, nodes, nodes)
    for i in range(HEADS // GROUP):
        heads = range(GROUP * i, GROUP * (i + 1))
        keys, values = [key_ref[h // per_group] for h in heads], [value_ref[h] for h in heads]
        for h, sums, _ in extend(
            heads, keys, values, gap_ref, query_ref, sums_ref, top_ref, scale
        ):
            attended_ref[h] = (sums[0:head_dim] / sums[head_dim : head_dim + 1]).astype(jnp.bfloat16)

    attended = attended_ref[...].reshape(width, nodes)
    mixed = lax.dot_general(
        attended, w_out_ref[...], (((0,), (0,)), ((), ())), preferred_element_type=jnp.float32
    )
    total = state_ref[...] + mixed
    normed = layer_norm(total, gain_ref[...]).astype(jnp.bfloat16)
    chunk = math.gcd(up_ref.shape[1], 512)
    for start in range(0, up_ref.shape[1], chunk):
        hidden = silu(dot(normed, up_ref[:, start : start + chunk])).astype(jnp.bfloat16)
        total = total + dot(hidden, down_ref[start : start + chunk, :])
    out_ref[...] = total.astype(jnp.bfloat16)


def cost(flops, size):
    return pl.CostEstimate(flops=flops, bytes_accessed=size, transcendentals=0)


def local(
    grid_rows,
    mesh_rows,
    edge_source,
    edge_target,
    edge_count,
    w_message,
    w_merge,
    gain_attn,
    w_qkv,
    window,
    w_out,
    gain_mlp,
    w_up,
    w_down,
):
    bands = lax.axis_size("band")
    inners = lax.axis_size("inner")
    devices = bands * inners
    grid_dev = grid_rows.shape[0]
    nodes, width = mesh_rows.shape
    cap = edge_source.shape[-1]
    head_dim = width // HEADS
    pairs = inners // 2
    half = width // 2
    f32, bf16, i32 = jnp.float32, jnp.bfloat16, jnp.int32
    edges = (edge_source, edge_target, jnp.transpose(edge_count, (0, 2, 1, 3)))

    def rows_of(*blocks):
        return jax.ShapeDtypeStruct((sum(n * cap + TILE for n in blocks), half), bf16)

    outgoing = [rows_of(pairs)] * 4 + [rows_of(3)] * (2 * pairs - 2) + [rows_of(pairs, 3)] * 2
    even, even_other, odd, odd_other, *cross, here, here_other = pl.pallas_call(
        functools.partial(message_kernel, pairs),
        out_shape=outgoing,
        in_specs=[ANY] * 5,
        out_specs=[ANY] * len(outgoing),
        scratch_shapes=[pltpu.VMEM(a.shape, bf16) for a in outgoing]
        + [
            pltpu.VMEM(edges[0].shape, i32),
            pltpu.VMEM(edges[1].shape, i32),
            pltpu.SMEM(edges[2].shape, i32),
            pltpu.VMEM(grid_rows.shape, bf16),
            pltpu.VMEM(w_message.shape, bf16),
            pltpu.VMEM((grid_dev, width), bf16),
            pltpu.VMEM((3 * inners * cap, grid_dev), bf16),
            pltpu.SemaphoreType.DMA((GRID_PARTS + 1,)),
            pltpu.SemaphoreType.DMA((3,)),
            pltpu.SemaphoreType.DMA((len(outgoing),)),
        ],
        compiler_params=params(MOST),
        cost_estimate=cost(2 * grid_dev * width * (width + 3 * inners * cap), 4 << 20),
        name="messages",
    )(grid_rows, w_message, *edges)
    beside = [(g, g ^ 1) for g in range(devices)]

    def bands_trade(odd_pairs, k=0):
        route = []
        for g in range(devices):
            b = g // inners
            t = (b - odd_pairs ^ 1) + odd_pairs
            route.append((g, t * inners + (g % inners ^ k) if 0 <= t < bands else g ^ 1))
        return route

    def chip_trade(p, k=0):
        return [(g, g ^ (2 * p + k)) for g in range(devices)]

    here_other = lax.ppermute(here_other, NODES, beside)
    cross[0::2] = [lax.ppermute(c, NODES, chip_trade(p + 1)) for p, c in enumerate(cross[0::2])]
    even = lax.ppermute(even, NODES, bands_trade(0))
    odd = lax.ppermute(odd, NODES, bands_trade(1))
    here_other, even_other, odd_other, *cross[1::2] = lax.optimization_barrier(
        (here_other, even_other, odd_other, *cross[1::2])
    )
    cross[1::2] = [lax.ppermute(c, NODES, chip_trade(p + 1, 1)) for p, c in enumerate(cross[1::2])]
    even_other = lax.ppermute(even_other, NODES, bands_trade(0, 1))
    odd_other = lax.ppermute(odd_other, NODES, bands_trade(1, 1))

    w_qkv, window, here = lax.optimization_barrier((w_qkv, window, here))
    head = jnp.arange(HEADS, dtype=i32)
    ahead = (window[None, :] > window[:, None]) | (
        (window[None, :] == window[:, None]) & (head[None, :] < head[:, None])
    )
    rank = jnp.sum(ahead.astype(i32), axis=1)
    sorted_to = rank[None, :] == head[:, None]
    plan = jnp.sum(jnp.where(sorted_to[None], jnp.stack([head, window])[:, None, :], 0), axis=2).astype(i32)
    w_query, w_key, w_value, early_left, early_right = pl.pallas_call(
        functools.partial(early_kernel, pairs),
        out_shape=[jax.ShapeDtypeStruct((width, width), bf16)] * 3
        + [jax.ShapeDtypeStruct((n, nodes, half), f32) for n in (pairs, 3)],
        in_specs=[VMEM] * 3 + [ANY],
        out_specs=[VMEM] * 5,
        compiler_params=params(24),
        cost_estimate=cost(1 << 28, 4 << 20),
        name="early",
    )(w_qkv, here, here_other, plan)
    def sums(arrays, early, kept, name):
        count = early.shape[0]
        return pl.pallas_call(
            functools.partial(sums_kernel, len(arrays), kept),
            out_shape=[jax.ShapeDtypeStruct((nodes, half), f32 if n == kept else bf16) for n in range(count)],
            in_specs=[VMEM] * (len(arrays) + 1),
            out_specs=[VMEM] * count,
            compiler_params=params(24),
            cost_estimate=cost(2 * nodes * half * len(arrays) * count * cap, 2 << 20),
            name=name,
        )(*arrays, early)

    left, *parts = sums([even, odd_other, odd, even_other], early_left, 0, "left")
    parts = [lax.ppermute(part, NODES, chip_trade(p + 1)) for p, part in enumerate(parts)]
    to_even, to_odd, right = sums(cross, early_right, 2, "right")
    from_even = lax.ppermute(to_even, NODES, bands_trade(0))
    from_odd = lax.ppermute(to_odd, NODES, bands_trade(1))

    state, normed = pl.pallas_call(
        merge_kernel,
        out_shape=[
            jax.ShapeDtypeStruct((nodes, width), f32),
            jax.ShapeDtypeStruct((nodes, width), bf16),
        ],
        in_specs=[VMEM] * (pairs + 6),
        out_specs=[VMEM] * 2,
        compiler_params=params(24),
        cost_estimate=cost(2 * nodes * width * width, 2 << 20),
        name="merge",
    )(left, *parts, right, from_even, from_odd, mesh_rows, w_merge, gain_attn.reshape(1, width))

    def chips_trade(odd_pairs):
        route = []
        for g in range(devices):
            t = (g // 2 - odd_pairs ^ 1) + odd_pairs
            route.append((g, 2 * t + g % 2 if 0 <= 2 * t < devices else g ^ 1))
        return route

    side = lax.ppermute(normed, NODES, beside)
    even = lax.ppermute(normed, NODES, chips_trade(0))
    side, normed = lax.optimization_barrier((side, normed))
    odd = lax.ppermute(normed, NODES, chips_trade(1))

    extra = head_dim + 16
    query, near, top = pl.pallas_call(
        near_kernel,
        out_shape=[
            jax.ShapeDtypeStruct((HEADS, LANES, nodes), bf16),
            jax.ShapeDtypeStruct((HEADS, extra, nodes), f32),
            jax.ShapeDtypeStruct((HEADS, 8, nodes), f32),
        ],
        in_specs=[VMEM] * 5 + [SMEM],
        out_specs=[VMEM] * 3,
        scratch_shapes=[
            pltpu.VMEM((width // LANES, 2 * nodes, LANES), bf16),
            pltpu.VMEM((HEADS, extra, 2 * nodes), bf16),
            pltpu.VMEM((2 * nodes, nodes), i32),
        ],
        compiler_params=params(32),
        cost_estimate=cost(8 << 30, 4 << 20),
        name="near",
    )(normed, side, w_query, w_key, w_value, plan)

    def outer(by_pair, block, near, top):
        return pl.pallas_call(
            functools.partial(outer_kernel, by_pair),
            out_shape=[
                jax.ShapeDtypeStruct((HEADS, extra, nodes), f32),
                jax.ShapeDtypeStruct((HEADS, 8, nodes), f32),
            ],
            in_specs=[VMEM] * 3 + [ANY] + [VMEM] * 3,
            out_specs=[VMEM] * 2,
            scratch_shapes=[
                pltpu.VMEM((width // LANES, nodes, LANES), bf16),
                pltpu.VMEM((HEADS, extra, nodes), bf16),
                pltpu.VMEM((nodes, nodes), f32),
                pltpu.SMEM((2, HEADS), i32),
                pltpu.SemaphoreType.DMA(()),
            ],
            compiler_params=params(24),
            cost_estimate=cost(8 * nodes * width * width, 3 << 20),
            name="pair" if by_pair else "other",
        )(block, w_key, w_value, plan, query, near, top)

    odd, near, top = lax.optimization_barrier((odd, near, top))
    second = lax.ppermute(odd, NODES, beside)
    near, top = outer(False, odd, near, top)
    even, near, top = lax.optimization_barrier((even, near, top))
    first = lax.ppermute(even, NODES, beside)
    near, top = outer(True, even, near, top)

    return pl.pallas_call(
        far_kernel,
        out_shape=jax.ShapeDtypeStruct((nodes, width), bf16),
        in_specs=[VMEM] * 12,
        out_specs=VMEM,
        scratch_shapes=[
            pltpu.VMEM((width // LANES, nodes, LANES), bf16),
            pltpu.VMEM((HEADS, extra, nodes), bf16),
            pltpu.VMEM((nodes, nodes), f32),
            pltpu.VMEM((HEADS, head_dim, nodes), bf16),
        ],
        compiler_params=params(40),
        cost_estimate=cost(8 << 30, 8 << 20),
        name="far",
    )(
        first, second, w_key, w_value,
        query, near, top, state, w_out, gain_mlp.reshape(1, width), w_up, w_down,
    )


def solution(mesh):
    placed = (
        P(("groups", "band", "inner"), None),
        P(("groups", "band", "inner"), None),
        P(("groups", "band"), "inner", None, None, None),
        P(("groups", "band"), "inner", None, None, None),
        P(("groups", "band"), "inner", None, None),
        P(),
        P(),
        P(),
        P(),
        P("groups"),
        P(),
        P(),
        P(),
        P(),
    )
    return jax.shard_map(
        local,
        mesh=mesh,
        in_specs=placed,
        out_specs=P(("groups", "band", "inner"), None),
        check_vma=False,
    )
```

```python
import functools
import math

import jax
import jax.numpy as jnp
from jax import lax
from jax.experimental import pallas as pl
from jax.experimental.pallas import tpu as pltpu
from jax.sharding import PartitionSpec as P

HEADS = 16
WMAX = 512
LANES = 128
NEAR = 128
TILE = 16
CAP = 128
GRID_PARTS = 2
MOST = 56
GROUP = 4

norm_eps = 1e-05
NODES = ("band", "inner")
VMEM = pl.BlockSpec(memory_space=pltpu.VMEM)
SMEM = pl.BlockSpec(memory_space=pltpu.SMEM)
ANY = pl.BlockSpec(memory_space=pl.ANY)


def params(mib):
    return pltpu.CompilerParams(vmem_limit_bytes=mib * 1024 * 1024)


def dot(a, b):
    return jnp.dot(a, b, preferred_element_type=jnp.float32)


def dot_t(a, b):
    return lax.dot_general(a, b, (((1,), (1,)), ((), ())), preferred_element_type=jnp.float32)


def silu(values):
    half = 0.5 * values
    return half + half * jnp.tanh(half)


def layer_norm(values, gain):
    center = values - jnp.mean(values, axis=-1, keepdims=True)
    spread = jnp.mean(center * center, axis=-1, keepdims=True)
    return center * lax.rsqrt(spread + norm_eps) * gain


def band_offsets():
    ahead = lax.rem(lax.axis_index("band"), 2) * 2
    return 2 - ahead, ahead, 1


def slot_columns(source_ref, blocks):
    sources = jnp.concatenate([source_ref[0, 0, o, pl.ds(j, 1), :] for o, j in blocks], axis=0)
    return jnp.transpose(sources.astype(jnp.float32)).astype(jnp.int32)


def target_tile(target_ref, count_ref, blocks, lanes):
    cap = target_ref.shape[-1]
    slot = lax.broadcasted_iota(jnp.int32, (1, cap), 1)
    targets = [
        jnp.where(slot < count_ref[0, o, 0, j], target_ref[0, 0, o, pl.ds(j, 1), :], -1) for o, j in blocks
    ]
    targets.append(jnp.full((TILE - len(blocks), cap), -1, jnp.int32))
    tile = jnp.concatenate(targets, axis=0).astype(jnp.float32).astype(jnp.bfloat16)
    return jnp.concatenate([tile] * (lanes // cap), axis=1)


def message_kernel(pair_count, grid_ref, w_ref, source_in, target_in, count_in, *refs):
    count = 4 + 2 * pair_count
    out_refs, out_vmems = refs[:count], refs[count : 2 * count]
    source_ref, target_ref, count_ref, grid_vmem, w_vmem, message_ref, pick_ref, in_sems, edge_sems, out_sems = refs[2 * count :]
    rows = grid_ref.shape[0]
    cap = source_ref.shape[-1]
    half = w_ref.shape[1] // 2
    part = rows // GRID_PARTS
    fetches = [pltpu.make_async_copy(w_ref, w_vmem, in_sems.at[GRID_PARTS])]
    for k in range(GRID_PARTS):
        span = pl.ds(k * part, part)
        fetches.append(pltpu.make_async_copy(grid_ref.at[span], grid_vmem.at[span], in_sems.at[k]))
    edges = ((source_in, source_ref), (target_in, target_ref), (count_in, count_ref))
    edge_fetches = [pltpu.make_async_copy(a, b, edge_sems.at[n]) for n, (a, b) in enumerate(edges)]
    for fetch in edge_fetches + fetches:
        fetch.start()
    for fetch in edge_fetches:
        fetch.wait()
    inner = lax.axis_index("inner")
    offsets = band_offsets()
    keys = [(t, p, k) for k in range(2) for t in range(3) for p in range(pair_count)]
    place = {(t, p, k): (offsets[t], inner ^ (2 * p + k)) for t, p, k in keys}
    by_slot = slot_columns(source_ref, [place[key] for key in keys])
    left, right = slice(0, half), slice(half, 2 * half)
    runs = [[([(t, p, k) for p in range(pair_count)], left)] for t in range(2) for k in range(2)]
    runs += [[([(t, p, k) for t in range(3)], right)] for p in range(1, pair_count) for k in range(2)]
    runs += [
        [([(2, p, k) for p in range(pair_count)], left), ([(t, 0, k) for t in range(3)], right)] for k in range(2)
    ]
    for out_vmem, parts in zip(out_vmems, runs):
        start = 0
        for chosen, _ in parts:
            start += len(chosen) * cap
            out_vmem[start : start + TILE, :] = target_tile(target_ref, count_ref, [place[key] for key in chosen], half)
            start += TILE
    row = lax.broadcasted_iota(jnp.int32, (cap, rows), 1)
    for m in range(len(keys)):
        pick_ref[m * cap : (m + 1) * cap, :] = jnp.where(row == by_slot[:, m : m + 1], 1.0, 0.0).astype(jnp.bfloat16)
    fetches[0].wait()
    for k in range(GRID_PARTS):
        span = pl.ds(k * part, part)
        fetches[k + 1].wait()
        message_ref[span] = silu(dot(grid_vmem[span], w_vmem[...])).astype(jnp.bfloat16)
    sends = []
    per_core = len(keys) // 2
    for k in range(2):
        first = k * per_core
        taken = dot(pick_ref[first * cap : (first + per_core) * cap, :], message_ref[...]).astype(jnp.bfloat16)
        for n in reversed(range(count)):
            start = 0
            if runs[n][0][0][0][2] != k:
                continue
            for chosen, lanes in runs[n]:
                for key in chosen:
                    m = keys.index(key) - first
                    out_vmems[n][start : start + cap, :] = taken[m * cap : (m + 1) * cap, lanes]
                    start += cap
                start += TILE
            send = pltpu.make_async_copy(out_vmems[n], out_refs[n], out_sems.at[n])
            send.start()
            sends.append(send)
    for send in sends:
        send.wait()


def node_sums(arrays, nodes):
    count = arrays[0][2]
    cap = CAP
    node = lax.broadcasted_iota(jnp.int32, (nodes, cap), 0)
    targets = [
        ref[start + count * cap : start + count * cap + TILE, 0:cap].astype(jnp.float32).astype(jnp.int32)
        for ref, start, _ in arrays
    ]
    for n in range(count):
        hits = [jnp.where(node == t[n : n + 1], 1.0, 0.0).astype(jnp.bfloat16) for t in targets]
        rows = [ref[start + n * cap : start + (n + 1) * cap, :] for ref, start, _ in arrays]
        yield n, dot(jnp.concatenate(hits, axis=1), jnp.concatenate(rows, axis=0))


def early_kernel(pair_count, w_ref, own_ref, other_ref, plan_ref, query_ref, key_ref, value_ref, left_ref, right_ref):
    width = w_ref.shape[0]
    head_dim = width // HEADS
    span = 3 * LANES
    def pick(c, along):
        shape = (LANES, span) if along else (span, LANES)
        to = lax.broadcasted_iota(jnp.int32, shape, 1 - along)
        column = lax.broadcasted_iota(jnp.int32, shape, along)
        wanted = to // head_dim * (3 * head_dim) + to % head_dim + c * head_dim
        return jnp.where(column == wanted, 1.0, 0.0).astype(jnp.bfloat16)

    for g in range(width // LANES):
        columns = w_ref[:, g * span : (g + 1) * span]
        part = slice(g * LANES, (g + 1) * LANES)
        query_ref[part, :] = dot_t(pick(0, 1), columns).astype(jnp.bfloat16)
        key_ref[:, part] = dot(columns, pick(1, 0)).astype(jnp.bfloat16)
        value_ref[part, :] = dot_t(pick(2, 1), columns).astype(jnp.bfloat16)
    start = 0
    for sum_ref in (left_ref, right_ref):
        count, nodes, _ = sum_ref.shape
        for n, total in node_sums([(own_ref, start, count), (other_ref, start, count)], nodes):
            sum_ref[n] = total
        start += count * CAP + TILE


def sums_kernel(array_count, kept, *refs):
    row_refs, early_ref, out_refs = refs[:array_count], refs[array_count], refs[array_count + 1 :]
    count, nodes, _ = early_ref.shape
    for n, total in node_sums([(r, 0, count) for r in row_refs], nodes):
        total = total + early_ref[n]
        out_refs[n][...] = total if n == kept else total.astype(jnp.bfloat16)


def merge_kernel(*refs):
    *part_refs, right_ref, even_ref, odd_ref, mesh_ref, w_ref, gain_ref, state_ref, normed_ref = refs
    left = functools.reduce(jnp.add, [r[...].astype(jnp.float32) for r in part_refs])
    right = right_ref[...] + even_ref[...].astype(jnp.float32) + odd_ref[...].astype(jnp.float32)
    total = jnp.concatenate([left, right], axis=1).astype(jnp.bfloat16)
    state = mesh_ref[...].astype(jnp.float32) + dot(total, w_ref[...])
    state_ref[...] = state
    normed_ref[...] = layer_norm(state, gain_ref[...]).astype(jnp.bfloat16)


def project_keys(rows, wk_ref, wv_ref, key_ref, value_ref, start):
    count = rows.shape[0]
    groups = key_ref.shape[0]
    heads = value_ref.shape[0]
    keys = dot(rows, wk_ref[...]).astype(jnp.bfloat16)
    for g in range(groups):
        key_ref[g, start : start + count, :] = keys[:, g * LANES : (g + 1) * LANES]
    values = dot_t(wv_ref[...], rows).astype(jnp.bfloat16)
    value_ref[:, 0 : values.shape[0] // heads, start : start + count] = values.reshape(
        heads, -1, count
    )


def near_kernel(
    own_ref, side_ref, wq_ref, wk_ref, wv_ref, plan_ref,
    query_ref, sums_ref, top_ref,
    key_ref, value_ref, gap_ref,
):
    nodes, width = own_ref.shape
    head_dim = width // HEADS
    per_group = LANES // head_dim
    odd = lax.rem(lax.axis_index("inner"), 2)
    side = 1 - 2 * odd
    first = odd * (nodes - NEAR)
    second = (1 - odd) * NEAR
    scale = head_dim ** (-0.5) / math.log(2.0)

    queries = dot_t(wq_ref[...], own_ref[...]).astype(jnp.bfloat16)
    part = lax.broadcasted_iota(jnp.int32, (LANES, nodes), 0) // head_dim
    for h in range(HEADS):
        g = h // per_group
        lanes = queries[g * LANES : (g + 1) * LANES]
        query_ref[h] = jnp.where(part == h % per_group, lanes, jnp.zeros_like(lanes))
    value_ref[:, head_dim:, :] = jnp.ones_like(value_ref[:, head_dim:, :])
    project_keys(own_ref[...], wk_ref, wv_ref, key_ref, value_ref, 0)
    project_keys(side_ref[pl.ds(pl.multiple_of(first, NEAR), NEAR), :], wk_ref, wv_ref, key_ref, value_ref, nodes)
    project_keys(
        side_ref[pl.ds(pl.multiple_of(second, NEAR), NEAR), :], wk_ref, wv_ref, key_ref, value_ref, nodes + NEAR
    )
    lag = lax.broadcasted_iota(jnp.int32, (nodes, nodes), 0) - lax.broadcasted_iota(
        jnp.int32, (nodes, nodes), 1
    )
    gap_ref[0:nodes] = jnp.abs(lag)
    gap_ref[nodes : nodes + NEAR] = jnp.abs(lag[0:NEAR] + (side * nodes + first))
    gap_ref[nodes + NEAR : 2 * nodes] = jnp.abs(lag[0:NEAR] + (side * nodes + second))

    def attend(heads, windows, rows):
        scores = [dot(key_ref[h // per_group, 0:rows, :], query_ref[h]) for h in heads]
        scores = [
            jnp.where(gap_ref[0:rows] <= w, x, -1e30) for w, x in zip(windows, scores)
        ]
        tops = [jnp.max(x, axis=0, keepdims=True) for x in scores]
        expos = [jnp.exp2((x - top) * scale).astype(jnp.bfloat16) for x, top in zip(scores, tops)]
        for h, w, top, expo in zip(heads, windows, tops, expos):
            sums_ref[h] = dot(value_ref[h, :, 0:rows], expo)
            top_ref[h, 0:1] = top
            top_ref[h, 1:2] = jnp.full((1, nodes), w.astype(jnp.float32))

    def together(i, carry):
        heads = [plan_ref[0, GROUP * i + k] for k in range(GROUP)]
        windows = [plan_ref[1, GROUP * i + k] for k in range(GROUP)]
        widest = windows[0]

        @pl.when(widest <= NEAR)
        def _():
            attend(heads, windows, nodes + NEAR)

        @pl.when(widest > NEAR)
        def _():
            attend(heads, windows, 2 * nodes)

        return carry

    lax.fori_loop(0, HEADS // GROUP, together, 0)


def gaps(device, start, rows, nodes):
    total = lax.axis_size("band") * lax.axis_size("inner")
    there = lax.axis_index("band") * lax.axis_size("inner") + lax.axis_index("inner") + device
    lag = lax.broadcasted_iota(jnp.int32, (rows, nodes), 0) - lax.broadcasted_iota(jnp.int32, (rows, nodes), 1)
    gap = jnp.where((there >= 0) & (there < total), jnp.abs(lag + (device * nodes + start)), 1 << 20)
    return gap.astype(jnp.float32)


def extend(heads, keys, values, gap_ref, query_ref, sums_ref, top_ref, scale):
    scores = [dot(k, query_ref[h]) for h, k in zip(heads, keys)]
    scores = [jnp.where(gap_ref[...] <= top_ref[h, 1:2, :], x, -1e30) for h, x in zip(heads, scores)]
    olds = [top_ref[h, 0:1, :] for h in heads]
    tops = [jnp.maximum(old, jnp.max(x, axis=0, keepdims=True)) for old, x in zip(olds, scores)]
    expos = [jnp.exp2((x - top) * scale).astype(jnp.bfloat16) for x, top in zip(scores, tops)]
    for h, v, old, top, expo in zip(heads, values, olds, tops, expos):
        yield h, sums_ref[h] * jnp.exp2((old - top) * scale) + dot(v, expo), top


def outer_kernel(
    by_pair, block_ref, wk_ref, wv_ref, plan_in, query_ref, sums_ref, top_ref,
    sums_out, top_out,
    key_ref, value_ref, gap_ref, plan_ref, sem,
):
    fetch = pltpu.make_async_copy(plan_in, plan_ref, sem)
    fetch.start()
    nodes, width = block_ref.shape
    head_dim = width // HEADS
    per_group = LANES // head_dim
    far = 2 - 4 * lax.rem(lax.axis_index("inner") // 2, 2)
    scale = head_dim ** (-0.5) / math.log(2.0)
    value_ref[:, head_dim:, :] = jnp.ones_like(value_ref[:, head_dim:, :])
    project_keys(block_ref[...], wk_ref, wv_ref, key_ref, value_ref, 0)
    gap_ref[...] = gaps(far if by_pair else -far, 0, nodes, nodes)
    fetch.wait()

    def wide(n):
        return plan_ref[1, n] > nodes

    def reach(first, last):
        heads = [plan_ref[0, n] for n in range(first, last)]
        keys, values = [key_ref[h // per_group] for h in heads], [value_ref[h] for h in heads]
        for h, sums, top in extend(
            heads, keys, values, gap_ref, query_ref, sums_ref, top_ref, scale
        ):
            sums_out[h] = sums
            top_out[h, 0:1] = top
            top_out[h, 1:2] = top_ref[h, 1:2]

    def leave(first, last):
        for n in range(first, last):
            h = plan_ref[0, n]
            sums_out[h] = sums_ref[h]
            top_out[h, 0:2] = top_ref[h, 0:2]

    @pl.when(wide(GROUP))
    def _():
        reach(0, 2 * GROUP)

    @pl.when(jnp.logical_not(wide(GROUP)))
    def _():
        reach(0, GROUP)
        leave(GROUP, 2 * GROUP)

    for first in range(2 * GROUP, HEADS, GROUP):
        pl.when(wide(first))(functools.partial(reach, first, first + GROUP))
        pl.when(jnp.logical_not(wide(first)))(functools.partial(leave, first, first + GROUP))


def far_kernel(
    first_ref, second_ref, wk_ref, wv_ref, query_ref, sums_ref, top_ref,
    state_ref, w_out_ref, gain_ref, up_ref, down_ref,
    out_ref,
    key_ref, value_ref, gap_ref, attended_ref,
):
    nodes, width = first_ref.shape
    head_dim = width // HEADS
    per_group = LANES // head_dim
    inner = lax.axis_index("inner")
    odd = lax.rem(inner, 2)
    scale = head_dim ** (-0.5) / math.log(2.0)
    value_ref[:, head_dim:, :] = jnp.ones_like(value_ref[:, head_dim:, :])
    by_even = odd == lax.rem(inner // 2 + 1, 2)
    project_keys(jnp.where(by_even, first_ref[...], second_ref[...]), wk_ref, wv_ref, key_ref, value_ref, 0)
    gap_ref[...] = gaps(2 * odd - 1, 0, nodes, nodes)
    for i in range(HEADS // (2 * GROUP)):
        heads = range(2 * GROUP * i, 2 * GROUP * (i + 1))
        keys, values = [key_ref[h // per_group] for h in heads], [value_ref[h] for h in heads]
        for h, sums, _ in extend(
            heads, keys, values, gap_ref, query_ref, sums_ref, top_ref, scale
        ):
            attended_ref[h] = (sums[0:head_dim] / sums[head_dim : head_dim + 1]).astype(jnp.bfloat16)

    attended = attended_ref[...].reshape(width, nodes)
    mixed = lax.dot_general(
        attended, w_out_ref[...], (((0,), (0,)), ((), ())), preferred_element_type=jnp.float32
    )
    total = state_ref[...] + mixed
    normed = layer_norm(total, gain_ref[...]).astype(jnp.bfloat16)
    chunk = math.gcd(up_ref.shape[1], 1024)
    for start in range(0, up_ref.shape[1], chunk):
        hidden = silu(dot(normed, up_ref[:, start : start + chunk])).astype(jnp.bfloat16)
        total = total + dot(hidden, down_ref[start : start + chunk, :])
    out_ref[...] = total.astype(jnp.bfloat16)


def cost(flops, size):
    return pl.CostEstimate(flops=flops, bytes_accessed=size, transcendentals=0)


def local(
    grid_rows,
    mesh_rows,
    edge_source,
    edge_target,
    edge_count,
    w_message,
    w_merge,
    gain_attn,
    w_qkv,
    window,
    w_out,
    gain_mlp,
    w_up,
    w_down,
):
    bands = lax.axis_size("band")
    inners = lax.axis_size("inner")
    devices = bands * inners
    grid_dev = grid_rows.shape[0]
    nodes, width = mesh_rows.shape
    cap = edge_source.shape[-1]
    head_dim = width // HEADS
    pairs = inners // 2
    half = width // 2
    f32, bf16, i32 = jnp.float32, jnp.bfloat16, jnp.int32
    edges = (edge_source, edge_target, jnp.transpose(edge_count, (0, 2, 1, 3)))

    def rows_of(*blocks):
        return jax.ShapeDtypeStruct((sum(n * cap + TILE for n in blocks), half), bf16)

    outgoing = [rows_of(pairs)] * 4 + [rows_of(3)] * (2 * pairs - 2) + [rows_of(pairs, 3)] * 2
    even, even_other, odd, odd_other, *cross, here, here_other = pl.pallas_call(
        functools.partial(message_kernel, pairs),
        out_shape=outgoing,
        in_specs=[ANY] * 5,
        out_specs=[ANY] * len(outgoing),
        scratch_shapes=[pltpu.VMEM(a.shape, bf16) for a in outgoing]
        + [
            pltpu.VMEM(edges[0].shape, i32),
            pltpu.VMEM(edges[1].shape, i32),
            pltpu.SMEM(edges[2].shape, i32),
            pltpu.VMEM(grid_rows.shape, bf16),
            pltpu.VMEM(w_message.shape, bf16),
            pltpu.VMEM((grid_dev, width), bf16),
            pltpu.VMEM((3 * inners * cap, grid_dev), bf16),
            pltpu.SemaphoreType.DMA((GRID_PARTS + 1,)),
            pltpu.SemaphoreType.DMA((3,)),
            pltpu.SemaphoreType.DMA((len(outgoing),)),
        ],
        compiler_params=params(MOST),
        cost_estimate=cost(2 * grid_dev * width * (width + 3 * inners * cap), 4 << 20),
        name="messages",
    )(grid_rows, w_message, *edges)
    beside = [(g, g ^ 1) for g in range(devices)]

    def bands_trade(odd_pairs, k=0):
        route = []
        for g in range(devices):
            b = g // inners
            t = (b - odd_pairs ^ 1) + odd_pairs
            route.append((g, t * inners + (g % inners ^ k) if 0 <= t < bands else g ^ 1))
        return route

    def chip_trade(p, k=0):
        return [(g, g ^ (2 * p + k)) for g in range(devices)]

    here_other = lax.ppermute(here_other, NODES, beside)
    cross[0::2] = [lax.ppermute(c, NODES, chip_trade(p + 1)) for p, c in enumerate(cross[0::2])]
    even = lax.ppermute(even, NODES, bands_trade(0))
    odd = lax.ppermute(odd, NODES, bands_trade(1))
    here_other, even_other, odd_other, *cross[1::2] = lax.optimization_barrier(
        (here_other, even_other, odd_other, *cross[1::2])
    )
    cross[1::2] = [lax.ppermute(c, NODES, chip_trade(p + 1, 1)) for p, c in enumerate(cross[1::2])]
    even_other = lax.ppermute(even_other, NODES, bands_trade(0, 1))
    odd_other = lax.ppermute(odd_other, NODES, bands_trade(1, 1))

    w_qkv, window, here = lax.optimization_barrier((w_qkv, window, here))
    head = jnp.arange(HEADS, dtype=i32)
    ahead = (window[None, :] > window[:, None]) | (
        (window[None, :] == window[:, None]) & (head[None, :] < head[:, None])
    )
    rank = jnp.sum(ahead.astype(i32), axis=1)
    sorted_to = rank[None, :] == head[:, None]
    plan = jnp.sum(jnp.where(sorted_to[None], jnp.stack([head, window])[:, None, :], 0), axis=2).astype(i32)
    w_query, w_key, w_value, early_left, early_right = pl.pallas_call(
        functools.partial(early_kernel, pairs),
        out_shape=[jax.ShapeDtypeStruct((width, width), bf16)] * 3
        + [jax.ShapeDtypeStruct((n, nodes, half), f32) for n in (pairs, 3)],
        in_specs=[VMEM] * 3 + [ANY],
        out_specs=[VMEM] * 5,
        compiler_params=params(24),
        cost_estimate=cost(1 << 28, 4 << 20),
        name="early",
    )(w_qkv, here, here_other, plan)
    def sums(arrays, early, kept, name):
        count = early.shape[0]
        return pl.pallas_call(
            functools.partial(sums_kernel, len(arrays), kept),
            out_shape=[jax.ShapeDtypeStruct((nodes, half), f32 if n == kept else bf16) for n in range(count)],
            in_specs=[VMEM] * (len(arrays) + 1),
            out_specs=[VMEM] * count,
            compiler_params=params(24),
            cost_estimate=cost(2 * nodes * half * len(arrays) * count * cap, 2 << 20),
            name=name,
        )(*arrays, early)

    left, *parts = sums([even, even_other, odd, odd_other], early_left, 0, "left")
    parts = [lax.ppermute(part, NODES, chip_trade(p + 1)) for p, part in enumerate(parts)]
    to_even, to_odd, right = sums(cross, early_right, 2, "right")
    from_even = lax.ppermute(to_even, NODES, bands_trade(0))
    from_odd = lax.ppermute(to_odd, NODES, bands_trade(1))

    state, normed = pl.pallas_call(
        merge_kernel,
        out_shape=[
            jax.ShapeDtypeStruct((nodes, width), f32),
            jax.ShapeDtypeStruct((nodes, width), bf16),
        ],
        in_specs=[VMEM] * (pairs + 6),
        out_specs=[VMEM] * 2,
        compiler_params=params(24),
        cost_estimate=cost(2 * nodes * width * width, 2 << 20),
        name="merge",
    )(left, *parts, right, from_even, from_odd, mesh_rows, w_merge, gain_attn.reshape(1, width))

    def chips_trade(odd_pairs):
        route = []
        for g in range(devices):
            t = (g // 2 - odd_pairs ^ 1) + odd_pairs
            route.append((g, 2 * t + g % 2 if 0 <= 2 * t < devices else g ^ 1))
        return route

    side = lax.ppermute(normed, NODES, beside)
    even = lax.ppermute(normed, NODES, chips_trade(0))
    side, normed = lax.optimization_barrier((side, normed))
    odd = lax.ppermute(normed, NODES, chips_trade(1))

    extra = head_dim + 16
    query, near, top = pl.pallas_call(
        near_kernel,
        out_shape=[
            jax.ShapeDtypeStruct((HEADS, LANES, nodes), bf16),
            jax.ShapeDtypeStruct((HEADS, extra, nodes), f32),
            jax.ShapeDtypeStruct((HEADS, 8, nodes), f32),
        ],
        in_specs=[VMEM] * 5 + [SMEM],
        out_specs=[VMEM] * 3,
        scratch_shapes=[
            pltpu.VMEM((width // LANES, 2 * nodes, LANES), bf16),
            pltpu.VMEM((HEADS, extra, 2 * nodes), bf16),
            pltpu.VMEM((2 * nodes, nodes), i32),
        ],
        compiler_params=params(32),
        cost_estimate=cost(8 << 30, 4 << 20),
        name="near",
    )(normed, side, w_query, w_key, w_value, plan)

    def outer(by_pair, block, near, top):
        return pl.pallas_call(
            functools.partial(outer_kernel, by_pair),
            out_shape=[
                jax.ShapeDtypeStruct((HEADS, extra, nodes), f32),
                jax.ShapeDtypeStruct((HEADS, 8, nodes), f32),
            ],
            in_specs=[VMEM] * 3 + [ANY] + [VMEM] * 3,
            out_specs=[VMEM] * 2,
            scratch_shapes=[
                pltpu.VMEM((width // LANES, nodes, LANES), bf16),
                pltpu.VMEM((HEADS, extra, nodes), bf16),
                pltpu.VMEM((nodes, nodes), f32),
                pltpu.SMEM((2, HEADS), i32),
                pltpu.SemaphoreType.DMA(()),
            ],
            compiler_params=params(24),
            cost_estimate=cost(8 * nodes * width * width, 3 << 20),
            name="pair" if by_pair else "other",
        )(block, w_key, w_value, plan, query, near, top)

    odd, near, top = lax.optimization_barrier((odd, near, top))
    second = lax.ppermute(odd, NODES, beside)
    near, top = outer(False, odd, near, top)
    even, near, top = lax.optimization_barrier((even, near, top))
    first = lax.ppermute(even, NODES, beside)
    near, top = outer(True, even, near, top)

    return pl.pallas_call(
        far_kernel,
        out_shape=jax.ShapeDtypeStruct((nodes, width), bf16),
        in_specs=[VMEM] * 12,
        out_specs=VMEM,
        scratch_shapes=[
            pltpu.VMEM((width // LANES, nodes, LANES), bf16),
            pltpu.VMEM((HEADS, extra, nodes), bf16),
            pltpu.VMEM((nodes, nodes), f32),
            pltpu.VMEM((HEADS, head_dim, nodes), bf16),
        ],
        compiler_params=params(40),
        cost_estimate=cost(8 << 30, 8 << 20),
        name="far",
    )(
        first, second, w_key, w_value,
        query, near, top, state, w_out, gain_mlp.reshape(1, width), w_up, w_down,
    )


def solution(mesh):
    placed = (
        P(("groups", "band", "inner"), None),
        P(("groups", "band", "inner"), None),
        P(("groups", "band"), "inner", None, None, None),
        P(("groups", "band"), "inner", None, None, None),
        P(("groups", "band"), "inner", None, None),
        P(),
        P(),
        P(),
        P(),
        P("groups"),
        P(),
        P(),
        P(),
        P(),
    )
    return jax.shard_map(
        local,
        mesh=mesh,
        in_specs=placed,
        out_specs=P(("groups", "band", "inner"), None),
        check_vma=False,
    )
```

```python
import functools
import math

import jax
import jax.numpy as jnp
from jax import lax
from jax.experimental import pallas as pl
from jax.experimental.pallas import tpu as pltpu
from jax.sharding import PartitionSpec as P

HEADS = 16
WMAX = 512
LANES = 128
NEAR = 128
TILE = 16
CAP = 128
GRID_PARTS = 1
MOST = 56
GROUP = 4

norm_eps = 1e-05
NODES = ("band", "inner")
VMEM = pl.BlockSpec(memory_space=pltpu.VMEM)
SMEM = pl.BlockSpec(memory_space=pltpu.SMEM)
ANY = pl.BlockSpec(memory_space=pl.ANY)


def params(mib):
    return pltpu.CompilerParams(vmem_limit_bytes=mib * 1024 * 1024)


def dot(a, b):
    return jnp.dot(a, b, preferred_element_type=jnp.float32)


def dot_t(a, b):
    return lax.dot_general(a, b, (((1,), (1,)), ((), ())), preferred_element_type=jnp.float32)


def silu(values):
    half = 0.5 * values
    return half + half * jnp.tanh(half)


def layer_norm(values, gain):
    center = values - jnp.mean(values, axis=-1, keepdims=True)
    spread = jnp.mean(center * center, axis=-1, keepdims=True)
    return center * lax.rsqrt(spread + norm_eps) * gain


def band_offsets():
    ahead = lax.rem(lax.axis_index("band"), 2) * 2
    return 2 - ahead, ahead, 1


def slot_columns(source_ref, blocks):
    sources = jnp.concatenate([source_ref[0, 0, o, pl.ds(j, 1), :] for o, j in blocks], axis=0)
    return jnp.transpose(sources.astype(jnp.float32)).astype(jnp.int32)


def target_tile(target_ref, count_ref, blocks, lanes):
    cap = target_ref.shape[-1]
    slot = lax.broadcasted_iota(jnp.int32, (1, cap), 1)
    targets = [
        jnp.where(slot < count_ref[0, o, 0, j], target_ref[0, 0, o, pl.ds(j, 1), :], -1) for o, j in blocks
    ]
    targets.append(jnp.full((TILE - len(blocks), cap), -1, jnp.int32))
    tile = jnp.concatenate(targets, axis=0).astype(jnp.float32).astype(jnp.bfloat16)
    return jnp.concatenate([tile] * (lanes // cap), axis=1)


def message_kernel(pair_count, grid_ref, w_ref, source_in, target_in, count_in, *refs):
    count = 4 + 2 * pair_count
    out_refs, out_vmems = refs[:count], refs[count : 2 * count]
    source_ref, target_ref, count_ref, grid_vmem, w_vmem, message_ref, pick_ref, in_sems, edge_sems, out_sems = refs[2 * count :]
    rows = grid_ref.shape[0]
    cap = source_ref.shape[-1]
    half = w_ref.shape[1] // 2
    part = rows // GRID_PARTS
    fetches = [pltpu.make_async_copy(w_ref, w_vmem, in_sems.at[GRID_PARTS])]
    for k in range(GRID_PARTS):
        span = pl.ds(k * part, part)
        fetches.append(pltpu.make_async_copy(grid_ref.at[span], grid_vmem.at[span], in_sems.at[k]))
    edges = ((source_in, source_ref), (target_in, target_ref), (count_in, count_ref))
    edge_fetches = [pltpu.make_async_copy(a, b, edge_sems.at[n]) for n, (a, b) in enumerate(edges)]
    for fetch in edge_fetches + fetches:
        fetch.start()
    for fetch in edge_fetches:
        fetch.wait()
    inner = lax.axis_index("inner")
    offsets = band_offsets()
    keys = [(t, p, k) for k in range(2) for t in range(3) for p in range(pair_count)]
    place = {(t, p, k): (offsets[t], inner ^ (2 * p + k)) for t, p, k in keys}
    by_slot = slot_columns(source_ref, [place[key] for key in keys])
    left, right = slice(0, half), slice(half, 2 * half)
    runs = [[([(t, p, k) for p in range(pair_count)], left)] for t in range(2) for k in range(2)]
    runs += [[([(t, p, k) for t in range(3)], right)] for p in range(1, pair_count) for k in range(2)]
    runs += [
        [([(2, p, k) for p in range(pair_count)], left), ([(t, 0, k) for t in range(3)], right)] for k in range(2)
    ]
    for out_vmem, parts in zip(out_vmems, runs):
        start = 0
        for chosen, _ in parts:
            start += len(chosen) * cap
            out_vmem[start : start + TILE, :] = target_tile(target_ref, count_ref, [place[key] for key in chosen], half)
            start += TILE
    row = lax.broadcasted_iota(jnp.int32, (cap, rows), 1)
    for m in range(len(keys)):
        pick_ref[m * cap : (m + 1) * cap, :] = jnp.where(row == by_slot[:, m : m + 1], 1.0, 0.0).astype(jnp.bfloat16)
    fetches[0].wait()
    for k in range(GRID_PARTS):
        span = pl.ds(k * part, part)
        fetches[k + 1].wait()
        message_ref[span] = silu(dot(grid_vmem[span], w_vmem[...])).astype(jnp.bfloat16)
    sends = []
    per_core = len(keys) // 2
    for k in range(2):
        first = k * per_core
        taken = dot(pick_ref[first * cap : (first + per_core) * cap, :], message_ref[...]).astype(jnp.bfloat16)
        for n in reversed(range(count)):
            start = 0
            if runs[n][0][0][0][2] != k:
                continue
            for chosen, lanes in runs[n]:
                for key in chosen:
                    m = keys.index(key) - first
                    out_vmems[n][start : start + cap, :] = taken[m * cap : (m + 1) * cap, lanes]
                    start += cap
                start += TILE
            send = pltpu.make_async_copy(out_vmems[n], out_refs[n], out_sems.at[n])
            send.start()
            sends.append(send)
    for send in sends:
        send.wait()


def node_sums(arrays, nodes):
    count = arrays[0][2]
    cap = CAP
    node = lax.broadcasted_iota(jnp.int32, (nodes, cap), 0)
    targets = [
        ref[start + count * cap : start + count * cap + TILE, 0:cap].astype(jnp.float32).astype(jnp.int32)
        for ref, start, _ in arrays
    ]
    for n in range(count):
        hits = [jnp.where(node == t[n : n + 1], 1.0, 0.0).astype(jnp.bfloat16) for t in targets]
        rows = [ref[start + n * cap : start + (n + 1) * cap, :] for ref, start, _ in arrays]
        yield n, dot(jnp.concatenate(hits, axis=1), jnp.concatenate(rows, axis=0))


def early_kernel(pair_count, w_ref, own_ref, other_ref, plan_ref, query_ref, key_ref, value_ref, left_ref, right_ref):
    width = w_ref.shape[0]
    head_dim = width // HEADS
    span = 3 * LANES
    def pick(c, along):
        shape = (LANES, span) if along else (span, LANES)
        to = lax.broadcasted_iota(jnp.int32, shape, 1 - along)
        column = lax.broadcasted_iota(jnp.int32, shape, along)
        wanted = to // head_dim * (3 * head_dim) + to % head_dim + c * head_dim
        return jnp.where(column == wanted, 1.0, 0.0).astype(jnp.bfloat16)

    for g in range(width // LANES):
        columns = w_ref[:, g * span : (g + 1) * span]
        part = slice(g * LANES, (g + 1) * LANES)
        query_ref[part, :] = dot_t(pick(0, 1), columns).astype(jnp.bfloat16)
        key_ref[:, part] = dot(columns, pick(1, 0)).astype(jnp.bfloat16)
        value_ref[part, :] = dot_t(pick(2, 1), columns).astype(jnp.bfloat16)
    start = 0
    for sum_ref in (left_ref, right_ref):
        count, nodes, _ = sum_ref.shape
        for n, total in node_sums([(own_ref, start, count), (other_ref, start, count)], nodes):
            sum_ref[n] = total
        start += count * CAP + TILE


def sums_kernel(array_count, kept, *refs):
    row_refs, early_ref, out_refs = refs[:array_count], refs[array_count], refs[array_count + 1 :]
    count, nodes, _ = early_ref.shape
    for n, total in node_sums([(r, 0, count) for r in row_refs], nodes):
        total = total + early_ref[n]
        out_refs[n][...] = total if n == kept else total.astype(jnp.bfloat16)


def merge_kernel(*refs):
    *part_refs, right_ref, even_ref, odd_ref, mesh_ref, w_ref, gain_ref, state_ref, normed_ref = refs
    left = functools.reduce(jnp.add, [r[...].astype(jnp.float32) for r in part_refs])
    right = right_ref[...] + even_ref[...].astype(jnp.float32) + odd_ref[...].astype(jnp.float32)
    total = jnp.concatenate([left, right], axis=1).astype(jnp.bfloat16)
    state = mesh_ref[...].astype(jnp.float32) + dot(total, w_ref[...])
    state_ref[...] = state
    normed_ref[...] = layer_norm(state, gain_ref[...]).astype(jnp.bfloat16)


def project_keys(rows, wk_ref, wv_ref, key_ref, value_ref, start):
    count = rows.shape[0]
    groups = key_ref.shape[0]
    heads = value_ref.shape[0]
    keys = dot(rows, wk_ref[...]).astype(jnp.bfloat16)
    for g in range(groups):
        key_ref[g, start : start + count, :] = keys[:, g * LANES : (g + 1) * LANES]
    values = dot_t(wv_ref[...], rows).astype(jnp.bfloat16)
    value_ref[:, 0 : values.shape[0] // heads, start : start + count] = values.reshape(
        heads, -1, count
    )


def near_kernel(
    own_ref, side_ref, wq_ref, wk_ref, wv_ref, plan_ref,
    query_ref, sums_ref, top_ref,
    key_ref, value_ref, gap_ref,
):
    nodes, width = own_ref.shape
    head_dim = width // HEADS
    per_group = LANES // head_dim
    odd = lax.rem(lax.axis_index("inner"), 2)
    side = 1 - 2 * odd
    first = odd * (nodes - NEAR)
    second = (1 - odd) * NEAR
    scale = head_dim ** (-0.5) / math.log(2.0)

    queries = dot_t(wq_ref[...], own_ref[...]).astype(jnp.bfloat16)
    part = lax.broadcasted_iota(jnp.int32, (LANES, nodes), 0) // head_dim
    for h in range(HEADS):
        g = h // per_group
        lanes = queries[g * LANES : (g + 1) * LANES]
        query_ref[h] = jnp.where(part == h % per_group, lanes, jnp.zeros_like(lanes))
    value_ref[:, head_dim:, :] = jnp.ones_like(value_ref[:, head_dim:, :])
    project_keys(own_ref[...], wk_ref, wv_ref, key_ref, value_ref, 0)
    project_keys(side_ref[pl.ds(pl.multiple_of(first, NEAR), NEAR), :], wk_ref, wv_ref, key_ref, value_ref, nodes)
    project_keys(
        side_ref[pl.ds(pl.multiple_of(second, NEAR), NEAR), :], wk_ref, wv_ref, key_ref, value_ref, nodes + NEAR
    )
    lag = lax.broadcasted_iota(jnp.int32, (nodes, nodes), 0) - lax.broadcasted_iota(
        jnp.int32, (nodes, nodes), 1
    )
    gap_ref[0:nodes] = jnp.abs(lag)
    gap_ref[nodes : nodes + NEAR] = jnp.abs(lag[0:NEAR] + (side * nodes + first))
    gap_ref[nodes + NEAR : 2 * nodes] = jnp.abs(lag[0:NEAR] + (side * nodes + second))

    def attend(heads, windows, rows):
        scores = [dot(key_ref[h // per_group, 0:rows, :], query_ref[h]) for h in heads]
        scores = [
            jnp.where(gap_ref[0:rows] <= w, x, -1e30) for w, x in zip(windows, scores)
        ]
        tops = [jnp.max(x, axis=0, keepdims=True) for x in scores]
        expos = [jnp.exp2((x - top) * scale).astype(jnp.bfloat16) for x, top in zip(scores, tops)]
        for h, w, top, expo in zip(heads, windows, tops, expos):
            sums_ref[h] = dot(value_ref[h, :, 0:rows], expo)
            top_ref[h, 0:1] = top
            top_ref[h, 1:2] = jnp.full((1, nodes), w.astype(jnp.float32))

    def together(i, carry):
        heads = [plan_ref[0, GROUP * i + k] for k in range(GROUP)]
        windows = [plan_ref[1, GROUP * i + k] for k in range(GROUP)]
        widest = windows[0]

        @pl.when(widest <= NEAR)
        def _():
            attend(heads, windows, nodes + NEAR)

        @pl.when(widest > NEAR)
        def _():
            attend(heads, windows, 2 * nodes)

        return carry

    lax.fori_loop(0, HEADS // GROUP, together, 0)


def gaps(device, start, rows, nodes):
    total = lax.axis_size("band") * lax.axis_size("inner")
    there = lax.axis_index("band") * lax.axis_size("inner") + lax.axis_index("inner") + device
    lag = lax.broadcasted_iota(jnp.int32, (rows, nodes), 0) - lax.broadcasted_iota(jnp.int32, (rows, nodes), 1)
    gap = jnp.where((there >= 0) & (there < total), jnp.abs(lag + (device * nodes + start)), 1 << 20)
    return gap.astype(jnp.float32)


def extend(heads, keys, values, gap_ref, query_ref, sums_ref, top_ref, scale):
    scores = [dot(k, query_ref[h]) for h, k in zip(heads, keys)]
    scores = [jnp.where(gap_ref[...] <= top_ref[h, 1:2, :], x, -1e30) for h, x in zip(heads, scores)]
    olds = [top_ref[h, 0:1, :] for h in heads]
    tops = [jnp.maximum(old, jnp.max(x, axis=0, keepdims=True)) for old, x in zip(olds, scores)]
    expos = [jnp.exp2((x - top) * scale).astype(jnp.bfloat16) for x, top in zip(scores, tops)]
    for h, v, old, top, expo in zip(heads, values, olds, tops, expos):
        yield h, sums_ref[h] * jnp.exp2((old - top) * scale) + dot(v, expo), top


def outer_kernel(
    by_pair, block_ref, wk_ref, wv_ref, plan_in, query_ref, sums_ref, top_ref,
    sums_out, top_out,
    key_ref, value_ref, gap_ref, plan_ref, sem,
):
    fetch = pltpu.make_async_copy(plan_in, plan_ref, sem)
    fetch.start()
    nodes, width = block_ref.shape
    head_dim = width // HEADS
    per_group = LANES // head_dim
    far = 2 - 4 * lax.rem(lax.axis_index("inner") // 2, 2)
    scale = head_dim ** (-0.5) / math.log(2.0)
    value_ref[:, head_dim:, :] = jnp.ones_like(value_ref[:, head_dim:, :])
    project_keys(block_ref[...], wk_ref, wv_ref, key_ref, value_ref, 0)
    gap_ref[...] = gaps(far if by_pair else -far, 0, nodes, nodes)
    fetch.wait()

    def wide(n):
        return plan_ref[1, n] > nodes

    def reach(first, last):
        heads = [plan_ref[0, n] for n in range(first, last)]
        keys, values = [key_ref[h // per_group] for h in heads], [value_ref[h] for h in heads]
        for h, sums, top in extend(
            heads, keys, values, gap_ref, query_ref, sums_ref, top_ref, scale
        ):
            sums_out[h] = sums
            top_out[h, 0:1] = top
            top_out[h, 1:2] = top_ref[h, 1:2]

    def leave(first, last):
        for n in range(first, last):
            h = plan_ref[0, n]
            sums_out[h] = sums_ref[h]
            top_out[h, 0:2] = top_ref[h, 0:2]

    @pl.when(wide(GROUP))
    def _():
        reach(0, 2 * GROUP)

    @pl.when(jnp.logical_not(wide(GROUP)))
    def _():
        reach(0, GROUP)
        leave(GROUP, 2 * GROUP)

    for first in range(2 * GROUP, HEADS, GROUP):
        pl.when(wide(first))(functools.partial(reach, first, first + GROUP))
        pl.when(jnp.logical_not(wide(first)))(functools.partial(leave, first, first + GROUP))


def far_kernel(
    first_ref, second_ref, wk_ref, wv_ref, query_ref, sums_ref, top_ref,
    state_ref, w_out_ref, gain_ref, up_ref, down_ref,
    out_ref,
    key_ref, value_ref, gap_ref, attended_ref,
):
    nodes, width = first_ref.shape
    head_dim = width // HEADS
    per_group = LANES // head_dim
    inner = lax.axis_index("inner")
    odd = lax.rem(inner, 2)
    scale = head_dim ** (-0.5) / math.log(2.0)
    value_ref[:, head_dim:, :] = jnp.ones_like(value_ref[:, head_dim:, :])
    by_even = odd == lax.rem(inner // 2 + 1, 2)
    project_keys(jnp.where(by_even, first_ref[...], second_ref[...]), wk_ref, wv_ref, key_ref, value_ref, 0)
    gap_ref[...] = gaps(2 * odd - 1, 0, nodes, nodes)
    heads = range(HEADS)
    keys, values = [key_ref[h // per_group] for h in heads], [value_ref[h] for h in heads]
    for h, sums, _ in extend(
        heads, keys, values, gap_ref, query_ref, sums_ref, top_ref, scale
    ):
        attended_ref[h] = (sums[0:head_dim] / sums[head_dim : head_dim + 1]).astype(jnp.bfloat16)

    attended = attended_ref[...].reshape(width, nodes)
    mixed = lax.dot_general(
        attended, w_out_ref[...], (((0,), (0,)), ((), ())), preferred_element_type=jnp.float32
    )
    total = state_ref[...] + mixed
    normed = layer_norm(total, gain_ref[...]).astype(jnp.bfloat16)
    hidden = silu(dot(normed, up_ref[...])).astype(jnp.bfloat16)
    total = total + dot(hidden, down_ref[...])
    out_ref[...] = total.astype(jnp.bfloat16)


def cost(flops, size):
    return pl.CostEstimate(flops=flops, bytes_accessed=size, transcendentals=0)


def local(
    grid_rows,
    mesh_rows,
    edge_source,
    edge_target,
    edge_count,
    w_message,
    w_merge,
    gain_attn,
    w_qkv,
    window,
    w_out,
    gain_mlp,
    w_up,
    w_down,
):
    bands = lax.axis_size("band")
    inners = lax.axis_size("inner")
    devices = bands * inners
    grid_dev = grid_rows.shape[0]
    nodes, width = mesh_rows.shape
    cap = edge_source.shape[-1]
    head_dim = width // HEADS
    pairs = inners // 2
    half = width // 2
    f32, bf16, i32 = jnp.float32, jnp.bfloat16, jnp.int32
    edges = (edge_source, edge_target, jnp.transpose(edge_count, (0, 2, 1, 3)))

    def rows_of(*blocks):
        return jax.ShapeDtypeStruct((sum(n * cap + TILE for n in blocks), half), bf16)

    outgoing = [rows_of(pairs)] * 4 + [rows_of(3)] * (2 * pairs - 2) + [rows_of(pairs, 3)] * 2
    even, even_other, odd, odd_other, *cross, here, here_other = pl.pallas_call(
        functools.partial(message_kernel, pairs),
        out_shape=outgoing,
        in_specs=[ANY] * 5,
        out_specs=[ANY] * len(outgoing),
        scratch_shapes=[pltpu.VMEM(a.shape, bf16) for a in outgoing]
        + [
            pltpu.VMEM(edges[0].shape, i32),
            pltpu.VMEM(edges[1].shape, i32),
            pltpu.SMEM(edges[2].shape, i32),
            pltpu.VMEM(grid_rows.shape, bf16),
            pltpu.VMEM(w_message.shape, bf16),
            pltpu.VMEM((grid_dev, width), bf16),
            pltpu.VMEM((3 * inners * cap, grid_dev), bf16),
            pltpu.SemaphoreType.DMA((GRID_PARTS + 1,)),
            pltpu.SemaphoreType.DMA((3,)),
            pltpu.SemaphoreType.DMA((len(outgoing),)),
        ],
        compiler_params=params(MOST),
        cost_estimate=cost(2 * grid_dev * width * (width + 3 * inners * cap), 4 << 20),
        name="messages",
    )(grid_rows, w_message, *edges)
    beside = [(g, g ^ 1) for g in range(devices)]

    def bands_trade(odd_pairs, k=0):
        route = []
        for g in range(devices):
            b = g // inners
            t = (b - odd_pairs ^ 1) + odd_pairs
            route.append((g, t * inners + (g % inners ^ k) if 0 <= t < bands else g ^ 1))
        return route

    def chip_trade(p, k=0):
        return [(g, g ^ (2 * p + k)) for g in range(devices)]

    here_other = lax.ppermute(here_other, NODES, beside)
    cross[0::2] = [lax.ppermute(c, NODES, chip_trade(p + 1)) for p, c in enumerate(cross[0::2])]
    even = lax.ppermute(even, NODES, bands_trade(0))
    odd = lax.ppermute(odd, NODES, bands_trade(1))
    here_other, even_other, odd_other, *cross[1::2] = lax.optimization_barrier(
        (here_other, even_other, odd_other, *cross[1::2])
    )
    cross[1::2] = [lax.ppermute(c, NODES, chip_trade(p + 1, 1)) for p, c in enumerate(cross[1::2])]
    even_other = lax.ppermute(even_other, NODES, bands_trade(0, 1))
    odd_other = lax.ppermute(odd_other, NODES, bands_trade(1, 1))

    w_qkv, window, here = lax.optimization_barrier((w_qkv, window, here))
    head = jnp.arange(HEADS, dtype=i32)
    ahead = (window[None, :] > window[:, None]) | (
        (window[None, :] == window[:, None]) & (head[None, :] < head[:, None])
    )
    rank = jnp.sum(ahead.astype(i32), axis=1)
    sorted_to = rank[None, :] == head[:, None]
    plan = jnp.sum(jnp.where(sorted_to[None], jnp.stack([head, window])[:, None, :], 0), axis=2).astype(i32)
    w_query, w_key, w_value, early_left, early_right = pl.pallas_call(
        functools.partial(early_kernel, pairs),
        out_shape=[jax.ShapeDtypeStruct((width, width), bf16)] * 3
        + [jax.ShapeDtypeStruct((n, nodes, half), f32) for n in (pairs, 3)],
        in_specs=[VMEM] * 3 + [ANY],
        out_specs=[VMEM] * 5,
        compiler_params=params(24),
        cost_estimate=cost(1 << 28, 4 << 20),
        name="early",
    )(w_qkv, here, here_other, plan)
    def sums(arrays, early, kept, name):
        count = early.shape[0]
        return pl.pallas_call(
            functools.partial(sums_kernel, len(arrays), kept),
            out_shape=[jax.ShapeDtypeStruct((nodes, half), f32 if n == kept else bf16) for n in range(count)],
            in_specs=[VMEM] * (len(arrays) + 1),
            out_specs=[VMEM] * count,
            compiler_params=params(24),
            cost_estimate=cost(2 * nodes * half * len(arrays) * count * cap, 2 << 20),
            name=name,
        )(*arrays, early)

    left, *parts = sums([even, even_other, odd, odd_other], early_left, 0, "left")
    parts = [lax.ppermute(part, NODES, chip_trade(p + 1)) for p, part in enumerate(parts)]
    to_even, to_odd, right = sums(cross, early_right, 2, "right")
    from_even = lax.ppermute(to_even, NODES, bands_trade(0))
    from_odd = lax.ppermute(to_odd, NODES, bands_trade(1))

    state, normed = pl.pallas_call(
        merge_kernel,
        out_shape=[
            jax.ShapeDtypeStruct((nodes, width), f32),
            jax.ShapeDtypeStruct((nodes, width), bf16),
        ],
        in_specs=[VMEM] * (pairs + 6),
        out_specs=[VMEM] * 2,
        compiler_params=params(24),
        cost_estimate=cost(2 * nodes * width * width, 2 << 20),
        name="merge",
    )(left, *parts, right, from_even, from_odd, mesh_rows, w_merge, gain_attn.reshape(1, width))

    def chips_trade(odd_pairs):
        route = []
        for g in range(devices):
            t = (g // 2 - odd_pairs ^ 1) + odd_pairs
            route.append((g, 2 * t + g % 2 if 0 <= 2 * t < devices else g ^ 1))
        return route

    side = lax.ppermute(normed, NODES, beside)
    even = lax.ppermute(normed, NODES, chips_trade(0))
    side, normed = lax.optimization_barrier((side, normed))
    odd = lax.ppermute(normed, NODES, chips_trade(1))

    extra = head_dim + 16
    query, near, top = pl.pallas_call(
        near_kernel,
        out_shape=[
            jax.ShapeDtypeStruct((HEADS, LANES, nodes), bf16),
            jax.ShapeDtypeStruct((HEADS, extra, nodes), f32),
            jax.ShapeDtypeStruct((HEADS, 8, nodes), f32),
        ],
        in_specs=[VMEM] * 5 + [SMEM],
        out_specs=[VMEM] * 3,
        scratch_shapes=[
            pltpu.VMEM((width // LANES, 2 * nodes, LANES), bf16),
            pltpu.VMEM((HEADS, extra, 2 * nodes), bf16),
            pltpu.VMEM((2 * nodes, nodes), i32),
        ],
        compiler_params=params(32),
        cost_estimate=cost(8 << 30, 4 << 20),
        name="near",
    )(normed, side, w_query, w_key, w_value, plan)

    def outer(by_pair, block, near, top):
        return pl.pallas_call(
            functools.partial(outer_kernel, by_pair),
            out_shape=[
                jax.ShapeDtypeStruct((HEADS, extra, nodes), f32),
                jax.ShapeDtypeStruct((HEADS, 8, nodes), f32),
            ],
            in_specs=[VMEM] * 3 + [ANY] + [VMEM] * 3,
            out_specs=[VMEM] * 2,
            scratch_shapes=[
                pltpu.VMEM((width // LANES, nodes, LANES), bf16),
                pltpu.VMEM((HEADS, extra, nodes), bf16),
                pltpu.VMEM((nodes, nodes), f32),
                pltpu.SMEM((2, HEADS), i32),
                pltpu.SemaphoreType.DMA(()),
            ],
            compiler_params=params(24),
            cost_estimate=cost(8 * nodes * width * width, 3 << 20),
            name="pair" if by_pair else "other",
        )(block, w_key, w_value, plan, query, near, top)

    odd, near, top = lax.optimization_barrier((odd, near, top))
    second = lax.ppermute(odd, NODES, beside)
    near, top = outer(False, odd, near, top)
    even, near, top = lax.optimization_barrier((even, near, top))
    first = lax.ppermute(even, NODES, beside)
    near, top = outer(True, even, near, top)

    return pl.pallas_call(
        far_kernel,
        out_shape=jax.ShapeDtypeStruct((nodes, width), bf16),
        in_specs=[VMEM] * 12,
        out_specs=VMEM,
        scratch_shapes=[
            pltpu.VMEM((width // LANES, nodes, LANES), bf16),
            pltpu.VMEM((HEADS, extra, nodes), bf16),
            pltpu.VMEM((nodes, nodes), f32),
            pltpu.VMEM((HEADS, head_dim, nodes), bf16),
        ],
        compiler_params=params(40),
        cost_estimate=cost(8 << 30, 8 << 20),
        name="far",
    )(
        first, second, w_key, w_value,
        query, near, top, state, w_out, gain_mlp.reshape(1, width), w_up, w_down,
    )


def solution(mesh):
    placed = (
        P(("groups", "band", "inner"), None),
        P(("groups", "band", "inner"), None),
        P(("groups", "band"), "inner", None, None, None),
        P(("groups", "band"), "inner", None, None, None),
        P(("groups", "band"), "inner", None, None),
        P(),
        P(),
        P(),
        P(),
        P("groups"),
        P(),
        P(),
        P(),
        P(),
    )
    return jax.shard_map(
        local,
        mesh=mesh,
        in_specs=placed,
        out_specs=P(("groups", "band", "inner"), None),
        check_vma=False,
    )
```

```python
import functools
import math

import jax
import jax.numpy as jnp
from jax import lax
from jax.experimental import pallas as pl
from jax.experimental.pallas import tpu as pltpu
from jax.sharding import PartitionSpec as P

HEADS = 16
WMAX = 512
LANES = 128
NEAR = 128
TILE = 16
CAP = 128
GRID_PARTS = 1
MOST = 56
GROUP = 4

norm_eps = 1e-05
NODES = ("band", "inner")
VMEM = pl.BlockSpec(memory_space=pltpu.VMEM)
SMEM = pl.BlockSpec(memory_space=pltpu.SMEM)
ANY = pl.BlockSpec(memory_space=pl.ANY)


def params(mib):
    return pltpu.CompilerParams(vmem_limit_bytes=mib * 1024 * 1024)


def dot(a, b):
    return jnp.dot(a, b, preferred_element_type=jnp.float32)


def dot_t(a, b):
    return lax.dot_general(a, b, (((1,), (1,)), ((), ())), preferred_element_type=jnp.float32)


def silu(values):
    half = 0.5 * values
    return half + half * jnp.tanh(half)


def layer_norm(values, gain):
    center = values - jnp.mean(values, axis=-1, keepdims=True)
    spread = jnp.mean(center * center, axis=-1, keepdims=True)
    return center * lax.rsqrt(spread + norm_eps) * gain


def band_offsets():
    ahead = lax.rem(lax.axis_index("band"), 2) * 2
    return 2 - ahead, ahead, 1


def slot_columns(source_ref, blocks):
    sources = jnp.concatenate([source_ref[0, 0, o, pl.ds(j, 1), :] for o, j in blocks], axis=0)
    return jnp.transpose(sources.astype(jnp.float32)).astype(jnp.int32)


def target_tile(target_ref, count_ref, blocks, lanes):
    cap = target_ref.shape[-1]
    slot = lax.broadcasted_iota(jnp.int32, (1, cap), 1)
    targets = [
        jnp.where(slot < count_ref[0, o, 0, j], target_ref[0, 0, o, pl.ds(j, 1), :], -1) for o, j in blocks
    ]
    targets.append(jnp.full((TILE - len(blocks), cap), -1, jnp.int32))
    tile = jnp.concatenate(targets, axis=0).astype(jnp.float32).astype(jnp.bfloat16)
    return jnp.concatenate([tile] * (lanes // cap), axis=1)


def message_kernel(pair_count, grid_ref, w_ref, source_in, target_in, count_in, *refs):
    count = 4 + 2 * pair_count
    out_refs, out_vmems = refs[:count], refs[count : 2 * count]
    source_ref, target_ref, count_ref, grid_vmem, w_vmem, message_ref, pick_ref, in_sems, edge_sems, out_sems = refs[2 * count :]
    rows = grid_ref.shape[0]
    cap = source_ref.shape[-1]
    half = w_ref.shape[1] // 2
    part = rows // GRID_PARTS
    fetches = [pltpu.make_async_copy(w_ref, w_vmem, in_sems.at[GRID_PARTS])]
    for k in range(GRID_PARTS):
        span = pl.ds(k * part, part)
        fetches.append(pltpu.make_async_copy(grid_ref.at[span], grid_vmem.at[span], in_sems.at[k]))
    edges = ((source_in, source_ref), (target_in, target_ref), (count_in, count_ref))
    edge_fetches = [pltpu.make_async_copy(a, b, edge_sems.at[n]) for n, (a, b) in enumerate(edges)]
    for fetch in edge_fetches + fetches:
        fetch.start()
    for fetch in edge_fetches:
        fetch.wait()
    inner = lax.axis_index("inner")
    offsets = band_offsets()
    keys = [(t, p, k) for k in range(2) for t in range(3) for p in range(pair_count)]
    place = {(t, p, k): (offsets[t], inner ^ (2 * p + k)) for t, p, k in keys}
    by_slot = slot_columns(source_ref, [place[key] for key in keys])
    left, right = slice(0, half), slice(half, 2 * half)
    runs = [[([(t, p, k) for p in range(pair_count)], left)] for t in range(2) for k in range(2)]
    runs += [[([(t, p, k) for t in range(3)], right)] for p in range(1, pair_count) for k in range(2)]
    runs += [
        [([(2, p, k) for p in range(pair_count)], left), ([(t, 0, k) for t in range(3)], right)] for k in range(2)
    ]
    for out_vmem, parts in zip(out_vmems, runs):
        start = 0
        for chosen, _ in parts:
            start += len(chosen) * cap
            out_vmem[start : start + TILE, :] = target_tile(target_ref, count_ref, [place[key] for key in chosen], half)
            start += TILE
    row = lax.broadcasted_iota(jnp.int32, (cap, rows), 1)
    for m in range(len(keys)):
        pick_ref[m * cap : (m + 1) * cap, :] = jnp.where(row == by_slot[:, m : m + 1], 1.0, 0.0).astype(jnp.bfloat16)
    fetches[0].wait()
    for k in range(GRID_PARTS):
        span = pl.ds(k * part, part)
        fetches[k + 1].wait()
        message_ref[span] = silu(dot(grid_vmem[span], w_vmem[...])).astype(jnp.bfloat16)
    sends = []
    per_core = len(keys) // 2
    for k in range(2):
        first = k * per_core
        taken = dot(pick_ref[first * cap : (first + per_core) * cap, :], message_ref[...]).astype(jnp.bfloat16)
        for n in reversed(range(count)):
            start = 0
            if runs[n][0][0][0][2] != k:
                continue
            for chosen, lanes in runs[n]:
                for key in chosen:
                    m = keys.index(key) - first
                    out_vmems[n][start : start + cap, :] = taken[m * cap : (m + 1) * cap, lanes]
                    start += cap
                start += TILE
            send = pltpu.make_async_copy(out_vmems[n], out_refs[n], out_sems.at[n])
            send.start()
            sends.append(send)
    for send in sends:
        send.wait()


def node_sums(arrays, nodes):
    count = arrays[0][2]
    cap = CAP
    node = lax.broadcasted_iota(jnp.int32, (nodes, cap), 0)
    targets = [
        ref[start + count * cap : start + count * cap + TILE, 0:cap].astype(jnp.float32).astype(jnp.int32)
        for ref, start, _ in arrays
    ]
    for n in range(count):
        hits = [jnp.where(node == t[n : n + 1], 1.0, 0.0).astype(jnp.bfloat16) for t in targets]
        rows = [ref[start + n * cap : start + (n + 1) * cap, :] for ref, start, _ in arrays]
        yield n, dot(jnp.concatenate(hits, axis=1), jnp.concatenate(rows, axis=0))


def early_kernel(pair_count, w_ref, own_ref, other_ref, plan_ref, query_ref, key_ref, value_ref, left_ref, right_ref):
    width = w_ref.shape[0]
    head_dim = width // HEADS
    span = 3 * LANES
    def pick(c, along):
        shape = (LANES, span) if along else (span, LANES)
        to = lax.broadcasted_iota(jnp.int32, shape, 1 - along)
        column = lax.broadcasted_iota(jnp.int32, shape, along)
        wanted = to // head_dim * (3 * head_dim) + to % head_dim + c * head_dim
        return jnp.where(column == wanted, 1.0, 0.0).astype(jnp.bfloat16)

    for g in range(width // LANES):
        columns = w_ref[:, g * span : (g + 1) * span]
        part = slice(g * LANES, (g + 1) * LANES)
        query_ref[part, :] = dot_t(pick(0, 1), columns).astype(jnp.bfloat16)
        key_ref[:, part] = dot(columns, pick(1, 0)).astype(jnp.bfloat16)
        value_ref[part, :] = dot_t(pick(2, 1), columns).astype(jnp.bfloat16)
    start = 0
    for sum_ref in (left_ref, right_ref):
        count, nodes, _ = sum_ref.shape
        for n, total in node_sums([(own_ref, start, count), (other_ref, start, count)], nodes):
            sum_ref[n] = total
        start += count * CAP + TILE


def sums_kernel(array_count, kept, *refs):
    row_refs, early_ref, out_refs = refs[:array_count], refs[array_count], refs[array_count + 1 :]
    count, nodes, _ = early_ref.shape
    for n, total in node_sums([(r, 0, count) for r in row_refs], nodes):
        total = total + early_ref[n]
        out_refs[n][...] = total if n == kept else total.astype(jnp.bfloat16)


def merge_kernel(*refs):
    *part_refs, right_ref, even_ref, odd_ref, mesh_ref, w_ref, gain_ref, state_ref, normed_ref = refs
    left = functools.reduce(jnp.add, [r[...].astype(jnp.float32) for r in part_refs])
    right = right_ref[...] + even_ref[...].astype(jnp.float32) + odd_ref[...].astype(jnp.float32)
    total = jnp.concatenate([left, right], axis=1).astype(jnp.bfloat16)
    state = mesh_ref[...].astype(jnp.float32) + dot(total, w_ref[...])
    state_ref[...] = state
    normed_ref[...] = layer_norm(state, gain_ref[...]).astype(jnp.bfloat16)


def project_keys(rows, wk_ref, wv_ref, key_ref, value_ref, start):
    count = rows.shape[0]
    groups = key_ref.shape[0]
    heads = value_ref.shape[0]
    keys = dot(rows, wk_ref[...]).astype(jnp.bfloat16)
    for g in range(groups):
        key_ref[g, start : start + count, :] = keys[:, g * LANES : (g + 1) * LANES]
    values = dot_t(wv_ref[...], rows).astype(jnp.bfloat16)
    value_ref[:, 0 : values.shape[0] // heads, start : start + count] = values.reshape(
        heads, -1, count
    )


def near_kernel(
    own_ref, side_ref, wq_ref, wk_ref, wv_ref, plan_ref,
    query_ref, sums_ref, top_ref,
    key_ref, value_ref, gap_ref,
):
    nodes, width = own_ref.shape
    head_dim = width // HEADS
    per_group = LANES // head_dim
    odd = lax.rem(lax.axis_index("inner"), 2)
    side = 1 - 2 * odd
    first = odd * (nodes - NEAR)
    second = (1 - odd) * NEAR
    scale = head_dim ** (-0.5) / math.log(2.0)

    queries = dot_t(wq_ref[...], own_ref[...]).astype(jnp.bfloat16)
    part = lax.broadcasted_iota(jnp.int32, (LANES, nodes), 0) // head_dim
    for h in range(HEADS):
        g = h // per_group
        lanes = queries[g * LANES : (g + 1) * LANES]
        query_ref[h] = jnp.where(part == h % per_group, lanes, jnp.zeros_like(lanes))
    value_ref[:, head_dim:, :] = jnp.ones_like(value_ref[:, head_dim:, :])
    project_keys(own_ref[...], wk_ref, wv_ref, key_ref, value_ref, 0)
    project_keys(side_ref[pl.ds(pl.multiple_of(first, NEAR), NEAR), :], wk_ref, wv_ref, key_ref, value_ref, nodes)
    project_keys(
        side_ref[pl.ds(pl.multiple_of(second, NEAR), NEAR), :], wk_ref, wv_ref, key_ref, value_ref, nodes + NEAR
    )
    lag = lax.broadcasted_iota(jnp.int32, (nodes, nodes), 0) - lax.broadcasted_iota(
        jnp.int32, (nodes, nodes), 1
    )
    gap_ref[0:nodes] = jnp.abs(lag)
    gap_ref[nodes : nodes + NEAR] = jnp.abs(lag[0:NEAR] + (side * nodes + first))
    gap_ref[nodes + NEAR : 2 * nodes] = jnp.abs(lag[0:NEAR] + (side * nodes + second))

    def attend(heads, windows, rows):
        scores = [dot(key_ref[h // per_group, 0:rows, :], query_ref[h]) for h in heads]
        scores = [
            jnp.where(gap_ref[0:rows] <= w, x, -1e30) for w, x in zip(windows, scores)
        ]
        tops = [jnp.max(x, axis=0, keepdims=True) for x in scores]
        expos = [jnp.exp2((x - top) * scale).astype(jnp.bfloat16) for x, top in zip(scores, tops)]
        for h, w, top, expo in zip(heads, windows, tops, expos):
            sums_ref[h] = dot(value_ref[h, :, 0:rows], expo)
            top_ref[h, 0:1] = top
            top_ref[h, 1:2] = jnp.full((1, nodes), w.astype(jnp.float32))

    def together(i, carry):
        heads = [plan_ref[0, GROUP * i + k] for k in range(GROUP)]
        windows = [plan_ref[1, GROUP * i + k] for k in range(GROUP)]
        widest = windows[0]

        @pl.when(widest <= NEAR)
        def _():
            attend(heads, windows, nodes + NEAR)

        @pl.when(widest > NEAR)
        def _():
            attend(heads, windows, 2 * nodes)

        return carry

    lax.fori_loop(0, HEADS // GROUP, together, 0)


def gaps(device, start, rows, nodes):
    total = lax.axis_size("band") * lax.axis_size("inner")
    there = lax.axis_index("band") * lax.axis_size("inner") + lax.axis_index("inner") + device
    lag = lax.broadcasted_iota(jnp.int32, (rows, nodes), 0) - lax.broadcasted_iota(jnp.int32, (rows, nodes), 1)
    gap = jnp.where((there >= 0) & (there < total), jnp.abs(lag + (device * nodes + start)), 1 << 20)
    return gap.astype(jnp.float32)


def extend(heads, keys, values, gap_ref, query_ref, sums_ref, top_ref, scale):
    scores = [dot(k, query_ref[h]) for h, k in zip(heads, keys)]
    scores = [jnp.where(gap_ref[...] <= top_ref[h, 1:2, :], x, -1e30) for h, x in zip(heads, scores)]
    olds = [top_ref[h, 0:1, :] for h in heads]
    tops = [jnp.maximum(old, jnp.max(x, axis=0, keepdims=True)) for old, x in zip(olds, scores)]
    expos = [jnp.exp2((x - top) * scale).astype(jnp.bfloat16) for x, top in zip(scores, tops)]
    for h, v, old, top, expo in zip(heads, values, olds, tops, expos):
        yield h, sums_ref[h] * jnp.exp2((old - top) * scale) + dot(v, expo), top


def outer_kernel(
    by_pair, block_ref, wk_ref, wv_ref, plan_in, query_ref, sums_ref, top_ref,
    sums_out, top_out,
    key_ref, value_ref, gap_ref, plan_ref, sem,
):
    fetch = pltpu.make_async_copy(plan_in, plan_ref, sem)
    fetch.start()
    nodes, width = block_ref.shape
    head_dim = width // HEADS
    per_group = LANES // head_dim
    far = 2 - 4 * lax.rem(lax.axis_index("inner") // 2, 2)
    scale = head_dim ** (-0.5) / math.log(2.0)
    value_ref[:, head_dim:, :] = jnp.ones_like(value_ref[:, head_dim:, :])
    project_keys(block_ref[...], wk_ref, wv_ref, key_ref, value_ref, 0)
    gap_ref[...] = gaps(far if by_pair else -far, 0, nodes, nodes)
    fetch.wait()

    def wide(n):
        return plan_ref[1, n] > nodes

    def reach(first, last):
        heads = [plan_ref[0, n] for n in range(first, last)]
        keys, values = [key_ref[h // per_group] for h in heads], [value_ref[h] for h in heads]
        for h, sums, top in extend(
            heads, keys, values, gap_ref, query_ref, sums_ref, top_ref, scale
        ):
            sums_out[h] = sums
            top_out[h, 0:1] = top
            top_out[h, 1:2] = top_ref[h, 1:2]

    def leave(first, last):
        for n in range(first, last):
            h = plan_ref[0, n]
            sums_out[h] = sums_ref[h]
            top_out[h, 0:2] = top_ref[h, 0:2]

    @pl.when(wide(GROUP))
    def _():
        reach(0, 2 * GROUP)

    @pl.when(jnp.logical_not(wide(GROUP)))
    def _():
        reach(0, GROUP)
        leave(GROUP, 2 * GROUP)

    for first in range(2 * GROUP, HEADS, GROUP):
        pl.when(wide(first))(functools.partial(reach, first, first + GROUP))
        pl.when(jnp.logical_not(wide(first)))(functools.partial(leave, first, first + GROUP))


def far_kernel(
    first_ref, second_ref, wk_ref, wv_ref, query_ref, sums_ref, top_ref,
    state_ref, w_out_ref, gain_ref, up_ref, down_ref,
    out_ref,
    key_ref, value_ref, gap_ref, attended_ref,
):
    nodes, width = first_ref.shape
    head_dim = width // HEADS
    per_group = LANES // head_dim
    inner = lax.axis_index("inner")
    odd = lax.rem(inner, 2)
    scale = head_dim ** (-0.5) / math.log(2.0)
    value_ref[:, head_dim:, :] = jnp.ones_like(value_ref[:, head_dim:, :])
    by_even = odd == lax.rem(inner // 2 + 1, 2)
    project_keys(jnp.where(by_even, first_ref[...], second_ref[...]), wk_ref, wv_ref, key_ref, value_ref, 0)
    gap_ref[...] = gaps(2 * odd - 1, 0, nodes, nodes)
    heads = range(HEADS)
    keys, values = [key_ref[h // per_group] for h in heads], [value_ref[h] for h in heads]
    for h, sums, _ in extend(
        heads, keys, values, gap_ref, query_ref, sums_ref, top_ref, scale
    ):
        attended_ref[h] = (sums[0:head_dim] / sums[head_dim : head_dim + 1]).astype(jnp.bfloat16)

    attended = attended_ref[...].reshape(width, nodes)
    mixed = lax.dot_general(
        attended, w_out_ref[...], (((0,), (0,)), ((), ())), preferred_element_type=jnp.float32
    )
    total = state_ref[...] + mixed
    normed = layer_norm(total, gain_ref[...]).astype(jnp.bfloat16)
    hidden = silu(dot(normed, up_ref[...])).astype(jnp.bfloat16)
    total = total + dot(hidden, down_ref[...])
    out_ref[...] = total.astype(jnp.bfloat16)


def cost(flops, size):
    return pl.CostEstimate(flops=flops, bytes_accessed=size, transcendentals=0)


def local(
    grid_rows,
    mesh_rows,
    edge_source,
    edge_target,
    edge_count,
    w_message,
    w_merge,
    gain_attn,
    w_qkv,
    window,
    w_out,
    gain_mlp,
    w_up,
    w_down,
):
    bands = lax.axis_size("band")
    inners = lax.axis_size("inner")
    devices = bands * inners
    grid_dev = grid_rows.shape[0]
    nodes, width = mesh_rows.shape
    cap = edge_source.shape[-1]
    head_dim = width // HEADS
    pairs = inners // 2
    half = width // 2
    f32, bf16, i32 = jnp.float32, jnp.bfloat16, jnp.int32
    edges = (edge_source, edge_target, jnp.transpose(edge_count, (0, 2, 1, 3)))

    def rows_of(*blocks):
        return jax.ShapeDtypeStruct((sum(n * cap + TILE for n in blocks), half), bf16)

    outgoing = [rows_of(pairs)] * 4 + [rows_of(3)] * (2 * pairs - 2) + [rows_of(pairs, 3)] * 2
    even, even_other, odd, odd_other, *cross, here, here_other = pl.pallas_call(
        functools.partial(message_kernel, pairs),
        out_shape=outgoing,
        in_specs=[ANY] * 5,
        out_specs=[ANY] * len(outgoing),
        scratch_shapes=[pltpu.VMEM(a.shape, bf16) for a in outgoing]
        + [
            pltpu.VMEM(edges[0].shape, i32),
            pltpu.VMEM(edges[1].shape, i32),
            pltpu.SMEM(edges[2].shape, i32),
            pltpu.VMEM(grid_rows.shape, bf16),
            pltpu.VMEM(w_message.shape, bf16),
            pltpu.VMEM((grid_dev, width), bf16),
            pltpu.VMEM((3 * inners * cap, grid_dev), bf16),
            pltpu.SemaphoreType.DMA((GRID_PARTS + 1,)),
            pltpu.SemaphoreType.DMA((3,)),
            pltpu.SemaphoreType.DMA((len(outgoing),)),
        ],
        compiler_params=params(MOST),
        cost_estimate=cost(2 * grid_dev * width * (width + 3 * inners * cap), 4 << 20),
        name="messages",
    )(grid_rows, w_message, *edges)
    beside = [(g, g ^ 1) for g in range(devices)]

    def bands_trade(odd_pairs, k=0):
        route = []
        for g in range(devices):
            b = g // inners
            t = (b - odd_pairs ^ 1) + odd_pairs
            route.append((g, t * inners + (g % inners ^ k) if 0 <= t < bands else g ^ 1))
        return route

    def chip_trade(p, k=0):
        return [(g, g ^ (2 * p + k)) for g in range(devices)]

    here_other = lax.ppermute(here_other, NODES, beside)
    cross[0::2] = [lax.ppermute(c, NODES, chip_trade(p + 1)) for p, c in enumerate(cross[0::2])]
    even = lax.ppermute(even, NODES, bands_trade(0))
    odd = lax.ppermute(odd, NODES, bands_trade(1))
    here_other, even_other, odd_other, *cross[1::2] = lax.optimization_barrier(
        (here_other, even_other, odd_other, *cross[1::2])
    )
    cross[1::2] = [lax.ppermute(c, NODES, chip_trade(p + 1, 1)) for p, c in enumerate(cross[1::2])]
    even_other = lax.ppermute(even_other, NODES, bands_trade(0, 1))
    odd_other = lax.ppermute(odd_other, NODES, bands_trade(1, 1))

    w_qkv, window, here = lax.optimization_barrier((w_qkv, window, here))
    head = jnp.arange(HEADS, dtype=i32)
    ahead = (window[None, :] > window[:, None]) | (
        (window[None, :] == window[:, None]) & (head[None, :] < head[:, None])
    )
    rank = jnp.sum(ahead.astype(i32), axis=1)
    sorted_to = rank[None, :] == head[:, None]
    plan = jnp.sum(jnp.where(sorted_to[None], jnp.stack([head, window])[:, None, :], 0), axis=2).astype(i32)
    w_query, w_key, w_value, early_left, early_right = pl.pallas_call(
        functools.partial(early_kernel, pairs),
        out_shape=[jax.ShapeDtypeStruct((width, width), bf16)] * 3
        + [jax.ShapeDtypeStruct((n, nodes, half), f32) for n in (pairs, 3)],
        in_specs=[VMEM] * 3 + [ANY],
        out_specs=[VMEM] * 5,
        compiler_params=params(24),
        cost_estimate=cost(1 << 28, 4 << 20),
        name="early",
    )(w_qkv, here, here_other, plan)
    def sums(arrays, early, kept, name):
        count = early.shape[0]
        return pl.pallas_call(
            functools.partial(sums_kernel, len(arrays), kept),
            out_shape=[jax.ShapeDtypeStruct((nodes, half), f32 if n == kept else bf16) for n in range(count)],
            in_specs=[VMEM] * (len(arrays) + 1),
            out_specs=[VMEM] * count,
            compiler_params=params(24),
            cost_estimate=cost(2 * nodes * half * len(arrays) * count * cap, 2 << 20),
            name=name,
        )(*arrays, early)

    left, *parts = sums([even, even_other, odd, odd_other], early_left, 0, "left")
    parts = [lax.ppermute(part, NODES, chip_trade(p + 1)) for p, part in enumerate(parts)]
    to_even, to_odd, right = sums(cross, early_right, 2, "right")
    from_even = lax.ppermute(to_even, NODES, bands_trade(0))
    from_odd = lax.ppermute(to_odd, NODES, bands_trade(1))

    state, normed = pl.pallas_call(
        merge_kernel,
        out_shape=[
            jax.ShapeDtypeStruct((nodes, width), f32),
            jax.ShapeDtypeStruct((nodes, width), bf16),
        ],
        in_specs=[VMEM] * (pairs + 6),
        out_specs=[VMEM] * 2,
        compiler_params=params(24),
        cost_estimate=cost(2 * nodes * width * width, 2 << 20),
        name="merge",
    )(left, *parts, right, from_even, from_odd, mesh_rows, w_merge, gain_attn.reshape(1, width))

    def chips_trade(odd_pairs):
        route = []
        for g in range(devices):
            t = (g // 2 - odd_pairs ^ 1) + odd_pairs
            route.append((g, 2 * t + g % 2 if 0 <= 2 * t < devices else g ^ 1))
        return route

    side = lax.ppermute(normed, NODES, beside)
    even = lax.ppermute(normed, NODES, chips_trade(0))
    odd = lax.ppermute(normed, NODES, chips_trade(1))

    extra = head_dim + 16
    query, near, top = pl.pallas_call(
        near_kernel,
        out_shape=[
            jax.ShapeDtypeStruct((HEADS, LANES, nodes), bf16),
            jax.ShapeDtypeStruct((HEADS, extra, nodes), f32),
            jax.ShapeDtypeStruct((HEADS, 8, nodes), f32),
        ],
        in_specs=[VMEM] * 5 + [SMEM],
        out_specs=[VMEM] * 3,
        scratch_shapes=[
            pltpu.VMEM((width // LANES, 2 * nodes, LANES), bf16),
            pltpu.VMEM((HEADS, extra, 2 * nodes), bf16),
            pltpu.VMEM((2 * nodes, nodes), i32),
        ],
        compiler_params=params(32),
        cost_estimate=cost(8 << 30, 4 << 20),
        name="near",
    )(normed, side, w_query, w_key, w_value, plan)

    def outer(by_pair, block, near, top):
        return pl.pallas_call(
            functools.partial(outer_kernel, by_pair),
            out_shape=[
                jax.ShapeDtypeStruct((HEADS, extra, nodes), f32),
                jax.ShapeDtypeStruct((HEADS, 8, nodes), f32),
            ],
            in_specs=[VMEM] * 3 + [ANY] + [VMEM] * 3,
            out_specs=[VMEM] * 2,
            scratch_shapes=[
                pltpu.VMEM((width // LANES, nodes, LANES), bf16),
                pltpu.VMEM((HEADS, extra, nodes), bf16),
                pltpu.VMEM((nodes, nodes), f32),
                pltpu.SMEM((2, HEADS), i32),
                pltpu.SemaphoreType.DMA(()),
            ],
            compiler_params=params(24),
            cost_estimate=cost(8 * nodes * width * width, 3 << 20),
            name="pair" if by_pair else "other",
        )(block, w_key, w_value, plan, query, near, top)

    odd, near, top = lax.optimization_barrier((odd, near, top))
    second = lax.ppermute(odd, NODES, beside)
    near, top = outer(False, odd, near, top)
    even, near, top = lax.optimization_barrier((even, near, top))
    first = lax.ppermute(even, NODES, beside)
    near, top = outer(True, even, near, top)

    return pl.pallas_call(
        far_kernel,
        out_shape=jax.ShapeDtypeStruct((nodes, width), bf16),
        in_specs=[VMEM] * 12,
        out_specs=VMEM,
        scratch_shapes=[
            pltpu.VMEM((width // LANES, nodes, LANES), bf16),
            pltpu.VMEM((HEADS, extra, nodes), bf16),
            pltpu.VMEM((nodes, nodes), f32),
            pltpu.VMEM((HEADS, head_dim, nodes), bf16),
        ],
        compiler_params=params(40),
        cost_estimate=cost(8 << 30, 8 << 20),
        name="far",
    )(
        first, second, w_key, w_value,
        query, near, top, state, w_out, gain_mlp.reshape(1, width), w_up, w_down,
    )


def solution(mesh):
    placed = (
        P(("groups", "band", "inner"), None),
        P(("groups", "band", "inner"), None),
        P(("groups", "band"), "inner", None, None, None),
        P(("groups", "band"), "inner", None, None, None),
        P(("groups", "band"), "inner", None, None),
        P(),
        P(),
        P(),
        P(),
        P("groups"),
        P(),
        P(),
        P(),
        P(),
    )
    return jax.shard_map(
        local,
        mesh=mesh,
        in_specs=placed,
        out_specs=P(("groups", "band", "inner"), None),
        check_vma=False,
    )
```

```python
import functools
import math

import jax
import jax.numpy as jnp
from jax import lax
from jax.experimental import pallas as pl
from jax.experimental.pallas import tpu as pltpu
from jax.sharding import PartitionSpec as P

HEADS = 16
WMAX = 512
LANES = 128
NEAR = 128
TILE = 16
CAP = 128
GRID_PARTS = 1
MOST = 56
GROUP = 4

norm_eps = 1e-05
NODES = ("band", "inner")
VMEM = pl.BlockSpec(memory_space=pltpu.VMEM)
SMEM = pl.BlockSpec(memory_space=pltpu.SMEM)
ANY = pl.BlockSpec(memory_space=pl.ANY)


def params(mib):
    return pltpu.CompilerParams(vmem_limit_bytes=mib * 1024 * 1024)


def dot(a, b):
    return jnp.dot(a, b, preferred_element_type=jnp.float32)


def dot_t(a, b):
    return lax.dot_general(a, b, (((1,), (1,)), ((), ())), preferred_element_type=jnp.float32)


def silu(values):
    half = 0.5 * values
    return half + half * jnp.tanh(half)


def layer_norm(values, gain):
    center = values - jnp.mean(values, axis=-1, keepdims=True)
    spread = jnp.mean(center * center, axis=-1, keepdims=True)
    return center * lax.rsqrt(spread + norm_eps) * gain


def band_offsets():
    ahead = lax.rem(lax.axis_index("band"), 2) * 2
    return 2 - ahead, ahead, 1


def slot_columns(source_ref, blocks):
    sources = jnp.concatenate([source_ref[0, 0, o, pl.ds(j, 1), :] for o, j in blocks], axis=0)
    return jnp.transpose(sources.astype(jnp.float32)).astype(jnp.int32)


def target_tile(target_ref, count_ref, blocks, lanes):
    cap = target_ref.shape[-1]
    slot = lax.broadcasted_iota(jnp.int32, (1, cap), 1)
    targets = [
        jnp.where(slot < count_ref[0, o, 0, j], target_ref[0, 0, o, pl.ds(j, 1), :], -1) for o, j in blocks
    ]
    targets.append(jnp.full((TILE - len(blocks), cap), -1, jnp.int32))
    tile = jnp.concatenate(targets, axis=0).astype(jnp.float32).astype(jnp.bfloat16)
    return jnp.concatenate([tile] * (lanes // cap), axis=1)


def message_kernel(pair_count, grid_ref, w_ref, source_in, target_in, count_in, *refs):
    count = 4 + 2 * pair_count
    out_refs, out_vmems = refs[:count], refs[count : 2 * count]
    source_ref, target_ref, count_ref, grid_vmem, w_vmem, message_ref, pick_ref, in_sems, edge_sems, out_sems = refs[2 * count :]
    rows = grid_ref.shape[0]
    cap = source_ref.shape[-1]
    half = w_ref.shape[1] // 2
    part = rows // GRID_PARTS
    fetches = [pltpu.make_async_copy(w_ref, w_vmem, in_sems.at[GRID_PARTS])]
    for k in range(GRID_PARTS):
        span = pl.ds(k * part, part)
        fetches.append(pltpu.make_async_copy(grid_ref.at[span], grid_vmem.at[span], in_sems.at[k]))
    edges = ((source_in, source_ref), (target_in, target_ref), (count_in, count_ref))
    edge_fetches = [pltpu.make_async_copy(a, b, edge_sems.at[n]) for n, (a, b) in enumerate(edges)]
    for fetch in edge_fetches + fetches:
        fetch.start()
    for fetch in edge_fetches:
        fetch.wait()
    inner = lax.axis_index("inner")
    offsets = band_offsets()
    keys = [(t, p, k) for k in range(2) for t in range(3) for p in range(pair_count)]
    place = {(t, p, k): (offsets[t], inner ^ (2 * p + k)) for t, p, k in keys}
    by_slot = slot_columns(source_ref, [place[key] for key in keys])
    left, right = slice(0, half), slice(half, 2 * half)
    runs = [[([(t, p, k) for p in range(pair_count)], left)] for t in range(2) for k in range(2)]
    runs += [[([(t, p, k) for t in range(3)], right)] for p in range(1, pair_count) for k in range(2)]
    runs += [
        [([(2, p, k) for p in range(pair_count)], left), ([(t, 0, k) for t in range(3)], right)] for k in range(2)
    ]
    for out_vmem, parts in zip(out_vmems, runs):
        start = 0
        for chosen, _ in parts:
            start += len(chosen) * cap
            out_vmem[start : start + TILE, :] = target_tile(target_ref, count_ref, [place[key] for key in chosen], half)
            start += TILE
    row = lax.broadcasted_iota(jnp.int32, (cap, rows), 1)
    for m in range(len(keys)):
        pick_ref[m * cap : (m + 1) * cap, :] = jnp.where(row == by_slot[:, m : m + 1], 1.0, 0.0).astype(jnp.bfloat16)
    fetches[0].wait()
    for k in range(GRID_PARTS):
        span = pl.ds(k * part, part)
        fetches[k + 1].wait()
        message_ref[span] = silu(dot(grid_vmem[span], w_vmem[...])).astype(jnp.bfloat16)
    sends = []
    per_core = len(keys) // 2
    for k in range(2):
        first = k * per_core
        taken = dot(pick_ref[first * cap : (first + per_core) * cap, :], message_ref[...]).astype(jnp.bfloat16)
        for n in reversed(range(count)):
            start = 0
            if runs[n][0][0][0][2] != k:
                continue
            for chosen, lanes in runs[n]:
                for key in chosen:
                    m = keys.index(key) - first
                    out_vmems[n][start : start + cap, :] = taken[m * cap : (m + 1) * cap, lanes]
                    start += cap
                start += TILE
            send = pltpu.make_async_copy(out_vmems[n], out_refs[n], out_sems.at[n])
            send.start()
            sends.append(send)
    for send in sends:
        send.wait()


def node_sums(arrays, nodes):
    count = arrays[0][2]
    cap = CAP
    node = lax.broadcasted_iota(jnp.int32, (nodes, cap), 0)
    targets = [
        ref[start + count * cap : start + count * cap + TILE, 0:cap].astype(jnp.float32).astype(jnp.int32)
        for ref, start, _ in arrays
    ]
    for n in range(count):
        hits = [jnp.where(node == t[n : n + 1], 1.0, 0.0).astype(jnp.bfloat16) for t in targets]
        rows = [ref[start + n * cap : start + (n + 1) * cap, :] for ref, start, _ in arrays]
        yield n, dot(jnp.concatenate(hits, axis=1), jnp.concatenate(rows, axis=0))


def early_kernel(pair_count, w_ref, own_ref, other_ref, plan_ref, query_ref, key_ref, value_ref, left_ref, right_ref):
    width = w_ref.shape[0]
    head_dim = width // HEADS
    span = 3 * LANES
    def pick(c, along):
        shape = (LANES, span) if along else (span, LANES)
        to = lax.broadcasted_iota(jnp.int32, shape, 1 - along)
        column = lax.broadcasted_iota(jnp.int32, shape, along)
        wanted = to // head_dim * (3 * head_dim) + to % head_dim + c * head_dim
        return jnp.where(column == wanted, 1.0, 0.0).astype(jnp.bfloat16)

    for g in range(width // LANES):
        columns = w_ref[:, g * span : (g + 1) * span]
        part = slice(g * LANES, (g + 1) * LANES)
        query_ref[part, :] = dot_t(pick(0, 1), columns).astype(jnp.bfloat16)
        key_ref[:, part] = dot(columns, pick(1, 0)).astype(jnp.bfloat16)
        value_ref[part, :] = dot_t(pick(2, 1), columns).astype(jnp.bfloat16)
    start = 0
    for sum_ref in (left_ref, right_ref):
        count, nodes, _ = sum_ref.shape
        for n, total in node_sums([(own_ref, start, count), (other_ref, start, count)], nodes):
            sum_ref[n] = total
        start += count * CAP + TILE


def sums_kernel(array_count, kept, *refs):
    row_refs, early_ref, out_refs = refs[:array_count], refs[array_count], refs[array_count + 1 :]
    count, nodes, _ = early_ref.shape
    for n, total in node_sums([(r, 0, count) for r in row_refs], nodes):
        total = total + early_ref[n]
        out_refs[n][...] = total if n == kept else total.astype(jnp.bfloat16)


def merge_kernel(*refs):
    *part_refs, right_ref, even_ref, odd_ref, mesh_ref, w_ref, gain_ref, state_ref, normed_ref = refs
    left = functools.reduce(jnp.add, [r[...].astype(jnp.float32) for r in part_refs])
    right = right_ref[...] + even_ref[...].astype(jnp.float32) + odd_ref[...].astype(jnp.float32)
    total = jnp.concatenate([left, right], axis=1).astype(jnp.bfloat16)
    state = mesh_ref[...].astype(jnp.float32) + dot(total, w_ref[...])
    state_ref[...] = state
    normed_ref[...] = layer_norm(state, gain_ref[...]).astype(jnp.bfloat16)


def project_keys(rows, wk_ref, wv_ref, key_ref, value_ref, start):
    count = rows.shape[0]
    groups = key_ref.shape[0]
    heads = value_ref.shape[0]
    keys = dot(rows, wk_ref[...]).astype(jnp.bfloat16)
    for g in range(groups):
        key_ref[g, start : start + count, :] = keys[:, g * LANES : (g + 1) * LANES]
    values = dot_t(wv_ref[...], rows).astype(jnp.bfloat16)
    value_ref[:, 0 : values.shape[0] // heads, start : start + count] = values.reshape(
        heads, -1, count
    )


def near_kernel(
    own_ref, side_ref, wq_ref, wk_ref, wv_ref, plan_ref,
    query_ref, sums_ref, top_ref,
    key_ref, value_ref, gap_ref,
):
    nodes, width = own_ref.shape
    head_dim = width // HEADS
    per_group = LANES // head_dim
    odd = lax.rem(lax.axis_index("inner"), 2)
    side = 1 - 2 * odd
    first = odd * (nodes - NEAR)
    second = (1 - odd) * NEAR
    scale = head_dim ** (-0.5) / math.log(2.0)

    queries = dot_t(wq_ref[...], own_ref[...]).astype(jnp.bfloat16)
    part = lax.broadcasted_iota(jnp.int32, (LANES, nodes), 0) // head_dim
    for h in range(HEADS):
        g = h // per_group
        lanes = queries[g * LANES : (g + 1) * LANES]
        query_ref[h] = jnp.where(part == h % per_group, lanes, jnp.zeros_like(lanes))
    value_ref[:, head_dim:, :] = jnp.ones_like(value_ref[:, head_dim:, :])
    project_keys(own_ref[...], wk_ref, wv_ref, key_ref, value_ref, 0)
    project_keys(side_ref[pl.ds(pl.multiple_of(first, NEAR), NEAR), :], wk_ref, wv_ref, key_ref, value_ref, nodes)
    project_keys(
        side_ref[pl.ds(pl.multiple_of(second, NEAR), NEAR), :], wk_ref, wv_ref, key_ref, value_ref, nodes + NEAR
    )
    lag = lax.broadcasted_iota(jnp.int32, (nodes, nodes), 0) - lax.broadcasted_iota(
        jnp.int32, (nodes, nodes), 1
    )
    gap_ref[0:nodes] = jnp.abs(lag)
    gap_ref[nodes : nodes + NEAR] = jnp.abs(lag[0:NEAR] + (side * nodes + first))
    gap_ref[nodes + NEAR : 2 * nodes] = jnp.abs(lag[0:NEAR] + (side * nodes + second))

    def attend(heads, windows, rows):
        scores = [dot(key_ref[h // per_group, 0:rows, :], query_ref[h]) for h in heads]
        scores = [
            jnp.where(gap_ref[0:rows] <= w, x, -1e30) for w, x in zip(windows, scores)
        ]
        tops = [jnp.max(x, axis=0, keepdims=True) for x in scores]
        expos = [jnp.exp2((x - top) * scale).astype(jnp.bfloat16) for x, top in zip(scores, tops)]
        for h, w, top, expo in zip(heads, windows, tops, expos):
            sums_ref[h] = dot(value_ref[h, :, 0:rows], expo)
            top_ref[h, 0:1] = top
            top_ref[h, 1:2] = jnp.full((1, nodes), w.astype(jnp.float32))

    def together(i, carry):
        heads = [plan_ref[0, GROUP * i + k] for k in range(GROUP)]
        windows = [plan_ref[1, GROUP * i + k] for k in range(GROUP)]
        widest = windows[0]

        @pl.when(widest <= NEAR)
        def _():
            attend(heads, windows, nodes + NEAR)

        @pl.when(widest > NEAR)
        def _():
            attend(heads, windows, 2 * nodes)

        return carry

    lax.fori_loop(0, HEADS // GROUP, together, 0)


def gaps(device, start, rows, nodes):
    total = lax.axis_size("band") * lax.axis_size("inner")
    there = lax.axis_index("band") * lax.axis_size("inner") + lax.axis_index("inner") + device
    lag = lax.broadcasted_iota(jnp.int32, (rows, nodes), 0) - lax.broadcasted_iota(jnp.int32, (rows, nodes), 1)
    gap = jnp.where((there >= 0) & (there < total), jnp.abs(lag + (device * nodes + start)), 1 << 20)
    return gap.astype(jnp.float32)


def extend(heads, keys, values, gap_ref, query_ref, sums_ref, top_ref, scale):
    scores = [dot(k, query_ref[h]) for h, k in zip(heads, keys)]
    scores = [jnp.where(gap_ref[...] <= top_ref[h, 1:2, :], x, -1e30) for h, x in zip(heads, scores)]
    olds = [top_ref[h, 0:1, :] for h in heads]
    tops = [jnp.maximum(old, jnp.max(x, axis=0, keepdims=True)) for old, x in zip(olds, scores)]
    expos = [jnp.exp2((x - top) * scale).astype(jnp.bfloat16) for x, top in zip(scores, tops)]
    for h, v, old, top, expo in zip(heads, values, olds, tops, expos):
        yield h, sums_ref[h] * jnp.exp2((old - top) * scale) + dot(v, expo), top


def outer_kernel(
    by_pair, block_ref, wk_ref, wv_ref, plan_in, query_ref, sums_ref, top_ref,
    sums_out, top_out,
    key_ref, value_ref, gap_ref, plan_ref, sem,
):
    fetch = pltpu.make_async_copy(plan_in, plan_ref, sem)
    fetch.start()
    nodes, width = block_ref.shape
    head_dim = width // HEADS
    per_group = LANES // head_dim
    far = 2 - 4 * lax.rem(lax.axis_index("inner") // 2, 2)
    scale = head_dim ** (-0.5) / math.log(2.0)
    value_ref[:, head_dim:, :] = jnp.ones_like(value_ref[:, head_dim:, :])
    project_keys(block_ref[...], wk_ref, wv_ref, key_ref, value_ref, 0)
    gap_ref[...] = gaps(far if by_pair else -far, 0, nodes, nodes)
    fetch.wait()

    def wide(n):
        return plan_ref[1, n] > nodes

    def reach(first, last):
        heads = [plan_ref[0, n] for n in range(first, last)]
        keys, values = [key_ref[h // per_group] for h in heads], [value_ref[h] for h in heads]
        for h, sums, top in extend(
            heads, keys, values, gap_ref, query_ref, sums_ref, top_ref, scale
        ):
            sums_out[h] = sums
            top_out[h, 0:1] = top
            top_out[h, 1:2] = top_ref[h, 1:2]

    def leave(first, last):
        for n in range(first, last):
            h = plan_ref[0, n]
            sums_out[h] = sums_ref[h]
            top_out[h, 0:2] = top_ref[h, 0:2]

    @pl.when(wide(GROUP))
    def _():
        reach(0, 2 * GROUP)

    @pl.when(jnp.logical_not(wide(GROUP)))
    def _():
        reach(0, GROUP)
        leave(GROUP, 2 * GROUP)

    for first in range(2 * GROUP, HEADS, GROUP):
        pl.when(wide(first))(functools.partial(reach, first, first + GROUP))
        pl.when(jnp.logical_not(wide(first)))(functools.partial(leave, first, first + GROUP))


def far_kernel(
    first_ref, second_ref, wk_ref, wv_ref, query_ref, sums_ref, top_ref,
    state_ref, w_out_ref, gain_ref, up_ref, down_ref,
    out_ref,
    key_ref, value_ref, gap_ref, attended_ref,
):
    nodes, width = first_ref.shape
    head_dim = width // HEADS
    per_group = LANES // head_dim
    inner = lax.axis_index("inner")
    odd = lax.rem(inner, 2)
    scale = head_dim ** (-0.5) / math.log(2.0)
    value_ref[:, head_dim:, :] = jnp.ones_like(value_ref[:, head_dim:, :])
    by_even = odd == lax.rem(inner // 2 + 1, 2)
    project_keys(jnp.where(by_even, first_ref[...], second_ref[...]), wk_ref, wv_ref, key_ref, value_ref, 0)
    gap_ref[...] = gaps(2 * odd - 1, 0, nodes, nodes)
    heads = range(HEADS)
    keys, values = [key_ref[h // per_group] for h in heads], [value_ref[h] for h in heads]
    for h, sums, _ in extend(
        heads, keys, values, gap_ref, query_ref, sums_ref, top_ref, scale
    ):
        attended_ref[h] = (sums[0:head_dim] / sums[head_dim : head_dim + 1]).astype(jnp.bfloat16)

    attended = attended_ref[...].reshape(width, nodes)
    mixed = lax.dot_general(
        attended, w_out_ref[...], (((0,), (0,)), ((), ())), preferred_element_type=jnp.float32
    )
    total = state_ref[...] + mixed
    normed = layer_norm(total, gain_ref[...]).astype(jnp.bfloat16)
    hidden = silu(dot(normed, up_ref[...])).astype(jnp.bfloat16)
    total = total + dot(hidden, down_ref[...])
    out_ref[...] = total.astype(jnp.bfloat16)


def cost(flops, size):
    return pl.CostEstimate(flops=flops, bytes_accessed=size, transcendentals=0)


def local(
    grid_rows,
    mesh_rows,
    edge_source,
    edge_target,
    edge_count,
    w_message,
    w_merge,
    gain_attn,
    w_qkv,
    window,
    w_out,
    gain_mlp,
    w_up,
    w_down,
):
    bands = lax.axis_size("band")
    inners = lax.axis_size("inner")
    devices = bands * inners
    grid_dev = grid_rows.shape[0]
    nodes, width = mesh_rows.shape
    cap = edge_source.shape[-1]
    head_dim = width // HEADS
    pairs = inners // 2
    half = width // 2
    f32, bf16, i32 = jnp.float32, jnp.bfloat16, jnp.int32
    edges = (edge_source, edge_target, jnp.transpose(edge_count, (0, 2, 1, 3)))

    def rows_of(*blocks):
        return jax.ShapeDtypeStruct((sum(n * cap + TILE for n in blocks), half), bf16)

    outgoing = [rows_of(pairs)] * 4 + [rows_of(3)] * (2 * pairs - 2) + [rows_of(pairs, 3)] * 2
    even, even_other, odd, odd_other, *cross, here, here_other = pl.pallas_call(
        functools.partial(message_kernel, pairs),
        out_shape=outgoing,
        in_specs=[ANY] * 5,
        out_specs=[ANY] * len(outgoing),
        scratch_shapes=[pltpu.VMEM(a.shape, bf16) for a in outgoing]
        + [
            pltpu.VMEM(edges[0].shape, i32),
            pltpu.VMEM(edges[1].shape, i32),
            pltpu.SMEM(edges[2].shape, i32),
            pltpu.VMEM(grid_rows.shape, bf16),
            pltpu.VMEM(w_message.shape, bf16),
            pltpu.VMEM((grid_dev, width), bf16),
            pltpu.VMEM((3 * inners * cap, grid_dev), bf16),
            pltpu.SemaphoreType.DMA((GRID_PARTS + 1,)),
            pltpu.SemaphoreType.DMA((3,)),
            pltpu.SemaphoreType.DMA((len(outgoing),)),
        ],
        compiler_params=params(MOST),
        cost_estimate=cost(2 * grid_dev * width * (width + 3 * inners * cap), 4 << 20),
        name="messages",
    )(grid_rows, w_message, *edges)
    beside = [(g, g ^ 1) for g in range(devices)]

    def bands_trade(odd_pairs, k=0):
        route = []
        for g in range(devices):
            b = g // inners
            t = (b - odd_pairs ^ 1) + odd_pairs
            route.append((g, t * inners + (g % inners ^ k) if 0 <= t < bands else g ^ 1))
        return route

    def chip_trade(p, k=0):
        return [(g, g ^ (2 * p + k)) for g in range(devices)]

    here_other = lax.ppermute(here_other, NODES, beside)
    cross[0::2] = [lax.ppermute(c, NODES, chip_trade(p + 1)) for p, c in enumerate(cross[0::2])]
    even = lax.ppermute(even, NODES, bands_trade(0))
    odd = lax.ppermute(odd, NODES, bands_trade(1))
    here_other, even_other, odd_other, *cross[1::2] = lax.optimization_barrier(
        (here_other, even_other, odd_other, *cross[1::2])
    )
    cross[1::2] = [lax.ppermute(c, NODES, chip_trade(p + 1, 1)) for p, c in enumerate(cross[1::2])]
    even_other = lax.ppermute(even_other, NODES, bands_trade(0, 1))
    odd_other = lax.ppermute(odd_other, NODES, bands_trade(1, 1))

    w_qkv, window, here = lax.optimization_barrier((w_qkv, window, here))
    head = jnp.arange(HEADS, dtype=i32)
    ahead = (window[None, :] > window[:, None]) | (
        (window[None, :] == window[:, None]) & (head[None, :] < head[:, None])
    )
    rank = jnp.sum(ahead.astype(i32), axis=1)
    sorted_to = rank[None, :] == head[:, None]
    plan = jnp.sum(jnp.where(sorted_to[None], jnp.stack([head, window])[:, None, :], 0), axis=2).astype(i32)
    w_query, w_key, w_value, early_left, early_right = pl.pallas_call(
        functools.partial(early_kernel, pairs),
        out_shape=[jax.ShapeDtypeStruct((width, width), bf16)] * 3
        + [jax.ShapeDtypeStruct((n, nodes, half), f32) for n in (pairs, 3)],
        in_specs=[VMEM] * 3 + [ANY],
        out_specs=[VMEM] * 5,
        compiler_params=params(24),
        cost_estimate=cost(1 << 28, 4 << 20),
        name="early",
    )(w_qkv, here, here_other, plan)
    def sums(arrays, early, kept, name):
        count = early.shape[0]
        return pl.pallas_call(
            functools.partial(sums_kernel, len(arrays), kept),
            out_shape=[jax.ShapeDtypeStruct((nodes, half), f32 if n == kept else bf16) for n in range(count)],
            in_specs=[VMEM] * (len(arrays) + 1),
            out_specs=[VMEM] * count,
            compiler_params=params(24),
            cost_estimate=cost(2 * nodes * half * len(arrays) * count * cap, 2 << 20),
            name=name,
        )(*arrays, early)

    left, *parts = sums([even, even_other, odd, odd_other], early_left, 0, "left")
    parts = [lax.ppermute(part, NODES, chip_trade(p + 1)) for p, part in enumerate(parts)]
    to_even, to_odd, right = sums(cross, early_right, 2, "right")
    from_even = lax.ppermute(to_even, NODES, bands_trade(0))
    from_odd = lax.ppermute(to_odd, NODES, bands_trade(1))

    state, normed = pl.pallas_call(
        merge_kernel,
        out_shape=[
            jax.ShapeDtypeStruct((nodes, width), f32),
            jax.ShapeDtypeStruct((nodes, width), bf16),
        ],
        in_specs=[VMEM] * (pairs + 6),
        out_specs=[VMEM] * 2,
        compiler_params=params(24),
        cost_estimate=cost(2 * nodes * width * width, 2 << 20),
        name="merge",
    )(left, *parts, right, from_even, from_odd, mesh_rows, w_merge, gain_attn.reshape(1, width))

    def chips_trade(odd_pairs):
        route = []
        for g in range(devices):
            t = (g // 2 - odd_pairs ^ 1) + odd_pairs
            route.append((g, 2 * t + g % 2 if 0 <= 2 * t < devices else g ^ 1))
        return route

    side = lax.ppermute(normed, NODES, beside)
    even = lax.ppermute(normed, NODES, chips_trade(0))
    side, normed = lax.optimization_barrier((side, normed))
    odd = lax.ppermute(normed, NODES, chips_trade(1))

    extra = head_dim + 16
    query, near, top = pl.pallas_call(
        near_kernel,
        out_shape=[
            jax.ShapeDtypeStruct((HEADS, LANES, nodes), bf16),
            jax.ShapeDtypeStruct((HEADS, extra, nodes), f32),
            jax.ShapeDtypeStruct((HEADS, 8, nodes), f32),
        ],
        in_specs=[VMEM] * 5 + [SMEM],
        out_specs=[VMEM] * 3,
        scratch_shapes=[
            pltpu.VMEM((width // LANES, 2 * nodes, LANES), bf16),
            pltpu.VMEM((HEADS, extra, 2 * nodes), bf16),
            pltpu.VMEM((2 * nodes, nodes), i32),
        ],
        compiler_params=params(32),
        cost_estimate=cost(8 << 30, 4 << 20),
        name="near",
    )(normed, side, w_query, w_key, w_value, plan)

    def outer(by_pair, block, near, top):
        return pl.pallas_call(
            functools.partial(outer_kernel, by_pair),
            out_shape=[
                jax.ShapeDtypeStruct((HEADS, extra, nodes), f32),
                jax.ShapeDtypeStruct((HEADS, 8, nodes), f32),
            ],
            in_specs=[VMEM] * 3 + [ANY] + [VMEM] * 3,
            out_specs=[VMEM] * 2,
            scratch_shapes=[
                pltpu.VMEM((width // LANES, nodes, LANES), bf16),
                pltpu.VMEM((HEADS, extra, nodes), bf16),
                pltpu.VMEM((nodes, nodes), f32),
                pltpu.SMEM((2, HEADS), i32),
                pltpu.SemaphoreType.DMA(()),
            ],
            compiler_params=params(24),
            cost_estimate=cost(8 * nodes * width * width, 3 << 20),
            name="pair" if by_pair else "other",
        )(block, w_key, w_value, plan, query, near, top)

    odd, near, top = lax.optimization_barrier((odd, near, top))
    second = lax.ppermute(odd, NODES, beside)
    near, top = outer(False, odd, near, top)
    even, second, near, top = lax.optimization_barrier((even, second, near, top))
    first = lax.ppermute(even, NODES, beside)
    near, top = outer(True, even, near, top)

    return pl.pallas_call(
        far_kernel,
        out_shape=jax.ShapeDtypeStruct((nodes, width), bf16),
        in_specs=[VMEM] * 12,
        out_specs=VMEM,
        scratch_shapes=[
            pltpu.VMEM((width // LANES, nodes, LANES), bf16),
            pltpu.VMEM((HEADS, extra, nodes), bf16),
            pltpu.VMEM((nodes, nodes), f32),
            pltpu.VMEM((HEADS, head_dim, nodes), bf16),
        ],
        compiler_params=params(40),
        cost_estimate=cost(8 << 30, 8 << 20),
        name="far",
    )(
        first, second, w_key, w_value,
        query, near, top, state, w_out, gain_mlp.reshape(1, width), w_up, w_down,
    )


def solution(mesh):
    placed = (
        P(("groups", "band", "inner"), None),
        P(("groups", "band", "inner"), None),
        P(("groups", "band"), "inner", None, None, None),
        P(("groups", "band"), "inner", None, None, None),
        P(("groups", "band"), "inner", None, None),
        P(),
        P(),
        P(),
        P(),
        P("groups"),
        P(),
        P(),
        P(),
        P(),
    )
    return jax.shard_map(
        local,
        mesh=mesh,
        in_specs=placed,
        out_specs=P(("groups", "band", "inner"), None),
        check_vma=False,
    )
```

```python
import functools
import math

import jax
import jax.numpy as jnp
from jax import lax
from jax.experimental import pallas as pl
from jax.experimental.pallas import tpu as pltpu
from jax.sharding import PartitionSpec as P

HEADS = 16
WMAX = 512
LANES = 128
NEAR = 128
TILE = 16
CAP = 128
GRID_PARTS = 1
MOST = 56
GROUP = 4

norm_eps = 1e-05
NODES = ("band", "inner")
VMEM = pl.BlockSpec(memory_space=pltpu.VMEM)
SMEM = pl.BlockSpec(memory_space=pltpu.SMEM)
ANY = pl.BlockSpec(memory_space=pl.ANY)


def params(mib):
    return pltpu.CompilerParams(vmem_limit_bytes=mib * 1024 * 1024)


def dot(a, b):
    return jnp.dot(a, b, preferred_element_type=jnp.float32)


def dot_t(a, b):
    return lax.dot_general(a, b, (((1,), (1,)), ((), ())), preferred_element_type=jnp.float32)


def silu(values):
    half = 0.5 * values
    return half + half * jnp.tanh(half)


def layer_norm(values, gain):
    center = values - jnp.mean(values, axis=-1, keepdims=True)
    spread = jnp.mean(center * center, axis=-1, keepdims=True)
    return center * lax.rsqrt(spread + norm_eps) * gain


def band_offsets():
    ahead = lax.rem(lax.axis_index("band"), 2) * 2
    return 2 - ahead, ahead, 1


def slot_columns(source_ref, blocks):
    sources = jnp.concatenate([source_ref[0, 0, o, pl.ds(j, 1), :] for o, j in blocks], axis=0)
    return jnp.transpose(sources.astype(jnp.float32)).astype(jnp.int32)


def target_tile(target_ref, count_ref, blocks, lanes):
    cap = target_ref.shape[-1]
    slot = lax.broadcasted_iota(jnp.int32, (1, cap), 1)
    targets = [
        jnp.where(slot < count_ref[0, o, 0, j], target_ref[0, 0, o, pl.ds(j, 1), :], -1) for o, j in blocks
    ]
    targets.append(jnp.full((TILE - len(blocks), cap), -1, jnp.int32))
    tile = jnp.concatenate(targets, axis=0).astype(jnp.float32).astype(jnp.bfloat16)
    return jnp.concatenate([tile] * (lanes // cap), axis=1)


def message_kernel(pair_count, grid_ref, w_ref, source_in, target_in, count_in, *refs):
    count = 4 + 2 * pair_count
    out_refs, out_vmems = refs[:count], refs[count : 2 * count]
    source_ref, target_ref, count_ref, grid_vmem, w_vmem, message_ref, pick_ref, in_sems, edge_sems, out_sems = refs[2 * count :]
    rows = grid_ref.shape[0]
    cap = source_ref.shape[-1]
    half = w_ref.shape[1] // 2
    part = rows // GRID_PARTS
    fetches = [pltpu.make_async_copy(w_ref, w_vmem, in_sems.at[GRID_PARTS])]
    for k in range(GRID_PARTS):
        span = pl.ds(k * part, part)
        fetches.append(pltpu.make_async_copy(grid_ref.at[span], grid_vmem.at[span], in_sems.at[k]))
    edges = ((source_in, source_ref), (target_in, target_ref), (count_in, count_ref))
    edge_fetches = [pltpu.make_async_copy(a, b, edge_sems.at[n]) for n, (a, b) in enumerate(edges)]
    for fetch in edge_fetches + fetches:
        fetch.start()
    for fetch in edge_fetches:
        fetch.wait()
    inner = lax.axis_index("inner")
    offsets = band_offsets()
    keys = [(t, p, k) for k in range(2) for t in range(3) for p in range(pair_count)]
    place = {(t, p, k): (offsets[t], inner ^ (2 * p + k)) for t, p, k in keys}
    by_slot = slot_columns(source_ref, [place[key] for key in keys])
    left, right = slice(0, half), slice(half, 2 * half)
    runs = [[([(t, p, k) for p in range(pair_count)], left)] for t in range(2) for k in range(2)]
    runs += [[([(t, p, k) for t in range(3)], right)] for p in range(1, pair_count) for k in range(2)]
    runs += [
        [([(2, p, k) for p in range(pair_count)], left), ([(t, 0, k) for t in range(3)], right)] for k in range(2)
    ]
    for out_vmem, parts in zip(out_vmems, runs):
        start = 0
        for chosen, _ in parts:
            start += len(chosen) * cap
            out_vmem[start : start + TILE, :] = target_tile(target_ref, count_ref, [place[key] for key in chosen], half)
            start += TILE
    row = lax.broadcasted_iota(jnp.int32, (cap, rows), 1)
    for m in range(len(keys)):
        pick_ref[m * cap : (m + 1) * cap, :] = jnp.where(row == by_slot[:, m : m + 1], 1.0, 0.0).astype(jnp.bfloat16)
    fetches[0].wait()
    for k in range(GRID_PARTS):
        span = pl.ds(k * part, part)
        fetches[k + 1].wait()
        message_ref[span] = silu(dot(grid_vmem[span], w_vmem[...])).astype(jnp.bfloat16)
    sends = []
    taken = dot(pick_ref[...], message_ref[...]).astype(jnp.bfloat16)
    for k in range(2):
        for n in reversed(range(count)):
            start = 0
            if runs[n][0][0][0][2] != k:
                continue
            for chosen, lanes in runs[n]:
                for key in chosen:
                    m = keys.index(key)
                    out_vmems[n][start : start + cap, :] = taken[m * cap : (m + 1) * cap, lanes]
                    start += cap
                start += TILE
            send = pltpu.make_async_copy(out_vmems[n], out_refs[n], out_sems.at[n])
            send.start()
            sends.append(send)
    for send in sends:
        send.wait()


def node_sums(arrays, nodes):
    count = arrays[0][2]
    cap = CAP
    node = lax.broadcasted_iota(jnp.int32, (nodes, cap), 0)
    targets = [
        ref[start + count * cap : start + count * cap + TILE, 0:cap].astype(jnp.float32).astype(jnp.int32)
        for ref, start, _ in arrays
    ]
    for n in range(count):
        hits = [jnp.where(node == t[n : n + 1], 1.0, 0.0).astype(jnp.bfloat16) for t in targets]
        rows = [ref[start + n * cap : start + (n + 1) * cap, :] for ref, start, _ in arrays]
        yield n, dot(jnp.concatenate(hits, axis=1), jnp.concatenate(rows, axis=0))


def early_kernel(pair_count, w_ref, own_ref, other_ref, plan_ref, query_ref, key_ref, value_ref, left_ref, right_ref):
    width = w_ref.shape[0]
    head_dim = width // HEADS
    span = 3 * LANES
    def pick(c, along):
        shape = (LANES, span) if along else (span, LANES)
        to = lax.broadcasted_iota(jnp.int32, shape, 1 - along)
        column = lax.broadcasted_iota(jnp.int32, shape, along)
        wanted = to // head_dim * (3 * head_dim) + to % head_dim + c * head_dim
        return jnp.where(column == wanted, 1.0, 0.0).astype(jnp.bfloat16)

    for g in range(width // LANES):
        columns = w_ref[:, g * span : (g + 1) * span]
        part = slice(g * LANES, (g + 1) * LANES)
        query_ref[part, :] = dot_t(pick(0, 1), columns).astype(jnp.bfloat16)
        key_ref[:, part] = dot(columns, pick(1, 0)).astype(jnp.bfloat16)
        value_ref[part, :] = dot_t(pick(2, 1), columns).astype(jnp.bfloat16)
    start = 0
    for sum_ref in (left_ref, right_ref):
        count, nodes, _ = sum_ref.shape
        for n, total in node_sums([(own_ref, start, count), (other_ref, start, count)], nodes):
            sum_ref[n] = total
        start += count * CAP + TILE


def sums_kernel(array_count, kept, *refs):
    row_refs, early_ref, out_refs = refs[:array_count], refs[array_count], refs[array_count + 1 :]
    count, nodes, _ = early_ref.shape
    for n, total in node_sums([(r, 0, count) for r in row_refs], nodes):
        total = total + early_ref[n]
        out_refs[n][...] = total if n == kept else total.astype(jnp.bfloat16)


def merge_kernel(*refs):
    *part_refs, right_ref, even_ref, odd_ref, mesh_ref, w_ref, gain_ref, state_ref, normed_ref = refs
    left = functools.reduce(jnp.add, [r[...].astype(jnp.float32) for r in part_refs])
    right = right_ref[...] + even_ref[...].astype(jnp.float32) + odd_ref[...].astype(jnp.float32)
    total = jnp.concatenate([left, right], axis=1).astype(jnp.bfloat16)
    state = mesh_ref[...].astype(jnp.float32) + dot(total, w_ref[...])
    state_ref[...] = state
    normed_ref[...] = layer_norm(state, gain_ref[...]).astype(jnp.bfloat16)


def project_keys(rows, wk_ref, wv_ref, key_ref, value_ref, start):
    count = rows.shape[0]
    groups = key_ref.shape[0]
    heads = value_ref.shape[0]
    keys = dot(rows, wk_ref[...]).astype(jnp.bfloat16)
    for g in range(groups):
        key_ref[g, start : start + count, :] = keys[:, g * LANES : (g + 1) * LANES]
    values = dot_t(wv_ref[...], rows).astype(jnp.bfloat16)
    value_ref[:, 0 : values.shape[0] // heads, start : start + count] = values.reshape(
        heads, -1, count
    )


def near_kernel(
    own_ref, side_ref, wq_ref, wk_ref, wv_ref, plan_ref,
    query_ref, sums_ref, top_ref,
    key_ref, value_ref, gap_ref,
):
    nodes, width = own_ref.shape
    head_dim = width // HEADS
    per_group = LANES // head_dim
    odd = lax.rem(lax.axis_index("inner"), 2)
    side = 1 - 2 * odd
    first = odd * (nodes - NEAR)
    second = (1 - odd) * NEAR
    scale = head_dim ** (-0.5) / math.log(2.0)

    queries = dot_t(wq_ref[...], own_ref[...]).astype(jnp.bfloat16)
    part = lax.broadcasted_iota(jnp.int32, (LANES, nodes), 0) // head_dim
    for h in range(HEADS):
        g = h // per_group
        lanes = queries[g * LANES : (g + 1) * LANES]
        query_ref[h] = jnp.where(part == h % per_group, lanes, jnp.zeros_like(lanes))
    value_ref[:, head_dim:, :] = jnp.ones_like(value_ref[:, head_dim:, :])
    project_keys(own_ref[...], wk_ref, wv_ref, key_ref, value_ref, 0)
    project_keys(side_ref[pl.ds(pl.multiple_of(first, NEAR), NEAR), :], wk_ref, wv_ref, key_ref, value_ref, nodes)
    project_keys(
        side_ref[pl.ds(pl.multiple_of(second, NEAR), NEAR), :], wk_ref, wv_ref, key_ref, value_ref, nodes + NEAR
    )
    lag = lax.broadcasted_iota(jnp.int32, (nodes, nodes), 0) - lax.broadcasted_iota(
        jnp.int32, (nodes, nodes), 1
    )
    gap_ref[0:nodes] = jnp.abs(lag)
    gap_ref[nodes : nodes + NEAR] = jnp.abs(lag[0:NEAR] + (side * nodes + first))
    gap_ref[nodes + NEAR : 2 * nodes] = jnp.abs(lag[0:NEAR] + (side * nodes + second))

    def attend(heads, windows, rows):
        scores = [dot(key_ref[h // per_group, 0:rows, :], query_ref[h]) for h in heads]
        scores = [
            jnp.where(gap_ref[0:rows] <= w, x, -1e30) for w, x in zip(windows, scores)
        ]
        tops = [jnp.max(x, axis=0, keepdims=True) for x in scores]
        expos = [jnp.exp2((x - top) * scale).astype(jnp.bfloat16) for x, top in zip(scores, tops)]
        for h, w, top, expo in zip(heads, windows, tops, expos):
            sums_ref[h] = dot(value_ref[h, :, 0:rows], expo)
            top_ref[h, 0:1] = top
            top_ref[h, 1:2] = jnp.full((1, nodes), w.astype(jnp.float32))

    def together(i, carry):
        heads = [plan_ref[0, GROUP * i + k] for k in range(GROUP)]
        windows = [plan_ref[1, GROUP * i + k] for k in range(GROUP)]
        widest = windows[0]

        @pl.when(widest <= NEAR)
        def _():
            attend(heads, windows, nodes + NEAR)

        @pl.when(widest > NEAR)
        def _():
            attend(heads, windows, 2 * nodes)

        return carry

    lax.fori_loop(0, HEADS // GROUP, together, 0)


def gaps(device, start, rows, nodes):
    total = lax.axis_size("band") * lax.axis_size("inner")
    there = lax.axis_index("band") * lax.axis_size("inner") + lax.axis_index("inner") + device
    lag = lax.broadcasted_iota(jnp.int32, (rows, nodes), 0) - lax.broadcasted_iota(jnp.int32, (rows, nodes), 1)
    gap = jnp.where((there >= 0) & (there < total), jnp.abs(lag + (device * nodes + start)), 1 << 20)
    return gap.astype(jnp.float32)


def extend(heads, keys, values, gap_ref, query_ref, sums_ref, top_ref, scale):
    scores = [dot(k, query_ref[h]) for h, k in zip(heads, keys)]
    scores = [jnp.where(gap_ref[...] <= top_ref[h, 1:2, :], x, -1e30) for h, x in zip(heads, scores)]
    olds = [top_ref[h, 0:1, :] for h in heads]
    tops = [jnp.maximum(old, jnp.max(x, axis=0, keepdims=True)) for old, x in zip(olds, scores)]
    expos = [jnp.exp2((x - top) * scale).astype(jnp.bfloat16) for x, top in zip(scores, tops)]
    for h, v, old, top, expo in zip(heads, values, olds, tops, expos):
        yield h, sums_ref[h] * jnp.exp2((old - top) * scale) + dot(v, expo), top


def outer_kernel(
    by_pair, block_ref, wk_ref, wv_ref, plan_in, query_ref, sums_ref, top_ref,
    sums_out, top_out,
    key_ref, value_ref, gap_ref, plan_ref, sem,
):
    fetch = pltpu.make_async_copy(plan_in, plan_ref, sem)
    fetch.start()
    nodes, width = block_ref.shape
    head_dim = width // HEADS
    per_group = LANES // head_dim
    far = 2 - 4 * lax.rem(lax.axis_index("inner") // 2, 2)
    scale = head_dim ** (-0.5) / math.log(2.0)
    value_ref[:, head_dim:, :] = jnp.ones_like(value_ref[:, head_dim:, :])
    project_keys(block_ref[...], wk_ref, wv_ref, key_ref, value_ref, 0)
    gap_ref[...] = gaps(far if by_pair else -far, 0, nodes, nodes)
    fetch.wait()

    def wide(n):
        return plan_ref[1, n] > nodes

    def reach(first, last):
        heads = [plan_ref[0, n] for n in range(first, last)]
        keys, values = [key_ref[h // per_group] for h in heads], [value_ref[h] for h in heads]
        for h, sums, top in extend(
            heads, keys, values, gap_ref, query_ref, sums_ref, top_ref, scale
        ):
            sums_out[h] = sums
            top_out[h, 0:1] = top
            top_out[h, 1:2] = top_ref[h, 1:2]

    def leave(first, last):
        for n in range(first, last):
            h = plan_ref[0, n]
            sums_out[h] = sums_ref[h]
            top_out[h, 0:2] = top_ref[h, 0:2]

    @pl.when(wide(GROUP))
    def _():
        reach(0, 2 * GROUP)

    @pl.when(jnp.logical_not(wide(GROUP)))
    def _():
        reach(0, GROUP)
        leave(GROUP, 2 * GROUP)

    for first in range(2 * GROUP, HEADS, GROUP):
        pl.when(wide(first))(functools.partial(reach, first, first + GROUP))
        pl.when(jnp.logical_not(wide(first)))(functools.partial(leave, first, first + GROUP))


def far_kernel(
    first_ref, second_ref, wk_ref, wv_ref, query_ref, sums_ref, top_ref,
    state_ref, w_out_ref, gain_ref, up_ref, down_ref,
    out_ref,
    key_ref, value_ref, gap_ref, attended_ref,
):
    nodes, width = first_ref.shape
    head_dim = width // HEADS
    per_group = LANES // head_dim
    inner = lax.axis_index("inner")
    odd = lax.rem(inner, 2)
    scale = head_dim ** (-0.5) / math.log(2.0)
    value_ref[:, head_dim:, :] = jnp.ones_like(value_ref[:, head_dim:, :])
    by_even = odd == lax.rem(inner // 2 + 1, 2)
    project_keys(jnp.where(by_even, first_ref[...], second_ref[...]), wk_ref, wv_ref, key_ref, value_ref, 0)
    gap_ref[...] = gaps(2 * odd - 1, 0, nodes, nodes)
    heads = range(HEADS)
    keys, values = [key_ref[h // per_group] for h in heads], [value_ref[h] for h in heads]
    for h, sums, _ in extend(
        heads, keys, values, gap_ref, query_ref, sums_ref, top_ref, scale
    ):
        attended_ref[h] = (sums[0:head_dim] / sums[head_dim : head_dim + 1]).astype(jnp.bfloat16)

    attended = attended_ref[...].reshape(width, nodes)
    mixed = lax.dot_general(
        attended, w_out_ref[...], (((0,), (0,)), ((), ())), preferred_element_type=jnp.float32
    )
    total = state_ref[...] + mixed
    normed = layer_norm(total, gain_ref[...]).astype(jnp.bfloat16)
    hidden = silu(dot(normed, up_ref[...])).astype(jnp.bfloat16)
    total = total + dot(hidden, down_ref[...])
    out_ref[...] = total.astype(jnp.bfloat16)


def cost(flops, size):
    return pl.CostEstimate(flops=flops, bytes_accessed=size, transcendentals=0)


def local(
    grid_rows,
    mesh_rows,
    edge_source,
    edge_target,
    edge_count,
    w_message,
    w_merge,
    gain_attn,
    w_qkv,
    window,
    w_out,
    gain_mlp,
    w_up,
    w_down,
):
    bands = lax.axis_size("band")
    inners = lax.axis_size("inner")
    devices = bands * inners
    grid_dev = grid_rows.shape[0]
    nodes, width = mesh_rows.shape
    cap = edge_source.shape[-1]
    head_dim = width // HEADS
    pairs = inners // 2
    half = width // 2
    f32, bf16, i32 = jnp.float32, jnp.bfloat16, jnp.int32
    edges = (edge_source, edge_target, jnp.transpose(edge_count, (0, 2, 1, 3)))

    def rows_of(*blocks):
        return jax.ShapeDtypeStruct((sum(n * cap + TILE for n in blocks), half), bf16)

    outgoing = [rows_of(pairs)] * 4 + [rows_of(3)] * (2 * pairs - 2) + [rows_of(pairs, 3)] * 2
    even, even_other, odd, odd_other, *cross, here, here_other = pl.pallas_call(
        functools.partial(message_kernel, pairs),
        out_shape=outgoing,
        in_specs=[ANY] * 5,
        out_specs=[ANY] * len(outgoing),
        scratch_shapes=[pltpu.VMEM(a.shape, bf16) for a in outgoing]
        + [
            pltpu.VMEM(edges[0].shape, i32),
            pltpu.VMEM(edges[1].shape, i32),
            pltpu.SMEM(edges[2].shape, i32),
            pltpu.VMEM(grid_rows.shape, bf16),
            pltpu.VMEM(w_message.shape, bf16),
            pltpu.VMEM((grid_dev, width), bf16),
            pltpu.VMEM((3 * inners * cap, grid_dev), bf16),
            pltpu.SemaphoreType.DMA((GRID_PARTS + 1,)),
            pltpu.SemaphoreType.DMA((3,)),
            pltpu.SemaphoreType.DMA((len(outgoing),)),
        ],
        compiler_params=params(MOST),
        cost_estimate=cost(2 * grid_dev * width * (width + 3 * inners * cap), 4 << 20),
        name="messages",
    )(grid_rows, w_message, *edges)
    beside = [(g, g ^ 1) for g in range(devices)]

    def bands_trade(odd_pairs, k=0):
        route = []
        for g in range(devices):
            b = g // inners
            t = (b - odd_pairs ^ 1) + odd_pairs
            route.append((g, t * inners + (g % inners ^ k) if 0 <= t < bands else g ^ 1))
        return route

    def chip_trade(p, k=0):
        return [(g, g ^ (2 * p + k)) for g in range(devices)]

    here_other = lax.ppermute(here_other, NODES, beside)
    cross[0::2] = [lax.ppermute(c, NODES, chip_trade(p + 1)) for p, c in enumerate(cross[0::2])]
    even = lax.ppermute(even, NODES, bands_trade(0))
    odd = lax.ppermute(odd, NODES, bands_trade(1))
    here_other, even_other, odd_other, *cross[1::2] = lax.optimization_barrier(
        (here_other, even_other, odd_other, *cross[1::2])
    )
    cross[1::2] = [lax.ppermute(c, NODES, chip_trade(p + 1, 1)) for p, c in enumerate(cross[1::2])]
    even_other = lax.ppermute(even_other, NODES, bands_trade(0, 1))
    odd_other = lax.ppermute(odd_other, NODES, bands_trade(1, 1))

    w_qkv, window, here = lax.optimization_barrier((w_qkv, window, here))
    head = jnp.arange(HEADS, dtype=i32)
    ahead = (window[None, :] > window[:, None]) | (
        (window[None, :] == window[:, None]) & (head[None, :] < head[:, None])
    )
    rank = jnp.sum(ahead.astype(i32), axis=1)
    sorted_to = rank[None, :] == head[:, None]
    plan = jnp.sum(jnp.where(sorted_to[None], jnp.stack([head, window])[:, None, :], 0), axis=2).astype(i32)
    w_query, w_key, w_value, early_left, early_right = pl.pallas_call(
        functools.partial(early_kernel, pairs),
        out_shape=[jax.ShapeDtypeStruct((width, width), bf16)] * 3
        + [jax.ShapeDtypeStruct((n, nodes, half), f32) for n in (pairs, 3)],
        in_specs=[VMEM] * 3 + [ANY],
        out_specs=[VMEM] * 5,
        compiler_params=params(24),
        cost_estimate=cost(1 << 28, 4 << 20),
        name="early",
    )(w_qkv, here, here_other, plan)
    def sums(arrays, early, kept, name):
        count = early.shape[0]
        return pl.pallas_call(
            functools.partial(sums_kernel, len(arrays), kept),
            out_shape=[jax.ShapeDtypeStruct((nodes, half), f32 if n == kept else bf16) for n in range(count)],
            in_specs=[VMEM] * (len(arrays) + 1),
            out_specs=[VMEM] * count,
            compiler_params=params(24),
            cost_estimate=cost(2 * nodes * half * len(arrays) * count * cap, 2 << 20),
            name=name,
        )(*arrays, early)

    left, *parts = sums([even, even_other, odd, odd_other], early_left, 0, "left")
    parts = [lax.ppermute(part, NODES, chip_trade(p + 1)) for p, part in enumerate(parts)]
    to_even, to_odd, right = sums(cross, early_right, 2, "right")
    from_even = lax.ppermute(to_even, NODES, bands_trade(0))
    from_odd = lax.ppermute(to_odd, NODES, bands_trade(1))

    state, normed = pl.pallas_call(
        merge_kernel,
        out_shape=[
            jax.ShapeDtypeStruct((nodes, width), f32),
            jax.ShapeDtypeStruct((nodes, width), bf16),
        ],
        in_specs=[VMEM] * (pairs + 6),
        out_specs=[VMEM] * 2,
        compiler_params=params(24),
        cost_estimate=cost(2 * nodes * width * width, 2 << 20),
        name="merge",
    )(left, *parts, right, from_even, from_odd, mesh_rows, w_merge, gain_attn.reshape(1, width))

    def chips_trade(odd_pairs):
        route = []
        for g in range(devices):
            t = (g // 2 - odd_pairs ^ 1) + odd_pairs
            route.append((g, 2 * t + g % 2 if 0 <= 2 * t < devices else g ^ 1))
        return route

    side = lax.ppermute(normed, NODES, beside)
    even = lax.ppermute(normed, NODES, chips_trade(0))
    side, normed = lax.optimization_barrier((side, normed))
    odd = lax.ppermute(normed, NODES, chips_trade(1))

    extra = head_dim + 16
    query, near, top = pl.pallas_call(
        near_kernel,
        out_shape=[
            jax.ShapeDtypeStruct((HEADS, LANES, nodes), bf16),
            jax.ShapeDtypeStruct((HEADS, extra, nodes), f32),
            jax.ShapeDtypeStruct((HEADS, 8, nodes), f32),
        ],
        in_specs=[VMEM] * 5 + [SMEM],
        out_specs=[VMEM] * 3,
        scratch_shapes=[
            pltpu.VMEM((width // LANES, 2 * nodes, LANES), bf16),
            pltpu.VMEM((HEADS, extra, 2 * nodes), bf16),
            pltpu.VMEM((2 * nodes, nodes), i32),
        ],
        compiler_params=params(32),
        cost_estimate=cost(8 << 30, 4 << 20),
        name="near",
    )(normed, side, w_query, w_key, w_value, plan)

    def outer(by_pair, block, near, top):
        return pl.pallas_call(
            functools.partial(outer_kernel, by_pair),
            out_shape=[
                jax.ShapeDtypeStruct((HEADS, extra, nodes), f32),
                jax.ShapeDtypeStruct((HEADS, 8, nodes), f32),
            ],
            in_specs=[VMEM] * 3 + [ANY] + [VMEM] * 3,
            out_specs=[VMEM] * 2,
            scratch_shapes=[
                pltpu.VMEM((width // LANES, nodes, LANES), bf16),
                pltpu.VMEM((HEADS, extra, nodes), bf16),
                pltpu.VMEM((nodes, nodes), f32),
                pltpu.SMEM((2, HEADS), i32),
                pltpu.SemaphoreType.DMA(()),
            ],
            compiler_params=params(24),
            cost_estimate=cost(8 * nodes * width * width, 3 << 20),
            name="pair" if by_pair else "other",
        )(block, w_key, w_value, plan, query, near, top)

    odd, near, top = lax.optimization_barrier((odd, near, top))
    second = lax.ppermute(odd, NODES, beside)
    near, top = outer(False, odd, near, top)
    even, second, near, top = lax.optimization_barrier((even, second, near, top))
    first = lax.ppermute(even, NODES, beside)
    near, top = outer(True, even, near, top)

    return pl.pallas_call(
        far_kernel,
        out_shape=jax.ShapeDtypeStruct((nodes, width), bf16),
        in_specs=[VMEM] * 12,
        out_specs=VMEM,
        scratch_shapes=[
            pltpu.VMEM((width // LANES, nodes, LANES), bf16),
            pltpu.VMEM((HEADS, extra, nodes), bf16),
            pltpu.VMEM((nodes, nodes), f32),
            pltpu.VMEM((HEADS, head_dim, nodes), bf16),
        ],
        compiler_params=params(40),
        cost_estimate=cost(8 << 30, 8 << 20),
        name="far",
    )(
        first, second, w_key, w_value,
        query, near, top, state, w_out, gain_mlp.reshape(1, width), w_up, w_down,
    )


def solution(mesh):
    placed = (
        P(("groups", "band", "inner"), None),
        P(("groups", "band", "inner"), None),
        P(("groups", "band"), "inner", None, None, None),
        P(("groups", "band"), "inner", None, None, None),
        P(("groups", "band"), "inner", None, None),
        P(),
        P(),
        P(),
        P(),
        P("groups"),
        P(),
        P(),
        P(),
        P(),
    )
    return jax.shard_map(
        local,
        mesh=mesh,
        in_specs=placed,
        out_specs=P(("groups", "band", "inner"), None),
        check_vma=False,
    )
```
